32 devices in a mesh: dp: 8 (over z, x), seq: 4 (over y, core).
Axes of the slice: x: 2, y: 2, z: 4, core: 2. Of those that a mesh axis runs over, the one named last changes fastest.
Arguments:
- stream: bfloat16 [8, 3, 512, 1024], P('dp', None, 'seq'), may hold values from -9 to 9
- encoded: bfloat16 [8, 512, 1024], P('dp', 'seq'), may hold values from -6 to 6
- cotangent: bfloat16 [8, 3, 512, 1024], P('dp', None, 'seq'), may hold values from -6 to 6
- lengths: int32 [8], P('dp'), may hold values from 65 to 512, as said below
- bucket_table: int32 [512], replicated, may hold values from 0 to 31, as said below
- w_query: bfloat16 [1024, 1024], replicated, may hold values from -0.1875 to 0.1875
- w_key: bfloat16 [1024, 1024], replicated, may hold values from -0.1875 to 0.1875
- w_value: bfloat16 [1024, 1024], replicated, may hold values from -0.1875 to 0.1875
- w_out: bfloat16 [1024, 1024], replicated, may hold values from -0.75 to 0.75
- c_query: bfloat16 [1024, 1024], replicated, may hold values from -0.1875 to 0.1875
- c_key: bfloat16 [1024, 1024], replicated, may hold values from -0.1875 to 0.1875
- c_value: bfloat16 [1024, 1024], replicated, may hold values from -0.1875 to 0.1875
- c_out: bfloat16 [1024, 1024], replicated, may hold values from -0.75 to 0.75
- w_in: bfloat16 [1024, 4096], replicated, may hold values from -0.1875 to 0.1875
- w_back: bfloat16 [4096, 1024], replicated, may hold values from -0.09375 to 0.09375
- gain_one: float32 [1024], replicated, may hold values from 0.25 to 1.75
- shift_one: float32 [1024], replicated, may hold values from -1.2 to 1.2
- gain_two: float32 [1024], replicated, may hold values from 0.25 to 1.75
- shift_two: float32 [1024], replicated, may hold values from -1.2 to 1.2
- gain_three: float32 [1024], replicated, may hold values from 0.25 to 1.75
- shift_three: float32 [1024], replicated, may hold values from -1.2 to 1.2
- position_bias: float32 [32, 16], replicated, may hold values from -4 to 4
Outputs:
- layer_output: bfloat16 [8, 3, 512, 1024], P('dp', None, 'seq')
- stream_grad: bfloat16 [8, 3, 512, 1024], P('dp', None, 'seq')
- encoded_grad: bfloat16 [8, 512, 1024], P('dp', 'seq')
- w_query_grad: float32 [1024, 1024], P('dp', 'seq')
- w_key_grad: float32 [1024, 1024], P('dp', 'seq')
- w_value_grad: float32 [1024, 1024], P('dp', 'seq')
- w_out_grad: float32 [1024, 1024], P('dp', 'seq')
- c_query_grad: float32 [1024, 1024], P('dp', 'seq')
- c_key_grad: float32 [1024, 1024], P('dp', 'seq')
- c_value_grad: float32 [1024, 1024], P('dp', 'seq')
- c_out_grad: float32 [1024, 1024], P('dp', 'seq')
- w_in_grad: float32 [1024, 4096], P('dp', 'seq')
- w_back_grad: float32 [4096, 1024], P('dp', 'seq')
- gain_one_grad: float32 [1024], replicated
- shift_one_grad: float32 [1024], replicated
- gain_two_grad: float32 [1024], replicated
- shift_two_grad: float32 [1024], replicated
- gain_three_grad: float32 [1024], replicated
- shift_three_grad: float32 [1024], replicated
- position_bias_grad: float32 [32, 16], replicated
- rms: float32 [4], replicated
The draws below stay inside these ranges and needn't reach their ends.
Inputs may be any that keep to these rules, and one draw needn't show every extreme that they name: `lengths`: each length lies in the upper half of one of the buckets 512 / 4, 256 and 512. In each aligned block of 1 row one row, drawn from the seed, is longer than 448; one row of all, drawn from the seed, has length 512. `bucket_table`: entry d is the bucket of distance d; it never falls as d grows, and entry 0 is 0.
All inputs are finite; a program needn't handle non-finite values.
Results may differ from the reference program's by a relative error of at most 0.025.
Values may be sent and summed in bfloat16 or wider, within the bound.
A program may use at most 256 MiB of HBM per device.

```python
import jax
import jax.numpy as jnp
from jax import lax

D = 1024
HEADS = 16
HEAD_DIM = 64
FF = 4096
NBUCKET = 32
LMAX = 512
R_DEV = 1
STREAMS = 3
ROWS = 8


def draw_stream(key, part):
    key = jax.random.fold_in(key, 11)
    placing = (jnp.arange(ROWS, dtype=jnp.float32) + 0.5) / ROWS
    row_scale = 0.6 + 0.9 * placing
    samples = jnp.clip(jax.random.normal(key, (ROWS, STREAMS, LMAX, D), jnp.float32), -6.0, 6.0)
    return (samples * row_scale[:, None, None, None]).astype(jnp.bfloat16)


def draw_lengths(key, part):
    key = jax.random.fold_in(key, 23)
    pick_key, span_key, row_key, long_key, top_key = jax.random.split(key, 5)
    bucket_pick = jax.random.randint(pick_key, (ROWS,), 0, 4)
    ceiling = jnp.where(bucket_pick == 0, LMAX // 4, jnp.where(bucket_pick == 1, LMAX // 2, LMAX))
    floor_len = ceiling // 2 + 1
    offsets = jax.random.randint(span_key, (ROWS,), 0, 1 << 20)
    drawn = floor_len + offsets % (ceiling - floor_len + 1)
    chosen = jax.random.randint(row_key, (ROWS // R_DEV,), 0, R_DEV)
    forced = jnp.arange(ROWS) % R_DEV == jnp.repeat(chosen, R_DEV)
    long_len = LMAX - LMAX // 8 + 1 + jax.random.randint(long_key, (ROWS,), 0, LMAX // 8)
    lengths = jnp.where(forced, long_len, drawn)
    top_row = jax.random.randint(top_key, (), 0, ROWS)
    lengths = jnp.where(jnp.arange(ROWS) == top_row, LMAX, lengths)
    return lengths.astype(jnp.int32)


def draw_bucket_table(key, part):
    key = jax.random.fold_in(key, 37)
    breaks = jax.random.permutation(key, LMAX - 1)[:NBUCKET - 1] + 1
    distances = jnp.arange(LMAX)
    return jnp.sum((distances[:, None] >= breaks[None, :]).astype(jnp.int32), axis=1).astype(jnp.int32)


def block_scale(stream_key, shape, shards, least, largest):
    gain = 1.0
    for position, parts in shards:
        heights = jax.random.uniform(jax.random.fold_in(jax.random.fold_in(stream_key, 6), position), (parts,), jnp.float32, least / len(shards), largest / len(shards))
        gain = gain * jnp.repeat(jnp.exp(heights), shape[position] // parts).reshape((-1,) + (1,) * (len(shape) - 1 - position))
    return gain


def scatter_about(stream_key, extent, deviation, bound, cuts=(), held_as=jnp.bfloat16):
    entries = jax.random.normal(stream_key, extent, jnp.float32) * deviation
    if len(cuts) > 0:
        entries = block_scale(stream_key, extent, cuts, -0.22, 0.18) * entries
    return jnp.clip(entries, min=-bound, max=bound).astype(held_as)


def setup_inputs(seed: int = 0) -> dict:
    keys = jax.random.split(jax.random.key(seed), 23)
    stream = draw_stream(jax.random.fold_in(keys[22], 71), 0)
    encoded = scatter_about(keys[1], (ROWS, LMAX, D), 1.0, 6.0, ((0, 8), (1, 4)))
    cotangent = scatter_about(keys[2], (ROWS, STREAMS, LMAX, D), 1.0, 6.0, ((0, 8), (2, 4)))
    lengths = draw_lengths(jax.random.fold_in(keys[22], 71), 0)
    bucket_table = draw_bucket_table(jax.random.fold_in(keys[22], 71), 0)
    w_query = scatter_about(keys[5], (D, D), D ** -0.5, 0.1875)
    w_key = scatter_about(keys[6], (D, D), D ** -0.5, 0.1875)
    w_value = scatter_about(keys[7], (D, D), D ** -0.5, 0.1875)
    w_out = scatter_about(keys[8], (D, D), (D // 16) ** -0.5, 0.75)
    c_query = scatter_about(keys[9], (D, D), D ** -0.5, 0.1875)
    c_key = scatter_about(keys[10], (D, D), D ** -0.5, 0.1875)
    c_value = scatter_about(keys[11], (D, D), D ** -0.5, 0.1875)
    c_out = scatter_about(keys[12], (D, D), (D // 16) ** -0.5, 0.75)
    w_in = scatter_about(keys[13], (D, FF), D ** -0.5, 0.1875)
    w_back = scatter_about(keys[14], (FF, D), FF ** -0.5, 0.09375)
    gain_one = jnp.clip(1.0 + 0.15 * jax.random.normal(keys[15], (D,), jnp.float32), 0.25, 1.75)
    shift_one = scatter_about(keys[16], (D,), 0.3, 1.2, (), jnp.float32)
    gain_two = jnp.clip(1.0 + 0.15 * jax.random.normal(keys[17], (D,), jnp.float32), 0.25, 1.75)
    shift_two = scatter_about(keys[18], (D,), 0.3, 1.2, (), jnp.float32)
    gain_three = jnp.clip(1.0 + 0.15 * jax.random.normal(keys[19], (D,), jnp.float32), 0.25, 1.75)
    shift_three = scatter_about(keys[20], (D,), 0.3, 1.2, (), jnp.float32)
    position_bias = scatter_about(keys[21], (NBUCKET, HEADS), 1.0, 4.0, (), jnp.float32)
    return {"stream": stream, "encoded": encoded, "cotangent": cotangent, "lengths": lengths, "bucket_table": bucket_table, "w_query": w_query, "w_key": w_key, "w_value": w_value, "w_out": w_out, "c_query": c_query, "c_key": c_key, "c_value": c_value, "c_out": c_out, "w_in": w_in, "w_back": w_back, "gain_one": gain_one, "shift_one": shift_one, "gain_two": gain_two, "shift_two": shift_two, "gain_three": gain_three, "shift_three": shift_three, "position_bias": position_bias}


@jax.custom_vjp
def low(v):
    return lax.optimization_barrier(v.astype(jnp.bfloat16)).astype(jnp.float32)

@jax.custom_vjp
def low_back(v):
    return v

def low_keep(v):
    return (low(v), None)

def low_pass(kept, grad):
    return (grad,)

def back_keep(v):
    return (v, None)

def back_low(kept, grad):
    return (low(grad),)
low.defvjp(low_keep, low_pass)
low_back.defvjp(back_keep, back_low)
epsilon = 1e-05
masked_score = -1e+30

def layer_norm(values, norm_gain, norm_shift):
    centre = lax.optimization_barrier(jnp.mean(values, axis=-1, keepdims=True))
    centred = values - centre
    spread = lax.optimization_barrier(jnp.mean(centred * centred, axis=-1, keepdims=True))
    return centred * lax.rsqrt(spread + epsilon) * norm_gain + norm_shift

def matmul(left_rows, right_rows):
    return jnp.dot(left_rows, right_rows, precision=lax.Precision.HIGHEST)

def split_heads(values):
    return values.reshape(values.shape[:-1] + (HEADS, HEAD_DIM))

def merge_heads(values):
    return values.reshape(values.shape[:-2] + (HEADS * HEAD_DIM,))

def sequence_forward(weights, inputs, source, length, bucket_table):
    w_query, w_key, w_value, w_out, c_query, c_key, c_value, c_out, w_in, w_back, gain_one, shift_one, gain_two, shift_two, gain_three, shift_three, position_bias = weights
    positions = jnp.arange(LMAX)
    valid_pos = positions < length
    pos_mask = valid_pos.astype(jnp.float32)[None, :, None]
    distance = positions[:, None] - positions[None, :]
    buckets = bucket_table[jnp.clip(distance, 0, LMAX - 1)]
    rel_bias = jnp.transpose(position_bias[buckets], (2, 0, 1))
    own_bias = position_bias[bucket_table[0]]
    queries = split_heads(low_back(low(matmul(inputs, w_query))))
    keys_all = split_heads(low_back(low(matmul(inputs, w_key))))
    values_all = split_heads(low_back(low(matmul(inputs, w_value))))
    main_keys = keys_all[0]
    main_values = values_all[0]

    def self_block(block_item):
        query_one, key_one, value_one, stream_id = block_item
        scores = jnp.einsum('thd,jhd->htj', query_one, main_keys, precision=lax.Precision.HIGHEST) * 0.125 + rel_bias
        scores = low_back(scores)
        allowed = jnp.where(stream_id == 0, distance >= 0, distance > 0) & valid_pos[None, :]
        scores = jnp.where(allowed[None], scores, masked_score)
        own_score = jnp.einsum('thd,thd->ht', query_one, key_one, precision=lax.Precision.HIGHEST) * 0.125 + own_bias[:, None]
        own_score = low_back(own_score)
        own_score = jnp.where(stream_id == 0, masked_score, own_score)
        row_top = jnp.maximum(lax.optimization_barrier(jnp.max(scores, axis=-1)), own_score)
        expo_main = jnp.exp(scores - row_top[..., None])
        expo_own = jnp.exp(own_score - row_top)
        row_total = lax.optimization_barrier(jnp.sum(expo_main, axis=-1)) + expo_own
        probs_main = low(expo_main / row_total[..., None])
        probs_own = expo_own / row_total
        context = jnp.einsum('htj,jhd->thd', probs_main, main_values, precision=lax.Precision.HIGHEST)
        return context + jnp.transpose(probs_own)[..., None] * value_one
    stream_ids = jnp.arange(STREAMS)
    context = lax.map(jax.checkpoint(self_block), (queries, keys_all, values_all, stream_ids))
    context = low_back(low(merge_heads(context)))
    attended = low_back(matmul(context, w_out))
    first_norm = low(layer_norm(inputs + attended, gain_one, shift_one))
    cross_queries = split_heads(low_back(low(matmul(first_norm, c_query))))
    cross_keys = split_heads(low_back(low(matmul(source, c_key))))
    cross_values = split_heads(low_back(low(matmul(source, c_value))))

    def cross_block(query_one):
        scores = jnp.einsum('thd,jhd->htj', query_one, cross_keys, precision=lax.Precision.HIGHEST) * 0.125
        scores = low_back(scores)
        scores = jnp.where(valid_pos[None, None, :], scores, masked_score)
        row_top = lax.optimization_barrier(jnp.max(scores, axis=-1, keepdims=True))
        expo_main = jnp.exp(scores - row_top)
        probs_main = low(expo_main / lax.optimization_barrier(jnp.sum(expo_main, axis=-1, keepdims=True)))
        return jnp.einsum('htj,jhd->thd', probs_main, cross_values, precision=lax.Precision.HIGHEST)
    cross_context = lax.map(jax.checkpoint(cross_block), cross_queries)
    cross_context = low_back(low(merge_heads(cross_context)))
    crossed = low_back(matmul(cross_context, c_out))
    second_norm = low(layer_norm(first_norm + crossed, gain_two, shift_two))
    ffn_inner = low_back(matmul(second_norm, w_in))
    activated = low(jax.nn.gelu(ffn_inner, approximate=False))
    ffn_out = low_back(matmul(activated, w_back))
    output = layer_norm(second_norm + ffn_out, gain_three, shift_three) * pos_mask
    stats = jnp.stack([jnp.sum(inputs * inputs * pos_mask), jnp.sum(attended * attended * pos_mask), jnp.sum(crossed * crossed * pos_mask), jnp.sum(ffn_out * ffn_out * pos_mask)])
    return (output, stats)

def reference(stream, encoded, cotangent, lengths, bucket_table, w_query, w_key, w_value, w_out, c_query, c_key, c_value, c_out, w_in, w_back, gain_one, shift_one, gain_two, shift_two, gain_three, shift_three, position_bias):
    weights = (w_query.astype(jnp.float32), w_key.astype(jnp.float32), w_value.astype(jnp.float32), w_out.astype(jnp.float32), c_query.astype(jnp.float32), c_key.astype(jnp.float32), c_value.astype(jnp.float32), c_out.astype(jnp.float32), w_in.astype(jnp.float32), w_back.astype(jnp.float32), gain_one, shift_one, gain_two, shift_two, gain_three, shift_three, position_bias)
    zero_grads = jax.tree.map(jnp.zeros_like, weights)

    def one_sequence(running, block_item):
        inputs, source, incoming, length = block_item

        def forward(params, values_in, source_in):
            return sequence_forward(params, values_in, source_in, length, bucket_table)
        result, pull_back, stats = jax.vjp(forward, weights, inputs.astype(jnp.float32), source.astype(jnp.float32), has_aux=True)
        grad_params, grad_inputs, grad_source = pull_back(incoming.astype(jnp.float32))
        summed = jax.tree.map(jnp.add, running[0], grad_params)
        return ((summed, running[1] + stats), (result.astype(jnp.bfloat16), grad_inputs.astype(jnp.bfloat16), grad_source.astype(jnp.bfloat16)))
    (grad_total, stat_total), (outputs, stream_grad, encoded_grad) = lax.scan(one_sequence, (zero_grads, jnp.zeros((4,), jnp.float32)), (stream, encoded, cotangent, lengths))
    token_count = jnp.sum(lengths).astype(jnp.float32) * STREAMS * D
    rms = jnp.sqrt(stat_total / token_count)
    return (outputs, stream_grad, encoded_grad, grad_total[0], grad_total[1], grad_total[2], grad_total[3], grad_total[4], grad_total[5], grad_total[6], grad_total[7], grad_total[8], grad_total[9], grad_total[10], grad_total[11], grad_total[12], grad_total[13], grad_total[14], grad_total[15], grad_total[16], rms)
```

```python
import jax
import jax.numpy as jnp
from jax import lax
from jax.sharding import PartitionSpec as P

HEADS = 16
HEAD_DIM = 64
NBUCKET = 32


epsilon = 1e-05
masked_score = -1e30


def layer_norm(values, norm_gain, norm_shift):
    centre = jnp.mean(values, axis=-1, keepdims=True)
    centred = values - centre
    spread = jnp.mean(centred * centred, axis=-1, keepdims=True)
    return centred * lax.rsqrt(spread + epsilon) * norm_gain + norm_shift


def norm_back(values, norm_gain, norm_shift, incoming):
    result, pull_back = jax.vjp(layer_norm, values, norm_gain, norm_shift)
    return pull_back(incoming)


def exact_gelu(values):
    return jax.nn.gelu(values, approximate=False)


def project(left_rows, weight):
    return jnp.dot(left_rows, weight, preferred_element_type=jnp.float32)


def weight_grad(left_rows, right_rows):
    return jnp.einsum("nd,ne->de", left_rows, right_rows, preferred_element_type=jnp.float32)


def back_project(grad_rows, weight):
    return jnp.einsum("ne,de->nd", grad_rows, weight, preferred_element_type=jnp.float32)


def per_device(
    stream,
    encoded,
    cotangent,
    lengths,
    bucket_table,
    w_query,
    w_key,
    w_value,
    w_out,
    c_query,
    c_key,
    c_value,
    c_out,
    w_in,
    w_back,
    gain_one,
    shift_one,
    gain_two,
    shift_two,
    gain_three,
    shift_three,
    position_bias,
):
    num_rows, num_streams, local_len, model_width = stream.shape
    full_len = local_len * lax.axis_size("seq")
    first_pos = lax.axis_index("seq") * local_len
    query_pos = first_pos + jnp.arange(local_len, dtype=jnp.int32)
    key_pos = jnp.arange(full_len, dtype=jnp.int32)
    valid_query = (query_pos[None, :] < lengths[:, None]).astype(jnp.float32)
    valid_key = key_pos[None, :] < lengths[:, None]
    distance = query_pos[:, None] - key_pos[None, :]
    starts = jnp.sum(
        (bucket_table[:, None] < jnp.arange(1, NBUCKET, dtype=jnp.int32)[None, :]).astype(jnp.int32),
        axis=0,
    )
    buckets = jnp.zeros_like(distance)
    for step in range(NBUCKET - 1):
        buckets = buckets + (distance >= starts[step]).astype(jnp.int32)
    bucket_ids = jnp.arange(NBUCKET, dtype=jnp.int32)
    one_hot = (buckets[:, :, None] == bucket_ids).astype(jnp.float32)
    rel_bias = jnp.einsum("tjb,bh->htj", one_hot, position_bias, precision=lax.Precision.HIGHEST)
    own_hot = (bucket_ids == bucket_table[0]).astype(jnp.float32)
    own_bias = jnp.dot(own_hot, position_bias, precision=lax.Precision.HIGHEST)
    stream_ids = jnp.arange(num_streams)
    allowed = jnp.where(stream_ids[:, None, None] == 0, distance[None] >= 0, distance[None] > 0)
    allowed = (allowed[None] & valid_key[:, None, None, :])[:, :, None]
    predicting = (stream_ids > 0)[None, :, None, None]
    cross_allowed = valid_key[:, None, None, None, :]
    head_shape = (num_rows, num_streams, local_len, HEADS, HEAD_DIM)
    flat_rows = stream.reshape(-1, model_width)
    source_rows = encoded.reshape(-1, model_width)
    row_mask = jnp.broadcast_to(
        valid_query[:, None, :], (num_rows, num_streams, local_len)
    ).reshape(-1, 1)

    def heads_of(block):
        return block.reshape(num_rows, full_len, HEADS, HEAD_DIM)

    queries = project(flat_rows, w_query).astype(jnp.bfloat16).reshape(head_shape)
    keys_local = project(flat_rows, w_key).astype(jnp.bfloat16).reshape(head_shape)
    values_local = project(flat_rows, w_value).astype(jnp.bfloat16).reshape(head_shape)
    main_key = keys_local[:, 0].reshape(num_rows, local_len, model_width)
    main_value = values_local[:, 0].reshape(num_rows, local_len, model_width)
    kept_keys, kept_values = (
        lax.all_gather(main_key, "seq", axis=1, tiled=True),
        lax.all_gather(main_value, "seq", axis=1, tiled=True),
    )

    def self_scores(key_block):
        raw_scores = jnp.einsum(
            "rstha,rjha->rshtj", queries, heads_of(key_block), preferred_element_type=jnp.float32
        )
        scores = jnp.where(allowed, raw_scores * 0.125 + rel_bias, masked_score)
        own_raw = jnp.einsum(
            "rstha,rstha->rsht", queries, keys_local, preferred_element_type=jnp.float32
        )
        own_score = jnp.where(
            predicting, own_raw * 0.125 + own_bias[None, None, :, None], masked_score
        )
        return (scores, own_score)

    scores, own_score = self_scores(kept_keys)
    row_top = jnp.maximum(jnp.max(scores, axis=-1), own_score)
    expo_main = jnp.exp(scores - row_top[..., None])
    expo_own = jnp.exp(own_score - row_top)
    row_total = jnp.sum(expo_main, axis=-1) + expo_own
    self_lse = row_top + jnp.log(row_total)
    probs_main = (expo_main / row_total[..., None]).astype(jnp.bfloat16)
    probs_own = expo_own / row_total
    own_weight = jnp.transpose(probs_own, (0, 1, 3, 2))[..., None]
    context = jnp.einsum(
        "rshtj,rjha->rstha", probs_main, heads_of(kept_values), preferred_element_type=jnp.float32
    )
    context = context + own_weight * values_local.astype(jnp.float32)
    context_low = context.astype(jnp.bfloat16).reshape(-1, model_width)
    attended = project(context_low, w_out)
    resid_one = flat_rows.astype(jnp.float32) + attended
    first_norm = layer_norm(resid_one, gain_one, shift_one).astype(jnp.bfloat16)
    cross_queries = project(first_norm, c_query).astype(jnp.bfloat16).reshape(head_shape)
    cross_key_local = (
        project(source_rows, c_key).astype(jnp.bfloat16).reshape(num_rows, local_len, model_width)
    )
    cross_value_local = (
        project(source_rows, c_value).astype(jnp.bfloat16).reshape(num_rows, local_len, model_width)
    )
    kept_cross_keys, kept_cross_values = (
        lax.all_gather(cross_key_local, "seq", axis=1, tiled=True),
        lax.all_gather(cross_value_local, "seq", axis=1, tiled=True),
    )

    def cross_scores(key_block):
        raw_scores = jnp.einsum(
            "rstha,rjha->rshtj",
            cross_queries,
            heads_of(key_block),
            preferred_element_type=jnp.float32,
        )
        return jnp.where(cross_allowed, raw_scores * 0.125, masked_score)

    cross_raw = cross_scores(kept_cross_keys)
    cross_top = jnp.max(cross_raw, axis=-1, keepdims=True)
    cross_expo = jnp.exp(cross_raw - cross_top)
    cross_total = jnp.sum(cross_expo, axis=-1, keepdims=True)
    cross_lse = cross_top + jnp.log(cross_total)
    cross_probs = (cross_expo / cross_total).astype(jnp.bfloat16)
    cross_context = jnp.einsum(
        "rshtj,rjha->rstha",
        cross_probs,
        heads_of(kept_cross_values),
        preferred_element_type=jnp.float32,
    )
    cross_low = cross_context.astype(jnp.bfloat16).reshape(-1, model_width)
    crossed = project(cross_low, c_out)
    resid_two = first_norm.astype(jnp.float32) + crossed
    second_norm = layer_norm(resid_two, gain_two, shift_two).astype(jnp.bfloat16)
    ffn_inner = project(second_norm, w_in)
    activated = exact_gelu(ffn_inner).astype(jnp.bfloat16)
    ffn_out = project(activated, w_back)
    resid_three = second_norm.astype(jnp.float32) + ffn_out
    layer_output = (layer_norm(resid_three, gain_three, shift_three) * row_mask).astype(
        jnp.bfloat16
    )
    input_wide = flat_rows.astype(jnp.float32)
    totals = lax.psum(
        (
            jnp.sum(input_wide * input_wide * row_mask),
            jnp.sum(attended * attended * row_mask),
            jnp.sum(crossed * crossed * row_mask),
            jnp.sum(ffn_out * ffn_out * row_mask),
            jnp.sum(row_mask),
        ),
        ("dp", "seq"),
    )
    rms = jnp.sqrt(
        jnp.stack([totals[0], totals[1], totals[2], totals[3]]) / (totals[4] * model_width)
    )
    key_block, value_block = (kept_keys, kept_values)
    cross_key_block, cross_value_block = (kept_cross_keys, kept_cross_values)
    d_output = cotangent.reshape(-1, model_width).astype(jnp.float32) * row_mask
    d_resid_three, d_gain_three, d_shift_three = norm_back(
        resid_three, gain_three, shift_three, d_output
    )
    d_ffn_out = d_resid_three.astype(jnp.bfloat16)
    g_back = weight_grad(activated, d_ffn_out)
    gelu_value, gelu_pull = jax.vjp(exact_gelu, ffn_inner)
    d_inner = gelu_pull(back_project(d_ffn_out, w_back))[0].astype(jnp.bfloat16)
    g_in = weight_grad(second_norm, d_inner)
    d_second = d_resid_three + back_project(d_inner, w_in)
    d_resid_two, d_gain_two, d_shift_two = norm_back(resid_two, gain_two, shift_two, d_second)
    d_crossed = d_resid_two.astype(jnp.bfloat16)
    g_cout = weight_grad(cross_low, d_crossed)
    d_cross_ctx = back_project(d_crossed, c_out).astype(jnp.bfloat16).reshape(head_shape)
    cross_back = jnp.exp(cross_scores(cross_key_block) - cross_lse)
    d_cross_probs = jnp.einsum(
        "rstha,rjha->rshtj",
        d_cross_ctx,
        heads_of(cross_value_block),
        preferred_element_type=jnp.float32,
    )
    cross_delta = jnp.sum(cross_back * d_cross_probs, axis=-1, keepdims=True)
    d_cross_scores = (cross_back * (d_cross_probs - cross_delta)).astype(jnp.bfloat16)
    d_cross_query = (
        (
            jnp.einsum(
                "rshtj,rjha->rstha",
                d_cross_scores,
                heads_of(cross_key_block),
                preferred_element_type=jnp.float32,
            )
            * 0.125
        )
        .astype(jnp.bfloat16)
        .reshape(-1, model_width)
    )
    cross_key_part = (
        jnp.einsum(
            "rshtj,rstha->rjha", d_cross_scores, cross_queries, preferred_element_type=jnp.float32
        )
        * 0.125
    ).reshape(num_rows, full_len, model_width)
    cross_value_part = jnp.einsum(
        "rshtj,rstha->rjha", cross_probs, d_cross_ctx, preferred_element_type=jnp.float32
    ).reshape(num_rows, full_len, model_width)
    d_cross_key, d_cross_value = (
        lax.psum_scatter(
            cross_key_part.astype(jnp.bfloat16), "seq", scatter_dimension=1, tiled=True
        ).astype(jnp.float32),
        lax.psum_scatter(
            cross_value_part.astype(jnp.bfloat16), "seq", scatter_dimension=1, tiled=True
        ).astype(jnp.float32),
    )
    d_cross_key = d_cross_key.astype(jnp.bfloat16).reshape(-1, model_width)
    d_cross_value = d_cross_value.astype(jnp.bfloat16).reshape(-1, model_width)
    g_ckey = weight_grad(source_rows, d_cross_key)
    g_cvalue = weight_grad(source_rows, d_cross_value)
    encoded_grad = (
        (back_project(d_cross_key, c_key) + back_project(d_cross_value, c_value))
        .astype(jnp.bfloat16)
        .reshape(encoded.shape)
    )
    g_cquery = weight_grad(first_norm, d_cross_query)
    d_first = d_resid_two + back_project(d_cross_query, c_query)
    d_resid_one, d_gain_one, d_shift_one = norm_back(resid_one, gain_one, shift_one, d_first)
    d_attended = d_resid_one.astype(jnp.bfloat16)
    g_out = weight_grad(context_low, d_attended)
    d_context = back_project(d_attended, w_out).astype(jnp.bfloat16).reshape(head_shape)
    scores_back, own_back = self_scores(key_block)
    p_main = jnp.exp(scores_back - self_lse[..., None])
    p_own = jnp.exp(own_back - self_lse)
    d_probs = jnp.einsum(
        "rstha,rjha->rshtj", d_context, heads_of(value_block), preferred_element_type=jnp.float32
    )
    d_probs_own = jnp.einsum(
        "rstha,rstha->rsht", d_context, values_local, preferred_element_type=jnp.float32
    )
    row_delta = jnp.sum(p_main * d_probs, axis=-1) + p_own * d_probs_own
    d_scores = (p_main * (d_probs - row_delta[..., None])).astype(jnp.bfloat16)
    d_own = (p_own * (d_probs_own - row_delta)).astype(jnp.bfloat16)
    own_grad = jnp.transpose(d_own, (0, 1, 3, 2))[..., None].astype(jnp.float32) * 0.125
    d_queries = jnp.einsum(
        "rshtj,rjha->rstha", d_scores, heads_of(key_block), preferred_element_type=jnp.float32
    ) * 0.125 + own_grad * keys_local.astype(jnp.float32)
    key_part = (
        jnp.einsum("rshtj,rstha->rjha", d_scores, queries, preferred_element_type=jnp.float32)
        * 0.125
    ).reshape(num_rows, full_len, model_width)
    value_part = jnp.einsum(
        "rshtj,rstha->rjha", probs_main, d_context, preferred_element_type=jnp.float32
    ).reshape(num_rows, full_len, model_width)
    d_main_key, d_main_value = (
        lax.psum_scatter(
            key_part.astype(jnp.bfloat16), "seq", scatter_dimension=1, tiled=True
        ).astype(jnp.float32),
        lax.psum_scatter(
            value_part.astype(jnp.bfloat16), "seq", scatter_dimension=1, tiled=True
        ).astype(jnp.float32),
    )
    stream_shape = (num_rows, num_streams, local_len, model_width)
    own_key_grad = (own_grad * queries.astype(jnp.float32)).reshape(stream_shape)
    own_value_grad = (
        jnp.transpose(p_own, (0, 1, 3, 2))[..., None] * d_context.astype(jnp.float32)
    ).reshape(stream_shape)
    d_keys = (
        jnp.concatenate([d_main_key[:, None], own_key_grad[:, 1:]], axis=1)
        .astype(jnp.bfloat16)
        .reshape(-1, model_width)
    )
    d_values = (
        jnp.concatenate([d_main_value[:, None], own_value_grad[:, 1:]], axis=1)
        .astype(jnp.bfloat16)
        .reshape(-1, model_width)
    )
    d_query_low = d_queries.astype(jnp.bfloat16).reshape(-1, model_width)
    g_query = weight_grad(flat_rows, d_query_low)
    g_key = weight_grad(flat_rows, d_keys)
    g_value = weight_grad(flat_rows, d_values)
    stream_grad = (
        (
            d_resid_one
            + back_project(d_query_low, w_query)
            + back_project(d_keys, w_key)
            + back_project(d_values, w_value)
        )
        .astype(jnp.bfloat16)
        .reshape(stream.shape)
    )
    score_sum = jnp.sum(d_scores.astype(jnp.float32), axis=(0, 1))
    table_part = jnp.einsum("htj,tjb->bh", score_sum, one_hot, precision=lax.Precision.HIGHEST)
    table_part = (
        table_part + own_hot[:, None] * jnp.sum(d_own.astype(jnp.float32), axis=(0, 1, 3))[None, :]
    )
    small_sums = lax.psum(
        (table_part, d_gain_one, d_shift_one, d_gain_two, d_shift_two, d_gain_three, d_shift_three),
        ("dp", "seq"),
    )
    def share_of(grads, rows_dim):
        low = grads.astype(jnp.bfloat16)
        low = lax.psum_scatter(low, "seq", scatter_dimension=rows_dim + 1, tiled=True)
        low = lax.psum_scatter(low, "dp", scatter_dimension=rows_dim, tiled=True)
        return low.astype(jnp.float32)

    square = share_of(
        jnp.stack([g_query, g_key, g_value, g_out, g_cquery, g_ckey, g_cvalue, g_cout]), 1
    )
    shares = tuple(square[i] for i in range(8)) + (share_of(g_in, 0), share_of(g_back, 0))
    return (
        layer_output.reshape(stream.shape),
        stream_grad,
        encoded_grad,
        shares[0],
        shares[1],
        shares[2],
        shares[3],
        shares[4],
        shares[5],
        shares[6],
        shares[7],
        shares[8],
        shares[9],
        small_sums[1],
        small_sums[2],
        small_sums[3],
        small_sums[4],
        small_sums[5],
        small_sums[6],
        small_sums[0],
        rms,
    )


def solution(mesh):
    placed = (
        P("dp", None, "seq", None),
        P("dp", "seq", None),
        P("dp", None, "seq", None),
        P("dp"),
        P(),
        P(),
        P(),
        P(),
        P(),
        P(),
        P(),
        P(),
        P(),
        P(),
        P(),
        P(),
        P(),
        P(),
        P(),
        P(),
        P(),
        P(),
    )
    return jax.shard_map(
        per_device,
        mesh=mesh,
        in_specs=placed,
        out_specs=(
            P("dp", None, "seq", None),
            P("dp", None, "seq", None),
            P("dp", "seq", None),
            P("dp", "seq"),
            P("dp", "seq"),
            P("dp", "seq"),
            P("dp", "seq"),
            P("dp", "seq"),
            P("dp", "seq"),
            P("dp", "seq"),
            P("dp", "seq"),
            P("dp", "seq"),
            P("dp", "seq"),
            P(),
            P(),
            P(),
            P(),
            P(),
            P(),
            P(),
            P(),
        ),
        check_vma=False,
    )
```

```python
import functools

import jax
import jax.numpy as jnp
from jax import lax
from jax.experimental import pallas as pl
from jax.experimental.pallas import tpu as pltpu
from jax.sharding import PartitionSpec as P

HEADS = 16
HEAD_DIM = 64
NBUCKET = 32
COLS = 256
SLOTS = 4


epsilon = 1e-05
masked_score = -1e30


def layer_norm(values, norm_gain, norm_shift):
    centre = jnp.mean(values, axis=-1, keepdims=True)
    centred = values - centre
    spread = jnp.mean(centred * centred, axis=-1, keepdims=True)
    return centred * lax.rsqrt(spread + epsilon) * norm_gain + norm_shift


def norm_back(values, norm_gain, norm_shift, incoming):
    result, pull_back = jax.vjp(layer_norm, values, norm_gain, norm_shift)
    return pull_back(incoming)


def exact_gelu(values):
    return jax.nn.gelu(values, approximate=False)


def project(left_rows, weight):
    return jnp.dot(left_rows, weight, preferred_element_type=jnp.float32)


def weight_grad(left_rows, right_rows):
    return jnp.einsum("nd,ne->de", left_rows, right_rows, preferred_element_type=jnp.float32)


def back_project(grad_rows, weight):
    return jnp.einsum("ne,de->nd", grad_rows, weight, preferred_element_type=jnp.float32)


MESH_ID = pl.DeviceIdType.MESH


def tile_dot(x_ref, x_start, y_ref, y_start, rows):
    left = x_ref[:, pl.ds(x_start, rows)]
    right = y_ref[:, pl.ds(y_start, COLS)]
    return lax.dot_general(
        left, right, (((0,), (0,)), ((), ())), preferred_element_type=jnp.float32
    )


def reduce_kernel(units, num_in, num_out, dp_size, *refs):
    ins, small_ref = refs[:num_in], refs[num_in]
    outs, small_out = refs[num_in + 1 : num_in + 1 + num_out], refs[num_in + 1 + num_out]
    sent, core_in, first_y, first_x, second, third, small_in = refs[num_in + num_out + 2 : -10]
    sems = refs[-10:]
    core_s, core_r, one_s, one_r, two_s, two_r, three_s, three_r, small_s, small_r = sems
    dp, sq = lax.axis_index("dp"), lax.axis_index("seq")
    core, ypos = sq % 2, sq // 2
    xpos, zpos = dp % 2, dp // 2
    depth = dp_size // 2
    chunk = 1024 // dp_size
    core_peer = (dp, sq + 1 - 2 * core)
    y_peer = (dp, sq + 2 - 4 * ypos)
    x_peer = (dp + 1 - 2 * xpos, sq)

    def z_peer(step):
        return ((zpos + step) % depth * 2 + xpos, sq)

    barrier = pltpu.get_barrier_semaphore()
    for peer in [core_peer, y_peer, x_peer] + [z_peer(step) for step in range(1, depth)]:
        pl.semaphore_signal(barrier, inc=1, device_id=peer, device_id_type=MESH_ID)
    pl.semaphore_wait(barrier, 2 + depth)

    def remote(src, dst, send_sem, recv_sem, peer):
        return pltpu.make_async_remote_copy(
            src_ref=src,
            dst_ref=dst,
            send_sem=send_sem,
            recv_sem=recv_sem,
            device_id=peer,
            device_id_type=MESH_ID,
        )

    def half_dots(unit, half, write):
        x_id, y_id, kind, part = units[unit]
        x_ref, y_ref = ins[x_id], ins[y_id]
        rows = chunk if kind == "back" else 256

        def body(step, carry):
            tile, side = step // 2, step % 2
            block = side * 2 + half
            x_start = tile * 256
            y_start = block * COLS
            if kind == "in":
                y_start = block * 1024 + part * COLS
            if kind == "back":
                x_start = tile * (4 * chunk) + part * chunk
            write(
                side,
                pl.ds(pl.multiple_of(tile * rows, rows), rows),
                tile_dot(
                    x_ref,
                    pl.multiple_of(x_start, 128),
                    y_ref,
                    pl.multiple_of(y_start, COLS),
                    rows,
                ),
            )
            return carry

        lax.fori_loop(0, 2 * (1024 // rows), body, 0)

    def core_copy(unit):
        return remote(
            sent.at[unit % SLOTS], core_in.at[unit], core_s.at[unit], core_r.at[unit], core_peer
        )

    def one_copy(unit):
        half = unit // 2
        if unit % 2 == 0:
            return remote(
                core_in.at[unit, 1 - ypos], first_y.at[half], one_s.at[unit], one_r.at[unit], y_peer
            )
        source = core_in.at[unit].reshape(2, depth, 2, chunk, COLS)
        return remote(
            source.at[:, :, 1 - xpos], first_x.at[half], one_s.at[unit], one_r.at[unit], x_peer
        )

    def two_copy(unit):
        half = unit // 2
        if unit % 2 == 0:
            source = first_y.at[half].reshape(depth, 2, chunk, COLS)
            return remote(
                source.at[:, 1 - xpos], second.at[unit], two_s.at[unit], two_r.at[unit], x_peer
            )
        return remote(
            first_x.at[half, 1 - ypos], second.at[unit], two_s.at[unit], two_r.at[unit], y_peer
        )

    def three_copy(unit, step):
        return remote(
            second.at[unit, (zpos + step) % depth],
            third.at[unit, step - 1],
            three_s.at[unit, step - 1],
            three_r.at[unit, step - 1],
            z_peer(step),
        )

    def products(unit):
        slot = unit % SLOTS
        if unit >= SLOTS:
            core_copy(unit - SLOTS).wait_send()

        def write(side, rows, value):
            sent[slot, side, rows, :] = value.astype(jnp.bfloat16)

        half_dots(unit, 1 - core, write)
        core_copy(unit).start()

    def core_sum(unit):
        core_copy(unit).wait_recv()

        def write(side, rows, value):
            old = core_in[unit, side, rows, :].astype(jnp.float32)
            core_in[unit, side, rows, :] = (value + old).astype(jnp.bfloat16)

        half_dots(unit, core, write)
        one_copy(unit).start()

    def plus(left, right):
        return (left.astype(jnp.float32) + right.astype(jnp.float32)).astype(jnp.bfloat16)

    def one_sum(unit):
        one_copy(unit).wait_recv()
        half = unit // 2
        if unit % 2 == 0:

            def body(step, carry):
                rows = pl.ds(pl.multiple_of(step * 128, 128), 128)
                first_y[half, rows, :] = plus(first_y[half, rows, :], core_in[unit, ypos, rows, :])
                return carry

            lax.fori_loop(0, 8, body, 0)
        else:
            def body(step, carry):
                side, layer = step // depth, step % depth
                rows = pl.ds(pl.multiple_of((layer * 2 + xpos) * chunk, chunk), chunk)
                first_x[half, side, layer] = plus(
                    first_x[half, side, layer], core_in[unit, side, rows, :]
                )
                return carry

            lax.fori_loop(0, 2 * depth, body, 0)
        two_copy(unit).start()

    def two_sum(unit):
        two_copy(unit).wait_recv()
        half = unit // 2

        def body(layer, carry):
            if unit % 2 == 0:
                rows = pl.ds(pl.multiple_of((layer * 2 + xpos) * chunk, chunk), chunk)
                old = first_y[half, rows, :]
            else:
                old = first_x[half, ypos, layer]
            second[unit, layer] = plus(second[unit, layer], old)
            return carry

        lax.fori_loop(0, depth, body, 0)

        def send(step, carry):
            three_copy(unit, step).start()
            return carry

        lax.fori_loop(1, depth, send, 0)

    def last_sum(unit):
        def body(step, total):
            three_copy(unit, step).wait_recv()
            return total + third[unit, step - 1].astype(jnp.float32)

        total = lax.fori_loop(1, depth, body, second[unit, zpos].astype(jnp.float32))
        x_id, y_id, kind, part = units[unit]
        if kind == "in":
            outs[8][:, part * COLS : (part + 1) * COLS] = total
        elif kind in ("back", "parted"):
            outs[9][part * chunk : (part + 1) * chunk, :] = total
        else:
            outs[part][...] = total

    bits = 0
    while (1 << bits) < dp_size:
        bits += 1
    small_out[...] = small_ref[...]

    def small_copy(step):
        if step == 0:
            peer = core_peer
        elif step == 1:
            peer = y_peer
        else:
            flip = 1 << (step - 2)
            peer = (dp + flip - 2 * flip * (dp // flip % 2), sq)
        return remote(small_out, small_in.at[step], small_s.at[step], small_r.at[step], peer)

    def small_step(step):
        small_copy(step).wait()
        small_out[...] = small_out[...] + small_in[step]

    count = len(units)
    pairs = count // 2
    small_copy(0).start()
    for turn in range(pairs + 5):
        for unit in (2 * turn, 2 * turn + 1):
            if unit < count:
                products(unit)
        for unit in (2 * turn - 2, 2 * turn - 1):
            if 0 <= unit < count:
                core_sum(unit)
        for unit in (2 * turn - 4, 2 * turn - 3):
            if 0 <= unit < count:
                one_sum(unit)
        for unit in (2 * turn - 6, 2 * turn - 5):
            if 0 <= unit < count:
                two_sum(unit)
        for unit in (2 * turn - 8, 2 * turn - 7):
            if 0 <= unit < count:
                last_sum(unit)
        if turn < bits + 2:
            small_step(turn)
            if turn + 1 < bits + 2:
                small_copy(turn + 1).start()
    for step in range(pairs + 5, bits + 2):
        small_step(step)
        if step + 1 < bits + 2:
            small_copy(step + 1).start()
    for unit in range(count):
        if unit >= count - SLOTS:
            core_copy(unit).wait_send()
        one_copy(unit).wait_send()
        two_copy(unit).wait_send()

        def drain(step, carry):
            three_copy(unit, step).wait_send()
            return carry

        lax.fori_loop(1, depth, drain, 0)


def reduce_grads(units, operands, small, dp_size):
    count = len(units)
    depth, chunk = dp_size // 2, 1024 // dp_size
    bits = dp_size.bit_length() - 1
    low = jnp.bfloat16
    out_shapes = [jax.ShapeDtypeStruct((chunk, COLS), jnp.float32)] * 8
    out_shapes.append(jax.ShapeDtypeStruct((chunk, 4 * COLS), jnp.float32))
    out_shapes.append(jax.ShapeDtypeStruct((4 * chunk, COLS), jnp.float32))
    out_shapes.append(jax.ShapeDtypeStruct(small.shape, jnp.float32))
    sem = pltpu.SemaphoreType.DMA
    vmem = pl.BlockSpec(memory_space=pltpu.VMEM)
    return pl.pallas_call(
        functools.partial(reduce_kernel, units, len(operands), 10, dp_size),
        out_shape=out_shapes,
        in_specs=[vmem] * (len(operands) + 1),
        out_specs=[vmem] * 11,
        scratch_shapes=[
            pltpu.VMEM((SLOTS, 2, 1024, COLS), low),
            pltpu.VMEM((count, 2, 1024, COLS), low),
            pltpu.VMEM((count // 2, 1024, COLS), low),
            pltpu.VMEM((count // 2, 2, depth, chunk, COLS), low),
            pltpu.VMEM((count, depth, chunk, COLS), low),
            pltpu.VMEM((count, depth - 1, chunk, COLS), low),
            pltpu.VMEM((bits + 2,) + small.shape, jnp.float32),
            sem((count,)),
            sem((count,)),
            sem((count,)),
            sem((count,)),
            sem((count,)),
            sem((count,)),
            sem((count, depth - 1)),
            sem((count, depth - 1)),
            sem((bits + 2,)),
            sem((bits + 2,)),
        ],
        compiler_params=pltpu.CompilerParams(
            collective_id=0, has_side_effects=True, vmem_limit_bytes=60 << 20
        ),
    )(*operands, small)


def per_device(
    stream,
    encoded,
    cotangent,
    lengths,
    bucket_table,
    w_query,
    w_key,
    w_value,
    w_out,
    c_query,
    c_key,
    c_value,
    c_out,
    w_in,
    w_back,
    gain_one,
    shift_one,
    gain_two,
    shift_two,
    gain_three,
    shift_three,
    position_bias,
):
    num_rows, num_streams, local_len, model_width = stream.shape
    full_len = local_len * lax.axis_size("seq")
    first_pos = lax.axis_index("seq") * local_len
    query_pos = first_pos + jnp.arange(local_len, dtype=jnp.int32)
    key_pos = jnp.arange(full_len, dtype=jnp.int32)
    valid_query = (query_pos[None, :] < lengths[:, None]).astype(jnp.float32)
    valid_key = key_pos[None, :] < lengths[:, None]
    distance = query_pos[:, None] - key_pos[None, :]
    starts = jnp.sum(
        (bucket_table[:, None] < jnp.arange(1, NBUCKET, dtype=jnp.int32)[None, :]).astype(jnp.int32),
        axis=0,
    )
    buckets = jnp.zeros_like(distance)
    for step in range(NBUCKET - 1):
        buckets = buckets + (distance >= starts[step]).astype(jnp.int32)
    bucket_ids = jnp.arange(NBUCKET, dtype=jnp.int32)
    one_hot = (buckets[:, :, None] == bucket_ids).astype(jnp.float32)
    rel_bias = jnp.einsum("tjb,bh->htj", one_hot, position_bias, precision=lax.Precision.HIGHEST)
    own_hot = (bucket_ids == bucket_table[0]).astype(jnp.float32)
    own_bias = jnp.dot(own_hot, position_bias, precision=lax.Precision.HIGHEST)
    stream_ids = jnp.arange(num_streams)
    allowed = jnp.where(stream_ids[:, None, None] == 0, distance[None] >= 0, distance[None] > 0)
    allowed = (allowed[None] & valid_key[:, None, None, :])[:, :, None]
    predicting = (stream_ids > 0)[None, :, None, None]
    cross_allowed = valid_key[:, None, None, None, :]
    head_shape = (num_rows, num_streams, local_len, HEADS, HEAD_DIM)
    flat_rows = stream.reshape(-1, model_width)
    source_rows = encoded.reshape(-1, model_width)
    row_mask = jnp.broadcast_to(
        valid_query[:, None, :], (num_rows, num_streams, local_len)
    ).reshape(-1, 1)

    def heads_of(block):
        return block.reshape(num_rows, full_len, HEADS, HEAD_DIM)

    queries = project(flat_rows, w_query).astype(jnp.bfloat16).reshape(head_shape)
    keys_local = project(flat_rows, w_key).astype(jnp.bfloat16).reshape(head_shape)
    values_local = project(flat_rows, w_value).astype(jnp.bfloat16).reshape(head_shape)
    main_key = keys_local[:, 0].reshape(num_rows, local_len, model_width)
    main_value = values_local[:, 0].reshape(num_rows, local_len, model_width)
    kept_keys, kept_values = (
        lax.all_gather(main_key, "seq", axis=1, tiled=True),
        lax.all_gather(main_value, "seq", axis=1, tiled=True),
    )

    def self_scores(key_block):
        raw_scores = jnp.einsum(
            "rstha,rjha->rshtj", queries, heads_of(key_block), preferred_element_type=jnp.float32
        )
        scores = jnp.where(allowed, raw_scores * 0.125 + rel_bias, masked_score)
        own_raw = jnp.einsum(
            "rstha,rstha->rsht", queries, keys_local, preferred_element_type=jnp.float32
        )
        own_score = jnp.where(
            predicting, own_raw * 0.125 + own_bias[None, None, :, None], masked_score
        )
        return (scores, own_score)

    scores, own_score = self_scores(kept_keys)
    row_top = jnp.maximum(jnp.max(scores, axis=-1), own_score)
    expo_main = jnp.exp(scores - row_top[..., None])
    expo_own = jnp.exp(own_score - row_top)
    row_total = jnp.sum(expo_main, axis=-1) + expo_own
    self_lse = row_top + jnp.log(row_total)
    probs_main = (expo_main / row_total[..., None]).astype(jnp.bfloat16)
    probs_own = expo_own / row_total
    own_weight = jnp.transpose(probs_own, (0, 1, 3, 2))[..., None]
    context = jnp.einsum(
        "rshtj,rjha->rstha", probs_main, heads_of(kept_values), preferred_element_type=jnp.float32
    )
    context = context + own_weight * values_local.astype(jnp.float32)
    context_low = context.astype(jnp.bfloat16).reshape(-1, model_width)
    attended = project(context_low, w_out)
    resid_one = flat_rows.astype(jnp.float32) + attended
    first_norm = layer_norm(resid_one, gain_one, shift_one).astype(jnp.bfloat16)
    cross_queries = project(first_norm, c_query).astype(jnp.bfloat16).reshape(head_shape)
    cross_key_local = (
        project(source_rows, c_key).astype(jnp.bfloat16).reshape(num_rows, local_len, model_width)
    )
    cross_value_local = (
        project(source_rows, c_value).astype(jnp.bfloat16).reshape(num_rows, local_len, model_width)
    )
    kept_cross_keys, kept_cross_values = (
        lax.all_gather(cross_key_local, "seq", axis=1, tiled=True),
        lax.all_gather(cross_value_local, "seq", axis=1, tiled=True),
    )

    def cross_scores(key_block):
        raw_scores = jnp.einsum(
            "rstha,rjha->rshtj",
            cross_queries,
            heads_of(key_block),
            preferred_element_type=jnp.float32,
        )
        return jnp.where(cross_allowed, raw_scores * 0.125, masked_score)

    cross_raw = cross_scores(kept_cross_keys)
    cross_top = jnp.max(cross_raw, axis=-1, keepdims=True)
    cross_expo = jnp.exp(cross_raw - cross_top)
    cross_total = jnp.sum(cross_expo, axis=-1, keepdims=True)
    cross_lse = cross_top + jnp.log(cross_total)
    cross_probs = (cross_expo / cross_total).astype(jnp.bfloat16)
    cross_context = jnp.einsum(
        "rshtj,rjha->rstha",
        cross_probs,
        heads_of(kept_cross_values),
        preferred_element_type=jnp.float32,
    )
    cross_low = cross_context.astype(jnp.bfloat16).reshape(-1, model_width)
    crossed = project(cross_low, c_out)
    resid_two = first_norm.astype(jnp.float32) + crossed
    second_norm = layer_norm(resid_two, gain_two, shift_two).astype(jnp.bfloat16)
    ffn_inner = project(second_norm, w_in)
    activated = exact_gelu(ffn_inner).astype(jnp.bfloat16)
    ffn_out = project(activated, w_back)
    resid_three = second_norm.astype(jnp.float32) + ffn_out
    layer_output = (layer_norm(resid_three, gain_three, shift_three) * row_mask).astype(
        jnp.bfloat16
    )
    input_wide = flat_rows.astype(jnp.float32)
    local_totals = (
        jnp.sum(input_wide * input_wide * row_mask),
        jnp.sum(attended * attended * row_mask),
        jnp.sum(crossed * crossed * row_mask),
        jnp.sum(ffn_out * ffn_out * row_mask),
        jnp.sum(row_mask),
    )
    key_block, value_block = (kept_keys, kept_values)
    cross_key_block, cross_value_block = (kept_cross_keys, kept_cross_values)
    d_output = cotangent.reshape(-1, model_width).astype(jnp.float32) * row_mask
    d_resid_three, d_gain_three, d_shift_three = norm_back(
        resid_three, gain_three, shift_three, d_output
    )
    d_ffn_out = d_resid_three.astype(jnp.bfloat16)
    gelu_value, gelu_pull = jax.vjp(exact_gelu, ffn_inner)
    d_inner = gelu_pull(back_project(d_ffn_out, w_back))[0].astype(jnp.bfloat16)
    d_second = d_resid_three + back_project(d_inner, w_in)
    d_resid_two, d_gain_two, d_shift_two = norm_back(resid_two, gain_two, shift_two, d_second)
    d_crossed = d_resid_two.astype(jnp.bfloat16)
    d_cross_ctx = back_project(d_crossed, c_out).astype(jnp.bfloat16).reshape(head_shape)
    cross_back = jnp.exp(cross_scores(cross_key_block) - cross_lse)
    d_cross_probs = jnp.einsum(
        "rstha,rjha->rshtj",
        d_cross_ctx,
        heads_of(cross_value_block),
        preferred_element_type=jnp.float32,
    )
    cross_delta = jnp.sum(cross_back * d_cross_probs, axis=-1, keepdims=True)
    d_cross_scores = (cross_back * (d_cross_probs - cross_delta)).astype(jnp.bfloat16)
    d_cross_query = (
        (
            jnp.einsum(
                "rshtj,rjha->rstha",
                d_cross_scores,
                heads_of(cross_key_block),
                preferred_element_type=jnp.float32,
            )
            * 0.125
        )
        .astype(jnp.bfloat16)
        .reshape(-1, model_width)
    )
    cross_key_part = (
        jnp.einsum(
            "rshtj,rstha->rjha", d_cross_scores, cross_queries, preferred_element_type=jnp.float32
        )
        * 0.125
    ).reshape(num_rows, full_len, model_width)
    cross_value_part = jnp.einsum(
        "rshtj,rstha->rjha", cross_probs, d_cross_ctx, preferred_element_type=jnp.float32
    ).reshape(num_rows, full_len, model_width)
    d_cross_key, d_cross_value = (
        lax.psum_scatter(
            cross_key_part.astype(jnp.bfloat16), "seq", scatter_dimension=1, tiled=True
        ).astype(jnp.float32),
        lax.psum_scatter(
            cross_value_part.astype(jnp.bfloat16), "seq", scatter_dimension=1, tiled=True
        ).astype(jnp.float32),
    )
    d_cross_key = d_cross_key.astype(jnp.bfloat16).reshape(-1, model_width)
    d_cross_value = d_cross_value.astype(jnp.bfloat16).reshape(-1, model_width)
    encoded_grad = (
        (back_project(d_cross_key, c_key) + back_project(d_cross_value, c_value))
        .astype(jnp.bfloat16)
        .reshape(encoded.shape)
    )
    d_first = d_resid_two + back_project(d_cross_query, c_query)
    d_resid_one, d_gain_one, d_shift_one = norm_back(resid_one, gain_one, shift_one, d_first)
    d_attended = d_resid_one.astype(jnp.bfloat16)
    d_context = back_project(d_attended, w_out).astype(jnp.bfloat16).reshape(head_shape)
    scores_back, own_back = self_scores(key_block)
    p_main = jnp.exp(scores_back - self_lse[..., None])
    p_own = jnp.exp(own_back - self_lse)
    d_probs = jnp.einsum(
        "rstha,rjha->rshtj", d_context, heads_of(value_block), preferred_element_type=jnp.float32
    )
    d_probs_own = jnp.einsum(
        "rstha,rstha->rsht", d_context, values_local, preferred_element_type=jnp.float32
    )
    row_delta = jnp.sum(p_main * d_probs, axis=-1) + p_own * d_probs_own
    d_scores = (p_main * (d_probs - row_delta[..., None])).astype(jnp.bfloat16)
    d_own = (p_own * (d_probs_own - row_delta)).astype(jnp.bfloat16)
    own_grad = jnp.transpose(d_own, (0, 1, 3, 2))[..., None].astype(jnp.float32) * 0.125
    d_queries = jnp.einsum(
        "rshtj,rjha->rstha", d_scores, heads_of(key_block), preferred_element_type=jnp.float32
    ) * 0.125 + own_grad * keys_local.astype(jnp.float32)
    key_part = (
        jnp.einsum("rshtj,rstha->rjha", d_scores, queries, preferred_element_type=jnp.float32)
        * 0.125
    ).reshape(num_rows, full_len, model_width)
    value_part = jnp.einsum(
        "rshtj,rstha->rjha", probs_main, d_context, preferred_element_type=jnp.float32
    ).reshape(num_rows, full_len, model_width)
    d_main_key, d_main_value = (
        lax.psum_scatter(
            key_part.astype(jnp.bfloat16), "seq", scatter_dimension=1, tiled=True
        ).astype(jnp.float32),
        lax.psum_scatter(
            value_part.astype(jnp.bfloat16), "seq", scatter_dimension=1, tiled=True
        ).astype(jnp.float32),
    )
    stream_shape = (num_rows, num_streams, local_len, model_width)
    own_key_grad = (own_grad * queries.astype(jnp.float32)).reshape(stream_shape)
    own_value_grad = (
        jnp.transpose(p_own, (0, 1, 3, 2))[..., None] * d_context.astype(jnp.float32)
    ).reshape(stream_shape)
    d_keys = (
        jnp.concatenate([d_main_key[:, None], own_key_grad[:, 1:]], axis=1)
        .astype(jnp.bfloat16)
        .reshape(-1, model_width)
    )
    d_values = (
        jnp.concatenate([d_main_value[:, None], own_value_grad[:, 1:]], axis=1)
        .astype(jnp.bfloat16)
        .reshape(-1, model_width)
    )
    d_query_low = d_queries.astype(jnp.bfloat16).reshape(-1, model_width)
    stream_grad = (
        (
            d_resid_one
            + back_project(d_query_low, w_query)
            + back_project(d_keys, w_key)
            + back_project(d_values, w_value)
        )
        .astype(jnp.bfloat16)
        .reshape(stream.shape)
    )
    score_sum = jnp.sum(d_scores.astype(jnp.float32), axis=(0, 1))
    table_part = jnp.einsum("htj,tjb->bh", score_sum, one_hot, precision=lax.Precision.HIGHEST)
    table_part = (
        table_part + own_hot[:, None] * jnp.sum(d_own.astype(jnp.float32), axis=(0, 1, 3))[None, :]
    )
    tail = jnp.concatenate(
        [table_part.reshape(-1), jnp.stack(local_totals), jnp.zeros((507,), jnp.float32)]
    )
    small = jnp.stack(
        [d_gain_one, d_shift_one, d_gain_two, d_shift_two, d_gain_three, d_shift_three, tail]
        + [jnp.zeros_like(tail)]
    )
    dp_size = lax.axis_size("dp")
    chunk = model_width // dp_size
    units = []
    operands = [d_ffn_out, second_norm, d_inner, cross_low, d_crossed, first_norm, d_cross_query]
    operands += [source_rows, d_cross_key, d_cross_value, context_low, d_attended]
    operands += [flat_rows, d_query_low, d_keys, d_values]
    if chunk % 128 == 0:
        operands.append(activated)
        for part in range(4):
            units.append((16, 0, "back", part))
    else:
        parted = jnp.transpose(activated.reshape(-1, dp_size, 4, chunk), (2, 0, 1, 3))
        parted = parted.reshape(4, -1, model_width)
        for part in range(4):
            operands.append(parted[part])
            units.append((16 + part, 0, "parted", part))
    for part in range(4):
        units.append((1, 2, "in", part))
    units += [(3, 4, "", 7), (5, 6, "", 4), (7, 8, "", 5), (7, 9, "", 6), (10, 11, "", 3)]
    units += [(12, 13, "", 0), (12, 14, "", 1), (12, 15, "", 2)]
    reduced = reduce_grads(tuple(units), operands, small, dp_size)
    shares, sums = reduced[:10], reduced[10]
    rms = jnp.sqrt(sums[6, 512:516] / (sums[6, 516] * model_width))
    return (
        layer_output.reshape(stream.shape),
        stream_grad,
        encoded_grad,
        shares[0],
        shares[1],
        shares[2],
        shares[3],
        shares[4],
        shares[5],
        shares[6],
        shares[7],
        shares[8],
        shares[9],
        sums[0],
        sums[1],
        sums[2],
        sums[3],
        sums[4],
        sums[5],
        sums[6, :512].reshape(NBUCKET, HEADS),
        rms,
    )


def solution(mesh):
    placed = (
        P("dp", None, "seq", None),
        P("dp", "seq", None),
        P("dp", None, "seq", None),
        P("dp"),
        P(),
        P(),
        P(),
        P(),
        P(),
        P(),
        P(),
        P(),
        P(),
        P(),
        P(),
        P(),
        P(),
        P(),
        P(),
        P(),
        P(),
        P(),
    )
    return jax.shard_map(
        per_device,
        mesh=mesh,
        in_specs=placed,
        out_specs=(
            P("dp", None, "seq", None),
            P("dp", None, "seq", None),
            P("dp", "seq", None),
            P("dp", "seq"),
            P("dp", "seq"),
            P("dp", "seq"),
            P("dp", "seq"),
            P("dp", "seq"),
            P("dp", "seq"),
            P("dp", "seq"),
            P("dp", "seq"),
            P("dp", "seq"),
            P("dp", "seq"),
            P(),
            P(),
            P(),
            P(),
            P(),
            P(),
            P(),
            P(),
        ),
        check_vma=False,
    )
```

```python
import functools

import jax
import jax.numpy as jnp
from jax import lax
from jax.experimental import pallas as pl
from jax.experimental.pallas import tpu as pltpu
from jax.sharding import PartitionSpec as P

HEADS = 16
HEAD_DIM = 64
NBUCKET = 32
COLS = 256
SLOTS = 4
epsilon = 1e-05
masked_score = -1e30


LOW = jnp.bfloat16
WIDE = jnp.float32
NN = (((1,), (0,)), ((), ()))
NT = (((1,), (1,)), ((), ()))


def dot(left, right, dims=NN):
    return lax.dot_general(left, right, dims, preferred_element_type=WIDE)


def flip(block):
    return jnp.transpose(block.astype(WIDE))


def places():
    dp, sq = lax.axis_index("dp"), lax.axis_index("seq")
    core, ypos = sq % 2, sq // 2
    return dp, sq, core, ypos, (dp, sq + 1 - 2 * core), (dp, sq + 2 - 4 * ypos)


def remote_copy(src, dst, send_sem, recv_sem, peer):
    return pltpu.make_async_remote_copy(
        src_ref=src,
        dst_ref=dst,
        send_sem=send_sem,
        recv_sem=recv_sem,
        device_id=peer,
        device_id_type=MESH_ID,
    )


def greet(peers):
    barrier = pltpu.get_barrier_semaphore()
    for peer in peers:
        pl.semaphore_signal(barrier, inc=1, device_id=peer, device_id_type=MESH_ID)
    pl.semaphore_wait(barrier, len(peers))


def tiles(count, size, body):
    def step(index, carry):
        body(pl.ds(pl.multiple_of(index * size, size), size))
        return carry

    lax.fori_loop(0, count, step, 0)


def project_to(dst, left, weight, scale=None):
    def body(cols):
        product = dot(left[...], weight[:, cols])
        if scale is not None:
            product = product * scale
        dst[:, cols] = product.astype(dst.dtype)

    tiles(dst.shape[1] // 256, 256, body)


def norm_stats(rows):
    centre = jnp.mean(rows, axis=-1, keepdims=True)
    centred = rows - centre
    spread = jnp.mean(centred * centred, axis=-1, keepdims=True)
    return centred, lax.rsqrt(spread + epsilon)


def norm_backward(rows, gain, incoming):
    centred, scale = norm_stats(rows)
    unit = centred * scale
    scaled = incoming * gain
    first = jnp.mean(scaled, axis=-1, keepdims=True)
    second = jnp.mean(scaled * unit, axis=-1, keepdims=True)
    grads = scale * (scaled - first - unit * second)
    d_gain = jnp.sum(incoming * unit, axis=0, keepdims=True)
    return grads, d_gain, jnp.sum(incoming, axis=0, keepdims=True)


def valid_rows(sq, length, count):
    position = sq * count + lax.broadcasted_iota(jnp.int32, (count, 1), 0)
    return (position < length).astype(WIDE)


def sum_squares(rows, mask):
    return jnp.sum(rows * rows * mask, axis=0, keepdims=True)


def half_rows(block, side):
    row = lax.broadcasted_iota(jnp.int32, block.shape, 0)
    return jnp.where(row // HEAD_DIM == side, block, 0.0).astype(LOW)


def half_lanes(block, side):
    lane = lax.broadcasted_iota(jnp.int32, block.shape, 1)
    return jnp.where(lane // HEAD_DIM == side, block.astype(WIDE), 0.0).astype(LOW)


def front_kernel(*refs):
    stream, encoded, length_ref, bias_table = refs[:4]
    gain_one, shift_one, gain_two, shift_two = refs[4:8]
    hbm_weights = refs[8:16]
    (query, own_key, own_value, main_key, main_value, context, resid_one, first_norm) = refs[16:24]
    (cross_query, cross_key, cross_value, cross_context, resid_two, second_norm) = refs[24:30]
    own_probs, stats, probs_out, cross_probs_out = refs[30:34]
    weights = refs[34:42]
    main_all, source_all, kept, bias, masks = refs[42:47]
    weight_sem, kept_sem, send_sem, recv_sem = refs[47:]
    w_query, w_key, w_value, w_out, c_query, c_key, c_value, c_out = weights
    dp, sq, core, ypos, core_peer, y_peer = places()
    length = length_ref[0]
    rows = stream.shape[1]
    full = main_all.shape[0] * rows
    loads = [
        pltpu.make_async_copy(src, dst, weight_sem.at[index])
        for index, (src, dst) in enumerate(zip(hbm_weights, weights))
    ]
    for load in loads:
        load.start()
    greet([core_peer, y_peer])
    sources = (stream.at[0], encoded)
    gathered = (main_all, source_all)
    firsts = []
    for index in range(2):
        for lane, peer in enumerate((y_peer, core_peer)):
            slot = index * 3 + lane
            firsts.append(
                remote_copy(
                    sources[index],
                    gathered[index].at[sq],
                    send_sem.at[slot],
                    recv_sem.at[slot],
                    peer,
                )
            )
            firsts[-1].start()
    main_all[sq] = stream[0]
    source_all[sq] = encoded[...]

    def passed_on(index):
        other = gathered[index].at[sq + 2 - 4 * ypos]
        slot = index * 3 + 2
        return remote_copy(other, other, send_sem.at[slot], recv_sem.at[slot], core_peer)

    flat = stream.reshape(3 * rows, stream.shape[2])
    loads[0].wait()
    project_to(query, flat, w_query, 0.125)
    firsts[0].wait_recv()
    passed_on(0).start()
    predicting = flat.at[rows:, :]
    loads[1].wait()
    project_to(own_key, predicting, w_key)
    loads[2].wait()
    project_to(own_value, predicting, w_value)
    firsts[1].wait_recv()
    passed_on(0).wait_recv()
    firsts[2].wait_recv()
    passed_on(1).start()
    wide_main = main_all.reshape(full, main_all.shape[2])
    project_to(main_key, wide_main, w_key)
    project_to(main_value, wide_main, w_value)

    key_row = lax.broadcasted_iota(jnp.int32, (full, rows), 0)
    distance = sq * rows + lax.broadcasted_iota(jnp.int32, (full, rows), 1) - key_row
    in_range = key_row < length
    masks[0] = jnp.where((distance >= 0) & in_range, 0.0, masked_score)
    masks[1] = jnp.where((distance > 0) & in_range, 0.0, masked_score)
    masks[2] = jnp.where(in_range, 0.0, masked_score)

    def kept_copy(pair, out):
        slot = pair % 2
        return pltpu.make_async_copy(kept.at[slot], out.at[pair], kept_sem.at[slot])

    def self_pair(pair, carry):
        @pl.when(pair >= 2)
        def _():
            kept_copy(pair - 2, probs_out).wait()

        slot = pair % 2
        cols = pl.ds(pl.multiple_of(pair * 128, 128), 128)
        keys = main_key[:, cols]
        query_t = flip(query[:, cols])
        value_t = flip(main_value[:, cols]).astype(LOW)
        own_key_t, own_value_t = flip(own_key[:, cols]), flip(own_value[:, cols])
        own_product = query_t[:, rows:] * own_key_t
        sides = []
        for side in range(2):
            head = 2 * pair + side
            span = slice(side * HEAD_DIM, (side + 1) * HEAD_DIM)
            scores = dot(keys, half_rows(query_t, side))
            own_bias = bias_table[head, :, full : full + 128][:, 0:1]
            own_score = jnp.sum(own_product[span], axis=0, keepdims=True) + own_bias
            for block in range(full // rows):
                start = pl.multiple_of((sq - block + full // rows - 1) * rows, 128)
                line = bias_table[head, :, pl.ds(start, 2 * rows)]
                wide = jnp.broadcast_to(line, (rows, 2 * rows))
                near = pltpu.roll(wide, 0, 1, stride=1, stride_axis=0)[:, rows:]
                part = slice(block * rows, (block + 1) * rows)
                for kind in range(2):
                    bias[kind, part, :] = near + masks[kind, part, :]
            owns = []
            for stream_id in range(3):
                lanes = slice(stream_id * rows, (stream_id + 1) * rows)
                score = scores[:, lanes] + bias[min(stream_id, 1)]
                top = jnp.max(score, axis=0, keepdims=True)
                if stream_id > 0:
                    own = own_score[:, (stream_id - 1) * rows : stream_id * rows]
                    top = jnp.maximum(top, own)
                expo = jnp.exp(score - top)
                total = jnp.sum(expo, axis=0, keepdims=True)
                if stream_id > 0:
                    expo_own = jnp.exp(own - top)
                    total = total + expo_own
                share = 1.0 / total
                kept[slot, side, :, lanes] = (expo * share).astype(LOW)
                owns.append(expo_own * share if stream_id > 0 else jnp.zeros_like(total))
            own_probs[head] = jnp.concatenate(owns, axis=1)
            mixed = dot(value_t[span], kept[slot, side])
            mixed_own = jnp.concatenate(owns[1:], axis=1) * own_value_t[span]
            sides.append(
                jnp.concatenate([mixed[:, :rows], mixed[:, rows:] + mixed_own], axis=1)
            )
        context[:, cols] = jnp.transpose(jnp.concatenate(sides, axis=0)).astype(LOW)
        kept_copy(pair, probs_out).start()
        return carry

    lax.fori_loop(0, HEADS // 2, self_pair, 0)
    for pair in range(HEADS // 2 - 2, HEADS // 2):
        kept_copy(pair, probs_out).wait()

    mask = valid_rows(sq, length, rows)
    loads[3].wait()
    project_to(resid_one, context, w_out)
    seen = jnp.zeros((1, stream.shape[2]), WIDE)
    branch = jnp.zeros((1, stream.shape[2]), WIDE)
    for stream_id in range(3):
        part = slice(stream_id * rows, (stream_id + 1) * rows)
        source, attended = stream[stream_id].astype(WIDE), resid_one[part, :]
        seen = seen + sum_squares(source, mask)
        branch = branch + sum_squares(attended, mask)
        total = source + attended
        resid_one[part, :] = total
        centred, scale = norm_stats(total)
        first_norm[part, :] = (centred * scale * gain_one[...] + shift_one[...]).astype(LOW)
    stats[0:1, :] = seen
    stats[1:2, :] = branch
    loads[4].wait()
    project_to(cross_query, first_norm, c_query, 0.125)
    firsts[3].wait_recv()
    passed_on(1).wait_recv()
    wide_source = source_all.reshape(full, source_all.shape[2])
    loads[5].wait()
    project_to(cross_key, wide_source, c_key)
    loads[6].wait()
    project_to(cross_value, wide_source, c_value)

    def cross_pair(pair, carry):
        @pl.when(pair >= 2)
        def _():
            kept_copy(pair - 2, cross_probs_out).wait()

        slot = pair % 2
        cols = pl.ds(pl.multiple_of(pair * 128, 128), 128)
        keys = cross_key[:, cols]
        query_t = flip(cross_query[:, cols])
        value_t = flip(cross_value[:, cols]).astype(LOW)
        sides = []
        for side in range(2):
            span = slice(side * HEAD_DIM, (side + 1) * HEAD_DIM)
            scores = dot(keys, half_rows(query_t, side))
            for stream_id in range(3):
                lanes = slice(stream_id * rows, (stream_id + 1) * rows)
                score = scores[:, lanes] + masks[2]
                expo = jnp.exp(score - jnp.max(score, axis=0, keepdims=True))
                share = 1.0 / jnp.sum(expo, axis=0, keepdims=True)
                kept[slot, side, :, lanes] = (expo * share).astype(LOW)
            sides.append(dot(value_t[span], kept[slot, side]))
        cross_context[:, cols] = jnp.transpose(jnp.concatenate(sides, axis=0)).astype(LOW)
        kept_copy(pair, cross_probs_out).start()
        return carry

    lax.fori_loop(0, HEADS // 2, cross_pair, 0)
    for pair in range(HEADS // 2 - 2, HEADS // 2):
        kept_copy(pair, cross_probs_out).wait()
    loads[7].wait()
    project_to(resid_two, cross_context, c_out)
    branch = jnp.zeros((1, stream.shape[2]), WIDE)
    for stream_id in range(3):
        part = slice(stream_id * rows, (stream_id + 1) * rows)
        crossed = resid_two[part, :]
        branch = branch + sum_squares(crossed, mask)
        total = first_norm[part, :].astype(WIDE) + crossed
        resid_two[part, :] = total
        centred, scale = norm_stats(total)
        second_norm[part, :] = (centred * scale * gain_two[...] + shift_two[...]).astype(LOW)
    stats[2:3, :] = branch
    for copy in firsts:
        copy.wait_send()
    for index in range(2):
        passed_on(index).wait_send()


def front(stream, encoded, length, bias_table, norms, weights):
    streams, rows, width = stream.shape
    seq = lax.axis_size("seq")
    full, tokens = seq * rows, streams * rows
    own = tokens - rows
    shape = jax.ShapeDtypeStruct
    pairs = HEADS // 2
    outs = [
        shape((tokens, width), LOW),
        shape((own, width), LOW),
        shape((own, width), LOW),
        shape((full, width), LOW),
        shape((full, width), LOW),
        shape((tokens, width), LOW),
        shape((tokens, width), WIDE),
        shape((tokens, width), LOW),
        shape((tokens, width), LOW),
        shape((full, width), LOW),
        shape((full, width), LOW),
        shape((tokens, width), LOW),
        shape((tokens, width), WIDE),
        shape((tokens, width), LOW),
        shape((HEADS, 1, tokens), WIDE),
        shape((3, width), WIDE),
        shape((pairs, 2, full, tokens), LOW),
        shape((pairs, 2, full, tokens), LOW),
    ]
    vmem = pl.BlockSpec(memory_space=pltpu.VMEM)
    smem = pl.BlockSpec(memory_space=pltpu.SMEM)
    hbm = pl.BlockSpec(memory_space=pl.ANY)
    sem = pltpu.SemaphoreType.DMA
    return pl.pallas_call(
        front_kernel,
        out_shape=outs,
        in_specs=[vmem, vmem, smem] + [vmem] * 5 + [hbm] * 8,
        out_specs=[vmem] * 16 + [hbm] * 2,
        scratch_shapes=[pltpu.VMEM(w.shape, LOW) for w in weights]
        + [
            pltpu.VMEM((seq, rows, width), LOW),
            pltpu.VMEM((seq, rows, width), LOW),
            pltpu.VMEM((2, 2, full, tokens), LOW),
            pltpu.VMEM((2, full, rows), WIDE),
            pltpu.VMEM((3, full, rows), WIDE),
            sem((8,)),
            sem((2,)),
            sem((6,)),
            sem((6,)),
        ],
        compiler_params=pltpu.CompilerParams(
            collective_id=1, has_side_effects=True, vmem_limit_bytes=60 << 20
        ),
    )(stream, encoded, length, bias_table, *norms, *weights)


def middle_kernel(*refs):
    second_norm, resid_two, cotangent, length_ref, gain_two, gain_three, shift_three = refs[:7]
    hbm_in, hbm_back = refs[7:9]
    output, activated, d_ffn, d_inner, d_resid, d_crossed, grads, stats = refs[9:17]
    w_in, w_back, slope, total, load_sem = refs[17:]
    sq = lax.axis_index("seq")
    length = length_ref[0]
    tokens, width = second_norm.shape
    rows = tokens // 3
    hidden = w_in.shape[1]
    size = 512
    steps = hidden // size

    def load_in(step):
        cols = pl.ds(pl.multiple_of(step * size, size), size)
        return pltpu.make_async_copy(hbm_in.at[:, cols], w_in.at[:, cols], load_sem.at[0, step])

    def load_back(step):
        cols = pl.ds(pl.multiple_of(step * size, size), size)
        return pltpu.make_async_copy(hbm_back.at[cols], w_back.at[cols], load_sem.at[1, step])

    for step in range(steps):
        load_in(step).start()
        load_back(step).start()
    total[...] = jnp.zeros_like(total)

    def forward(step, carry):
        cols = pl.ds(pl.multiple_of(step * size, size), size)
        load_in(step).wait()
        inner = dot(second_norm[...], w_in[:, cols])
        phi = 0.5 + 0.5 * lax.erf(inner * (0.5**0.5))
        bell = jnp.exp(inner * inner * -0.5) * (0.5 / jnp.pi) ** 0.5
        value = (inner * phi).astype(LOW)
        activated[:, cols] = value
        slope[:, cols] = (phi + inner * bell).astype(LOW)
        load_back(step).wait()
        total[...] += dot(value, w_back[cols, :])
        return carry

    lax.fori_loop(0, steps, forward, 0)
    mask = valid_rows(sq, length, rows)
    branch = jnp.zeros((1, width), WIDE)
    d_gain = jnp.zeros((1, width), WIDE)
    d_shift = jnp.zeros((1, width), WIDE)
    for stream_id in range(3):
        part = slice(stream_id * rows, (stream_id + 1) * rows)
        ffn = total[part, :]
        branch = branch + sum_squares(ffn, mask)
        resid = second_norm[part, :].astype(WIDE) + ffn
        centred, scale = norm_stats(resid)
        normed = centred * scale * gain_three[...] + shift_three[...]
        output[part, :] = (normed * mask).astype(LOW)
        incoming = cotangent[part, :].astype(WIDE) * mask
        back, gain_part, shift_part = norm_backward(resid, gain_three[...], incoming)
        d_gain, d_shift = d_gain + gain_part, d_shift + shift_part
        total[part, :] = back
        d_ffn[part, :] = back.astype(LOW)
    stats[...] = branch
    grads[2:3, :] = d_gain
    grads[3:4, :] = d_shift

    def backward(step, carry):
        cols = pl.ds(pl.multiple_of(step * size, size), size)
        d_act = dot(d_ffn[...], w_back[cols, :], NT)
        d_in = (d_act * slope[:, cols].astype(WIDE)).astype(LOW)
        d_inner[:, cols] = d_in
        total[...] += dot(d_in, w_in[:, cols], NT)
        return carry

    lax.fori_loop(0, steps, backward, 0)
    d_gain = jnp.zeros((1, width), WIDE)
    d_shift = jnp.zeros((1, width), WIDE)
    for stream_id in range(3):
        part = slice(stream_id * rows, (stream_id + 1) * rows)
        back, gain_part, shift_part = norm_backward(
            resid_two[part, :], gain_two[...], total[part, :]
        )
        d_gain, d_shift = d_gain + gain_part, d_shift + shift_part
        d_resid[part, :] = back
        d_crossed[part, :] = back.astype(LOW)
    grads[0:1, :] = d_gain
    grads[1:2, :] = d_shift


def middle(second_norm, resid_two, cotangent, length, gain_two, gain_three, shift_three, w_in, w_back):
    tokens, width = second_norm.shape
    hidden = w_in.shape[1]
    shape = jax.ShapeDtypeStruct
    vmem = pl.BlockSpec(memory_space=pltpu.VMEM)
    smem = pl.BlockSpec(memory_space=pltpu.SMEM)
    hbm = pl.BlockSpec(memory_space=pl.ANY)
    return pl.pallas_call(
        middle_kernel,
        out_shape=[
            shape((tokens, width), LOW),
            shape((tokens, hidden), LOW),
            shape((tokens, width), LOW),
            shape((tokens, hidden), LOW),
            shape((tokens, width), WIDE),
            shape((tokens, width), LOW),
            shape((4, width), WIDE),
            shape((1, width), WIDE),
        ],
        in_specs=[vmem] * 3 + [smem] + [vmem] * 3 + [hbm] * 2,
        out_specs=[vmem] * 8,
        scratch_shapes=[
            pltpu.VMEM(w_in.shape, LOW),
            pltpu.VMEM(w_back.shape, LOW),
            pltpu.VMEM((tokens, hidden), LOW),
            pltpu.VMEM((tokens, width), WIDE),
            pltpu.SemaphoreType.DMA((2, hidden // 512)),
        ],
        compiler_params=pltpu.CompilerParams(vmem_limit_bytes=60 << 20),
    )(second_norm, resid_two, cotangent, length, gain_two, gain_three, shift_three, w_in, w_back)


def rear_kernel(*refs):
    d_crossed, d_resid_two, cross_key, cross_value, cross_query, resid_one = refs[:6]
    main_key, main_value, query, own_key, own_value, own_probs, gain_one = refs[6:13]
    hbm_weights = refs[13:21]
    cross_probs, probs = refs[21:23]
    (d_cross_query, d_cross_key, d_cross_value, encoded_grad, d_attended) = refs[23:28]
    (d_query, d_key, d_value, stream_grad, grads, bias_sums, own_sums) = refs[28:35]
    weights = refs[35:43]
    kept, d_context, d_resid, parts, near_in, far_in = refs[43:49]
    weight_sem, kept_sem, core_s, core_r, far_s, far_r = refs[49:]
    c_out, c_query, w_out, w_query, w_key, w_value, c_key, c_value = weights
    dp, sq, core, ypos, core_peer, y_peer = places()
    tokens, width = query.shape
    rows = tokens // 3
    full = main_key.shape[0]
    pairs = HEADS // 2
    loads = [
        pltpu.make_async_copy(src, dst, weight_sem.at[index])
        for index, (src, dst) in enumerate(zip(hbm_weights, weights))
    ]

    def fetch(pair, source, base):
        slot = (pair + base) % 2
        return pltpu.make_async_copy(source.at[pair], kept.at[slot], kept_sem.at[slot])

    loads[0].start()
    fetch(0, cross_probs, 0).start()
    for load in loads[1:]:
        load.start()
    greet([core_peer, y_peer])
    loads[0].wait()

    def back_to(dst, left, weight, scale=None):
        def body(cols):
            dst[:, cols] = dot(left[...], weight[cols, :], NT).astype(dst.dtype)

        tiles(width // 256, 256, body)

    back_to(d_context, d_crossed, c_out)

    def core_copy(index):
        view = parts.at[index].reshape(2, 2, rows, width)
        return remote_copy(
            view.at[:, 1 - core], near_in.at[index], core_s.at[index], core_r.at[index], core_peer
        )

    def far_copy(index):
        return remote_copy(
            near_in.at[index, 1 - ypos], far_in.at[index], far_s.at[index], far_r.at[index], y_peer
        )

    def near_sum(index):
        core_copy(index).wait_recv()
        for side in range(2):
            mine = parts[index, side * 2 + core].astype(WIDE)
            near_in[index, side] = (near_in[index, side].astype(WIDE) + mine).astype(LOW)
        far_copy(index).start()

    def far_sum(index):
        far_copy(index).wait_recv()
        return (near_in[index, ypos].astype(WIDE) + far_in[index].astype(WIDE)).astype(LOW)

    def store_part(index, cols, block):
        for part in range(full // rows):
            parts[index, part, :, cols] = block[part * rows : (part + 1) * rows].astype(LOW)

    def cross_pair(pair, carry):
        fetch(pair, cross_probs, 0).wait()

        @pl.when(pair + 1 < pairs)
        def _():
            fetch(pair + 1, cross_probs, 0).start()

        slot = pair % 2
        cols = pl.ds(pl.multiple_of(pair * 128, 128), 128)
        values = cross_value[:, cols]
        key_t = flip(cross_key[:, cols]).astype(LOW)
        queries, d_ctx = cross_query[:, cols], d_context[:, cols]
        d_ctx_t = flip(d_ctx)
        d_query_t, d_scores = [], []
        for side in range(2):
            span = slice(side * HEAD_DIM, (side + 1) * HEAD_DIM)
            d_prob = dot(values, half_rows(d_ctx_t, side))
            prob = kept[slot, side].astype(WIDE)
            delta = jnp.sum(prob * d_prob, axis=0, keepdims=True)
            d_score = (prob * (d_prob - delta)).astype(LOW)
            d_query_t.append(dot(key_t[span], d_score))
            d_scores.append(d_score)
        d_cross_query[:, cols] = (
            jnp.transpose(jnp.concatenate(d_query_t, axis=0)) * 0.125
        ).astype(LOW)
        both = jnp.concatenate(d_scores, axis=1)
        split = jnp.concatenate([half_lanes(queries, 0), half_lanes(queries, 1)], axis=0)
        store_part(0, cols, dot(both, split))
        both = jnp.concatenate([kept[slot, 0], kept[slot, 1]], axis=1)
        split = jnp.concatenate([half_lanes(d_ctx, 0), half_lanes(d_ctx, 1)], axis=0)
        store_part(1, cols, dot(both, split))
        return carry

    lax.fori_loop(0, pairs, cross_pair, 0)
    fetch(0, probs, 0).start()
    core_copy(0).start()
    core_copy(1).start()
    loads[1].wait()
    back_to(d_resid, d_cross_query, c_query)
    d_gain = jnp.zeros((1, width), WIDE)
    d_shift = jnp.zeros((1, width), WIDE)
    for stream_id in range(3):
        part = slice(stream_id * rows, (stream_id + 1) * rows)
        back, gain_part, shift_part = norm_backward(
            resid_one[part, :], gain_one[...], d_resid[part, :] + d_resid_two[part, :]
        )
        d_gain, d_shift = d_gain + gain_part, d_shift + shift_part
        d_resid[part, :] = back
        d_attended[part, :] = back.astype(LOW)
    grads[0:1, :] = d_gain
    grads[1:2, :] = d_shift
    near_sum(0)
    near_sum(1)
    loads[2].wait()
    back_to(d_context, d_attended, w_out)
    line = lax.broadcasted_iota(jnp.int32, (rows, rows), 0)
    turned = (line + lax.broadcasted_iota(jnp.int32, (rows, rows), 1) == rows - 1).astype(LOW)

    def self_pair(pair, carry):
        fetch(pair, probs, 0).wait()

        @pl.when(pair + 1 < pairs)
        def _():
            fetch(pair + 1, probs, 0).start()

        slot = pair % 2
        cols = pl.ds(pl.multiple_of(pair * 128, 128), 128)
        values = main_value[:, cols]
        key_t = flip(main_key[:, cols]).astype(LOW)
        queries, d_ctx = query[:, cols], d_context[:, cols]
        d_ctx_t, query_t = flip(d_ctx), flip(queries)
        own_key_t, own_value_t = flip(own_key[:, cols]), flip(own_value[:, cols])
        own_product = d_ctx_t[:, rows:] * own_value_t
        d_query_t, d_scores, d_own_key, d_own_value = [], [], [], []
        for side in range(2):
            head = 2 * pair + side
            span = slice(side * HEAD_DIM, (side + 1) * HEAD_DIM)
            d_prob = dot(values, half_rows(d_ctx_t, side))
            prob = kept[slot, side].astype(WIDE)
            prob_own = own_probs[head][:, rows:]
            d_prob_own = jnp.sum(own_product[span], axis=0, keepdims=True)
            delta = jnp.sum(prob * d_prob, axis=0, keepdims=True)
            delta = jnp.concatenate(
                [delta[:, :rows], delta[:, rows:] + prob_own * d_prob_own], axis=1
            )
            d_score = (prob * (d_prob - delta)).astype(LOW)
            d_own = (prob_own * (d_prob_own - delta[:, rows:])).astype(LOW).astype(WIDE)
            own_sums[head] = d_own
            mixed = dot(key_t[span], d_score)
            d_query_t.append(
                jnp.concatenate(
                    [mixed[:, :rows], mixed[:, rows:] + d_own * own_key_t[span]], axis=1
                )
            )
            d_scores.append(d_score)
            d_own_key.append(d_own * query_t[span, rows:])
            d_own_value.append(prob_own * d_ctx_t[span, rows:])
            wide = d_score.astype(WIDE)
            summed = wide[:, :rows] + wide[:, rows : 2 * rows] + wide[:, 2 * rows :]
            mirrored = dot(summed.astype(LOW), turned)
            for block in range(full // rows):
                piece = mirrored[block * rows : (block + 1) * rows]
                piece = jnp.concatenate([piece, jnp.zeros_like(piece)], axis=1)
                aligned = pltpu.roll(piece, 0, 1, stride=1, stride_axis=0)
                bias_sums[head, block : block + 1, :] = jnp.sum(aligned, axis=0, keepdims=True)
        d_query[:, cols] = (jnp.transpose(jnp.concatenate(d_query_t, axis=0)) * 0.125).astype(LOW)
        d_key[rows:, cols] = jnp.transpose(jnp.concatenate(d_own_key, axis=0)).astype(LOW)
        d_value[rows:, cols] = jnp.transpose(jnp.concatenate(d_own_value, axis=0)).astype(LOW)
        both = jnp.concatenate(d_scores, axis=1)
        split = jnp.concatenate([half_lanes(queries, 0), half_lanes(queries, 1)], axis=0)
        store_part(2, cols, dot(both, split))
        both = jnp.concatenate([kept[slot, 0], kept[slot, 1]], axis=1)
        split = jnp.concatenate([half_lanes(d_ctx, 0), half_lanes(d_ctx, 1)], axis=0)
        store_part(3, cols, dot(both, split))
        return carry

    lax.fori_loop(0, pairs, self_pair, 0)
    core_copy(2).start()
    core_copy(3).start()
    d_cross_key[...] = far_sum(0)
    d_cross_value[...] = far_sum(1)
    loads[6].wait()
    loads[7].wait()

    def source_body(cols):
        grad = dot(d_cross_key[...], c_key[cols, :], NT)
        grad = grad + dot(d_cross_value[...], c_value[cols, :], NT)
        encoded_grad[:, cols] = grad.astype(LOW)

    tiles(width // 256, 256, source_body)
    near_sum(2)
    near_sum(3)
    loads[3].wait()

    def query_body(cols):
        d_resid[:, cols] += dot(d_query[...], w_query[cols, :], NT)

    tiles(width // 256, 256, query_body)
    d_key[:rows, :] = far_sum(2)
    d_value[:rows, :] = far_sum(3)
    loads[4].wait()
    loads[5].wait()

    def last_body(cols):
        grad = d_resid[:, cols] + dot(d_key[...], w_key[cols, :], NT)
        grad = grad + dot(d_value[...], w_value[cols, :], NT)
        stream_grad[:, cols] = grad.astype(LOW)

    tiles(width // 256, 256, last_body)
    for index in range(4):
        core_copy(index).wait_send()
        far_copy(index).wait_send()


def rear(acts, gain_one, weights, cross_probs, probs):
    d_crossed, d_resid_two, cross_key = acts[:3]
    tokens, width = d_crossed.shape
    full = cross_key.shape[0]
    rows = tokens // 3
    shape = jax.ShapeDtypeStruct
    vmem = pl.BlockSpec(memory_space=pltpu.VMEM)
    hbm = pl.BlockSpec(memory_space=pl.ANY)
    sem = pltpu.SemaphoreType.DMA
    blocks = full // rows
    return pl.pallas_call(
        rear_kernel,
        out_shape=[
            shape((tokens, width), LOW),
            shape((rows, width), LOW),
            shape((rows, width), LOW),
            shape((rows, width), LOW),
            shape((tokens, width), LOW),
            shape((tokens, width), LOW),
            shape((tokens, width), LOW),
            shape((tokens, width), LOW),
            shape((tokens, width), LOW),
            shape((2, width), WIDE),
            shape((HEADS, blocks, 2 * rows), WIDE),
            shape((HEADS, 1, tokens - rows), WIDE),
        ],
        in_specs=[vmem] * 13 + [hbm] * 10,
        out_specs=[vmem] * 12,
        scratch_shapes=[pltpu.VMEM(w.shape, LOW) for w in weights]
        + [
            pltpu.VMEM((2, 2, full, tokens), LOW),
            pltpu.VMEM((tokens, width), LOW),
            pltpu.VMEM((tokens, width), WIDE),
            pltpu.VMEM((4, blocks, rows, width), LOW),
            pltpu.VMEM((4, 2, rows, width), LOW),
            pltpu.VMEM((4, rows, width), LOW),
            sem((8,)),
            sem((2,)),
            sem((4,)),
            sem((4,)),
            sem((4,)),
            sem((4,)),
        ],
        compiler_params=pltpu.CompilerParams(
            collective_id=2, has_side_effects=True, vmem_limit_bytes=60 << 20
        ),
    )(*acts, gain_one, *weights, cross_probs, probs)


MESH_ID = pl.DeviceIdType.MESH


def tile_dot(x_ref, x_start, y_ref, y_start, rows):
    left = x_ref[:, pl.ds(x_start, rows)]
    right = y_ref[:, pl.ds(y_start, COLS)]
    return lax.dot_general(
        left, right, (((0,), (0,)), ((), ())), preferred_element_type=jnp.float32
    )


def reduce_kernel(units, num_in, num_out, dp_size, *refs):
    ins, small_ref = refs[:num_in], refs[num_in]
    outs, small_out = refs[num_in + 1 : num_in + 1 + num_out], refs[num_in + 1 + num_out]
    sent, core_in, first_y, first_x, second, third, small_in = refs[num_in + num_out + 2 : -10]
    sems = refs[-10:]
    core_s, core_r, one_s, one_r, two_s, two_r, three_s, three_r, small_s, small_r = sems
    dp, sq = lax.axis_index("dp"), lax.axis_index("seq")
    core, ypos = sq % 2, sq // 2
    xpos, zpos = dp % 2, dp // 2
    depth = dp_size // 2
    chunk = 1024 // dp_size
    core_peer = (dp, sq + 1 - 2 * core)
    y_peer = (dp, sq + 2 - 4 * ypos)
    x_peer = (dp + 1 - 2 * xpos, sq)

    def z_peer(step):
        return ((zpos + step) % depth * 2 + xpos, sq)

    barrier = pltpu.get_barrier_semaphore()
    for peer in [core_peer, y_peer, x_peer] + [z_peer(step) for step in range(1, depth)]:
        pl.semaphore_signal(barrier, inc=1, device_id=peer, device_id_type=MESH_ID)
    pl.semaphore_wait(barrier, 2 + depth)

    def remote(src, dst, send_sem, recv_sem, peer):
        return pltpu.make_async_remote_copy(
            src_ref=src,
            dst_ref=dst,
            send_sem=send_sem,
            recv_sem=recv_sem,
            device_id=peer,
            device_id_type=MESH_ID,
        )

    def half_dots(unit, half, write):
        x_id, y_id, kind, part = units[unit]
        x_ref, y_ref = ins[x_id], ins[y_id]
        rows = chunk if kind == "back" else 256

        def body(step, carry):
            tile, side = step // 2, step % 2
            block = side * 2 + half
            x_start = tile * 256
            y_start = block * COLS
            if kind == "in":
                y_start = block * 1024 + part * COLS
            if kind == "back":
                x_start = tile * (4 * chunk) + part * chunk
            write(
                side,
                pl.ds(pl.multiple_of(tile * rows, rows), rows),
                tile_dot(
                    x_ref,
                    pl.multiple_of(x_start, 128),
                    y_ref,
                    pl.multiple_of(y_start, COLS),
                    rows,
                ),
            )
            return carry

        lax.fori_loop(0, 2 * (1024 // rows), body, 0)

    def core_copy(unit):
        return remote(
            sent.at[unit % SLOTS], core_in.at[unit], core_s.at[unit], core_r.at[unit], core_peer
        )

    def one_copy(unit):
        half = unit // 2
        if unit % 2 == 0:
            return remote(
                core_in.at[unit, 1 - ypos], first_y.at[half], one_s.at[unit], one_r.at[unit], y_peer
            )
        source = core_in.at[unit].reshape(2, depth, 2, chunk, COLS)
        return remote(
            source.at[:, :, 1 - xpos], first_x.at[half], one_s.at[unit], one_r.at[unit], x_peer
        )

    def two_copy(unit):
        half = unit // 2
        if unit % 2 == 0:
            source = first_y.at[half].reshape(depth, 2, chunk, COLS)
            return remote(
                source.at[:, 1 - xpos], second.at[unit], two_s.at[unit], two_r.at[unit], x_peer
            )
        return remote(
            first_x.at[half, 1 - ypos], second.at[unit], two_s.at[unit], two_r.at[unit], y_peer
        )

    def three_copy(unit, step):
        return remote(
            second.at[unit, (zpos + step) % depth],
            third.at[unit, step - 1],
            three_s.at[unit, step - 1],
            three_r.at[unit, step - 1],
            z_peer(step),
        )

    def products(unit):
        slot = unit % SLOTS
        if unit >= SLOTS:
            core_copy(unit - SLOTS).wait_send()

        def write(side, rows, value):
            sent[slot, side, rows, :] = value.astype(jnp.bfloat16)

        half_dots(unit, 1 - core, write)
        core_copy(unit).start()

    def core_sum(unit):
        core_copy(unit).wait_recv()

        def write(side, rows, value):
            old = core_in[unit, side, rows, :].astype(jnp.float32)
            core_in[unit, side, rows, :] = (value + old).astype(jnp.bfloat16)

        half_dots(unit, core, write)
        one_copy(unit).start()

    def plus(left, right):
        return (left.astype(jnp.float32) + right.astype(jnp.float32)).astype(jnp.bfloat16)

    def one_sum(unit):
        one_copy(unit).wait_recv()
        half = unit // 2
        if unit % 2 == 0:

            def body(step, carry):
                rows = pl.ds(pl.multiple_of(step * 128, 128), 128)
                first_y[half, rows, :] = plus(first_y[half, rows, :], core_in[unit, ypos, rows, :])
                return carry

            lax.fori_loop(0, 8, body, 0)
        else:
            def body(step, carry):
                side, layer = step // depth, step % depth
                rows = pl.ds(pl.multiple_of((layer * 2 + xpos) * chunk, chunk), chunk)
                first_x[half, side, layer] = plus(
                    first_x[half, side, layer], core_in[unit, side, rows, :]
                )
                return carry

            lax.fori_loop(0, 2 * depth, body, 0)
        two_copy(unit).start()

    def two_sum(unit):
        two_copy(unit).wait_recv()
        half = unit // 2

        def body(layer, carry):
            if unit % 2 == 0:
                rows = pl.ds(pl.multiple_of((layer * 2 + xpos) * chunk, chunk), chunk)
                old = first_y[half, rows, :]
            else:
                old = first_x[half, ypos, layer]
            second[unit, layer] = plus(second[unit, layer], old)
            return carry

        lax.fori_loop(0, depth, body, 0)

        def send(step, carry):
            three_copy(unit, step).start()
            return carry

        lax.fori_loop(1, depth, send, 0)

    def last_sum(unit):
        def body(step, total):
            three_copy(unit, step).wait_recv()
            return total + third[unit, step - 1].astype(jnp.float32)

        total = lax.fori_loop(1, depth, body, second[unit, zpos].astype(jnp.float32))
        x_id, y_id, kind, part = units[unit]
        if kind == "in":
            outs[8][:, part * COLS : (part + 1) * COLS] = total
        elif kind in ("back", "parted"):
            outs[9][part * chunk : (part + 1) * chunk, :] = total
        else:
            outs[part][...] = total

    bits = 0
    while (1 << bits) < dp_size:
        bits += 1
    small_out[...] = small_ref[...]

    def small_copy(step):
        if step == 0:
            peer = core_peer
        elif step == 1:
            peer = y_peer
        else:
            flip = 1 << (step - 2)
            peer = (dp + flip - 2 * flip * (dp // flip % 2), sq)
        return remote(small_out, small_in.at[step], small_s.at[step], small_r.at[step], peer)

    def small_step(step):
        small_copy(step).wait()
        small_out[...] = small_out[...] + small_in[step]

    count = len(units)
    pairs = count // 2
    small_copy(0).start()
    for turn in range(pairs + 5):
        for unit in (2 * turn, 2 * turn + 1):
            if unit < count:
                products(unit)
        for unit in (2 * turn - 2, 2 * turn - 1):
            if 0 <= unit < count:
                core_sum(unit)
        for unit in (2 * turn - 4, 2 * turn - 3):
            if 0 <= unit < count:
                one_sum(unit)
        for unit in (2 * turn - 6, 2 * turn - 5):
            if 0 <= unit < count:
                two_sum(unit)
        for unit in (2 * turn - 8, 2 * turn - 7):
            if 0 <= unit < count:
                last_sum(unit)
        if turn < bits + 2:
            small_step(turn)
            if turn + 1 < bits + 2:
                small_copy(turn + 1).start()
    for step in range(pairs + 5, bits + 2):
        small_step(step)
        if step + 1 < bits + 2:
            small_copy(step + 1).start()
    for unit in range(count):
        if unit >= count - SLOTS:
            core_copy(unit).wait_send()
        one_copy(unit).wait_send()
        two_copy(unit).wait_send()

        def drain(step, carry):
            three_copy(unit, step).wait_send()
            return carry

        lax.fori_loop(1, depth, drain, 0)


def reduce_grads(units, operands, small, dp_size):
    count = len(units)
    depth, chunk = dp_size // 2, 1024 // dp_size
    bits = dp_size.bit_length() - 1
    low = jnp.bfloat16
    out_shapes = [jax.ShapeDtypeStruct((chunk, COLS), jnp.float32)] * 8
    out_shapes.append(jax.ShapeDtypeStruct((chunk, 4 * COLS), jnp.float32))
    out_shapes.append(jax.ShapeDtypeStruct((4 * chunk, COLS), jnp.float32))
    out_shapes.append(jax.ShapeDtypeStruct(small.shape, jnp.float32))
    sem = pltpu.SemaphoreType.DMA
    vmem = pl.BlockSpec(memory_space=pltpu.VMEM)
    return pl.pallas_call(
        functools.partial(reduce_kernel, units, len(operands), 10, dp_size),
        out_shape=out_shapes,
        in_specs=[vmem] * (len(operands) + 1),
        out_specs=[vmem] * 11,
        scratch_shapes=[
            pltpu.VMEM((SLOTS, 2, 1024, COLS), low),
            pltpu.VMEM((count, 2, 1024, COLS), low),
            pltpu.VMEM((count // 2, 1024, COLS), low),
            pltpu.VMEM((count // 2, 2, depth, chunk, COLS), low),
            pltpu.VMEM((count, depth, chunk, COLS), low),
            pltpu.VMEM((count, depth - 1, chunk, COLS), low),
            pltpu.VMEM((bits + 2,) + small.shape, jnp.float32),
            sem((count,)),
            sem((count,)),
            sem((count,)),
            sem((count,)),
            sem((count,)),
            sem((count,)),
            sem((count, depth - 1)),
            sem((count, depth - 1)),
            sem((bits + 2,)),
            sem((bits + 2,)),
        ],
        compiler_params=pltpu.CompilerParams(
            collective_id=0, has_side_effects=True, vmem_limit_bytes=60 << 20
        ),
    )(*operands, small)


def per_device(
    stream,
    encoded,
    cotangent,
    lengths,
    bucket_table,
    w_query,
    w_key,
    w_value,
    w_out,
    c_query,
    c_key,
    c_value,
    c_out,
    w_in,
    w_back,
    gain_one,
    shift_one,
    gain_two,
    shift_two,
    gain_three,
    shift_three,
    position_bias,
):
    num_rows, num_streams, local_len, model_width = stream.shape
    full_len = local_len * lax.axis_size("seq")
    sq = lax.axis_index("seq")
    dp_size = lax.axis_size("dp")
    chunk = model_width // dp_size
    bucket_ids = jnp.arange(NBUCKET, dtype=jnp.int32)
    exact = lax.Precision.HIGHEST
    table_hot = (bucket_table[:, None] == bucket_ids[None, :]).astype(jnp.float32)
    by_distance = jnp.einsum("db,bh->hd", table_hot, position_bias, precision=exact)
    bias_table = jnp.concatenate([jnp.zeros_like(by_distance), by_distance], axis=1)[:, None, :]
    flat_rows = stream.reshape(-1, model_width)
    source_rows = encoded.reshape(-1, model_width)
    flat_cotangent = cotangent.reshape(-1, model_width)

    def line(values):
        return values.reshape(1, model_width)

    fronts = front(
        stream.reshape(num_streams, local_len, model_width),
        source_rows,
        lengths,
        bias_table,
        (line(gain_one), line(shift_one), line(gain_two), line(shift_two)),
        (w_query, w_key, w_value, w_out, c_query, c_key, c_value, c_out),
    )
    query, own_key, own_value, main_key, main_value, context_low, resid_one, first_norm = fronts[:8]
    cross_query, cross_key, cross_value, cross_low, resid_two, second_norm = fronts[8:14]
    own_probs, front_stats, probs, cross_probs = fronts[14:]
    layer_output, activated, d_ffn_out, d_inner, d_resid_two, d_crossed, mid_grads, ffn_stat = middle(
        second_norm,
        resid_two,
        flat_cotangent,
        lengths,
        line(gain_two),
        line(gain_three),
        line(shift_three),
        w_in,
        w_back,
    )
    rears = rear(
        (
            d_crossed,
            d_resid_two,
            cross_key,
            cross_value,
            cross_query,
            resid_one,
            main_key,
            main_value,
            query,
            own_key,
            own_value,
            own_probs,
        ),
        line(gain_one),
        (c_out, c_query, w_out, w_query, w_key, w_value, c_key, c_value),
        cross_probs,
        probs,
    )
    d_cross_query, d_cross_key, d_cross_value, encoded_grad, d_attended = rears[:5]
    d_query_low, d_keys, d_values, stream_grad, rear_grads, bias_sums, own_sums = rears[5:]

    blocks = full_len // local_len
    place = jnp.arange(2 * local_len, dtype=jnp.int32)
    reach = (sq - jnp.arange(blocks, dtype=jnp.int32))[:, None] * local_len + (
        local_len - 1 - place[None, :]
    )
    first_of = jnp.sum((bucket_table[:, None] < bucket_ids[None, :]).astype(jnp.int32), axis=0)
    next_of = jnp.sum((bucket_table[:, None] <= bucket_ids[None, :]).astype(jnp.int32), axis=0)
    window_hot = (reach[..., None] >= first_of) & (reach[..., None] < next_of)
    table_part = jnp.einsum(
        "hkv,kvb->bh", bias_sums, window_hot.astype(jnp.float32), precision=exact
    )
    own_hot = (bucket_ids == bucket_table[0]).astype(jnp.float32)
    table_part = table_part + own_hot[:, None] * jnp.sum(own_sums, axis=(1, 2))[None, :]
    position = sq * local_len + jnp.arange(local_len)
    count = num_streams * jnp.sum((position < lengths[0]).astype(jnp.float32))
    stats = jnp.concatenate([jnp.sum(front_stats, axis=1), jnp.sum(ffn_stat, axis=1), count[None]])
    tail = jnp.concatenate([table_part.reshape(-1), stats, jnp.zeros((507,), jnp.float32)])
    small = jnp.concatenate([rear_grads, mid_grads, tail[None], jnp.zeros_like(tail)[None]])
    units = []
    operands = [d_ffn_out, second_norm, d_inner, cross_low, d_crossed, first_norm, d_cross_query]
    operands += [source_rows, d_cross_key, d_cross_value, context_low, d_attended]
    operands += [flat_rows, d_query_low, d_keys, d_values]
    if chunk % 128 == 0:
        operands.append(activated)
        for part in range(4):
            units.append((16, 0, "back", part))
    else:
        parted = jnp.transpose(activated.reshape(-1, dp_size, 4, chunk), (2, 0, 1, 3))
        parted = parted.reshape(4, -1, model_width)
        for part in range(4):
            operands.append(parted[part])
            units.append((16 + part, 0, "parted", part))
    for part in range(4):
        units.append((1, 2, "in", part))
    units += [(3, 4, "", 7), (5, 6, "", 4), (7, 8, "", 5), (7, 9, "", 6), (10, 11, "", 3)]
    units += [(12, 13, "", 0), (12, 14, "", 1), (12, 15, "", 2)]
    reduced = reduce_grads(tuple(units), operands, small, dp_size)
    shares, sums = reduced[:10], reduced[10]
    rms = jnp.sqrt(sums[6, 512:516] / (sums[6, 516] * model_width))
    return (
        layer_output.reshape(stream.shape),
        stream_grad.reshape(stream.shape),
        encoded_grad.reshape(encoded.shape),
        shares[0],
        shares[1],
        shares[2],
        shares[3],
        shares[4],
        shares[5],
        shares[6],
        shares[7],
        shares[8],
        shares[9],
        sums[0],
        sums[1],
        sums[2],
        sums[3],
        sums[4],
        sums[5],
        sums[6, :512].reshape(NBUCKET, HEADS),
        rms,
    )


def solution(mesh):
    placed = (
        P("dp", None, "seq", None),
        P("dp", "seq", None),
        P("dp", None, "seq", None),
        P("dp"),
        P(),
        P(),
        P(),
        P(),
        P(),
        P(),
        P(),
        P(),
        P(),
        P(),
        P(),
        P(),
        P(),
        P(),
        P(),
        P(),
        P(),
        P(),
    )
    return jax.shard_map(
        per_device,
        mesh=mesh,
        in_specs=placed,
        out_specs=(
            P("dp", None, "seq", None),
            P("dp", None, "seq", None),
            P("dp", "seq", None),
            P("dp", "seq"),
            P("dp", "seq"),
            P("dp", "seq"),
            P("dp", "seq"),
            P("dp", "seq"),
            P("dp", "seq"),
            P("dp", "seq"),
            P("dp", "seq"),
            P("dp", "seq"),
            P("dp", "seq"),
            P(),
            P(),
            P(),
            P(),
            P(),
            P(),
            P(),
            P(),
        ),
        check_vma=False,
    )
```

```python
import functools

import jax
import jax.numpy as jnp
from jax import lax
from jax.experimental import pallas as pl
from jax.experimental.pallas import tpu as pltpu
from jax.sharding import PartitionSpec as P

HEADS = 16
HEAD_DIM = 64
NBUCKET = 32
COLS = 256
SLOTS = 3
RING = 6
LATE = 8
epsilon = 1e-05
masked_score = -1e30


LOW = jnp.bfloat16
WIDE = jnp.float32
NN = (((1,), (0,)), ((), ()))
NT = (((1,), (1,)), ((), ()))


def dot(left, right, dims=NN):
    return lax.dot_general(left, right, dims, preferred_element_type=WIDE)


def flip(block):
    return jnp.transpose(block.astype(WIDE))


def places():
    dp, sq = lax.axis_index("dp"), lax.axis_index("seq")
    core, ypos = sq % 2, sq // 2
    return dp, sq, core, ypos, (dp, sq + 1 - 2 * core), (dp, sq + 2 - 4 * ypos)


def remote_copy(src, dst, send_sem, recv_sem, peer):
    return pltpu.make_async_remote_copy(
        src_ref=src,
        dst_ref=dst,
        send_sem=send_sem,
        recv_sem=recv_sem,
        device_id=peer,
        device_id_type=MESH_ID,
    )


def greet(peers):
    barrier = pltpu.get_barrier_semaphore()
    for peer in peers:
        pl.semaphore_signal(barrier, inc=1, device_id=peer, device_id_type=MESH_ID)
    pl.semaphore_wait(barrier, len(peers))


def tiles(count, size, body):
    def step(index, carry):
        body(pl.ds(pl.multiple_of(index * size, size), size))
        return carry

    lax.fori_loop(0, count, step, 0)


def project_to(dst, left, weight, scale=None):
    def body(cols):
        product = dot(left[...], weight[:, cols])
        if scale is not None:
            product = product * scale
        dst[:, cols] = product.astype(dst.dtype)

    tiles(dst.shape[1] // 256, 256, body)


def norm_stats(rows):
    centre = jnp.mean(rows, axis=-1, keepdims=True)
    centred = rows - centre
    spread = jnp.mean(centred * centred, axis=-1, keepdims=True)
    return centred, lax.rsqrt(spread + epsilon)


def norm_backward(rows, gain, incoming):
    centred, scale = norm_stats(rows)
    unit = centred * scale
    scaled = incoming * gain
    first = jnp.mean(scaled, axis=-1, keepdims=True)
    second = jnp.mean(scaled * unit, axis=-1, keepdims=True)
    grads = scale * (scaled - first - unit * second)
    d_gain = jnp.sum(incoming * unit, axis=0, keepdims=True)
    return grads, d_gain, jnp.sum(incoming, axis=0, keepdims=True)


def valid_rows(sq, length, count):
    position = sq * count + lax.broadcasted_iota(jnp.int32, (count, 1), 0)
    return (position < length).astype(WIDE)


def sum_squares(rows, mask):
    return jnp.sum(rows * rows * mask, axis=0, keepdims=True)


def half_rows(block, side):
    row = lax.broadcasted_iota(jnp.int32, block.shape, 0)
    return jnp.where(row // HEAD_DIM == side, block, 0.0).astype(LOW)


def half_lanes(block, side):
    lane = lax.broadcasted_iota(jnp.int32, block.shape, 1)
    return jnp.where(lane // HEAD_DIM == side, block.astype(WIDE), 0.0).astype(LOW)


def front_kernel(*refs):
    stream, encoded, length_ref, bias_table = refs[:4]
    gain_one, shift_one, gain_two, shift_two = refs[4:8]
    hbm_weights = refs[8:16]
    (query, own_key, own_value, main_key, main_value, context, resid_one, first_norm) = refs[16:24]
    (cross_query, cross_key, cross_value, cross_context, resid_two, second_norm) = refs[24:30]
    own_probs, stats, probs_out, cross_probs_out = refs[30:34]
    weights = refs[34:42]
    main_all, source_all, kept, bias, masks = refs[42:47]
    weight_sem, kept_sem, send_sem, recv_sem = refs[47:]
    w_query, w_key, w_value, w_out, c_query, c_key, c_value, c_out = weights
    dp, sq, core, ypos, core_peer, y_peer = places()
    length = length_ref[0]
    rows = stream.shape[1]
    full = main_all.shape[0] * rows
    loads = [
        pltpu.make_async_copy(src, dst, weight_sem.at[index])
        for index, (src, dst) in enumerate(zip(hbm_weights, weights))
    ]
    for load in loads:
        load.start()
    greet([core_peer, y_peer])
    sources = (stream.at[0], encoded)
    gathered = (main_all, source_all)
    firsts = []
    for index in range(2):
        for lane, peer in enumerate((y_peer, core_peer)):
            slot = index * 3 + lane
            firsts.append(
                remote_copy(
                    sources[index],
                    gathered[index].at[sq],
                    send_sem.at[slot],
                    recv_sem.at[slot],
                    peer,
                )
            )
            firsts[-1].start()
    main_all[sq] = stream[0]
    source_all[sq] = encoded[...]

    def passed_on(index):
        other = gathered[index].at[sq + 2 - 4 * ypos]
        slot = index * 3 + 2
        return remote_copy(other, other, send_sem.at[slot], recv_sem.at[slot], core_peer)

    flat = stream.reshape(3 * rows, stream.shape[2])
    loads[0].wait()
    project_to(query, flat, w_query, 0.125)
    firsts[0].wait_recv()
    passed_on(0).start()
    predicting = flat.at[rows:, :]
    loads[1].wait()
    project_to(own_key, predicting, w_key)
    loads[2].wait()
    project_to(own_value, predicting, w_value)
    firsts[1].wait_recv()
    passed_on(0).wait_recv()
    firsts[2].wait_recv()
    passed_on(1).start()
    wide_main = main_all.reshape(full, main_all.shape[2])
    project_to(main_key, wide_main, w_key)
    project_to(main_value, wide_main, w_value)

    key_row = lax.broadcasted_iota(jnp.int32, (full, rows), 0)
    distance = sq * rows + lax.broadcasted_iota(jnp.int32, (full, rows), 1) - key_row
    in_range = key_row < length
    masks[0] = jnp.where((distance >= 0) & in_range, 0.0, masked_score)
    masks[1] = jnp.where((distance > 0) & in_range, 0.0, masked_score)
    masks[2] = jnp.where(in_range, 0.0, masked_score)

    def kept_copy(pair, out):
        slot = pair % 2
        return pltpu.make_async_copy(kept.at[slot], out.at[pair], kept_sem.at[slot])

    def self_pair(pair, carry):
        @pl.when(pair >= 2)
        def _():
            kept_copy(pair - 2, probs_out).wait()

        slot = pair % 2
        cols = pl.ds(pl.multiple_of(pair * 128, 128), 128)
        keys = main_key[:, cols]
        query_t = flip(query[:, cols])
        value_t = flip(main_value[:, cols]).astype(LOW)
        own_key_t, own_value_t = flip(own_key[:, cols]), flip(own_value[:, cols])
        own_product = query_t[:, rows:] * own_key_t
        sides = []
        for side in range(2):
            head = 2 * pair + side
            span = slice(side * HEAD_DIM, (side + 1) * HEAD_DIM)
            scores = dot(keys, half_rows(query_t, side))
            own_bias = bias_table[head, :, full : full + 128][:, 0:1]
            own_score = jnp.sum(own_product[span], axis=0, keepdims=True) + own_bias
            for block in range(full // rows):
                start = pl.multiple_of((sq - block + full // rows - 1) * rows, 128)
                line = bias_table[head, :, pl.ds(start, 2 * rows)]
                wide = jnp.broadcast_to(line, (rows, 2 * rows))
                near = pltpu.roll(wide, 0, 1, stride=1, stride_axis=0)[:, rows:]
                part = slice(block * rows, (block + 1) * rows)
                for kind in range(2):
                    bias[kind, part, :] = near + masks[kind, part, :]
            owns = []
            for stream_id in range(3):
                lanes = slice(stream_id * rows, (stream_id + 1) * rows)
                score = scores[:, lanes] + bias[min(stream_id, 1)]
                top = jnp.max(score, axis=0, keepdims=True)
                if stream_id > 0:
                    own = own_score[:, (stream_id - 1) * rows : stream_id * rows]
                    top = jnp.maximum(top, own)
                expo = jnp.exp(score - top)
                total = jnp.sum(expo, axis=0, keepdims=True)
                if stream_id > 0:
                    expo_own = jnp.exp(own - top)
                    total = total + expo_own
                share = 1.0 / total
                kept[slot, side, :, lanes] = (expo * share).astype(LOW)
                owns.append(expo_own * share if stream_id > 0 else jnp.zeros_like(total))
            own_probs[head] = jnp.concatenate(owns, axis=1)
            mixed = dot(value_t[span], kept[slot, side])
            mixed_own = jnp.concatenate(owns[1:], axis=1) * own_value_t[span]
            sides.append(
                jnp.concatenate([mixed[:, :rows], mixed[:, rows:] + mixed_own], axis=1)
            )
        context[:, cols] = jnp.transpose(jnp.concatenate(sides, axis=0)).astype(LOW)
        kept_copy(pair, probs_out).start()
        return carry

    lax.fori_loop(0, HEADS // 2, self_pair, 0)
    for pair in range(HEADS // 2 - 2, HEADS // 2):
        kept_copy(pair, probs_out).wait()

    mask = valid_rows(sq, length, rows)
    loads[3].wait()
    project_to(resid_one, context, w_out)
    seen = jnp.zeros((1, stream.shape[2]), WIDE)
    branch = jnp.zeros((1, stream.shape[2]), WIDE)
    for stream_id in range(3):
        part = slice(stream_id * rows, (stream_id + 1) * rows)
        source, attended = stream[stream_id].astype(WIDE), resid_one[part, :]
        seen = seen + sum_squares(source, mask)
        branch = branch + sum_squares(attended, mask)
        total = source + attended
        resid_one[part, :] = total
        centred, scale = norm_stats(total)
        first_norm[part, :] = (centred * scale * gain_one[...] + shift_one[...]).astype(LOW)
    stats[0:1, :] = seen
    stats[1:2, :] = branch
    loads[4].wait()
    project_to(cross_query, first_norm, c_query, 0.125)
    firsts[3].wait_recv()
    passed_on(1).wait_recv()
    wide_source = source_all.reshape(full, source_all.shape[2])
    loads[5].wait()
    project_to(cross_key, wide_source, c_key)
    loads[6].wait()
    project_to(cross_value, wide_source, c_value)

    def cross_pair(pair, carry):
        @pl.when(pair >= 2)
        def _():
            kept_copy(pair - 2, cross_probs_out).wait()

        slot = pair % 2
        cols = pl.ds(pl.multiple_of(pair * 128, 128), 128)
        keys = cross_key[:, cols]
        query_t = flip(cross_query[:, cols])
        value_t = flip(cross_value[:, cols]).astype(LOW)
        sides = []
        for side in range(2):
            span = slice(side * HEAD_DIM, (side + 1) * HEAD_DIM)
            scores = dot(keys, half_rows(query_t, side))
            for stream_id in range(3):
                lanes = slice(stream_id * rows, (stream_id + 1) * rows)
                score = scores[:, lanes] + masks[2]
                expo = jnp.exp(score - jnp.max(score, axis=0, keepdims=True))
                share = 1.0 / jnp.sum(expo, axis=0, keepdims=True)
                kept[slot, side, :, lanes] = (expo * share).astype(LOW)
            sides.append(dot(value_t[span], kept[slot, side]))
        cross_context[:, cols] = jnp.transpose(jnp.concatenate(sides, axis=0)).astype(LOW)
        kept_copy(pair, cross_probs_out).start()
        return carry

    lax.fori_loop(0, HEADS // 2, cross_pair, 0)
    for pair in range(HEADS // 2 - 2, HEADS // 2):
        kept_copy(pair, cross_probs_out).wait()
    loads[7].wait()
    project_to(resid_two, cross_context, c_out)
    branch = jnp.zeros((1, stream.shape[2]), WIDE)
    for stream_id in range(3):
        part = slice(stream_id * rows, (stream_id + 1) * rows)
        crossed = resid_two[part, :]
        branch = branch + sum_squares(crossed, mask)
        total = first_norm[part, :].astype(WIDE) + crossed
        resid_two[part, :] = total
        centred, scale = norm_stats(total)
        second_norm[part, :] = (centred * scale * gain_two[...] + shift_two[...]).astype(LOW)
    stats[2:3, :] = branch
    for copy in firsts:
        copy.wait_send()
    for index in range(2):
        passed_on(index).wait_send()


def front(stream, encoded, length, bias_table, norms, weights):
    streams, rows, width = stream.shape
    seq = lax.axis_size("seq")
    full, tokens = seq * rows, streams * rows
    own = tokens - rows
    shape = jax.ShapeDtypeStruct
    pairs = HEADS // 2
    outs = [
        shape((tokens, width), LOW),
        shape((own, width), LOW),
        shape((own, width), LOW),
        shape((full, width), LOW),
        shape((full, width), LOW),
        shape((tokens, width), LOW),
        shape((tokens, width), WIDE),
        shape((tokens, width), LOW),
        shape((tokens, width), LOW),
        shape((full, width), LOW),
        shape((full, width), LOW),
        shape((tokens, width), LOW),
        shape((tokens, width), WIDE),
        shape((tokens, width), LOW),
        shape((HEADS, 1, tokens), WIDE),
        shape((3, width), WIDE),
        shape((pairs, 2, full, tokens), LOW),
        shape((pairs, 2, full, tokens), LOW),
    ]
    vmem = pl.BlockSpec(memory_space=pltpu.VMEM)
    smem = pl.BlockSpec(memory_space=pltpu.SMEM)
    hbm = pl.BlockSpec(memory_space=pl.ANY)
    sem = pltpu.SemaphoreType.DMA
    return pl.pallas_call(
        front_kernel,
        out_shape=outs,
        in_specs=[vmem, vmem, smem] + [vmem] * 5 + [hbm] * 8,
        out_specs=[vmem] * 16 + [hbm] * 2,
        scratch_shapes=[pltpu.VMEM(w.shape, LOW) for w in weights]
        + [
            pltpu.VMEM((seq, rows, width), LOW),
            pltpu.VMEM((seq, rows, width), LOW),
            pltpu.VMEM((2, 2, full, tokens), LOW),
            pltpu.VMEM((2, full, rows), WIDE),
            pltpu.VMEM((3, full, rows), WIDE),
            sem((8,)),
            sem((2,)),
            sem((6,)),
            sem((6,)),
        ],
        compiler_params=pltpu.CompilerParams(
            collective_id=1, has_side_effects=True, vmem_limit_bytes=60 << 20
        ),
    )(stream, encoded, length, bias_table, *norms, *weights)


def middle_kernel(*refs):
    second_norm, resid_two, cotangent, length_ref, gain_two, gain_three, shift_three = refs[:7]
    hbm_in, hbm_back = refs[7:9]
    output, activated, d_ffn, d_inner, d_resid, d_crossed, grads, stats = refs[9:17]
    w_in, w_back, slope, total, load_sem = refs[17:]
    sq = lax.axis_index("seq")
    length = length_ref[0]
    tokens, width = second_norm.shape
    rows = tokens // 3
    hidden = w_in.shape[1]
    size = 512
    steps = hidden // size

    def load_in(step):
        cols = pl.ds(pl.multiple_of(step * size, size), size)
        return pltpu.make_async_copy(hbm_in.at[:, cols], w_in.at[:, cols], load_sem.at[0, step])

    def load_back(step):
        cols = pl.ds(pl.multiple_of(step * size, size), size)
        return pltpu.make_async_copy(hbm_back.at[cols], w_back.at[cols], load_sem.at[1, step])

    for step in range(steps):
        load_in(step).start()
        load_back(step).start()
    total[...] = jnp.zeros_like(total)

    def forward(step, carry):
        cols = pl.ds(pl.multiple_of(step * size, size), size)
        load_in(step).wait()
        inner = dot(second_norm[...], w_in[:, cols])
        phi = 0.5 + 0.5 * lax.erf(inner * (0.5**0.5))
        bell = jnp.exp(inner * inner * -0.5) * (0.5 / jnp.pi) ** 0.5
        value = (inner * phi).astype(LOW)
        activated[:, cols] = value
        slope[:, cols] = (phi + inner * bell).astype(LOW)
        load_back(step).wait()
        total[...] += dot(value, w_back[cols, :])
        return carry

    lax.fori_loop(0, steps, forward, 0)
    mask = valid_rows(sq, length, rows)
    branch = jnp.zeros((1, width), WIDE)
    d_gain = jnp.zeros((1, width), WIDE)
    d_shift = jnp.zeros((1, width), WIDE)
    for stream_id in range(3):
        part = slice(stream_id * rows, (stream_id + 1) * rows)
        ffn = total[part, :]
        branch = branch + sum_squares(ffn, mask)
        resid = second_norm[part, :].astype(WIDE) + ffn
        centred, scale = norm_stats(resid)
        normed = centred * scale * gain_three[...] + shift_three[...]
        output[part, :] = (normed * mask).astype(LOW)
        incoming = cotangent[part, :].astype(WIDE) * mask
        back, gain_part, shift_part = norm_backward(resid, gain_three[...], incoming)
        d_gain, d_shift = d_gain + gain_part, d_shift + shift_part
        total[part, :] = back
        d_ffn[part, :] = back.astype(LOW)
    stats[...] = branch
    grads[2:3, :] = d_gain
    grads[3:4, :] = d_shift

    def backward(step, carry):
        cols = pl.ds(pl.multiple_of(step * size, size), size)
        d_act = dot(d_ffn[...], w_back[cols, :], NT)
        d_in = (d_act * slope[:, cols].astype(WIDE)).astype(LOW)
        d_inner[:, cols] = d_in
        total[...] += dot(d_in, w_in[:, cols], NT)
        return carry

    lax.fori_loop(0, steps, backward, 0)
    d_gain = jnp.zeros((1, width), WIDE)
    d_shift = jnp.zeros((1, width), WIDE)
    for stream_id in range(3):
        part = slice(stream_id * rows, (stream_id + 1) * rows)
        back, gain_part, shift_part = norm_backward(
            resid_two[part, :], gain_two[...], total[part, :]
        )
        d_gain, d_shift = d_gain + gain_part, d_shift + shift_part
        d_resid[part, :] = back
        d_crossed[part, :] = back.astype(LOW)
    grads[0:1, :] = d_gain
    grads[1:2, :] = d_shift


def middle(second_norm, resid_two, cotangent, length, gain_two, gain_three, shift_three, w_in, w_back):
    tokens, width = second_norm.shape
    hidden = w_in.shape[1]
    shape = jax.ShapeDtypeStruct
    vmem = pl.BlockSpec(memory_space=pltpu.VMEM)
    smem = pl.BlockSpec(memory_space=pltpu.SMEM)
    hbm = pl.BlockSpec(memory_space=pl.ANY)
    return pl.pallas_call(
        middle_kernel,
        out_shape=[
            shape((tokens, width), LOW),
            shape((tokens, hidden), LOW),
            shape((tokens, width), LOW),
            shape((tokens, hidden), LOW),
            shape((tokens, width), WIDE),
            shape((tokens, width), LOW),
            shape((4, width), WIDE),
            shape((1, width), WIDE),
        ],
        in_specs=[vmem] * 3 + [smem] + [vmem] * 3 + [hbm] * 2,
        out_specs=[vmem] * 8,
        scratch_shapes=[
            pltpu.VMEM(w_in.shape, LOW),
            pltpu.VMEM(w_back.shape, LOW),
            pltpu.VMEM((tokens, hidden), LOW),
            pltpu.VMEM((tokens, width), WIDE),
            pltpu.SemaphoreType.DMA((2, hidden // 512)),
        ],
        compiler_params=pltpu.CompilerParams(vmem_limit_bytes=60 << 20),
    )(second_norm, resid_two, cotangent, length, gain_two, gain_three, shift_three, w_in, w_back)


def rear_kernel(units, dp_size, *refs):
    d_crossed, cross_query, resid_one, query, own_key, own_value, own_probs, gain_one = refs[:8]
    d_ffn, second_norm, cross_context, first_norm, mid_grads, mid_stats, window_hot = refs[8:15]
    hbm_inner, hbm_activated, hbm_context, hbm_stream, hbm_source, hbm_resid = refs[15:21]
    hbm_sides, hbm_weights = refs[21:25], refs[25:33]
    cross_probs, probs = refs[33:35]
    encoded_grad, stream_grad, small_out = refs[35:38]
    shares, in_share, back_share = refs[38:46], refs[46], refs[47]
    (d_cross_query, d_cross_key, d_cross_value, d_attended) = refs[48:52]
    (d_query, d_key, d_value, bias_sums, small_in) = refs[52:57]
    d_inner, activated = refs[57:59]
    weights = refs[59:62]
    kept, d_context, d_resid, parts, near_in, far_in, sides_held = refs[62:69]
    weight_sem, kept_sem, core_s, core_r, far_s, far_r, small_s, small_r = refs[69:77]
    held = (0, 1, 2, 0, 1, 2, 1, 2)
    c_out, c_query, w_out, w_query, w_key, w_value, c_key, c_value = [weights[i] for i in held]
    chunk = 1024 // dp_size

    def emit(unit, total):
        part = unit[3]
        if unit[2] == "in":
            in_share[:, part * COLS : (part + 1) * COLS] = total
        elif unit[2] in ("back", "parted"):
            back_share[part * chunk : (part + 1) * chunk, :] = total
        else:
            shares[part][...] = total

    operands = (d_ffn, second_norm, d_inner, activated, cross_context, d_crossed, first_norm)
    operands += (d_cross_query, d_attended, d_cross_key, d_cross_value, d_query, d_key, d_value)
    turn, drain = reducer(units, operands, emit, refs[77:], dp_size)
    small_copy, small_step = small_sums(small_out, small_in, small_s, small_r, dp_size)
    dp, sq, core, ypos, core_peer, y_peer = places()
    tokens, width = query.shape
    rows = tokens // 3
    full = sides_held.shape[1]
    blocks = full // rows
    keys_held, values_held = sides_held.at[0], sides_held.at[1]
    pairs = HEADS // 2
    loads = [
        pltpu.make_async_copy(src, weights[held[index]], weight_sem.at[index])
        for index, src in enumerate(hbm_weights)
    ]

    def load_extra(index, src, dst):
        return pltpu.make_async_copy(src, dst, weight_sem.at[12 + index])

    early = [
        load_extra(0, hbm_activated, activated),
        load_extra(1, hbm_inner, d_inner),
        load_extra(2, hbm_resid, d_resid),
    ]
    late = [
        load_extra(3, hbm_context, activated.at[:, :width]),
        load_extra(4, hbm_stream, activated.at[:, width : 2 * width]),
        load_extra(5, hbm_source, activated.at[:rows, 2 * width : 3 * width]),
    ]

    def load_side(index):
        return pltpu.make_async_copy(
            hbm_sides[index], sides_held.at[index % 2], weight_sem.at[8 + index]
        )

    def fetch(pair, source, base):
        slot = (pair + base) % 2
        return pltpu.make_async_copy(source.at[pair], kept.at[slot], kept_sem.at[slot])

    early[0].start()
    early[1].start()
    loads[0].start()
    fetch(0, cross_probs, 0).start()
    load_side(0).start()
    load_side(1).start()
    loads[1].start()
    loads[2].start()
    early[2].start()
    greet(reduce_peers(dp_size))
    early[0].wait()
    early[1].wait()
    turn(0)
    turn(1)
    loads[0].wait()

    def back_to(dst, left, weight, add=False):
        def body(cols):
            product = dot(left[...], weight[cols, :], NT)
            if add:
                product = product + dst[:, cols]
            dst[:, cols] = product.astype(dst.dtype)

        tiles(width // 256, 256, body)

    back_to(d_context, d_crossed, c_out)
    loads[3].start()

    def core_copy(index):
        view = parts.at[index % 2].reshape(2, 2, rows, width)
        return remote_copy(
            view.at[:, 1 - core], near_in.at[index], core_s.at[index], core_r.at[index], core_peer
        )

    def far_copy(index):
        return remote_copy(
            near_in.at[index, 1 - ypos], far_in.at[index], far_s.at[index], far_r.at[index], y_peer
        )

    def near_sum(index):
        core_copy(index).wait_recv()
        for side in range(2):
            mine = parts[index % 2, side * 2 + core].astype(WIDE)
            near_in[index, side] = (near_in[index, side].astype(WIDE) + mine).astype(LOW)
        far_copy(index).start()

    def far_sum(index):
        far_copy(index).wait_recv()
        return (near_in[index, ypos].astype(WIDE) + far_in[index].astype(WIDE)).astype(LOW)

    def store_part(index, cols, block):
        for part in range(full // rows):
            parts[index % 2, part, :, cols] = block[part * rows : (part + 1) * rows].astype(LOW)

    def cross_pair(pair, carry):
        fetch(pair, cross_probs, 0).wait()

        @pl.when(pair + 1 < pairs)
        def _():
            fetch(pair + 1, cross_probs, 0).start()

        slot = pair % 2
        cols = pl.ds(pl.multiple_of(pair * 128, 128), 128)
        values = values_held[:, cols]
        key_t = flip(keys_held[:, cols]).astype(LOW)
        queries, d_ctx = cross_query[:, cols], d_context[:, cols]
        d_ctx_t = flip(d_ctx)
        d_query_t, d_scores = [], []
        for side in range(2):
            span = slice(side * HEAD_DIM, (side + 1) * HEAD_DIM)
            d_prob = dot(values, half_rows(d_ctx_t, side))
            prob = kept[slot, side].astype(WIDE)
            delta = jnp.sum(prob * d_prob, axis=0, keepdims=True)
            d_score = (prob * (d_prob - delta)).astype(LOW)
            d_query_t.append(dot(key_t[span], d_score))
            d_scores.append(d_score)
        d_cross_query[:, cols] = (
            jnp.transpose(jnp.concatenate(d_query_t, axis=0)) * 0.125
        ).astype(LOW)
        both = jnp.concatenate(d_scores, axis=1)
        split = jnp.concatenate([half_lanes(queries, 0), half_lanes(queries, 1)], axis=0)
        store_part(0, cols, dot(both, split))
        both = jnp.concatenate([kept[slot, 0], kept[slot, 1]], axis=1)
        split = jnp.concatenate([half_lanes(d_ctx, 0), half_lanes(d_ctx, 1)], axis=0)
        store_part(1, cols, dot(both, split))
        return carry

    load_side(0).wait()
    load_side(1).wait()
    lax.fori_loop(0, pairs // 2, cross_pair, 0)
    turn(2)
    lax.fori_loop(pairs // 2, pairs, cross_pair, 0)
    fetch(0, probs, 0).start()
    load_side(2).start()
    load_side(3).start()
    core_copy(0).start()
    core_copy(1).start()
    loads[1].wait()
    early[2].wait()
    back_to(d_resid, d_cross_query, c_query, True)
    loads[6].start()
    d_gain = jnp.zeros((1, width), WIDE)
    d_shift = jnp.zeros((1, width), WIDE)
    for stream_id in range(3):
        part = slice(stream_id * rows, (stream_id + 1) * rows)
        back, gain_part, shift_part = norm_backward(
            resid_one[part, :], gain_one[...], d_resid[part, :]
        )
        d_gain, d_shift = d_gain + gain_part, d_shift + shift_part
        d_resid[part, :] = back
        d_attended[part, :] = back.astype(LOW)
    lines = [d_gain, d_shift] + [mid_grads[row : row + 1, :] for row in range(4)]
    for row, line in enumerate(lines):
        for piece in range(8):
            small_out[8 * row + piece : 8 * row + piece + 1, :] = line[
                :, 128 * piece : 128 * (piece + 1)
            ]
    small_out[64:72, :] = mid_stats[...]
    small_out[72:80, :] = jnp.zeros((8, 128), WIDE)
    near_sum(0)
    near_sum(1)
    turn(3)
    loads[2].wait()
    back_to(d_context, d_attended, w_out)
    loads[7].start()
    core_copy(0).wait_send()
    core_copy(1).wait_send()
    line = lax.broadcasted_iota(jnp.int32, (rows, rows), 0)
    turned = (line + lax.broadcasted_iota(jnp.int32, (rows, rows), 1) == rows - 1).astype(LOW)

    def self_pair(pair, carry):
        fetch(pair, probs, 0).wait()

        @pl.when(pair + 1 < pairs)
        def _():
            fetch(pair + 1, probs, 0).start()

        slot = pair % 2
        cols = pl.ds(pl.multiple_of(pair * 128, 128), 128)
        values = values_held[:, cols]
        key_t = flip(keys_held[:, cols]).astype(LOW)
        queries, d_ctx = query[:, cols], d_context[:, cols]
        d_ctx_t, query_t = flip(d_ctx), flip(queries)
        own_key_t, own_value_t = flip(own_key[:, cols]), flip(own_value[:, cols])
        own_product = d_ctx_t[:, rows:] * own_value_t
        d_query_t, d_scores, d_own_key, d_own_value = [], [], [], []
        for side in range(2):
            head = 2 * pair + side
            span = slice(side * HEAD_DIM, (side + 1) * HEAD_DIM)
            d_prob = dot(values, half_rows(d_ctx_t, side))
            prob = kept[slot, side].astype(WIDE)
            prob_own = own_probs[head][:, rows:]
            d_prob_own = jnp.sum(own_product[span], axis=0, keepdims=True)
            delta = jnp.sum(prob * d_prob, axis=0, keepdims=True)
            delta = jnp.concatenate(
                [delta[:, :rows], delta[:, rows:] + prob_own * d_prob_own], axis=1
            )
            d_score = (prob * (d_prob - delta)).astype(LOW)
            d_own = (prob_own * (d_prob_own - delta[:, rows:])).astype(LOW).astype(WIDE)
            bias_sums[head, blocks : blocks + 1, :] = d_own
            mixed = dot(key_t[span], d_score)
            d_query_t.append(
                jnp.concatenate(
                    [mixed[:, :rows], mixed[:, rows:] + d_own * own_key_t[span]], axis=1
                )
            )
            d_scores.append(d_score)
            d_own_key.append(d_own * query_t[span, rows:])
            d_own_value.append(prob_own * d_ctx_t[span, rows:])
            wide = d_score.astype(WIDE)
            summed = wide[:, :rows] + wide[:, rows : 2 * rows] + wide[:, 2 * rows :]
            mirrored = dot(summed.astype(LOW), turned)
            for block in range(full // rows):
                piece = mirrored[block * rows : (block + 1) * rows]
                piece = jnp.concatenate([piece, jnp.zeros_like(piece)], axis=1)
                aligned = pltpu.roll(piece, 0, 1, stride=1, stride_axis=0)
                bias_sums[head, block : block + 1, :] = jnp.sum(aligned, axis=0, keepdims=True)
        d_query[:, cols] = (jnp.transpose(jnp.concatenate(d_query_t, axis=0)) * 0.125).astype(LOW)
        d_key[rows:, cols] = jnp.transpose(jnp.concatenate(d_own_key, axis=0)).astype(LOW)
        d_value[rows:, cols] = jnp.transpose(jnp.concatenate(d_own_value, axis=0)).astype(LOW)
        both = jnp.concatenate(d_scores, axis=1)
        split = jnp.concatenate([half_lanes(queries, 0), half_lanes(queries, 1)], axis=0)
        store_part(2, cols, dot(both, split))
        both = jnp.concatenate([kept[slot, 0], kept[slot, 1]], axis=1)
        split = jnp.concatenate([half_lanes(d_ctx, 0), half_lanes(d_ctx, 1)], axis=0)
        store_part(3, cols, dot(both, split))
        return carry

    load_side(2).wait()
    load_side(3).wait()
    lax.fori_loop(0, pairs // 2, self_pair, 0)
    turn(4)
    for load in late:
        load.start()
    lax.fori_loop(pairs // 2, pairs, self_pair, 0)
    core_copy(2).start()
    core_copy(3).start()
    d_cross_key[...] = far_sum(0)
    d_cross_value[...] = far_sum(1)
    for load in late:
        load.wait()
    turn(5)
    loads[6].wait()
    loads[7].wait()

    def source_body(cols):
        grad = dot(d_cross_key[...], c_key[cols, :], NT)
        grad = grad + dot(d_cross_value[...], c_value[cols, :], NT)
        encoded_grad[:, cols] = grad.astype(LOW)

    tiles(width // 256, 256, source_body)
    loads[4].start()
    loads[5].start()
    near_sum(2)
    near_sum(3)
    loads[3].wait()

    def query_body(cols):
        d_resid[:, cols] += dot(d_query[...], w_query[cols, :], NT)

    tiles(width // 256, 256, query_body)
    turn(6)
    table = jnp.zeros((HEADS, 128), WIDE)
    for block in range(blocks + 1):
        rest = bias_sums[:, block, :]
        for _ in range(3):
            part = rest.astype(LOW)
            rest = rest - part.astype(WIDE)
            table = table + dot(part, window_hot[block])
    small_out[48:64, :] = table
    small_copy(0).start()
    d_key[:rows, :] = far_sum(2)
    d_value[:rows, :] = far_sum(3)
    turn(7)
    loads[4].wait()
    loads[5].wait()

    def last_body(cols):
        grad = d_resid[:, cols] + dot(d_key[...], w_key[cols, :], NT)
        grad = grad + dot(d_value[...], w_value[cols, :], NT)
        stream_grad[:, cols] = grad.astype(LOW)

    tiles(width // 256, 256, last_body)
    for index in range(4):
        if index >= 2:
            core_copy(index).wait_send()
        far_copy(index).wait_send()
    last = len(units) // 2 + 4
    for index in range(8, last):
        turn(index)
        if index - 8 <= dp_size.bit_length():
            small_step(index - 8)
    for step in range(last - 8, dp_size.bit_length() + 1):
        small_step(step)
    drain()


def rear(acts, hbm_acts, sides, weights, cross_probs, probs, units, dp_size):
    tokens, width = acts[0].shape
    full = sides[0].shape[0]
    rows = tokens // 3
    shape = jax.ShapeDtypeStruct
    vmem = pl.BlockSpec(memory_space=pltpu.VMEM)
    hbm = pl.BlockSpec(memory_space=pl.ANY)
    sem = pltpu.SemaphoreType.DMA
    blocks = full // rows
    chunk = width // dp_size
    steps = dp_size.bit_length() + 1
    return pl.pallas_call(
        functools.partial(rear_kernel, units, dp_size),
        out_shape=[
            shape((rows, width), LOW),
            shape((tokens, width), LOW),
            shape((80, 128), WIDE),
        ]
        + [shape((chunk, COLS), WIDE)] * 8
        + [shape((chunk, 4 * COLS), WIDE), shape((4 * chunk, COLS), WIDE)],
        in_specs=[vmem] * len(acts) + [hbm] * (len(hbm_acts) + 14),
        out_specs=[vmem] * 13,
        scratch_shapes=[
            pltpu.VMEM((tokens, width), LOW),
            pltpu.VMEM((rows, width), LOW),
            pltpu.VMEM((rows, width), LOW),
            pltpu.VMEM((tokens, width), LOW),
            pltpu.VMEM((tokens, width), LOW),
            pltpu.VMEM((tokens, width), LOW),
            pltpu.VMEM((tokens, width), LOW),
            pltpu.VMEM((HEADS, blocks + 1, 2 * rows), WIDE),
            pltpu.VMEM((steps, 80, 128), WIDE),
            pltpu.VMEM((tokens, 4 * width), LOW),
            pltpu.VMEM((tokens, 4 * width), LOW),
        ]
        + [pltpu.VMEM(w.shape, LOW) for w in weights[:3]]
        + [
            pltpu.VMEM((2, 2, full, tokens), LOW),
            pltpu.VMEM((tokens, width), LOW),
            pltpu.VMEM((tokens, width), WIDE),
            pltpu.VMEM((2, blocks, rows, width), LOW),
            pltpu.VMEM((4, 2, rows, width), LOW),
            pltpu.VMEM((4, rows, width), LOW),
            pltpu.VMEM((2, full, width), LOW),
            sem((18,)),
            sem((2,)),
            sem((4,)),
            sem((4,)),
            sem((4,)),
            sem((4,)),
            sem((steps,)),
            sem((steps,)),
        ]
        + reduce_buffers(len(units), dp_size),
        compiler_params=pltpu.CompilerParams(
            collective_id=2, has_side_effects=True, vmem_limit_bytes=63 << 20
        ),
    )(*acts, *hbm_acts, *sides, *weights, cross_probs, probs)


MESH_ID = pl.DeviceIdType.MESH


def tile_dot(x_ref, x_start, y_ref, y_start, rows, tokens):
    left = x_ref[:tokens, pl.ds(x_start, rows)]
    right = y_ref[:tokens, pl.ds(y_start, COLS)]
    return lax.dot_general(
        left, right, (((0,), (0,)), ((), ())), preferred_element_type=jnp.float32
    )


def reduce_peers(dp_size):
    dp, sq, core, ypos, core_peer, y_peer = places()
    xpos, zpos = dp % 2, dp // 2
    depth = dp_size // 2
    peers = [core_peer, y_peer, (dp + 1 - 2 * xpos, sq)]
    return peers + [((zpos + step) % depth * 2 + xpos, sq) for step in range(1, depth)]


def reducer(units, ins, emit, buffers, dp_size):
    sent, core_in, first_y, first_x, second, third = buffers[:6]
    core_s, core_r, one_s, one_r, two_s, two_r, three_s, three_r = buffers[6:14]
    core_free, one_free, two_free = buffers[14:]
    dp, sq, core, ypos, core_peer, y_peer = places()
    xpos, zpos = dp % 2, dp // 2
    depth = dp_size // 2
    chunk = 1024 // dp_size
    x_peer = (dp + 1 - 2 * xpos, sq)
    count = len(units)
    remote = remote_copy

    def z_peer(step):
        return ((zpos + step) % depth * 2 + xpos, sq)

    def half_dots(unit, half, write):
        x_id, y_id, kind, part, base, tokens = units[unit]
        x_ref, y_ref = ins[x_id], ins[y_id]
        rows = chunk if kind == "back" else 256

        def body(step, carry):
            tile, side = step // 2, step % 2
            block = side * 2 + half
            x_start = base + tile * 256
            y_start = block * COLS
            if kind == "in":
                y_start = block * 1024 + part * COLS
            if kind == "back":
                x_start = tile * (4 * chunk) + part * chunk
            write(
                side,
                pl.ds(pl.multiple_of(tile * rows, rows), rows),
                tile_dot(
                    x_ref,
                    pl.multiple_of(x_start, 128),
                    y_ref,
                    pl.multiple_of(y_start, COLS),
                    rows,
                    tokens,
                ),
            )
            return carry

        lax.fori_loop(0, 2 * (1024 // rows), body, 0)

    def core_copy(unit):
        return remote(
            sent.at[unit % SLOTS], core_in.at[unit % RING], core_s.at[unit], core_r.at[unit], core_peer
        )

    def one_copy(unit):
        half = unit // 2 % (RING // 2)
        if unit % 2 == 0:
            return remote(
                core_in.at[unit % RING, 1 - ypos], first_y.at[half], one_s.at[unit], one_r.at[unit], y_peer
            )
        source = core_in.at[unit % RING].reshape(2, depth, 2, chunk, COLS)
        return remote(
            source.at[:, :, 1 - xpos], first_x.at[half], one_s.at[unit], one_r.at[unit], x_peer
        )

    def two_copy(unit):
        half = unit // 2 % (RING // 2)
        if unit % 2 == 0:
            source = first_y.at[half].reshape(depth, 2, chunk, COLS)
            return remote(
                source.at[:, 1 - xpos], second.at[unit % LATE], two_s.at[unit], two_r.at[unit], x_peer
            )
        return remote(
            first_x.at[half, 1 - ypos], second.at[unit % LATE], two_s.at[unit], two_r.at[unit], y_peer
        )

    def three_copy(unit, step):
        return remote(
            second.at[unit % LATE, (zpos + step) % depth],
            third.at[unit, step - 1],
            three_s.at[unit, step - 1],
            three_r.at[unit, step - 1],
            z_peer(step),
        )

    def products(unit):
        slot = unit % SLOTS
        if unit >= SLOTS:
            core_copy(unit - SLOTS).wait_send()

        def write(side, rows, value):
            sent[slot, side, rows, :] = value.astype(jnp.bfloat16)

        half_dots(unit, 1 - core, write)
        if unit >= RING:
            pl.semaphore_wait(core_free, 1)
        core_copy(unit).start()

    def allow(unit, ring, free, peer):
        if unit + ring < count:
            pl.semaphore_signal(free, inc=1, device_id=peer, device_id_type=MESH_ID)

    def core_sum(unit):
        core_copy(unit).wait_recv()

        def write(side, rows, value):
            old = core_in[unit % RING, side, rows, :].astype(jnp.float32)
            core_in[unit % RING, side, rows, :] = (value + old).astype(jnp.bfloat16)

        half_dots(unit, core, write)
        if unit >= RING:
            pl.semaphore_wait(one_free.at[unit % 2], 1)
        one_copy(unit).start()

    def plus(left, right):
        return (left.astype(jnp.float32) + right.astype(jnp.float32)).astype(jnp.bfloat16)

    def one_sum(unit):
        one_copy(unit).wait_recv()
        half = unit // 2 % (RING // 2)
        if unit % 2 == 0:

            def body(step, carry):
                rows = pl.ds(pl.multiple_of(step * 128, 128), 128)
                first_y[half, rows, :] = plus(first_y[half, rows, :], core_in[unit % RING, ypos, rows, :])
                return carry

            lax.fori_loop(0, 8, body, 0)
        else:
            def body(step, carry):
                side, layer = step // depth, step % depth
                rows = pl.ds(pl.multiple_of((layer * 2 + xpos) * chunk, chunk), chunk)
                first_x[half, side, layer] = plus(
                    first_x[half, side, layer], core_in[unit % RING, side, rows, :]
                )
                return carry

            lax.fori_loop(0, 2 * depth, body, 0)
        if unit >= LATE:
            pl.semaphore_wait(two_free.at[unit % 2], 1)
        two_copy(unit).start()
        one_copy(unit).wait_send()
        allow(unit, RING, core_free, core_peer)

    def two_sum(unit):
        two_copy(unit).wait_recv()
        half = unit // 2 % (RING // 2)

        def body(layer, carry):
            if unit % 2 == 0:
                rows = pl.ds(pl.multiple_of((layer * 2 + xpos) * chunk, chunk), chunk)
                old = first_y[half, rows, :]
            else:
                old = first_x[half, ypos, layer]
            second[unit % LATE, layer] = plus(second[unit % LATE, layer], old)
            return carry

        lax.fori_loop(0, depth, body, 0)
        two_copy(unit).wait_send()
        allow(unit, RING, one_free.at[unit % 2], (y_peer, x_peer)[unit % 2])

        def send(step, carry):
            three_copy(unit, step).start()
            return carry

        lax.fori_loop(1, depth, send, 0)

    def last_sum(unit):
        def body(step, total):
            three_copy(unit, step).wait_recv()
            return total + third[unit, step - 1].astype(jnp.float32)

        total = lax.fori_loop(1, depth, body, second[unit % LATE, zpos].astype(jnp.float32))
        emit(units[unit], total)

        def sent_out(step, carry):
            three_copy(unit, step).wait_send()
            return carry

        lax.fori_loop(1, depth, sent_out, 0)
        allow(unit, LATE, two_free.at[unit % 2], (x_peer, y_peer)[unit % 2])

    def turn(index):
        for stage, lag in ((products, 0), (core_sum, 1), (one_sum, 2), (two_sum, 3), (last_sum, 4)):
            for unit in (2 * (index - lag), 2 * (index - lag) + 1):
                if 0 <= unit < count:
                    stage(unit)

    def drain():
        for unit in range(count - SLOTS, count):
            core_copy(unit).wait_send()

    return turn, drain


def reduce_buffers(count, dp_size):
    depth, chunk = dp_size // 2, 1024 // dp_size
    sem = pltpu.SemaphoreType.DMA
    credit = pltpu.SemaphoreType.REGULAR
    return [
        pltpu.VMEM((SLOTS, 2, 1024, COLS), LOW),
        pltpu.VMEM((RING, 2, 1024, COLS), LOW),
        pltpu.VMEM((RING // 2, 1024, COLS), LOW),
        pltpu.VMEM((RING // 2, 2, depth, chunk, COLS), LOW),
        pltpu.VMEM((LATE, depth, chunk, COLS), LOW),
        pltpu.VMEM((count, depth - 1, chunk, COLS), LOW),
    ] + [sem((count,))] * 6 + [sem((count, depth - 1))] * 2 + [credit, credit((2,)), credit((2,))]


def small_sums(small, small_in, small_s, small_r, dp_size):
    dp, sq, core, ypos, core_peer, y_peer = places()

    def copy(step):
        flip = 1 << max(step - 2, 0)
        peer = (dp + flip - 2 * flip * (dp // flip % 2), sq)
        peer = (core_peer, y_peer, peer)[min(step, 2)]
        return remote_copy(small, small_in.at[step], small_s.at[step], small_r.at[step], peer)

    def advance(step):
        copy(step).wait()
        small[...] = small[...] + small_in[step]
        if step < dp_size.bit_length():
            copy(step + 1).start()

    return copy, advance


def per_device(
    stream,
    encoded,
    cotangent,
    lengths,
    bucket_table,
    w_query,
    w_key,
    w_value,
    w_out,
    c_query,
    c_key,
    c_value,
    c_out,
    w_in,
    w_back,
    gain_one,
    shift_one,
    gain_two,
    shift_two,
    gain_three,
    shift_three,
    position_bias,
):
    num_rows, num_streams, local_len, model_width = stream.shape
    full_len = local_len * lax.axis_size("seq")
    sq = lax.axis_index("seq")
    dp_size = lax.axis_size("dp")
    chunk = model_width // dp_size
    bucket_ids = jnp.arange(NBUCKET, dtype=jnp.int32)
    exact = lax.Precision.HIGHEST
    table_hot = (bucket_table[:, None] == bucket_ids[None, :]).astype(jnp.float32)
    by_distance = jnp.einsum("db,bh->hd", table_hot, position_bias, precision=exact)
    bias_table = jnp.concatenate([jnp.zeros_like(by_distance), by_distance], axis=1)[:, None, :]
    flat_rows = stream.reshape(-1, model_width)
    source_rows = encoded.reshape(-1, model_width)
    flat_cotangent = cotangent.reshape(-1, model_width)

    def line(values):
        return values.reshape(1, model_width)

    fronts = front(
        stream.reshape(num_streams, local_len, model_width),
        source_rows,
        lengths,
        bias_table,
        (line(gain_one), line(shift_one), line(gain_two), line(shift_two)),
        (w_query, w_key, w_value, w_out, c_query, c_key, c_value, c_out),
    )
    query, own_key, own_value, main_key, main_value, context_low, resid_one, first_norm = fronts[:8]
    cross_query, cross_key, cross_value, cross_low, resid_two, second_norm = fronts[8:14]
    own_probs, front_stats, probs, cross_probs = fronts[14:]
    layer_output, activated, d_ffn_out, d_inner, d_resid_two, d_crossed, mid_grads, ffn_stat = middle(
        second_norm,
        resid_two,
        flat_cotangent,
        lengths,
        line(gain_two),
        line(gain_three),
        line(shift_three),
        w_in,
        w_back,
    )
    blocks = full_len // local_len
    place = jnp.arange(2 * local_len, dtype=jnp.int32)
    reach = (sq - jnp.arange(blocks, dtype=jnp.int32))[:, None] * local_len + (
        local_len - 1 - place[None, :]
    )
    reach = jnp.concatenate([reach, jnp.zeros((1, 2 * local_len), jnp.int32)])
    lane_ids = jnp.arange(128, dtype=jnp.int32)
    first_of = jnp.sum((bucket_table[:, None] < lane_ids[None, :]).astype(jnp.int32), axis=0)
    next_of = jnp.sum((bucket_table[:, None] <= lane_ids[None, :]).astype(jnp.int32), axis=0)
    window_hot = (reach[..., None] >= first_of) & (reach[..., None] < next_of)
    position = sq * local_len + jnp.arange(local_len)
    count = num_streams * jnp.sum((position < lengths[0]).astype(jnp.float32))
    mid_stats = jnp.concatenate([front_stats, ffn_stat]).reshape(4, -1, 128).sum(axis=1)
    mid_stats = jnp.concatenate([mid_stats, jnp.full((4, 128), count / 128)])
    units = []
    tokens = num_streams * local_len
    spread = activated
    if chunk % 128 != 0:
        spread = activated.reshape(-1, dp_size, 4, chunk)
        spread = jnp.transpose(spread, (0, 2, 1, 3)).reshape(activated.shape)
    for part in range(4):
        if chunk % 128 == 0:
            units.append((3, 0, "back", part, 0, tokens))
        else:
            units.append((3, 0, "parted", part, part * model_width, tokens))
        units.append((1, 2, "in", part, 0, tokens))
    units += [(4, 5, "", 7, 0, tokens), (6, 7, "", 4, 0, tokens), (3, 8, "", 3, 0, tokens)]
    units += [(3, 9, "", 5, 2 * model_width, local_len), (3, 10, "", 6, 2 * model_width, local_len)]
    units += [(3, 11 + part, "", part, model_width, tokens) for part in range(3)]
    rears = rear(
        (
            d_crossed,
            cross_query,
            resid_one,
            query,
            own_key,
            own_value,
            own_probs,
            line(gain_one),
            d_ffn_out,
            second_norm,
            cross_low,
            first_norm,
            mid_grads,
            mid_stats,
            window_hot.astype(jnp.bfloat16),
        ),
        (d_inner, spread, context_low, flat_rows, source_rows, d_resid_two),
        (cross_key, cross_value, main_key, main_value),
        (c_out, c_query, w_out, w_query, w_key, w_value, c_key, c_value),
        cross_probs,
        probs,
        tuple(units),
        dp_size,
    )
    encoded_grad, stream_grad, sums = rears[:3]
    shares = rears[3:]
    wide_sums = sums[:48].reshape(6, model_width)
    rms = jnp.sqrt(jnp.sum(sums[64:68], axis=1) / (jnp.sum(sums[68]) * model_width))
    return (
        layer_output.reshape(stream.shape),
        stream_grad.reshape(stream.shape),
        encoded_grad.reshape(encoded.shape),
        shares[0],
        shares[1],
        shares[2],
        shares[3],
        shares[4],
        shares[5],
        shares[6],
        shares[7],
        shares[8],
        shares[9],
        wide_sums[0],
        wide_sums[1],
        wide_sums[2],
        wide_sums[3],
        wide_sums[4],
        wide_sums[5],
        jnp.transpose(sums[48:64, :NBUCKET]),
        rms,
    )


def solution(mesh):
    placed = (
        P("dp", None, "seq", None),
        P("dp", "seq", None),
        P("dp", None, "seq", None),
        P("dp"),
        P(),
        P(),
        P(),
        P(),
        P(),
        P(),
        P(),
        P(),
        P(),
        P(),
        P(),
        P(),
        P(),
        P(),
        P(),
        P(),
        P(),
        P(),
    )
    return jax.shard_map(
        per_device,
        mesh=mesh,
        in_specs=placed,
        out_specs=(
            P("dp", None, "seq", None),
            P("dp", None, "seq", None),
            P("dp", "seq", None),
            P("dp", "seq"),
            P("dp", "seq"),
            P("dp", "seq"),
            P("dp", "seq"),
            P("dp", "seq"),
            P("dp", "seq"),
            P("dp", "seq"),
            P("dp", "seq"),
            P("dp", "seq"),
            P("dp", "seq"),
            P(),
            P(),
            P(),
            P(),
            P(),
            P(),
            P(),
            P(),
        ),
        check_vma=False,
    )
```

```python
import functools

import jax
import jax.numpy as jnp
from jax import lax
from jax.experimental import pallas as pl
from jax.experimental.pallas import tpu as pltpu
from jax.sharding import PartitionSpec as P

HEADS = 16
HEAD_DIM = 64
NBUCKET = 32
COLS = 256
SLOTS = 2
RING = 6
RING_ONE = 5
COLORS = "yxyxzxyxyxzxyxzxyxyxzxyxzxyxyxyx"
epsilon = 1e-05
masked_score = -1e30


LOW = jnp.bfloat16
WIDE = jnp.float32
NN = (((1,), (0,)), ((), ()))
NT = (((1,), (1,)), ((), ()))


def dot(left, right, dims=NN):
    return lax.dot_general(left, right, dims, preferred_element_type=WIDE)


def flip(block):
    return jnp.transpose(block.astype(WIDE))


def places():
    dp, sq = lax.axis_index("dp"), lax.axis_index("seq")
    core, ypos = sq % 2, sq // 2
    return dp, sq, core, ypos, (dp, sq + 1 - 2 * core), (dp, sq + 2 - 4 * ypos)


def remote_copy(src, dst, send_sem, recv_sem, peer):
    return pltpu.make_async_remote_copy(
        src_ref=src,
        dst_ref=dst,
        send_sem=send_sem,
        recv_sem=recv_sem,
        device_id=peer,
        device_id_type=MESH_ID,
    )


def greet(peers):
    barrier = pltpu.get_barrier_semaphore()
    for peer in peers:
        pl.semaphore_signal(barrier, inc=1, device_id=peer, device_id_type=MESH_ID)
    pl.semaphore_wait(barrier, len(peers))


def tiles(count, size, body):
    def step(index, carry):
        body(pl.ds(pl.multiple_of(index * size, size), size))
        return carry

    lax.fori_loop(0, count, step, 0)


def project_to(dst, left, weight, scale=None):
    product = dot(left[...], weight[...])
    if scale is not None:
        product = product * scale
    dst[...] = product.astype(dst.dtype)


def norm_stats(rows):
    centre = jnp.mean(rows, axis=-1, keepdims=True)
    centred = rows - centre
    spread = jnp.mean(centred * centred, axis=-1, keepdims=True)
    return centred, lax.rsqrt(spread + epsilon)


def norm_backward(unit, scale, gain, incoming):
    scaled = incoming * gain
    first = jnp.mean(scaled, axis=-1, keepdims=True)
    second = jnp.mean(scaled * unit, axis=-1, keepdims=True)
    grads = scale * (scaled - first - unit * second)
    d_gain = jnp.sum(incoming * unit, axis=0, keepdims=True)
    return grads, d_gain, jnp.sum(incoming, axis=0, keepdims=True)


def valid_rows(sq, length, count):
    position = sq * count + lax.broadcasted_iota(jnp.int32, (count, 1), 0)
    return (position < length).astype(WIDE)


def sum_squares(rows, mask):
    return jnp.sum(rows * rows * mask, axis=0, keepdims=True)


def half_rows(block, side):
    row = lax.broadcasted_iota(jnp.int32, block.shape, 0)
    return jnp.where(row // HEAD_DIM == side, block, 0.0).astype(LOW)


def half_lanes(block, side):
    lane = lax.broadcasted_iota(jnp.int32, block.shape, 1)
    return jnp.where(lane // HEAD_DIM == side, block.astype(WIDE), 0.0).astype(LOW)


def front_kernel(*refs):
    stream, encoded, length_ref, bias_table = refs[:4]
    gain_one, shift_one, gain_two, shift_two = refs[4:8]
    hbm_weights = refs[8:16]
    (query, own_key, own_value, main_key, main_value, context, unit_one, first_norm) = refs[16:24]
    (cross_query, cross_key, cross_value, cross_context, unit_two, second_norm) = refs[24:30]
    scales, own_probs, stats, probs_out, cross_probs_out = refs[30:35]
    weights = refs[35:43]
    main_all, source_all, kept, bias, masks, branch_out = refs[43:49]
    weight_sem, kept_sem, send_sem, recv_sem = refs[49:]
    w_query, w_key, w_value, w_out, c_query, c_key, c_value, c_out = weights
    dp, sq, core, ypos, core_peer, y_peer = places()
    length = length_ref[0]
    rows = stream.shape[1]
    full = main_all.shape[0] * rows
    loads = [
        pltpu.make_async_copy(src, dst, weight_sem.at[index])
        for index, (src, dst) in enumerate(zip(hbm_weights, weights))
    ]
    for load in loads:
        load.start()
    greet([core_peer, y_peer])
    sources = (stream.at[0], encoded)
    gathered = (main_all, source_all)
    firsts = []
    for index in range(2):
        for lane, peer in enumerate((y_peer, core_peer)):
            slot = index * 3 + lane
            firsts.append(
                remote_copy(
                    sources[index],
                    gathered[index].at[sq],
                    send_sem.at[slot],
                    recv_sem.at[slot],
                    peer,
                )
            )
            firsts[-1].start()
    main_all[sq] = stream[0]
    source_all[sq] = encoded[...]

    def passed_on(index):
        other = gathered[index].at[sq + 2 - 4 * ypos]
        slot = index * 3 + 2
        return remote_copy(other, other, send_sem.at[slot], recv_sem.at[slot], core_peer)

    flat = stream.reshape(3 * rows, stream.shape[2])
    loads[0].wait()
    project_to(query, flat, w_query, 0.125)
    firsts[0].wait_recv()
    passed_on(0).start()
    predicting = flat.at[rows:, :]
    loads[1].wait()
    project_to(own_key, predicting, w_key)
    loads[2].wait()
    project_to(own_value, predicting, w_value)
    firsts[1].wait_recv()
    passed_on(0).wait_recv()
    firsts[2].wait_recv()
    passed_on(1).start()
    wide_main = main_all.reshape(full, main_all.shape[2])
    project_to(main_key, wide_main, w_key)
    project_to(main_value, wide_main, w_value)

    key_row = lax.broadcasted_iota(jnp.int32, (full, rows), 0)
    distance = sq * rows + lax.broadcasted_iota(jnp.int32, (full, rows), 1) - key_row
    in_range = key_row < length
    masks[0] = jnp.where((distance >= 0) & in_range, 0.0, masked_score)
    masks[1] = jnp.where((distance > 0) & in_range, 0.0, masked_score)
    masks[2] = jnp.where(in_range, 0.0, masked_score)

    def kept_copy(pair, out):
        slot = pair % 2
        return pltpu.make_async_copy(kept.at[slot], out.at[pair], kept_sem.at[slot])

    def self_pair(pair, carry):
        @pl.when(pair >= 2)
        def _():
            kept_copy(pair - 2, probs_out).wait()

        slot = pair % 2
        cols = pl.ds(pl.multiple_of(pair * 128, 128), 128)
        keys = main_key[:, cols]
        query_t = flip(query[:, cols])
        value_t = flip(main_value[:, cols]).astype(LOW)
        own_key_t, own_value_t = flip(own_key[:, cols]), flip(own_value[:, cols])
        own_product = query_t[:, rows:] * own_key_t
        sides = []
        for side in range(2):
            head = 2 * pair + side
            span = slice(side * HEAD_DIM, (side + 1) * HEAD_DIM)
            scores = dot(keys, half_rows(query_t, side))
            own_bias = bias_table[head, :, full : full + 128][:, 0:1]
            own_score = jnp.sum(own_product[span], axis=0, keepdims=True) + own_bias
            for block in range(full // rows):
                start = pl.multiple_of((sq - block + full // rows - 1) * rows, 128)
                line = bias_table[head, :, pl.ds(start, 2 * rows)]
                wide = jnp.broadcast_to(line, (rows, 2 * rows))
                near = pltpu.roll(wide, 0, 1, stride=1, stride_axis=0)[:, rows:]
                part = slice(block * rows, (block + 1) * rows)
                for kind in range(2):
                    bias[kind, part, :] = near + masks[kind, part, :]
            owns = []
            for stream_id in range(3):
                lanes = slice(stream_id * rows, (stream_id + 1) * rows)
                score = scores[:, lanes] + bias[min(stream_id, 1)]
                top = jnp.max(score, axis=0, keepdims=True)
                if stream_id > 0:
                    own = own_score[:, (stream_id - 1) * rows : stream_id * rows]
                    top = jnp.maximum(top, own)
                expo = jnp.exp(score - top)
                total = jnp.sum(expo, axis=0, keepdims=True)
                if stream_id > 0:
                    expo_own = jnp.exp(own - top)
                    total = total + expo_own
                share = 1.0 / total
                kept[slot, side, :, lanes] = (expo * share).astype(LOW)
                owns.append(expo_own * share if stream_id > 0 else jnp.zeros_like(total))
            own_probs[head] = jnp.concatenate(owns, axis=1)
            mixed = dot(value_t[span], kept[slot, side])
            mixed_own = jnp.concatenate(owns[1:], axis=1) * own_value_t[span]
            sides.append(
                jnp.concatenate([mixed[:, :rows], mixed[:, rows:] + mixed_own], axis=1)
            )
        context[:, cols] = jnp.transpose(jnp.concatenate(sides, axis=0)).astype(LOW)
        kept_copy(pair, probs_out).start()
        return carry

    lax.fori_loop(0, HEADS // 2, self_pair, 0)
    for pair in range(HEADS // 2 - 2, HEADS // 2):
        kept_copy(pair, probs_out).wait()

    mask = valid_rows(sq, length, rows)
    loads[3].wait()
    project_to(branch_out, context, w_out)
    seen = jnp.zeros((1, stream.shape[2]), WIDE)
    branch = jnp.zeros((1, stream.shape[2]), WIDE)
    for stream_id in range(3):
        part = slice(stream_id * rows, (stream_id + 1) * rows)
        source, attended = stream[stream_id].astype(WIDE), branch_out[part, :]
        seen = seen + sum_squares(source, mask)
        branch = branch + sum_squares(attended, mask)
        centred, scale = norm_stats(source + attended)
        unit = centred * scale
        unit_one[part, :] = unit.astype(LOW)
        scales[0, part, :] = jnp.broadcast_to(scale, (rows, 128))
        first_norm[part, :] = (unit * gain_one[...] + shift_one[...]).astype(LOW)
    stats[0:1, :] = seen
    stats[1:2, :] = branch
    loads[4].wait()
    project_to(cross_query, first_norm, c_query, 0.125)
    firsts[3].wait_recv()
    passed_on(1).wait_recv()
    wide_source = source_all.reshape(full, source_all.shape[2])
    loads[5].wait()
    project_to(cross_key, wide_source, c_key)
    loads[6].wait()
    project_to(cross_value, wide_source, c_value)

    def cross_pair(pair, carry):
        @pl.when(pair >= 2)
        def _():
            kept_copy(pair - 2, cross_probs_out).wait()

        slot = pair % 2
        cols = pl.ds(pl.multiple_of(pair * 128, 128), 128)
        keys = cross_key[:, cols]
        query_t = flip(cross_query[:, cols])
        value_t = flip(cross_value[:, cols]).astype(LOW)
        sides = []
        for side in range(2):
            span = slice(side * HEAD_DIM, (side + 1) * HEAD_DIM)
            scores = dot(keys, half_rows(query_t, side))
            for stream_id in range(3):
                lanes = slice(stream_id * rows, (stream_id + 1) * rows)
                score = scores[:, lanes] + masks[2]
                expo = jnp.exp(score - jnp.max(score, axis=0, keepdims=True))
                share = 1.0 / jnp.sum(expo, axis=0, keepdims=True)
                kept[slot, side, :, lanes] = (expo * share).astype(LOW)
            sides.append(dot(value_t[span], kept[slot, side]))
        cross_context[:, cols] = jnp.transpose(jnp.concatenate(sides, axis=0)).astype(LOW)
        kept_copy(pair, cross_probs_out).start()
        return carry

    lax.fori_loop(0, HEADS // 2, cross_pair, 0)
    for pair in range(HEADS // 2 - 2, HEADS // 2):
        kept_copy(pair, cross_probs_out).wait()
    loads[7].wait()
    project_to(branch_out, cross_context, c_out)
    branch = jnp.zeros((1, stream.shape[2]), WIDE)
    for stream_id in range(3):
        part = slice(stream_id * rows, (stream_id + 1) * rows)
        crossed = branch_out[part, :]
        branch = branch + sum_squares(crossed, mask)
        centred, scale = norm_stats(first_norm[part, :].astype(WIDE) + crossed)
        unit = centred * scale
        unit_two[part, :] = unit.astype(LOW)
        scales[1, part, :] = jnp.broadcast_to(scale, (rows, 128))
        second_norm[part, :] = (unit * gain_two[...] + shift_two[...]).astype(LOW)
    stats[2:3, :] = branch
    for copy in firsts:
        copy.wait_send()
    for index in range(2):
        passed_on(index).wait_send()


def front(stream, encoded, length, bias_table, norms, weights):
    streams, rows, width = stream.shape
    seq = lax.axis_size("seq")
    full, tokens = seq * rows, streams * rows
    own = tokens - rows
    shape = jax.ShapeDtypeStruct
    pairs = HEADS // 2
    outs = [
        shape((tokens, width), LOW),
        shape((own, width), LOW),
        shape((own, width), LOW),
        shape((full, width), LOW),
        shape((full, width), LOW),
        shape((tokens, width), LOW),
        shape((tokens, width), LOW),
        shape((tokens, width), LOW),
        shape((tokens, width), LOW),
        shape((full, width), LOW),
        shape((full, width), LOW),
        shape((tokens, width), LOW),
        shape((tokens, width), LOW),
        shape((tokens, width), LOW),
        shape((2, tokens, 128), WIDE),
        shape((HEADS, 1, tokens), WIDE),
        shape((3, width), WIDE),
        shape((pairs, 2, full, tokens), LOW),
        shape((pairs, 2, full, tokens), LOW),
    ]
    vmem = pl.BlockSpec(memory_space=pltpu.VMEM)
    smem = pl.BlockSpec(memory_space=pltpu.SMEM)
    hbm = pl.BlockSpec(memory_space=pl.ANY)
    sem = pltpu.SemaphoreType.DMA
    return pl.pallas_call(
        front_kernel,
        out_shape=outs,
        in_specs=[vmem, vmem, smem] + [vmem] * 5 + [hbm] * 8,
        out_specs=[vmem] * 17 + [hbm] * 2,
        scratch_shapes=[pltpu.VMEM(w.shape, LOW) for w in weights]
        + [
            pltpu.VMEM((seq, rows, width), LOW),
            pltpu.VMEM((seq, rows, width), LOW),
            pltpu.VMEM((2, 2, full, tokens), LOW),
            pltpu.VMEM((2, full, rows), WIDE),
            pltpu.VMEM((3, full, rows), WIDE),
            pltpu.VMEM((tokens, width), WIDE),
            sem((8,)),
            sem((2,)),
            sem((6,)),
            sem((6,)),
        ],
        compiler_params=pltpu.CompilerParams(
            collective_id=1, has_side_effects=True, vmem_limit_bytes=60 << 20
        ),
    )(stream, encoded, length, bias_table, *norms, *weights)


def middle_kernel(*refs):
    second_norm, unit_two, scales, cotangent, length_ref, gain_two, gain_three = refs[:7]
    shift_three, hbm_in, hbm_back = refs[7:10]
    output, activated, d_ffn, d_inner, d_resid, d_crossed, grads, stats = refs[10:18]
    w_in, w_back, slope, total, load_sem = refs[18:]
    sq = lax.axis_index("seq")
    length = length_ref[0]
    tokens, width = second_norm.shape
    rows = tokens // 3
    hidden = w_in.shape[1]
    size = 512
    steps = hidden // size

    def load_in(step):
        cols = pl.ds(pl.multiple_of(step * size, size), size)
        return pltpu.make_async_copy(hbm_in.at[:, cols], w_in.at[:, cols], load_sem.at[0, step])

    def load_back(step):
        cols = pl.ds(pl.multiple_of(step * size, size), size)
        return pltpu.make_async_copy(hbm_back.at[cols], w_back.at[cols], load_sem.at[1, step])

    for step in range(steps):
        load_in(step).start()
        load_back(step).start()
    total[...] = jnp.zeros_like(total)

    def forward(step, carry):
        cols = pl.ds(pl.multiple_of(step * size, size), size)
        load_in(step).wait()
        inner = dot(second_norm[...], w_in[:, cols])
        phi = 0.5 + 0.5 * lax.erf(inner * (0.5**0.5))
        bell = jnp.exp(inner * inner * -0.5) * (0.5 / jnp.pi) ** 0.5
        value = (inner * phi).astype(LOW)
        activated[:, cols] = value
        slope[:, cols] = (phi + inner * bell).astype(LOW)
        load_back(step).wait()
        total[...] += dot(value, w_back[cols, :])
        return carry

    lax.fori_loop(0, steps, forward, 0)
    mask = valid_rows(sq, length, rows)
    branch = jnp.zeros((1, width), WIDE)
    d_gain = jnp.zeros((1, width), WIDE)
    d_shift = jnp.zeros((1, width), WIDE)
    for stream_id in range(3):
        part = slice(stream_id * rows, (stream_id + 1) * rows)
        ffn = total[part, :]
        branch = branch + sum_squares(ffn, mask)
        resid = second_norm[part, :].astype(WIDE) + ffn
        centred, scale = norm_stats(resid)
        unit = centred * scale
        normed = unit * gain_three[...] + shift_three[...]
        output[part, :] = (normed * mask).astype(LOW)
        incoming = cotangent[part, :].astype(WIDE) * mask
        back, gain_part, shift_part = norm_backward(unit, scale, gain_three[...], incoming)
        d_gain, d_shift = d_gain + gain_part, d_shift + shift_part
        total[part, :] = back
        d_ffn[part, :] = back.astype(LOW)
    stats[...] = branch
    grads[2:3, :] = d_gain
    grads[3:4, :] = d_shift

    def backward(step, carry):
        cols = pl.ds(pl.multiple_of(step * size, size), size)
        d_act = dot(d_ffn[...], w_back[cols, :], NT)
        d_in = (d_act * slope[:, cols].astype(WIDE)).astype(LOW)
        d_inner[:, cols] = d_in
        total[...] += dot(d_in, w_in[:, cols], NT)
        return carry

    lax.fori_loop(0, steps, backward, 0)
    d_gain = jnp.zeros((1, width), WIDE)
    d_shift = jnp.zeros((1, width), WIDE)
    for stream_id in range(3):
        part = slice(stream_id * rows, (stream_id + 1) * rows)
        unit, scale = unit_two[part, :].astype(WIDE), scales[1, part, 0:1]
        back, gain_part, shift_part = norm_backward(
            unit, scale, gain_two[...], total[part, :]
        )
        d_gain, d_shift = d_gain + gain_part, d_shift + shift_part
        d_resid[part, :] = back
        d_crossed[part, :] = back.astype(LOW)
    grads[0:1, :] = d_gain
    grads[1:2, :] = d_shift


def middle(second_norm, unit_two, scales, cotangent, length, norms, w_in, w_back):
    tokens, width = second_norm.shape
    hidden = w_in.shape[1]
    shape = jax.ShapeDtypeStruct
    vmem = pl.BlockSpec(memory_space=pltpu.VMEM)
    smem = pl.BlockSpec(memory_space=pltpu.SMEM)
    hbm = pl.BlockSpec(memory_space=pl.ANY)
    return pl.pallas_call(
        middle_kernel,
        out_shape=[
            shape((tokens, width), LOW),
            shape((tokens, hidden), LOW),
            shape((tokens, width), LOW),
            shape((tokens, hidden), LOW),
            shape((tokens, width), WIDE),
            shape((tokens, width), LOW),
            shape((4, width), WIDE),
            shape((1, width), WIDE),
        ],
        in_specs=[vmem] * 4 + [smem] + [vmem] * 3 + [hbm] * 2,
        out_specs=[vmem] * 8,
        scratch_shapes=[
            pltpu.VMEM(w_in.shape, LOW),
            pltpu.VMEM(w_back.shape, LOW),
            pltpu.VMEM((tokens, hidden), LOW),
            pltpu.VMEM((tokens, width), WIDE),
            pltpu.SemaphoreType.DMA((2, hidden // 512)),
        ],
        compiler_params=pltpu.CompilerParams(vmem_limit_bytes=60 << 20),
    )(second_norm, unit_two, scales, cotangent, length, *norms, w_in, w_back)


def rear_kernel(units, dp_size, *refs):
    d_crossed, cross_query, unit_one, query, own_key, own_value, own_probs, gain_one = refs[:8]
    d_ffn, second_norm, cross_context, first_norm, mid_grads, mid_stats, window_hot = refs[8:15]
    scales, refs = refs[15], refs[:15] + refs[16:]
    hbm_inner, hbm_activated, hbm_context, hbm_stream, hbm_source, hbm_resid = refs[15:21]
    hbm_sides, hbm_weights = refs[21:25], refs[25:33]
    cross_probs, probs = refs[33:35]
    encoded_grad, stream_grad, small_out = refs[35:38]
    shares, in_share, back_share = refs[38:46], refs[46], refs[47]
    (d_cross_query, d_cross_key, d_cross_value, d_attended) = refs[48:52]
    (d_query, d_key, d_value, bias_sums, small_in) = refs[52:57]
    d_inner, activated = refs[57:59]
    weights = refs[59:62]
    kept, d_context, d_resid, parts, near_in, far_in, sides_held = refs[62:69]
    weight_sem, kept_sem, core_s, core_r, far_s, far_r, small_s, small_r = refs[69:77]
    held = (0, 1, 2, 0, 1, 2, 1, 2)
    c_out, c_query, w_out, w_query, w_key, w_value, c_key, c_value = [weights[i] for i in held]
    chunk = 1024 // dp_size

    def emit(unit, item, total):
        part, cols = unit[3], slice(item * 128, (item + 1) * 128)
        if unit[2] == "in":
            in_share[:, part * COLS + item * 128 : part * COLS + (item + 1) * 128] = total
        elif unit[2] in ("back", "parted"):
            back_share[part * chunk : (part + 1) * chunk, cols] = total
        else:
            shares[part][:, cols] = total

    operands = (d_ffn, second_norm, d_inner, activated, cross_context, d_crossed, first_norm)
    operands += (d_cross_query, d_attended, d_cross_key, d_cross_value, d_query, d_key, d_value)
    turn, drain = reducer(units, COLORS, operands, emit, refs[77:], dp_size)
    small_copy, small_step = small_sums(small_out, small_in, small_s, small_r, dp_size)
    dp, sq, core, ypos, core_peer, y_peer = places()
    tokens, width = query.shape
    rows = tokens // 3
    full = sides_held.shape[1]
    blocks = full // rows
    keys_held, values_held = sides_held.at[0], sides_held.at[1]
    pairs = HEADS // 2
    loads = [
        pltpu.make_async_copy(src, weights[held[index]], weight_sem.at[index])
        for index, src in enumerate(hbm_weights)
    ]

    def load_extra(index, src, dst):
        return pltpu.make_async_copy(src, dst, weight_sem.at[12 + index])

    early = [
        load_extra(0, hbm_activated, activated),
        load_extra(1, hbm_inner, d_inner),
        load_extra(2, hbm_resid, d_resid),
    ]
    late = [
        load_extra(3, hbm_context, activated.at[:, :width]),
        load_extra(4, hbm_stream, activated.at[:, width : 2 * width]),
        load_extra(5, hbm_source, activated.at[:rows, 2 * width : 3 * width]),
    ]

    def load_side(index):
        return pltpu.make_async_copy(
            hbm_sides[index], sides_held.at[index % 2], weight_sem.at[8 + index]
        )

    def fetch(pair, source, base):
        slot = (pair + base) % 2
        return pltpu.make_async_copy(source.at[pair], kept.at[slot], kept_sem.at[slot])

    early[0].start()
    early[1].start()
    loads[0].start()
    fetch(0, cross_probs, 0).start()
    load_side(0).start()
    load_side(1).start()
    loads[1].start()
    loads[2].start()
    early[2].start()
    greet(reduce_peers(dp_size))
    early[0].wait()
    early[1].wait()
    turn(0)
    turn(1)
    loads[0].wait()

    def back_to(dst, left, weight, add=False):
        def body(cols):
            product = dot(left[...], weight[cols, :], NT)
            if add:
                product = product + dst[:, cols]
            dst[:, cols] = product.astype(dst.dtype)

        tiles(width // 256, 256, body)

    back_to(d_context, d_crossed, c_out)
    loads[3].start()

    def core_copy(index):
        view = parts.at[index % 2].reshape(2, 2, rows, width)
        return remote_copy(
            view.at[:, 1 - core], near_in.at[index], core_s.at[index], core_r.at[index], core_peer
        )

    def far_copy(index):
        return remote_copy(
            near_in.at[index, 1 - ypos], far_in.at[index], far_s.at[index], far_r.at[index], y_peer
        )

    def near_sum(index):
        core_copy(index).wait_recv()
        for side in range(2):
            mine = parts[index % 2, side * 2 + core].astype(WIDE)
            near_in[index, side] = (near_in[index, side].astype(WIDE) + mine).astype(LOW)
        far_copy(index).start()

    def far_sum(index):
        far_copy(index).wait_recv()
        return (near_in[index, ypos].astype(WIDE) + far_in[index].astype(WIDE)).astype(LOW)

    def store_part(index, cols, block):
        for part in range(full // rows):
            parts[index % 2, part, :, cols] = block[part * rows : (part + 1) * rows].astype(LOW)

    def cross_pair(pair, carry):
        fetch(pair, cross_probs, 0).wait()

        @pl.when(pair + 1 < pairs)
        def _():
            fetch(pair + 1, cross_probs, 0).start()

        slot = pair % 2
        cols = pl.ds(pl.multiple_of(pair * 128, 128), 128)
        values = values_held[:, cols]
        key_t = flip(keys_held[:, cols]).astype(LOW)
        queries, d_ctx = cross_query[:, cols], d_context[:, cols]
        d_ctx_t = flip(d_ctx)
        d_query_t, d_scores = [], []
        for side in range(2):
            span = slice(side * HEAD_DIM, (side + 1) * HEAD_DIM)
            d_prob = dot(values, half_rows(d_ctx_t, side))
            prob = kept[slot, side].astype(WIDE)
            delta = jnp.sum(prob * d_prob, axis=0, keepdims=True)
            d_score = (prob * (d_prob - delta)).astype(LOW)
            d_query_t.append(dot(key_t[span], d_score))
            d_scores.append(d_score)
        d_cross_query[:, cols] = (
            jnp.transpose(jnp.concatenate(d_query_t, axis=0)) * 0.125
        ).astype(LOW)
        both = jnp.concatenate(d_scores, axis=1)
        split = jnp.concatenate([half_lanes(queries, 0), half_lanes(queries, 1)], axis=0)
        store_part(0, cols, dot(both, split))
        both = jnp.concatenate([kept[slot, 0], kept[slot, 1]], axis=1)
        split = jnp.concatenate([half_lanes(d_ctx, 0), half_lanes(d_ctx, 1)], axis=0)
        store_part(1, cols, dot(both, split))
        return carry

    load_side(0).wait()
    load_side(1).wait()
    lax.fori_loop(0, pairs // 2, cross_pair, 0)
    turn(2)
    turn(3)
    lax.fori_loop(pairs // 2, pairs, cross_pair, 0)
    fetch(0, probs, 0).start()
    load_side(2).start()
    load_side(3).start()
    core_copy(0).start()
    core_copy(1).start()
    turn(4)
    turn(5)
    loads[1].wait()
    early[2].wait()
    back_to(d_resid, d_cross_query, c_query, True)
    loads[6].start()
    d_gain = jnp.zeros((1, width), WIDE)
    d_shift = jnp.zeros((1, width), WIDE)
    for stream_id in range(3):
        part = slice(stream_id * rows, (stream_id + 1) * rows)
        unit, scale = unit_one[part, :].astype(WIDE), scales[0, part, 0:1]
        back, gain_part, shift_part = norm_backward(
            unit, scale, gain_one[...], d_resid[part, :]
        )
        d_gain, d_shift = d_gain + gain_part, d_shift + shift_part
        d_resid[part, :] = back
        d_attended[part, :] = back.astype(LOW)
    lines = [d_gain, d_shift] + [mid_grads[row : row + 1, :] for row in range(4)]
    for row, line in enumerate(lines):
        for piece in range(8):
            small_out[8 * row + piece : 8 * row + piece + 1, :] = line[
                :, 128 * piece : 128 * (piece + 1)
            ]
    small_out[64:72, :] = mid_stats[...]
    small_out[72:80, :] = jnp.zeros((8, 128), WIDE)
    near_sum(0)
    near_sum(1)
    turn(6)
    turn(7)
    loads[2].wait()
    back_to(d_context, d_attended, w_out)
    loads[7].start()
    core_copy(0).wait_send()
    core_copy(1).wait_send()
    line = lax.broadcasted_iota(jnp.int32, (rows, rows), 0)
    turned = (line + lax.broadcasted_iota(jnp.int32, (rows, rows), 1) == rows - 1).astype(LOW)

    def self_pair(pair, carry):
        fetch(pair, probs, 0).wait()

        @pl.when(pair + 1 < pairs)
        def _():
            fetch(pair + 1, probs, 0).start()

        slot = pair % 2
        cols = pl.ds(pl.multiple_of(pair * 128, 128), 128)
        values = values_held[:, cols]
        key_t = flip(keys_held[:, cols]).astype(LOW)
        queries, d_ctx = query[:, cols], d_context[:, cols]
        d_ctx_t, query_t = flip(d_ctx), flip(queries)
        own_key_t, own_value_t = flip(own_key[:, cols]), flip(own_value[:, cols])
        own_product = d_ctx_t[:, rows:] * own_value_t
        d_query_t, d_scores, d_own_key, d_own_value = [], [], [], []
        for side in range(2):
            head = 2 * pair + side
            span = slice(side * HEAD_DIM, (side + 1) * HEAD_DIM)
            d_prob = dot(values, half_rows(d_ctx_t, side))
            prob = kept[slot, side].astype(WIDE)
            prob_own = own_probs[head][:, rows:]
            d_prob_own = jnp.sum(own_product[span], axis=0, keepdims=True)
            delta = jnp.sum(prob * d_prob, axis=0, keepdims=True)
            delta = jnp.concatenate(
                [delta[:, :rows], delta[:, rows:] + prob_own * d_prob_own], axis=1
            )
            d_score = (prob * (d_prob - delta)).astype(LOW)
            d_own = (prob_own * (d_prob_own - delta[:, rows:])).astype(LOW).astype(WIDE)
            bias_sums[head, blocks : blocks + 1, :] = d_own
            mixed = dot(key_t[span], d_score)
            d_query_t.append(
                jnp.concatenate(
                    [mixed[:, :rows], mixed[:, rows:] + d_own * own_key_t[span]], axis=1
                )
            )
            d_scores.append(d_score)
            d_own_key.append(d_own * query_t[span, rows:])
            d_own_value.append(prob_own * d_ctx_t[span, rows:])
            wide = d_score.astype(WIDE)
            summed = wide[:, :rows] + wide[:, rows : 2 * rows] + wide[:, 2 * rows :]
            mirrored = dot(summed.astype(LOW), turned)
            for block in range(full // rows):
                piece = mirrored[block * rows : (block + 1) * rows]
                piece = jnp.concatenate([piece, jnp.zeros_like(piece)], axis=1)
                aligned = pltpu.roll(piece, 0, 1, stride=1, stride_axis=0)
                bias_sums[head, block : block + 1, :] = jnp.sum(aligned, axis=0, keepdims=True)
        d_query[:, cols] = (jnp.transpose(jnp.concatenate(d_query_t, axis=0)) * 0.125).astype(LOW)
        d_key[rows:, cols] = jnp.transpose(jnp.concatenate(d_own_key, axis=0)).astype(LOW)
        d_value[rows:, cols] = jnp.transpose(jnp.concatenate(d_own_value, axis=0)).astype(LOW)
        both = jnp.concatenate(d_scores, axis=1)
        split = jnp.concatenate([half_lanes(queries, 0), half_lanes(queries, 1)], axis=0)
        store_part(2, cols, dot(both, split))
        both = jnp.concatenate([kept[slot, 0], kept[slot, 1]], axis=1)
        split = jnp.concatenate([half_lanes(d_ctx, 0), half_lanes(d_ctx, 1)], axis=0)
        store_part(3, cols, dot(both, split))
        return carry

    load_side(2).wait()
    load_side(3).wait()
    quarter = pairs // 4
    lax.fori_loop(0, quarter, self_pair, 0)
    turn(8)
    for load in late:
        load.start()
    lax.fori_loop(quarter, 2 * quarter, self_pair, 0)
    turn(9)
    lax.fori_loop(2 * quarter, 3 * quarter, self_pair, 0)
    for load in late:
        load.wait()
    turn(10)
    lax.fori_loop(3 * quarter, pairs, self_pair, 0)
    core_copy(2).start()
    core_copy(3).start()
    d_cross_key[...] = far_sum(0)
    d_cross_value[...] = far_sum(1)
    turn(11)
    near_sum(2)
    near_sum(3)
    turn(12)
    loads[6].wait()
    loads[7].wait()

    def source_body(cols):
        grad = dot(d_cross_key[...], c_key[cols, :], NT)
        grad = grad + dot(d_cross_value[...], c_value[cols, :], NT)
        encoded_grad[:, cols] = grad.astype(LOW)

    tiles(width // 256, 256, source_body)
    loads[4].start()
    loads[5].start()
    loads[3].wait()

    def query_body(cols):
        d_resid[:, cols] += dot(d_query[...], w_query[cols, :], NT)

    turn(13)
    tiles(width // 256, 256, query_body)
    table = jnp.zeros((HEADS, 128), WIDE)
    for block in range(blocks + 1):
        rest = bias_sums[:, block, :]
        for _ in range(3):
            part = rest.astype(LOW)
            rest = rest - part.astype(WIDE)
            table = table + dot(part, window_hot[block])
    small_out[48:64, :] = table
    small_copy(0).start()
    d_key[:rows, :] = far_sum(2)
    d_value[:rows, :] = far_sum(3)
    turn(14)
    turn(15)
    loads[4].wait()
    loads[5].wait()

    def last_body(cols):
        grad = d_resid[:, cols] + dot(d_key[...], w_key[cols, :], NT)
        grad = grad + dot(d_value[...], w_value[cols, :], NT)
        stream_grad[:, cols] = grad.astype(LOW)

    tiles(width // 256, 256, last_body)
    for index in range(4):
        if index >= 2:
            core_copy(index).wait_send()
        far_copy(index).wait_send()
    last = len(units) + 9
    for index in range(16, last):
        turn(index)
        if index % 2 == 0 and (index - 16) // 2 <= dp_size.bit_length():
            small_step((index - 16) // 2)
    for step in range((last - 15) // 2, dp_size.bit_length() + 1):
        small_step(step)
    drain()


def rear(acts, hbm_acts, sides, weights, cross_probs, probs, units, dp_size):
    tokens, width = acts[0].shape
    full = sides[0].shape[0]
    rows = tokens // 3
    shape = jax.ShapeDtypeStruct
    vmem = pl.BlockSpec(memory_space=pltpu.VMEM)
    hbm = pl.BlockSpec(memory_space=pl.ANY)
    sem = pltpu.SemaphoreType.DMA
    blocks = full // rows
    chunk = width // dp_size
    steps = dp_size.bit_length() + 1
    return pl.pallas_call(
        functools.partial(rear_kernel, units, dp_size),
        out_shape=[
            shape((rows, width), LOW),
            shape((tokens, width), LOW),
            shape((80, 128), WIDE),
        ]
        + [shape((chunk, COLS), WIDE)] * 8
        + [shape((chunk, 4 * COLS), WIDE), shape((4 * chunk, COLS), WIDE)],
        in_specs=[vmem] * len(acts) + [hbm] * (len(hbm_acts) + 14),
        out_specs=[vmem] * 13,
        scratch_shapes=[
            pltpu.VMEM((tokens, width), LOW),
            pltpu.VMEM((rows, width), LOW),
            pltpu.VMEM((rows, width), LOW),
            pltpu.VMEM((tokens, width), LOW),
            pltpu.VMEM((tokens, width), LOW),
            pltpu.VMEM((tokens, width), LOW),
            pltpu.VMEM((tokens, width), LOW),
            pltpu.VMEM((HEADS, blocks + 1, 2 * rows), WIDE),
            pltpu.VMEM((steps, 80, 128), WIDE),
            pltpu.VMEM((tokens, 4 * width), LOW),
            pltpu.VMEM((tokens, 4 * width), LOW),
        ]
        + [pltpu.VMEM(w.shape, LOW) for w in weights[:3]]
        + [
            pltpu.VMEM((2, 2, full, tokens), LOW),
            pltpu.VMEM((tokens, width), LOW),
            pltpu.VMEM((tokens, width), WIDE),
            pltpu.VMEM((2, blocks, rows, width), LOW),
            pltpu.VMEM((4, 2, rows, width), LOW),
            pltpu.VMEM((4, rows, width), LOW),
            pltpu.VMEM((2, full, width), LOW),
            sem((18,)),
            sem((2,)),
            sem((4,)),
            sem((4,)),
            sem((4,)),
            sem((4,)),
            sem((steps,)),
            sem((steps,)),
        ]
        + reduce_buffers(COLORS, dp_size),
        compiler_params=pltpu.CompilerParams(
            collective_id=2, has_side_effects=True, vmem_limit_bytes=63 << 20
        ),
    )(*acts, *hbm_acts, *sides, *weights, cross_probs, probs)


MESH_ID = pl.DeviceIdType.MESH


def reduce_peers(dp_size):
    dp, sq, core, ypos, core_peer, y_peer = places()
    xpos, zpos = dp % 2, dp // 2
    depth = dp_size // 2
    peers = [core_peer, y_peer, (dp + 1 - 2 * xpos, sq)]
    return peers + [((zpos + step) % depth * 2 + xpos, sq) for step in range(1, depth)]


def reducer(units, colors, ins, emit, buffers, dp_size):
    sent, core_in, first_y, first_x, second_y, second_x, third = buffers[:7]
    z_in, z_half, z_last = buffers[7:10]
    core_s, core_r, one_s, one_r, two_s, two_r, three_s, three_r = buffers[10:18]
    core_free, one_free, two_free = buffers[18:]
    dp, sq, core, ypos, core_peer, y_peer = places()
    xpos, zpos = dp % 2, dp // 2
    depth = dp_size // 2
    chunk = 1024 // dp_size
    x_peer = (dp + 1 - 2 * xpos, sq)
    count = len(units)
    remote = remote_copy
    nth = [colors[:item].count(colors[item]) for item in range(2 * count)]
    order = [item - colors[:item].count("z") for item in range(2 * count)]
    firsts = {"y": first_y, "x": first_x}
    seconds = {"y": second_y, "x": second_x}
    color_id = {"y": 0, "x": RING_ONE}
    first_peer = {"y": y_peer, "x": x_peer}
    second_peer = {"y": x_peer, "x": y_peer}

    def z_peer(step):
        return ((zpos + step) % depth * 2 + xpos, sq)

    def half_dots(unit, half, write):
        x_id, y_id, kind, part, base, tokens = units[unit]
        x_ref, y_ref = ins[x_id], ins[y_id]
        if kind == "back":
            starts = [device * 4 * chunk + part * chunk for device in range(dp_size)]
            left = jnp.concatenate([x_ref[:tokens, s : s + chunk] for s in starts], axis=1)
        else:
            left = x_ref[:tokens, base : base + 1024]
        for side in range(2):
            start = (side * 2 + half) * COLS
            if kind == "in":
                start = (side * 2 + half) * 1024 + part * COLS
            right = y_ref[:tokens, pl.ds(pl.multiple_of(start, COLS), COLS)]
            value = lax.dot_general(
                left, right, (((0,), (0,)), ((), ())), preferred_element_type=WIDE
            )
            write(0, side, value[:, :128])
            write(1, side, value[:, 128:])

    def landed(item):
        return core_in.at[item // 2 % RING, item % 2]

    def core_copy(unit):
        return remote(
            sent.at[unit % SLOTS],
            core_in.at[unit % RING],
            core_s.at[unit],
            core_r.at[unit],
            core_peer,
        )

    def one_copy(item):
        color, source = colors[item], landed(item)
        if color == "y":
            source = source.at[1 - ypos]
        else:
            source = source.reshape(2, depth, 2, chunk, 128).at[:, :, 1 - xpos]
        return remote(
            source,
            firsts[color].at[nth[item] % RING_ONE],
            one_s.at[item],
            one_r.at[item],
            first_peer[color],
        )

    def two_copy(item):
        color = colors[item]
        source = firsts[color].at[nth[item] % RING_ONE]
        if color == "y":
            source = source.reshape(depth, 2, chunk, 128).at[:, 1 - xpos]
        else:
            source = source.at[1 - ypos]
        return remote(
            source,
            seconds[color].at[nth[item] % RING_ONE],
            two_s.at[item],
            two_r.at[item],
            second_peer[color],
        )

    def three_copy(item, step):
        color = colors[item]
        return remote(
            seconds[color].at[nth[item] % RING_ONE, (zpos + step) % depth],
            third.at[order[item], step - 1],
            three_s.at[item, step - 1],
            three_r.at[item, step - 1],
            z_peer(step),
        )

    def z_copy(item, step):
        source = landed(item).reshape(2, depth, 2 * chunk, 128)
        return remote(
            source.at[:, (zpos + step) % depth],
            z_in.at[nth[item], step - 1],
            three_s.at[item, step - 1],
            three_r.at[item, step - 1],
            z_peer(step),
        )

    def zy_copy(item):
        return remote(
            z_in.at[nth[item], 0, 1 - ypos],
            z_half.at[nth[item]],
            one_s.at[item],
            one_r.at[item],
            y_peer,
        )

    def zx_copy(item):
        source = z_half.at[nth[item]].reshape(2, chunk, 128)
        return remote(
            source.at[1 - xpos], z_last.at[nth[item]], two_s.at[item], two_r.at[item], x_peer
        )

    def take(free, slot):
        pl.semaphore_wait(free.at[slot], 1)

    def allow(free, slot, peer):
        pl.semaphore_signal(free.at[slot], inc=1, device_id=peer, device_id_type=MESH_ID)

    def steps(action):
        def body(step, carry):
            action(step)
            return carry

        lax.fori_loop(1, depth, body, 0)

    def plus(left, right):
        return (left.astype(WIDE) + right.astype(WIDE)).astype(LOW)

    def products(unit):
        slot = unit % SLOTS
        if unit >= SLOTS:
            core_copy(unit - SLOTS).wait_send()

        def write(item, side, value):
            sent[slot, item, side] = value.astype(LOW)

        half_dots(unit, 1 - core, write)
        if unit >= RING:
            for item in range(2):
                take(core_free, unit % RING * 2 + item)
        core_copy(unit).start()

    def core_sum(unit):
        core_copy(unit).wait_recv()
        slot = unit % RING

        def write(item, side, value):
            old = core_in[slot, item, side].astype(WIDE)
            core_in[slot, item, side] = (value + old).astype(LOW)

        half_dots(unit, core, write)
        for item in (2 * unit, 2 * unit + 1):
            color = colors[item]
            if color == "z":
                steps(lambda step: z_copy(item, step).start())
                continue
            if nth[item] >= RING_ONE:
                take(one_free, color_id[color] + nth[item] % RING_ONE)
            one_copy(item).start()

    def core_done(item):
        if item // 2 + RING < count:
            allow(core_free, item // 2 % RING * 2 + item % 2, core_peer)

    def one_sum(item):
        color = colors[item]
        if color == "z":
            return
        one_copy(item).wait_recv()
        slot, base, own = nth[item] % RING_ONE, item // 2 % RING, item % 2
        if color == "y":

            def body(step, carry):
                rows = pl.ds(pl.multiple_of(step * 256, 256), 256)
                first_y[slot, rows, :] = plus(
                    first_y[slot, rows, :], core_in[base, own, ypos, rows, :]
                )
                return carry

            lax.fori_loop(0, 4, body, 0)
        else:

            def body(layer, carry):
                rows = pl.ds(pl.multiple_of((layer * 2 + xpos) * chunk, chunk), chunk)
                for side in range(2):
                    first_x[slot, side, layer] = plus(
                        first_x[slot, side, layer], core_in[base, own, side, rows, :]
                    )
                return carry

            lax.fori_loop(0, depth, body, 0)
        if nth[item] >= RING_ONE:
            take(two_free, color_id[color] + nth[item] % RING_ONE)
        two_copy(item).start()
        one_copy(item).wait_send()
        core_done(item)

    def z_sum(item):
        base, own = item // 2 % RING, item % 2
        rows = pl.ds(pl.multiple_of(zpos * 2 * chunk, 2 * chunk), 2 * chunk)
        steps(lambda step: z_copy(item, step).wait_recv())
        for side in range(2):

            def body(step, total):
                return total + z_in[nth[item], step - 1, side].astype(WIDE)

            mine = core_in[base, own, side, rows, :].astype(WIDE)
            z_in[nth[item], 0, side] = lax.fori_loop(1, depth, body, mine).astype(LOW)
        zy_copy(item).start()
        steps(lambda step: z_copy(item, step).wait_send())
        core_done(item)

    def two_sum(item):
        color = colors[item]
        if color == "z":
            z_sum(item)
            return
        two_copy(item).wait_recv()
        slot = nth[item] % RING_ONE
        second = seconds[color]

        def body(layer, carry):
            if color == "y":
                rows = pl.ds(pl.multiple_of((layer * 2 + xpos) * chunk, chunk), chunk)
                old = first_y[slot, rows, :]
            else:
                old = first_x[slot, ypos, layer]
            second[slot, layer] = plus(second[slot, layer], old)
            return carry

        lax.fori_loop(0, depth, body, 0)
        steps(lambda step: three_copy(item, step).start())
        two_copy(item).wait_send()
        if nth[item] + RING_ONE < colors.count(color):
            allow(one_free, color_id[color] + slot, first_peer[color])

    def last_sum(item):
        color = colors[item]
        if color == "z":
            zy_copy(item).wait_recv()
            z_half[nth[item]] = plus(z_half[nth[item]], z_in[nth[item], 0, ypos])
            zx_copy(item).start()
            zy_copy(item).wait_send()
            return
        slot = nth[item] % RING_ONE

        def body(step, total):
            three_copy(item, step).wait_recv()
            return total + third[order[item], step - 1].astype(WIDE)

        total = lax.fori_loop(1, depth, body, seconds[color][slot, zpos].astype(WIDE))
        emit(units[item // 2], item % 2, total)
        steps(lambda step: three_copy(item, step).wait_send())
        if nth[item] + RING_ONE < colors.count(color):
            allow(two_free, color_id[color] + slot, second_peer[color])

    def z_end(item):
        if colors[item] == "z":
            zx_copy(item).wait_recv()
            rows = pl.ds(pl.multiple_of(xpos * chunk, chunk), chunk)
            mine = z_half[nth[item], rows, :].astype(WIDE)
            emit(units[item // 2], item % 2, mine + z_last[nth[item]].astype(WIDE))
            zx_copy(item).wait_send()

    def turn(index):
        for stage, lag in ((products, 0), (core_sum, 1)):
            if 0 <= index - lag < count:
                stage(index - lag)
        for stage, lag in ((one_sum, 3), (two_sum, 5), (last_sum, 7), (z_end, 9)):
            for item in (2 * (index - lag), 2 * (index - lag) + 1):
                if 0 <= item < 2 * count:
                    stage(item)

    def drain():
        for unit in range(count - SLOTS, count):
            core_copy(unit).wait_send()

    return turn, drain


def reduce_buffers(colors, dp_size):
    depth, chunk = dp_size // 2, 1024 // dp_size
    count, slow = len(colors), max(colors.count("z"), 1)
    sem = pltpu.SemaphoreType.DMA
    credit = pltpu.SemaphoreType.REGULAR
    return (
        [
            pltpu.VMEM((SLOTS, 2, 2, 1024, 128), LOW),
            pltpu.VMEM((RING, 2, 2, 1024, 128), LOW),
            pltpu.VMEM((RING_ONE, 1024, 128), LOW),
            pltpu.VMEM((RING_ONE, 2, depth, chunk, 128), LOW),
            pltpu.VMEM((RING_ONE, depth, chunk, 128), LOW),
            pltpu.VMEM((RING_ONE, depth, chunk, 128), LOW),
            pltpu.VMEM((count - colors.count("z"), depth - 1, chunk, 128), LOW),
            pltpu.VMEM((slow, depth - 1, 2, 2 * chunk, 128), LOW),
            pltpu.VMEM((slow, 2 * chunk, 128), LOW),
            pltpu.VMEM((slow, chunk, 128), LOW),
        ]
        + [sem((count // 2,))] * 2
        + [sem((count,))] * 4
        + [sem((count, depth - 1))] * 2
        + [credit((2 * RING,)), credit((2 * RING_ONE,)), credit((2 * RING_ONE,))]
    )


def small_sums(small, small_in, small_s, small_r, dp_size):
    dp, sq, core, ypos, core_peer, y_peer = places()

    def copy(step):
        flip = 1 << max(step - 2, 0)
        peer = (dp + flip - 2 * flip * (dp // flip % 2), sq)
        peer = (core_peer, y_peer, peer)[min(step, 2)]
        return remote_copy(small, small_in.at[step], small_s.at[step], small_r.at[step], peer)

    def advance(step):
        copy(step).wait()
        small[...] = small[...] + small_in[step]
        if step < dp_size.bit_length():
            copy(step + 1).start()

    return copy, advance


def per_device(
    stream,
    encoded,
    cotangent,
    lengths,
    bucket_table,
    w_query,
    w_key,
    w_value,
    w_out,
    c_query,
    c_key,
    c_value,
    c_out,
    w_in,
    w_back,
    gain_one,
    shift_one,
    gain_two,
    shift_two,
    gain_three,
    shift_three,
    position_bias,
):
    num_rows, num_streams, local_len, model_width = stream.shape
    full_len = local_len * lax.axis_size("seq")
    sq = lax.axis_index("seq")
    dp_size = lax.axis_size("dp")
    chunk = model_width // dp_size
    bucket_ids = jnp.arange(NBUCKET, dtype=jnp.int32)
    exact = lax.Precision.HIGHEST
    table_hot = (bucket_table[:, None] == bucket_ids[None, :]).astype(jnp.float32)
    by_distance = jnp.einsum("db,bh->hd", table_hot, position_bias, precision=exact)
    bias_table = jnp.concatenate([jnp.zeros_like(by_distance), by_distance], axis=1)[:, None, :]
    flat_rows = stream.reshape(-1, model_width)
    source_rows = encoded.reshape(-1, model_width)
    flat_cotangent = cotangent.reshape(-1, model_width)

    def line(values):
        return values.reshape(1, model_width)

    fronts = front(
        stream.reshape(num_streams, local_len, model_width),
        source_rows,
        lengths,
        bias_table,
        (line(gain_one), line(shift_one), line(gain_two), line(shift_two)),
        (w_query, w_key, w_value, w_out, c_query, c_key, c_value, c_out),
    )
    query, own_key, own_value, main_key, main_value, context_low, unit_one, first_norm = fronts[:8]
    cross_query, cross_key, cross_value, cross_low, unit_two, second_norm = fronts[8:14]
    scales, own_probs, front_stats, probs, cross_probs = fronts[14:]
    layer_output, activated, d_ffn_out, d_inner, d_resid_two, d_crossed, mid_grads, ffn_stat = middle(
        second_norm,
        unit_two,
        scales,
        flat_cotangent,
        lengths,
        (line(gain_two), line(gain_three), line(shift_three)),
        w_in,
        w_back,
    )
    blocks = full_len // local_len
    place = jnp.arange(2 * local_len, dtype=jnp.int32)
    reach = (sq - jnp.arange(blocks, dtype=jnp.int32))[:, None] * local_len + (
        local_len - 1 - place[None, :]
    )
    reach = jnp.concatenate([reach, jnp.zeros((1, 2 * local_len), jnp.int32)])
    lane_ids = jnp.arange(128, dtype=jnp.int32)
    first_of = jnp.sum((bucket_table[:, None] < lane_ids[None, :]).astype(jnp.int32), axis=0)
    next_of = jnp.sum((bucket_table[:, None] <= lane_ids[None, :]).astype(jnp.int32), axis=0)
    window_hot = (reach[..., None] >= first_of) & (reach[..., None] < next_of)
    position = sq * local_len + jnp.arange(local_len)
    count = num_streams * jnp.sum((position < lengths[0]).astype(jnp.float32))
    mid_stats = jnp.concatenate([front_stats, ffn_stat]).reshape(4, -1, 128).sum(axis=1)
    mid_stats = jnp.concatenate([mid_stats, jnp.full((4, 128), count / 128)])
    units = []
    tokens = num_streams * local_len
    spread = activated
    if chunk % 128 != 0:
        spread = activated.reshape(-1, dp_size, 4, chunk)
        spread = jnp.transpose(spread, (0, 2, 1, 3)).reshape(activated.shape)
    for part in range(4):
        if chunk % 128 == 0:
            units.append((3, 0, "back", part, 0, tokens))
        else:
            units.append((3, 0, "parted", part, part * model_width, tokens))
        units.append((1, 2, "in", part, 0, tokens))
    units += [(4, 5, "", 7, 0, tokens), (6, 7, "", 4, 0, tokens), (3, 8, "", 3, 0, tokens)]
    units += [(3, 9, "", 5, 2 * model_width, local_len), (3, 10, "", 6, 2 * model_width, local_len)]
    units += [(3, 11 + part, "", part, model_width, tokens) for part in range(3)]
    rears = rear(
        (
            d_crossed,
            cross_query,
            unit_one,
            query,
            own_key,
            own_value,
            own_probs,
            line(gain_one),
            d_ffn_out,
            second_norm,
            cross_low,
            first_norm,
            mid_grads,
            mid_stats,
            window_hot.astype(jnp.bfloat16),
            scales,
        ),
        (d_inner, spread, context_low, flat_rows, source_rows, d_resid_two),
        (cross_key, cross_value, main_key, main_value),
        (c_out, c_query, w_out, w_query, w_key, w_value, c_key, c_value),
        cross_probs,
        probs,
        tuple(units),
        dp_size,
    )
    encoded_grad, stream_grad, sums = rears[:3]
    shares = rears[3:]
    wide_sums = sums[:48].reshape(6, model_width)
    rms = jnp.sqrt(jnp.sum(sums[64:68], axis=1) / (jnp.sum(sums[68]) * model_width))
    return (
        layer_output.reshape(stream.shape),
        stream_grad.reshape(stream.shape),
        encoded_grad.reshape(encoded.shape),
        shares[0],
        shares[1],
        shares[2],
        shares[3],
        shares[4],
        shares[5],
        shares[6],
        shares[7],
        shares[8],
        shares[9],
        wide_sums[0],
        wide_sums[1],
        wide_sums[2],
        wide_sums[3],
        wide_sums[4],
        wide_sums[5],
        jnp.transpose(sums[48:64, :NBUCKET]),
        rms,
    )


def solution(mesh):
    placed = (
        P("dp", None, "seq", None),
        P("dp", "seq", None),
        P("dp", None, "seq", None),
        P("dp"),
        P(),
        P(),
        P(),
        P(),
        P(),
        P(),
        P(),
        P(),
        P(),
        P(),
        P(),
        P(),
        P(),
        P(),
        P(),
        P(),
        P(),
        P(),
    )
    return jax.shard_map(
        per_device,
        mesh=mesh,
        in_specs=placed,
        out_specs=(
            P("dp", None, "seq", None),
            P("dp", None, "seq", None),
            P("dp", "seq", None),
            P("dp", "seq"),
            P("dp", "seq"),
            P("dp", "seq"),
            P("dp", "seq"),
            P("dp", "seq"),
            P("dp", "seq"),
            P("dp", "seq"),
            P("dp", "seq"),
            P("dp", "seq"),
            P("dp", "seq"),
            P(),
            P(),
            P(),
            P(),
            P(),
            P(),
            P(),
            P(),
        ),
        check_vma=False,
    )
```

```python
import functools

import jax
import jax.numpy as jnp
from jax import lax
from jax.experimental import pallas as pl
from jax.experimental.pallas import tpu as pltpu
from jax.sharding import PartitionSpec as P

HEADS = 16
HEAD_DIM = 64
NBUCKET = 32
COLS = 256
SLOTS = 2
RING = 6
RING_ONE = 5
COLORS = "yxyxzxyxyxzxyxzxyxyxzxyxzxyxyxyx"
epsilon = 1e-05
masked_score = -1e30


LOW = jnp.bfloat16
WIDE = jnp.float32
NN = (((1,), (0,)), ((), ()))
NT = (((1,), (1,)), ((), ()))


def dot(left, right, dims=NN):
    return lax.dot_general(left, right, dims, preferred_element_type=WIDE)


def flip(block):
    return jnp.transpose(block.astype(WIDE))


def places():
    dp, sq = lax.axis_index("dp"), lax.axis_index("seq")
    core, ypos = sq % 2, sq // 2
    return dp, sq, core, ypos, (dp, sq + 1 - 2 * core), (dp, sq + 2 - 4 * ypos)


def remote_copy(src, dst, send_sem, recv_sem, peer):
    return pltpu.make_async_remote_copy(
        src_ref=src,
        dst_ref=dst,
        send_sem=send_sem,
        recv_sem=recv_sem,
        device_id=peer,
        device_id_type=MESH_ID,
    )


def greet(peers):
    barrier = pltpu.get_barrier_semaphore()
    for peer in peers:
        pl.semaphore_signal(barrier, inc=1, device_id=peer, device_id_type=MESH_ID)
    pl.semaphore_wait(barrier, len(peers))


def tiles(count, size, body):
    def step(index, carry):
        body(pl.ds(pl.multiple_of(index * size, size), size))
        return carry

    lax.fori_loop(0, count, step, 0)


def project_to(dst, left, weight, scale=None):
    product = dot(left[...], weight[...])
    if scale is not None:
        product = product * scale
    dst[...] = product.astype(dst.dtype)


def norm_stats(rows):
    centre = jnp.mean(rows, axis=-1, keepdims=True)
    centred = rows - centre
    spread = jnp.mean(centred * centred, axis=-1, keepdims=True)
    return centred, lax.rsqrt(spread + epsilon)


def norm_backward(unit, scale, gain, incoming):
    scaled = incoming * gain
    first = jnp.mean(scaled, axis=-1, keepdims=True)
    second = jnp.mean(scaled * unit, axis=-1, keepdims=True)
    grads = scale * (scaled - first - unit * second)
    d_gain = jnp.sum(incoming * unit, axis=0, keepdims=True)
    return grads, d_gain, jnp.sum(incoming, axis=0, keepdims=True)


def valid_rows(sq, length, count):
    position = sq * count + lax.broadcasted_iota(jnp.int32, (count, 1), 0)
    return (position < length).astype(WIDE)


def sum_squares(rows, mask):
    return jnp.sum(rows * rows * mask, axis=0, keepdims=True)


def half_rows(block, side):
    row = lax.broadcasted_iota(jnp.int32, block.shape, 0)
    return jnp.where(row // HEAD_DIM == side, block, 0.0).astype(LOW)


def half_lanes(block, side):
    lane = lax.broadcasted_iota(jnp.int32, block.shape, 1)
    return jnp.where(lane // HEAD_DIM == side, block.astype(WIDE), 0.0).astype(LOW)


def front_kernel(*refs):
    stream, encoded, length_ref, bucket_row, position_bias = refs[:5]
    gain_one, shift_one, gain_two, shift_two = refs[5:9]
    hbm_weights = refs[9:17]
    outs, probs_out, cross_probs_out = refs[17:34], refs[34], refs[35]
    held, refs = refs[36:53], refs[53:]
    (query, own_key, own_value, main_key, main_value, context, unit_one, first_norm) = held[:8]
    (cross_query, cross_key, cross_value, cross_context, unit_two, second_norm) = held[8:14]
    scales, own_probs, stats = held[14:]
    weights = refs[:8]
    main_all, source_all, kept, bias, masks, branch_out, bias_table = refs[8:15]
    weight_sem, kept_sem, send_sem, recv_sem, out_sem = refs[15:]
    stores = [
        pltpu.make_async_copy(src, dst, out_sem.at[index])
        for index, (src, dst) in enumerate(zip(held, outs))
    ]
    w_query, w_key, w_value, w_out, c_query, c_key, c_value, c_out = weights
    dp, sq, core, ypos, core_peer, y_peer = places()
    length = length_ref[0]
    rows = stream.shape[1]
    full = main_all.shape[0] * rows
    loads = [
        pltpu.make_async_copy(src, dst, weight_sem.at[index])
        for index, (src, dst) in enumerate(zip(hbm_weights, weights))
    ]
    for load in loads:
        load.start()
    greet([core_peer, y_peer])
    sources = (stream.at[0], encoded)
    gathered = (main_all, source_all)
    firsts = []
    for index in range(2):
        for lane, peer in enumerate((y_peer, core_peer)):
            slot = index * 3 + lane
            firsts.append(
                remote_copy(
                    sources[index],
                    gathered[index].at[sq],
                    send_sem.at[slot],
                    recv_sem.at[slot],
                    peer,
                )
            )
    firsts[0].start()
    firsts[1].start()
    main_all[sq] = stream[0]
    source_all[sq] = encoded[...]
    bucket = lax.broadcasted_iota(jnp.int32, (NBUCKET, full), 0)
    table_hot = (bucket == bucket_row[...]).astype(WIDE).astype(LOW)
    by_distance = jnp.zeros((HEADS, full), WIDE)
    rest = position_bias[...]
    for _ in range(3):
        part = rest.astype(LOW)
        rest = rest - part.astype(WIDE)
        by_distance = by_distance + dot(part, table_hot, (((0,), (0,)), ((), ())))
    bias_table[...] = jnp.zeros_like(bias_table)
    for head in range(HEADS):
        bias_table[head, :, full:] = by_distance[head : head + 1]

    def passed_on(index):
        other = gathered[index].at[sq + 2 - 4 * ypos]
        slot = index * 3 + 2
        return remote_copy(other, other, send_sem.at[slot], recv_sem.at[slot], core_peer)

    flat = stream.reshape(3 * rows, stream.shape[2])
    loads[0].wait()
    project_to(query, flat, w_query, 0.125)
    stores[0].start()
    predicting = flat.at[rows:, :]
    loads[1].wait()
    project_to(own_key, predicting, w_key)
    loads[2].wait()
    project_to(own_value, predicting, w_value)
    key_row = lax.broadcasted_iota(jnp.int32, (full, rows), 0)
    distance = sq * rows + lax.broadcasted_iota(jnp.int32, (full, rows), 1) - key_row
    in_range = key_row < length
    masks[0] = jnp.where((distance >= 0) & in_range, 0.0, masked_score)
    masks[1] = jnp.where((distance > 0) & in_range, 0.0, masked_score)
    masks[2] = jnp.where(in_range, 0.0, masked_score)
    firsts[0].wait_recv()
    passed_on(0).start()
    firsts[2].start()
    firsts[3].start()
    stores[1].start()
    stores[2].start()
    firsts[1].wait_recv()
    passed_on(0).wait_recv()
    wide_main = main_all.reshape(full, main_all.shape[2])
    project_to(main_key, wide_main, w_key)
    project_to(main_value, wide_main, w_value)
    stores[3].start()
    stores[4].start()

    def kept_copy(pair, out):
        slot = pair % 2
        return pltpu.make_async_copy(kept.at[slot], out.at[pair], kept_sem.at[slot])

    def self_pair(pair, carry):
        @pl.when(pair >= 2)
        def _():
            kept_copy(pair - 2, probs_out).wait()

        slot = pair % 2
        cols = pl.ds(pl.multiple_of(pair * 128, 128), 128)
        keys = main_key[:, cols]
        query_t = flip(query[:, cols])
        value_t = flip(main_value[:, cols]).astype(LOW)
        own_key_t, own_value_t = flip(own_key[:, cols]), flip(own_value[:, cols])
        own_product = query_t[:, rows:] * own_key_t
        sides = []
        for side in range(2):
            head = 2 * pair + side
            span = slice(side * HEAD_DIM, (side + 1) * HEAD_DIM)
            scores = dot(keys, half_rows(query_t, side))
            own_bias = bias_table[head, :, full : full + 128][:, 0:1]
            own_score = jnp.sum(own_product[span], axis=0, keepdims=True) + own_bias
            for block in range(full // rows):
                start = pl.multiple_of((sq - block + full // rows - 1) * rows, 128)
                line = bias_table[head, :, pl.ds(start, 2 * rows)]
                wide = jnp.broadcast_to(line, (rows, 2 * rows))
                near = pltpu.roll(wide, 0, 1, stride=1, stride_axis=0)[:, rows:]
                part = slice(block * rows, (block + 1) * rows)
                for kind in range(2):
                    bias[kind, part, :] = near + masks[kind, part, :]
            owns = []
            for stream_id in range(3):
                lanes = slice(stream_id * rows, (stream_id + 1) * rows)
                score = scores[:, lanes] + bias[min(stream_id, 1)]
                top = jnp.max(score, axis=0, keepdims=True)
                if stream_id > 0:
                    own = own_score[:, (stream_id - 1) * rows : stream_id * rows]
                    top = jnp.maximum(top, own)
                expo = jnp.exp(score - top)
                total = jnp.sum(expo, axis=0, keepdims=True)
                if stream_id > 0:
                    expo_own = jnp.exp(own - top)
                    total = total + expo_own
                share = 1.0 / total
                kept[slot, side, :, lanes] = (expo * share).astype(LOW)
                owns.append(expo_own * share if stream_id > 0 else jnp.zeros_like(total))
            own_probs[head] = jnp.concatenate(owns, axis=1)
            mixed = dot(value_t[span], kept[slot, side])
            mixed_own = jnp.concatenate(owns[1:], axis=1) * own_value_t[span]
            sides.append(
                jnp.concatenate([mixed[:, :rows], mixed[:, rows:] + mixed_own], axis=1)
            )
        context[:, cols] = jnp.transpose(jnp.concatenate(sides, axis=0)).astype(LOW)
        kept_copy(pair, probs_out).start()
        return carry

    lax.fori_loop(0, HEADS // 2, self_pair, 0)
    for pair in range(HEADS // 2 - 2, HEADS // 2):
        kept_copy(pair, probs_out).wait()
    stores[5].start()
    stores[15].start()

    mask = valid_rows(sq, length, rows)
    loads[3].wait()
    project_to(branch_out, context, w_out)
    firsts[2].wait_recv()
    passed_on(1).start()
    seen = jnp.zeros((1, stream.shape[2]), WIDE)
    branch = jnp.zeros((1, stream.shape[2]), WIDE)
    for stream_id in range(3):
        part = slice(stream_id * rows, (stream_id + 1) * rows)
        source, attended = stream[stream_id].astype(WIDE), branch_out[part, :]
        seen = seen + sum_squares(source, mask)
        branch = branch + sum_squares(attended, mask)
        centred, scale = norm_stats(source + attended)
        unit = centred * scale
        unit_one[part, :] = unit.astype(LOW)
        scales[0, part, :] = jnp.broadcast_to(scale, (rows, 128))
        first_norm[part, :] = (unit * gain_one[...] + shift_one[...]).astype(LOW)
    stats[0:1, :] = seen
    stats[1:2, :] = branch
    loads[4].wait()
    project_to(cross_query, first_norm, c_query, 0.125)
    for index in (6, 7, 8):
        stores[index].start()
    firsts[3].wait_recv()
    passed_on(1).wait_recv()
    wide_source = source_all.reshape(full, source_all.shape[2])
    loads[5].wait()
    project_to(cross_key, wide_source, c_key)
    loads[6].wait()
    project_to(cross_value, wide_source, c_value)
    stores[9].start()
    stores[10].start()

    def cross_pair(pair, carry):
        @pl.when(pair >= 2)
        def _():
            kept_copy(pair - 2, cross_probs_out).wait()

        slot = pair % 2
        cols = pl.ds(pl.multiple_of(pair * 128, 128), 128)
        keys = cross_key[:, cols]
        query_t = flip(cross_query[:, cols])
        value_t = flip(cross_value[:, cols]).astype(LOW)
        sides = []
        for side in range(2):
            span = slice(side * HEAD_DIM, (side + 1) * HEAD_DIM)
            scores = dot(keys, half_rows(query_t, side))
            for stream_id in range(3):
                lanes = slice(stream_id * rows, (stream_id + 1) * rows)
                score = scores[:, lanes] + masks[2]
                expo = jnp.exp(score - jnp.max(score, axis=0, keepdims=True))
                share = 1.0 / jnp.sum(expo, axis=0, keepdims=True)
                kept[slot, side, :, lanes] = (expo * share).astype(LOW)
            sides.append(dot(value_t[span], kept[slot, side]))
        cross_context[:, cols] = jnp.transpose(jnp.concatenate(sides, axis=0)).astype(LOW)
        kept_copy(pair, cross_probs_out).start()
        return carry

    lax.fori_loop(0, HEADS // 2, cross_pair, 0)
    for pair in range(HEADS // 2 - 2, HEADS // 2):
        kept_copy(pair, cross_probs_out).wait()
    stores[11].start()
    loads[7].wait()
    project_to(branch_out, cross_context, c_out)
    branch = jnp.zeros((1, stream.shape[2]), WIDE)
    for stream_id in range(3):
        part = slice(stream_id * rows, (stream_id + 1) * rows)
        crossed = branch_out[part, :]
        branch = branch + sum_squares(crossed, mask)
        centred, scale = norm_stats(first_norm[part, :].astype(WIDE) + crossed)
        unit = centred * scale
        unit_two[part, :] = unit.astype(LOW)
        scales[1, part, :] = jnp.broadcast_to(scale, (rows, 128))
        second_norm[part, :] = (unit * gain_two[...] + shift_two[...]).astype(LOW)
    stats[2:3, :] = branch
    for index in (12, 13, 14, 16):
        stores[index].start()
    for store in stores:
        store.wait()
    for copy in firsts:
        copy.wait_send()
    for index in range(2):
        passed_on(index).wait_send()


def front(stream, encoded, length, bucket_row, position_bias, norms, weights):
    streams, rows, width = stream.shape
    seq = lax.axis_size("seq")
    full, tokens = seq * rows, streams * rows
    own = tokens - rows
    shape = jax.ShapeDtypeStruct
    pairs = HEADS // 2
    outs = [
        shape((tokens, width), LOW),
        shape((own, width), LOW),
        shape((own, width), LOW),
        shape((full, width), LOW),
        shape((full, width), LOW),
        shape((tokens, width), LOW),
        shape((tokens, width), LOW),
        shape((tokens, width), LOW),
        shape((tokens, width), LOW),
        shape((full, width), LOW),
        shape((full, width), LOW),
        shape((tokens, width), LOW),
        shape((tokens, width), LOW),
        shape((tokens, width), LOW),
        shape((2, tokens, 128), WIDE),
        shape((HEADS, 1, tokens), WIDE),
        shape((3, width), WIDE),
        shape((pairs, 2, full, tokens), LOW),
        shape((pairs, 2, full, tokens), LOW),
    ]
    vmem = pl.BlockSpec(memory_space=pltpu.VMEM)
    smem = pl.BlockSpec(memory_space=pltpu.SMEM)
    hbm = pl.BlockSpec(memory_space=pl.ANY)
    sem = pltpu.SemaphoreType.DMA
    return pl.pallas_call(
        front_kernel,
        out_shape=outs,
        in_specs=[vmem, vmem, smem] + [vmem] * 6 + [hbm] * 8,
        out_specs=[hbm] * 19,
        scratch_shapes=[pltpu.VMEM(out.shape, out.dtype) for out in outs[:17]]
        + [pltpu.VMEM(w.shape, LOW) for w in weights]
        + [
            pltpu.VMEM((seq, rows, width), LOW),
            pltpu.VMEM((seq, rows, width), LOW),
            pltpu.VMEM((2, 2, full, tokens), LOW),
            pltpu.VMEM((2, full, rows), WIDE),
            pltpu.VMEM((3, full, rows), WIDE),
            pltpu.VMEM((tokens, width), WIDE),
            pltpu.VMEM((HEADS, 1, 2 * full), WIDE),
            sem((8,)),
            sem((2,)),
            sem((6,)),
            sem((6,)),
            sem((17,)),
        ],
        compiler_params=pltpu.CompilerParams(
            collective_id=1, has_side_effects=True, vmem_limit_bytes=60 << 20
        ),
    )(stream, encoded, length, bucket_row, position_bias, *norms, *weights)


def middle_kernel(*refs):
    second_norm, cotangent, length_ref, gain_three, shift_three, hbm_in, hbm_back = refs[:7]
    outs, grads, stats = refs[7:12], refs[12], refs[13]
    output, activated, d_ffn, slope, total = refs[14:19]
    w_in, w_back, load_sem, out_sem = refs[19:]
    sq = lax.axis_index("seq")
    length = length_ref[0]
    tokens, width = second_norm.shape
    rows = tokens // 3
    hidden = w_in.shape[1]
    size = 1024
    steps = hidden // size
    stores = [
        pltpu.make_async_copy(src, dst, out_sem.at[index])
        for index, (src, dst) in enumerate(zip(refs[14:19], outs))
    ]

    def load_in(step):
        cols = pl.ds(pl.multiple_of(step * size, size), size)
        return pltpu.make_async_copy(hbm_in.at[:, cols], w_in.at[:, cols], load_sem.at[0, step])

    def load_back(step):
        cols = pl.ds(pl.multiple_of(step * size, size), size)
        return pltpu.make_async_copy(hbm_back.at[cols], w_back.at[cols], load_sem.at[1, step])

    for step in range(steps):
        load_in(step).start()
        load_back(step).start()
    total[...] = jnp.zeros_like(total)

    def forward(step, carry):
        cols = pl.ds(pl.multiple_of(step * size, size), size)
        load_in(step).wait()
        inner = dot(second_norm[...], w_in[:, cols])
        phi = 0.5 + 0.5 * lax.erf(inner * (0.5**0.5))
        bell = jnp.exp(inner * inner * -0.5) * (0.5 / jnp.pi) ** 0.5
        value = (inner * phi).astype(LOW)
        activated[:, cols] = value
        slope[:, cols] = (phi + inner * bell).astype(LOW)
        load_back(step).wait()
        total[...] += dot(value, w_back[cols, :])
        return carry

    lax.fori_loop(0, steps, forward, 0)
    stores[1].start()
    stores[3].start()
    mask = valid_rows(sq, length, rows)
    branch = jnp.zeros((1, width), WIDE)
    d_gain = jnp.zeros((1, width), WIDE)
    d_shift = jnp.zeros((1, width), WIDE)
    for stream_id in range(3):
        part = slice(stream_id * rows, (stream_id + 1) * rows)
        ffn = total[part, :]
        branch = branch + sum_squares(ffn, mask)
        resid = second_norm[part, :].astype(WIDE) + ffn
        centred, scale = norm_stats(resid)
        unit = centred * scale
        normed = unit * gain_three[...] + shift_three[...]
        output[part, :] = (normed * mask).astype(LOW)
        incoming = cotangent[part, :].astype(WIDE) * mask
        back, gain_part, shift_part = norm_backward(unit, scale, gain_three[...], incoming)
        d_gain, d_shift = d_gain + gain_part, d_shift + shift_part
        total[part, :] = back
        d_ffn[part, :] = back.astype(LOW)
    stats[...] = branch
    grads[0:1, :] = d_gain
    grads[1:2, :] = d_shift
    for index in (0, 2, 4):
        stores[index].start()
    for store in stores:
        store.wait()


def middle(second_norm, cotangent, length, norms, w_in, w_back):
    tokens, width = second_norm.shape
    hidden = w_in.shape[1]
    shape = jax.ShapeDtypeStruct
    vmem = pl.BlockSpec(memory_space=pltpu.VMEM)
    smem = pl.BlockSpec(memory_space=pltpu.SMEM)
    hbm = pl.BlockSpec(memory_space=pl.ANY)
    outs = [
        shape((tokens, width), LOW),
        shape((tokens, hidden), LOW),
        shape((tokens, width), LOW),
        shape((tokens, hidden), LOW),
        shape((tokens, width), WIDE),
    ]
    return pl.pallas_call(
        middle_kernel,
        out_shape=outs + [shape((2, width), WIDE), shape((1, width), WIDE)],
        in_specs=[vmem] * 2 + [smem] + [vmem] * 2 + [hbm] * 2,
        out_specs=[hbm] * 5 + [vmem] * 2,
        scratch_shapes=[pltpu.VMEM(out.shape, out.dtype) for out in outs]
        + [
            pltpu.VMEM(w_in.shape, LOW),
            pltpu.VMEM(w_back.shape, LOW),
            pltpu.SemaphoreType.DMA((2, hidden // 1024)),
            pltpu.SemaphoreType.DMA((5,)),
        ],
        compiler_params=pltpu.CompilerParams(vmem_limit_bytes=60 << 20),
    )(second_norm, cotangent, length, *norms, w_in, w_back)


def rear_kernel(units, dp_size, *refs):
    cross_query, unit_one, query, own_key, own_value, own_probs, gain_one = refs[:7]
    refs = (None,) + refs
    d_ffn, second_norm, cross_context, first_norm, mid_grads, ffn_stat, front_stats = refs[8:15]
    scales, gain_two, bucket_row, length_ref = refs[15:19]
    refs = refs[:15] + refs[19:]
    hbm_slope, hbm_activated, hbm_context, hbm_stream, hbm_source, hbm_resid = refs[15:21]
    hbm_unit, refs = refs[21], refs[:21] + refs[22:]
    hbm_sides, hbm_weights = refs[21:25], refs[25:33]
    hbm_ffn, refs = refs[33:35], refs[:33] + refs[35:]
    cross_probs, probs = refs[33:35]
    encoded_grad, stream_grad, small_out = refs[35:38]
    shares, in_share, back_share = refs[38:46], refs[46], refs[47]
    (d_cross_query, d_cross_key, d_cross_value, d_attended) = refs[48:52]
    (d_query, d_key, d_value, bias_sums, small_in) = refs[52:57]
    d_inner, activated = refs[57:59]
    weights = refs[59:62]
    kept, d_context, d_resid, parts, near_in, far_in, sides_held = refs[62:69]
    d_crossed, ffn_sem, refs = refs[69], refs[70], refs[:69] + refs[71:]
    weight_sem, kept_sem, core_s, core_r, far_s, far_r, small_s, small_r = refs[69:77]
    held = (0, 1, 2, 0, 1, 2, 1, 2)
    c_out, c_query, w_out, w_query, w_key, w_value, c_key, c_value = [weights[i] for i in held]
    chunk = 1024 // dp_size

    def emit(unit, item, total):
        part, cols = unit[3], slice(item * 128, (item + 1) * 128)
        if unit[2] == "in":
            in_share[:, part * COLS + item * 128 : part * COLS + (item + 1) * 128] = total
        elif unit[2] in ("back", "parted"):
            back_share[part * chunk : (part + 1) * chunk, cols] = total
        else:
            shares[part][:, cols] = total

    operands = (d_ffn, second_norm, d_inner, activated, cross_context, d_crossed, first_norm)
    operands += (d_cross_query, d_attended, d_cross_key, d_cross_value, d_query, d_key, d_value)
    turn, drain = reducer(units, COLORS, operands, emit, refs[77:], dp_size)
    small_copy, small_step = small_sums(small_out, small_in, small_s, small_r, dp_size)
    dp, sq, core, ypos, core_peer, y_peer = places()
    tokens, width = query.shape
    rows = tokens // 3
    full = sides_held.shape[1]
    blocks = full // rows
    keys_held, values_held = sides_held.at[0], sides_held.at[1]
    pairs = HEADS // 2
    loads = [
        pltpu.make_async_copy(src, weights[held[index]], weight_sem.at[index])
        for index, src in enumerate(hbm_weights)
    ]

    def load_extra(index, src, dst):
        return pltpu.make_async_copy(src, dst, weight_sem.at[12 + index])

    early = [
        load_extra(0, hbm_activated, activated),
        load_extra(1, hbm_slope, d_inner),
        load_extra(2, hbm_resid, d_resid),
        load_extra(6, hbm_unit, d_context),
    ]
    late = [
        load_extra(3, hbm_context, activated.at[:, :width]),
        load_extra(4, hbm_stream, activated.at[:, width : 2 * width]),
        load_extra(5, hbm_source, activated.at[:rows, 2 * width : 3 * width]),
    ]

    def load_side(index):
        return pltpu.make_async_copy(
            hbm_sides[index], sides_held.at[index % 2], weight_sem.at[8 + index]
        )

    def fetch(pair, source, base):
        slot = (pair + base) % 2
        return pltpu.make_async_copy(source.at[pair], kept.at[slot], kept_sem.at[slot])

    def keep_lines(base, lines):
        for row, line in enumerate(lines):
            for piece in range(8):
                at = 8 * (base + row) + piece
                small_out[at : at + 1, :] = line[:, 128 * piece : 128 * (piece + 1)]

    def ffn_load(index):
        span = pl.ds(index // 2 * width, width)
        source = hbm_ffn[0].at[span] if index % 2 == 0 else hbm_ffn[1].at[:, span]
        return pltpu.make_async_copy(source, weights[index % 3], ffn_sem.at[index])

    early[0].start()
    early[1].start()
    for index in range(3):
        ffn_load(index).start()
    early[2].start()
    early[3].start()
    fetch(0, cross_probs, 0).start()
    load_side(0).start()
    load_side(1).start()
    greet(reduce_peers(dp_size))
    early[0].wait()
    turn(0)
    early[1].wait()
    early[2].wait()
    ffn_steps = hbm_ffn[0].shape[0] // width
    for step in range(ffn_steps):
        span = slice(step * width, (step + 1) * width)
        ffn_load(2 * step).wait()
        d_act = dot(d_ffn[...], weights[2 * step % 3][...], NT)
        d_inner[:, span] = (d_act * d_inner[:, span].astype(WIDE)).astype(LOW)
        ffn_load(2 * step + 1).wait()
        d_resid[...] += dot(d_inner[:, span], weights[(2 * step + 1) % 3][...], NT)
        for index in (2 * step + 3, 2 * step + 4):
            if index < 2 * ffn_steps:
                ffn_load(index).start()
        turn(1 + step)
    for index in range(3):
        loads[index].start()
    early[3].wait()
    d_gain_two = jnp.zeros((1, width), WIDE)
    d_shift_two = jnp.zeros((1, width), WIDE)
    for stream_id in range(3):
        part = slice(stream_id * rows, (stream_id + 1) * rows)
        unit, scale = d_context[part, :].astype(WIDE), scales[1, part, 0:1]
        back, gain_part, shift_part = norm_backward(unit, scale, gain_two[...], d_resid[part, :])
        d_gain_two, d_shift_two = d_gain_two + gain_part, d_shift_two + shift_part
        d_resid[part, :] = back
        d_crossed[part, :] = back.astype(LOW)
    keep_lines(2, [d_gain_two, d_shift_two])
    loads[0].wait()

    def back_to(dst, left, weight, add=False):
        def body(cols):
            product = dot(left[...], weight[cols, :], NT)
            if add:
                product = product + dst[:, cols]
            dst[:, cols] = product.astype(dst.dtype)

        tiles(width // 256, 256, body)

    back_to(d_context, d_crossed, c_out)
    loads[3].start()

    def core_copy(index):
        view = parts.at[index % 2].reshape(2, 2, rows, width)
        return remote_copy(
            view.at[:, 1 - core], near_in.at[index], core_s.at[index], core_r.at[index], core_peer
        )

    def far_copy(index):
        return remote_copy(
            near_in.at[index, 1 - ypos], far_in.at[index], far_s.at[index], far_r.at[index], y_peer
        )

    def near_sum(index):
        core_copy(index).wait_recv()
        for side in range(2):
            mine = parts[index % 2, side * 2 + core].astype(WIDE)
            near_in[index, side] = (near_in[index, side].astype(WIDE) + mine).astype(LOW)
        far_copy(index).start()

    def far_sum(index):
        far_copy(index).wait_recv()
        return (near_in[index, ypos].astype(WIDE) + far_in[index].astype(WIDE)).astype(LOW)

    def store_part(index, cols, block):
        for part in range(full // rows):
            parts[index % 2, part, :, cols] = block[part * rows : (part + 1) * rows].astype(LOW)

    def cross_pair(pair, carry):
        fetch(pair, cross_probs, 0).wait()

        @pl.when(pair + 1 < pairs)
        def _():
            fetch(pair + 1, cross_probs, 0).start()

        slot = pair % 2
        cols = pl.ds(pl.multiple_of(pair * 128, 128), 128)
        values = values_held[:, cols]
        key_t = flip(keys_held[:, cols]).astype(LOW)
        queries, d_ctx = cross_query[:, cols], d_context[:, cols]
        d_ctx_t = flip(d_ctx)
        d_query_t, d_scores = [], []
        for side in range(2):
            span = slice(side * HEAD_DIM, (side + 1) * HEAD_DIM)
            d_prob = dot(values, half_rows(d_ctx_t, side))
            prob = kept[slot, side].astype(WIDE)
            delta = jnp.sum(prob * d_prob, axis=0, keepdims=True)
            d_score = (prob * (d_prob - delta)).astype(LOW)
            d_query_t.append(dot(key_t[span], d_score))
            d_scores.append(d_score)
        d_cross_query[:, cols] = (
            jnp.transpose(jnp.concatenate(d_query_t, axis=0)) * 0.125
        ).astype(LOW)
        both = jnp.concatenate(d_scores, axis=1)
        split = jnp.concatenate([half_lanes(queries, 0), half_lanes(queries, 1)], axis=0)
        store_part(0, cols, dot(both, split))
        both = jnp.concatenate([kept[slot, 0], kept[slot, 1]], axis=1)
        split = jnp.concatenate([half_lanes(d_ctx, 0), half_lanes(d_ctx, 1)], axis=0)
        store_part(1, cols, dot(both, split))
        return carry

    load_side(0).wait()
    load_side(1).wait()
    lax.fori_loop(0, pairs // 2, cross_pair, 0)
    turn(5)
    lax.fori_loop(pairs // 2, pairs, cross_pair, 0)
    fetch(0, probs, 0).start()
    load_side(2).start()
    load_side(3).start()
    core_copy(0).start()
    core_copy(1).start()
    turn(6)
    loads[1].wait()
    back_to(d_resid, d_cross_query, c_query, True)
    loads[6].start()
    d_gain = jnp.zeros((1, width), WIDE)
    d_shift = jnp.zeros((1, width), WIDE)
    for stream_id in range(3):
        part = slice(stream_id * rows, (stream_id + 1) * rows)
        unit, scale = unit_one[part, :].astype(WIDE), scales[0, part, 0:1]
        back, gain_part, shift_part = norm_backward(
            unit, scale, gain_one[...], d_resid[part, :]
        )
        d_gain, d_shift = d_gain + gain_part, d_shift + shift_part
        d_resid[part, :] = back
        d_attended[part, :] = back.astype(LOW)
    keep_lines(0, [d_gain, d_shift])
    keep_lines(4, [mid_grads[row : row + 1, :] for row in range(2)])
    for row, line in enumerate([front_stats[row : row + 1, :] for row in range(3)] + [ffn_stat[...]]):
        folded = line[:, :128]
        for piece in range(1, 8):
            folded = folded + line[:, 128 * piece : 128 * (piece + 1)]
        small_out[64 + row : 65 + row, :] = folded
    mask = valid_rows(sq, length_ref[0], rows)
    count = jnp.sum(jnp.broadcast_to(mask, (rows, 128)), axis=0, keepdims=True)
    small_out[68:69, :] = count * (3.0 / 128.0)
    small_out[69:80, :] = jnp.zeros((11, 128), WIDE)
    near_sum(0)
    near_sum(1)
    turn(7)
    loads[2].wait()
    back_to(d_context, d_attended, w_out)
    loads[7].start()
    core_copy(0).wait_send()
    core_copy(1).wait_send()
    line = lax.broadcasted_iota(jnp.int32, (rows, rows), 0)
    turned = (line + lax.broadcasted_iota(jnp.int32, (rows, rows), 1) == rows - 1).astype(LOW)

    def self_pair(pair, carry):
        fetch(pair, probs, 0).wait()

        @pl.when(pair + 1 < pairs)
        def _():
            fetch(pair + 1, probs, 0).start()

        slot = pair % 2
        cols = pl.ds(pl.multiple_of(pair * 128, 128), 128)
        values = values_held[:, cols]
        key_t = flip(keys_held[:, cols]).astype(LOW)
        queries, d_ctx = query[:, cols], d_context[:, cols]
        d_ctx_t, query_t = flip(d_ctx), flip(queries)
        own_key_t, own_value_t = flip(own_key[:, cols]), flip(own_value[:, cols])
        own_product = d_ctx_t[:, rows:] * own_value_t
        d_query_t, d_scores, d_own_key, d_own_value = [], [], [], []
        for side in range(2):
            head = 2 * pair + side
            span = slice(side * HEAD_DIM, (side + 1) * HEAD_DIM)
            d_prob = dot(values, half_rows(d_ctx_t, side))
            prob = kept[slot, side].astype(WIDE)
            prob_own = own_probs[head][:, rows:]
            d_prob_own = jnp.sum(own_product[span], axis=0, keepdims=True)
            delta = jnp.sum(prob * d_prob, axis=0, keepdims=True)
            delta = jnp.concatenate(
                [delta[:, :rows], delta[:, rows:] + prob_own * d_prob_own], axis=1
            )
            d_score = (prob * (d_prob - delta)).astype(LOW)
            d_own = (prob_own * (d_prob_own - delta[:, rows:])).astype(LOW).astype(WIDE)
            bias_sums[head, blocks : blocks + 1, :] = d_own
            mixed = dot(key_t[span], d_score)
            d_query_t.append(
                jnp.concatenate(
                    [mixed[:, :rows], mixed[:, rows:] + d_own * own_key_t[span]], axis=1
                )
            )
            d_scores.append(d_score)
            d_own_key.append(d_own * query_t[span, rows:])
            d_own_value.append(prob_own * d_ctx_t[span, rows:])
            wide = d_score.astype(WIDE)
            summed = wide[:, :rows] + wide[:, rows : 2 * rows] + wide[:, 2 * rows :]
            mirrored = dot(summed.astype(LOW), turned)
            for block in range(full // rows):
                piece = mirrored[block * rows : (block + 1) * rows]
                piece = jnp.concatenate([piece, jnp.zeros_like(piece)], axis=1)
                aligned = pltpu.roll(piece, 0, 1, stride=1, stride_axis=0)
                bias_sums[head, block : block + 1, :] = jnp.sum(aligned, axis=0, keepdims=True)
        d_query[:, cols] = (jnp.transpose(jnp.concatenate(d_query_t, axis=0)) * 0.125).astype(LOW)
        d_key[rows:, cols] = jnp.transpose(jnp.concatenate(d_own_key, axis=0)).astype(LOW)
        d_value[rows:, cols] = jnp.transpose(jnp.concatenate(d_own_value, axis=0)).astype(LOW)
        both = jnp.concatenate(d_scores, axis=1)
        split = jnp.concatenate([half_lanes(queries, 0), half_lanes(queries, 1)], axis=0)
        store_part(2, cols, dot(both, split))
        both = jnp.concatenate([kept[slot, 0], kept[slot, 1]], axis=1)
        split = jnp.concatenate([half_lanes(d_ctx, 0), half_lanes(d_ctx, 1)], axis=0)
        store_part(3, cols, dot(both, split))
        return carry

    load_side(2).wait()
    load_side(3).wait()
    quarter = pairs // 4
    lax.fori_loop(0, quarter, self_pair, 0)
    turn(8)
    for load in late:
        load.start()
    lax.fori_loop(quarter, 2 * quarter, self_pair, 0)
    turn(9)
    lax.fori_loop(2 * quarter, 3 * quarter, self_pair, 0)
    for load in late:
        load.wait()
    turn(10)
    lax.fori_loop(3 * quarter, pairs, self_pair, 0)
    core_copy(2).start()
    core_copy(3).start()
    d_cross_key[...] = far_sum(0)
    d_cross_value[...] = far_sum(1)
    turn(11)
    near_sum(2)
    near_sum(3)
    turn(12)
    loads[6].wait()
    loads[7].wait()

    def source_body(cols):
        grad = dot(d_cross_key[...], c_key[cols, :], NT)
        grad = grad + dot(d_cross_value[...], c_value[cols, :], NT)
        encoded_grad[:, cols] = grad.astype(LOW)

    tiles(width // 256, 256, source_body)
    loads[4].start()
    loads[5].start()
    loads[3].wait()

    def query_body(cols):
        d_resid[:, cols] += dot(d_query[...], w_query[cols, :], NT)

    turn(13)
    tiles(width // 256, 256, query_body)
    bucket = lax.broadcasted_iota(jnp.int32, (128, full), 0)
    ones = jnp.ones((8, full), LOW)
    below = (bucket_row[...] < bucket).astype(WIDE).astype(LOW)
    upto = (bucket_row[...] <= bucket).astype(WIDE).astype(LOW)
    first, after = dot(ones, below, NT)[0:1], dot(ones, upto, NT)[0:1]
    lane = lax.broadcasted_iota(jnp.int32, (2 * rows, 128), 0)
    table = jnp.zeros((HEADS, 128), WIDE)
    for block in range(blocks + 1):
        reach = ((sq - block) * rows + rows - 1 - lane).astype(WIDE)
        if block == blocks:
            reach = jnp.zeros((2 * rows, 128), WIDE)
        window_hot = ((reach >= first) & (reach < after)).astype(WIDE).astype(LOW)
        rest = bias_sums[:, block, :]
        for _ in range(3):
            part = rest.astype(LOW)
            rest = rest - part.astype(WIDE)
            table = table + dot(part, window_hot)
    small_out[48:64, :] = table
    small_copy(0).start()
    d_key[:rows, :] = far_sum(2)
    d_value[:rows, :] = far_sum(3)
    turn(14)
    turn(15)
    loads[4].wait()
    loads[5].wait()

    def last_body(cols):
        grad = d_resid[:, cols] + dot(d_key[...], w_key[cols, :], NT)
        grad = grad + dot(d_value[...], w_value[cols, :], NT)
        stream_grad[:, cols] = grad.astype(LOW)

    tiles(width // 256, 256, last_body)
    for index in range(4):
        if index >= 2:
            core_copy(index).wait_send()
        far_copy(index).wait_send()
    last = len(units) + 9
    for index in range(16, last):
        turn(index)
        if index % 2 == 0 and (index - 16) // 2 <= dp_size.bit_length():
            small_step((index - 16) // 2)
    for step in range((last - 15) // 2, dp_size.bit_length() + 1):
        small_step(step)
    drain()


def rear(acts, hbm_acts, sides, weights, ffn_weights, cross_probs, probs, units, dp_size):
    tokens, width = acts[0].shape
    full = sides[0].shape[0]
    rows = tokens // 3
    shape = jax.ShapeDtypeStruct
    vmem = pl.BlockSpec(memory_space=pltpu.VMEM)
    smem = pl.BlockSpec(memory_space=pltpu.SMEM)
    hbm = pl.BlockSpec(memory_space=pl.ANY)
    sem = pltpu.SemaphoreType.DMA
    blocks = full // rows
    chunk = width // dp_size
    steps = dp_size.bit_length() + 1
    return pl.pallas_call(
        functools.partial(rear_kernel, units, dp_size),
        out_shape=[
            shape((rows, width), LOW),
            shape((tokens, width), LOW),
            shape((80, 128), WIDE),
        ]
        + [shape((chunk, COLS), WIDE)] * 8
        + [shape((chunk, 4 * COLS), WIDE), shape((4 * chunk, COLS), WIDE)],
        in_specs=[vmem] * (len(acts) - 1) + [smem] + [hbm] * (len(hbm_acts) + 16),
        out_specs=[vmem] * 13,
        scratch_shapes=[
            pltpu.VMEM((tokens, width), LOW),
            pltpu.VMEM((rows, width), LOW),
            pltpu.VMEM((rows, width), LOW),
            pltpu.VMEM((tokens, width), LOW),
            pltpu.VMEM((tokens, width), LOW),
            pltpu.VMEM((tokens, width), LOW),
            pltpu.VMEM((tokens, width), LOW),
            pltpu.VMEM((HEADS, blocks + 1, 2 * rows), WIDE),
            pltpu.VMEM((steps, 80, 128), WIDE),
            pltpu.VMEM((tokens, 4 * width), LOW),
            pltpu.VMEM((tokens, 4 * width), LOW),
        ]
        + [pltpu.VMEM(w.shape, LOW) for w in weights[:3]]
        + [
            pltpu.VMEM((2, 2, full, tokens), LOW),
            pltpu.VMEM((tokens, width), LOW),
            pltpu.VMEM((tokens, width), WIDE),
            pltpu.VMEM((2, blocks, rows, width), LOW),
            pltpu.VMEM((4, 2, rows, width), LOW),
            pltpu.VMEM((4, rows, width), LOW),
            pltpu.VMEM((2, full, width), LOW),
            pltpu.VMEM((tokens, width), LOW),
            sem((8,)),
            sem((19,)),
            sem((2,)),
            sem((4,)),
            sem((4,)),
            sem((4,)),
            sem((4,)),
            sem((steps,)),
            sem((steps,)),
        ]
        + reduce_buffers(COLORS, dp_size),
        compiler_params=pltpu.CompilerParams(
            collective_id=2, has_side_effects=True, vmem_limit_bytes=63 << 20
        ),
    )(*acts, *hbm_acts, *sides, *weights, *ffn_weights, cross_probs, probs)


def finish_kernel(num, *refs):
    ins, sums = refs[:num], refs[num]
    outs, lines, table, rms, sems = refs[num + 1 : 2 * num + 1], refs[-9:-3], *refs[-3:]
    copies = [
        pltpu.make_async_copy(src, dst, sems.at[index])
        for index, (src, dst) in enumerate(zip(ins, outs))
    ]
    for copy in copies:
        copy.start()
    for row, line in enumerate(lines):
        line[...] = sums[8 * row : 8 * row + 8, :]
    wide = jnp.concatenate([sums[48:64, :], jnp.zeros((112, 128), WIDE)], axis=0)
    table[...] = jnp.transpose(wide)[:NBUCKET, :HEADS]
    totals = jnp.sum(sums[64:72, :], axis=1, keepdims=True)
    rms[...] = jnp.broadcast_to(jnp.sqrt(totals / (totals[4:5] * 1024.0)), (8, 128))
    for copy in copies:
        copy.wait()


def finish(arrays, sums):
    shape = jax.ShapeDtypeStruct
    vmem = pl.BlockSpec(memory_space=pltpu.VMEM)
    hbm = pl.BlockSpec(memory_space=pl.ANY)
    num = len(arrays)
    return pl.pallas_call(
        functools.partial(finish_kernel, num),
        out_shape=[shape(array.shape, array.dtype) for array in arrays]
        + [shape((8, 128), WIDE)] * 6
        + [shape((NBUCKET, HEADS), WIDE), shape((8, 128), WIDE)],
        in_specs=[hbm] * num + [vmem],
        out_specs=[hbm] * num + [vmem] * 8,
        scratch_shapes=[pltpu.SemaphoreType.DMA((num,))],
        compiler_params=pltpu.CompilerParams(vmem_limit_bytes=8 << 20),
    )(*arrays, sums)


MESH_ID = pl.DeviceIdType.MESH


def reduce_peers(dp_size):
    dp, sq, core, ypos, core_peer, y_peer = places()
    xpos, zpos = dp % 2, dp // 2
    depth = dp_size // 2
    peers = [core_peer, y_peer, (dp + 1 - 2 * xpos, sq)]
    return peers + [((zpos + step) % depth * 2 + xpos, sq) for step in range(1, depth)]


def reducer(units, colors, ins, emit, buffers, dp_size):
    sent, core_in, first_y, first_x, second_y, second_x, third = buffers[:7]
    z_in, z_half, z_last = buffers[7:10]
    core_s, core_r, one_s, one_r, two_s, two_r, three_s, three_r = buffers[10:18]
    core_free, one_free, two_free = buffers[18:]
    dp, sq, core, ypos, core_peer, y_peer = places()
    xpos, zpos = dp % 2, dp // 2
    depth = dp_size // 2
    chunk = 1024 // dp_size
    x_peer = (dp + 1 - 2 * xpos, sq)
    count = len(units)
    remote = remote_copy
    nth = [colors[:item].count(colors[item]) for item in range(2 * count)]
    order = [item - colors[:item].count("z") for item in range(2 * count)]
    firsts = {"y": first_y, "x": first_x}
    seconds = {"y": second_y, "x": second_x}
    color_id = {"y": 0, "x": RING_ONE}
    first_peer = {"y": y_peer, "x": x_peer}
    second_peer = {"y": x_peer, "x": y_peer}

    def z_peer(step):
        return ((zpos + step) % depth * 2 + xpos, sq)

    def half_dots(unit, half, write):
        x_id, y_id, kind, part, base, tokens = units[unit]
        x_ref, y_ref = ins[x_id], ins[y_id]
        if kind == "back":
            starts = [device * 4 * chunk + part * chunk for device in range(dp_size)]
            left = jnp.concatenate([x_ref[:tokens, s : s + chunk] for s in starts], axis=1)
        else:
            left = x_ref[:tokens, base : base + 1024]
        for side in range(2):
            start = (side * 2 + half) * COLS
            if kind == "in":
                start = (side * 2 + half) * 1024 + part * COLS
            right = y_ref[:tokens, pl.ds(pl.multiple_of(start, COLS), COLS)]
            value = lax.dot_general(
                left, right, (((0,), (0,)), ((), ())), preferred_element_type=WIDE
            )
            write(0, side, value[:, :128])
            write(1, side, value[:, 128:])

    def landed(item):
        return core_in.at[item // 2 % RING, item % 2]

    def core_copy(unit):
        return remote(
            sent.at[unit % SLOTS],
            core_in.at[unit % RING],
            core_s.at[unit],
            core_r.at[unit],
            core_peer,
        )

    def one_copy(item):
        color, source = colors[item], landed(item)
        if color == "y":
            source = source.at[1 - ypos]
        else:
            source = source.reshape(2, depth, 2, chunk, 128).at[:, :, 1 - xpos]
        return remote(
            source,
            firsts[color].at[nth[item] % RING_ONE],
            one_s.at[item],
            one_r.at[item],
            first_peer[color],
        )

    def two_copy(item):
        color = colors[item]
        source = firsts[color].at[nth[item] % RING_ONE]
        if color == "y":
            source = source.reshape(depth, 2, chunk, 128).at[:, 1 - xpos]
        else:
            source = source.at[1 - ypos]
        return remote(
            source,
            seconds[color].at[nth[item] % RING_ONE],
            two_s.at[item],
            two_r.at[item],
            second_peer[color],
        )

    def three_copy(item, step):
        color = colors[item]
        return remote(
            seconds[color].at[nth[item] % RING_ONE, (zpos + step) % depth],
            third.at[order[item], step - 1],
            three_s.at[item, step - 1],
            three_r.at[item, step - 1],
            z_peer(step),
        )

    def z_copy(item, step):
        source = landed(item).reshape(2, depth, 2 * chunk, 128)
        return remote(
            source.at[:, (zpos + step) % depth],
            z_in.at[nth[item], step - 1],
            three_s.at[item, step - 1],
            three_r.at[item, step - 1],
            z_peer(step),
        )

    def zy_copy(item):
        return remote(
            z_in.at[nth[item], 0, 1 - ypos],
            z_half.at[nth[item]],
            one_s.at[item],
            one_r.at[item],
            y_peer,
        )

    def zx_copy(item):
        source = z_half.at[nth[item]].reshape(2, chunk, 128)
        return remote(
            source.at[1 - xpos], z_last.at[nth[item]], two_s.at[item], two_r.at[item], x_peer
        )

    def take(free, slot):
        pl.semaphore_wait(free.at[slot], 1)

    def allow(free, slot, peer):
        pl.semaphore_signal(free.at[slot], inc=1, device_id=peer, device_id_type=MESH_ID)

    def steps(action):
        def body(step, carry):
            action(step)
            return carry

        lax.fori_loop(1, depth, body, 0)

    def plus(left, right):
        return (left.astype(WIDE) + right.astype(WIDE)).astype(LOW)

    def products(unit):
        slot = unit % SLOTS
        if unit >= SLOTS:
            core_copy(unit - SLOTS).wait_send()

        def write(item, side, value):
            sent[slot, item, side] = value.astype(LOW)

        half_dots(unit, 1 - core, write)
        if unit >= RING:
            for item in range(2):
                take(core_free, unit % RING * 2 + item)
        core_copy(unit).start()

    def core_sum(unit):
        core_copy(unit).wait_recv()
        slot = unit % RING

        def write(item, side, value):
            old = core_in[slot, item, side].astype(WIDE)
            core_in[slot, item, side] = (value + old).astype(LOW)

        half_dots(unit, core, write)
        for item in (2 * unit, 2 * unit + 1):
            color = colors[item]
            if color == "z":
                steps(lambda step: z_copy(item, step).start())
                continue
            if nth[item] >= RING_ONE:
                take(one_free, color_id[color] + nth[item] % RING_ONE)
            one_copy(item).start()

    def core_done(item):
        if item // 2 + RING < count:
            allow(core_free, item // 2 % RING * 2 + item % 2, core_peer)

    def one_sum(item):
        color = colors[item]
        if color == "z":
            return
        one_copy(item).wait_recv()
        slot, base, own = nth[item] % RING_ONE, item // 2 % RING, item % 2
        if color == "y":

            def body(step, carry):
                rows = pl.ds(pl.multiple_of(step * 256, 256), 256)
                first_y[slot, rows, :] = plus(
                    first_y[slot, rows, :], core_in[base, own, ypos, rows, :]
                )
                return carry

            lax.fori_loop(0, 4, body, 0)
        else:

            def body(layer, carry):
                rows = pl.ds(pl.multiple_of((layer * 2 + xpos) * chunk, chunk), chunk)
                for side in range(2):
                    first_x[slot, side, layer] = plus(
                        first_x[slot, side, layer], core_in[base, own, side, rows, :]
                    )
                return carry

            lax.fori_loop(0, depth, body, 0)
        if nth[item] >= RING_ONE:
            take(two_free, color_id[color] + nth[item] % RING_ONE)
        two_copy(item).start()
        one_copy(item).wait_send()
        core_done(item)

    def z_sum(item):
        base, own = item // 2 % RING, item % 2
        rows = pl.ds(pl.multiple_of(zpos * 2 * chunk, 2 * chunk), 2 * chunk)
        steps(lambda step: z_copy(item, step).wait_recv())
        for side in range(2):

            def body(step, total):
                return total + z_in[nth[item], step - 1, side].astype(WIDE)

            mine = core_in[base, own, side, rows, :].astype(WIDE)
            z_in[nth[item], 0, side] = lax.fori_loop(1, depth, body, mine).astype(LOW)
        zy_copy(item).start()
        steps(lambda step: z_copy(item, step).wait_send())
        core_done(item)

    def two_sum(item):
        color = colors[item]
        if color == "z":
            z_sum(item)
            return
        two_copy(item).wait_recv()
        slot = nth[item] % RING_ONE
        second = seconds[color]

        def body(layer, carry):
            if color == "y":
                rows = pl.ds(pl.multiple_of((layer * 2 + xpos) * chunk, chunk), chunk)
                old = first_y[slot, rows, :]
            else:
                old = first_x[slot, ypos, layer]
            second[slot, layer] = plus(second[slot, layer], old)
            return carry

        lax.fori_loop(0, depth, body, 0)
        steps(lambda step: three_copy(item, step).start())
        two_copy(item).wait_send()
        if nth[item] + RING_ONE < colors.count(color):
            allow(one_free, color_id[color] + slot, first_peer[color])

    def last_sum(item):
        color = colors[item]
        if color == "z":
            zy_copy(item).wait_recv()
            z_half[nth[item]] = plus(z_half[nth[item]], z_in[nth[item], 0, ypos])
            zx_copy(item).start()
            zy_copy(item).wait_send()
            return
        slot = nth[item] % RING_ONE

        def body(step, total):
            three_copy(item, step).wait_recv()
            return total + third[order[item], step - 1].astype(WIDE)

        total = lax.fori_loop(1, depth, body, seconds[color][slot, zpos].astype(WIDE))
        emit(units[item // 2], item % 2, total)
        steps(lambda step: three_copy(item, step).wait_send())
        if nth[item] + RING_ONE < colors.count(color):
            allow(two_free, color_id[color] + slot, second_peer[color])

    def z_end(item):
        if colors[item] == "z":
            zx_copy(item).wait_recv()
            rows = pl.ds(pl.multiple_of(xpos * chunk, chunk), chunk)
            mine = z_half[nth[item], rows, :].astype(WIDE)
            emit(units[item // 2], item % 2, mine + z_last[nth[item]].astype(WIDE))
            zx_copy(item).wait_send()

    def turn(index):
        for stage, lag in ((products, 0), (core_sum, 1)):
            if 0 <= index - lag < count:
                stage(index - lag)
        for stage, lag in ((one_sum, 3), (two_sum, 5), (last_sum, 7), (z_end, 9)):
            for item in (2 * (index - lag), 2 * (index - lag) + 1):
                if 0 <= item < 2 * count:
                    stage(item)

    def drain():
        for unit in range(count - SLOTS, count):
            core_copy(unit).wait_send()

    return turn, drain


def reduce_buffers(colors, dp_size):
    depth, chunk = dp_size // 2, 1024 // dp_size
    count, slow = len(colors), max(colors.count("z"), 1)
    sem = pltpu.SemaphoreType.DMA
    credit = pltpu.SemaphoreType.REGULAR
    return (
        [
            pltpu.VMEM((SLOTS, 2, 2, 1024, 128), LOW),
            pltpu.VMEM((RING, 2, 2, 1024, 128), LOW),
            pltpu.VMEM((RING_ONE, 1024, 128), LOW),
            pltpu.VMEM((RING_ONE, 2, depth, chunk, 128), LOW),
            pltpu.VMEM((RING_ONE, depth, chunk, 128), LOW),
            pltpu.VMEM((RING_ONE, depth, chunk, 128), LOW),
            pltpu.VMEM((count - colors.count("z"), depth - 1, chunk, 128), LOW),
            pltpu.VMEM((slow, depth - 1, 2, 2 * chunk, 128), LOW),
            pltpu.VMEM((slow, 2 * chunk, 128), LOW),
            pltpu.VMEM((slow, chunk, 128), LOW),
        ]
        + [sem((count // 2,))] * 2
        + [sem((count,))] * 4
        + [sem((count, depth - 1))] * 2
        + [credit((2 * RING,)), credit((2 * RING_ONE,)), credit((2 * RING_ONE,))]
    )


def small_sums(small, small_in, small_s, small_r, dp_size):
    dp, sq, core, ypos, core_peer, y_peer = places()

    def copy(step):
        flip = 1 << max(step - 2, 0)
        peer = (dp + flip - 2 * flip * (dp // flip % 2), sq)
        peer = (core_peer, y_peer, peer)[min(step, 2)]
        return remote_copy(small, small_in.at[step], small_s.at[step], small_r.at[step], peer)

    def advance(step):
        copy(step).wait()
        small[...] = small[...] + small_in[step]
        if step < dp_size.bit_length():
            copy(step + 1).start()

    return copy, advance


def per_device(
    stream,
    encoded,
    cotangent,
    lengths,
    bucket_table,
    w_query,
    w_key,
    w_value,
    w_out,
    c_query,
    c_key,
    c_value,
    c_out,
    w_in,
    w_back,
    gain_one,
    shift_one,
    gain_two,
    shift_two,
    gain_three,
    shift_three,
    position_bias,
):
    num_rows, num_streams, local_len, model_width = stream.shape
    full_len = local_len * lax.axis_size("seq")
    dp_size = lax.axis_size("dp")
    chunk = model_width // dp_size
    bucket_row = bucket_table.reshape(1, full_len)
    flat_rows = stream.reshape(-1, model_width)
    source_rows = encoded.reshape(-1, model_width)
    flat_cotangent = cotangent.reshape(-1, model_width)

    def line(values):
        return values.reshape(1, model_width)

    fronts = front(
        stream.reshape(num_streams, local_len, model_width),
        source_rows,
        lengths,
        bucket_row,
        position_bias,
        (line(gain_one), line(shift_one), line(gain_two), line(shift_two)),
        (w_query, w_key, w_value, w_out, c_query, c_key, c_value, c_out),
    )
    query, own_key, own_value, main_key, main_value, context_low, unit_one, first_norm = fronts[:8]
    cross_query, cross_key, cross_value, cross_low, unit_two, second_norm = fronts[8:14]
    scales, own_probs, front_stats, probs, cross_probs = fronts[14:]
    layer_output, activated, d_ffn_out, slope, d_resid_three, mid_grads, ffn_stat = middle(
        second_norm,
        flat_cotangent,
        lengths,
        (line(gain_three), line(shift_three)),
        w_in,
        w_back,
    )
    units = []
    tokens = num_streams * local_len
    spread = activated
    if chunk % 128 != 0:
        spread = activated.reshape(-1, dp_size, 4, chunk)
        spread = jnp.transpose(spread, (0, 2, 1, 3)).reshape(activated.shape)
    for part in range(4):
        if chunk % 128 == 0:
            units.append((3, 0, "back", part, 0, tokens))
        else:
            units.append((3, 0, "parted", part, part * model_width, tokens))
    for part in range(4):
        units.append((1, 2, "in", part, 0, tokens))
    units += [(4, 5, "", 7, 0, tokens), (6, 7, "", 4, 0, tokens), (3, 8, "", 3, 0, tokens)]
    units += [(3, 9, "", 5, 2 * model_width, local_len), (3, 10, "", 6, 2 * model_width, local_len)]
    units += [(3, 11 + part, "", part, model_width, tokens) for part in range(3)]
    rears = rear(
        (
            cross_query,
            unit_one,
            query,
            own_key,
            own_value,
            own_probs,
            line(gain_one),
            d_ffn_out,
            second_norm,
            cross_low,
            first_norm,
            mid_grads,
            ffn_stat,
            front_stats,
            scales,
            line(gain_two),
            bucket_row,
            lengths,
        ),
        (slope, spread, context_low, flat_rows, source_rows, d_resid_three, unit_two),
        (cross_key, cross_value, main_key, main_value),
        (c_out, c_query, w_out, w_query, w_key, w_value, c_key, c_value),
        (w_back, w_in),
        cross_probs,
        probs,
        tuple(units),
        dp_size,
    )
    ends = finish(list(rears[:2]) + list(rears[3:]), rears[2])
    encoded_grad, stream_grad = ends[:2]
    shares, lines, table_grad = ends[2:12], ends[12:18], ends[18]
    rms = ends[19][:4, 0]
    return (
        layer_output.reshape(stream.shape),
        stream_grad.reshape(stream.shape),
        encoded_grad.reshape(encoded.shape),
        shares[0],
        shares[1],
        shares[2],
        shares[3],
        shares[4],
        shares[5],
        shares[6],
        shares[7],
        shares[8],
        shares[9],
        lines[0].reshape(model_width),
        lines[1].reshape(model_width),
        lines[2].reshape(model_width),
        lines[3].reshape(model_width),
        lines[4].reshape(model_width),
        lines[5].reshape(model_width),
        table_grad,
        rms,
    )


def solution(mesh):
    placed = (
        P("dp", None, "seq", None),
        P("dp", "seq", None),
        P("dp", None, "seq", None),
        P("dp"),
        P(),
        P(),
        P(),
        P(),
        P(),
        P(),
        P(),
        P(),
        P(),
        P(),
        P(),
        P(),
        P(),
        P(),
        P(),
        P(),
        P(),
        P(),
    )
    return jax.shard_map(
        per_device,
        mesh=mesh,
        in_specs=placed,
        out_specs=(
            P("dp", None, "seq", None),
            P("dp", None, "seq", None),
            P("dp", "seq", None),
            P("dp", "seq"),
            P("dp", "seq"),
            P("dp", "seq"),
            P("dp", "seq"),
            P("dp", "seq"),
            P("dp", "seq"),
            P("dp", "seq"),
            P("dp", "seq"),
            P("dp", "seq"),
            P("dp", "seq"),
            P(),
            P(),
            P(),
            P(),
            P(),
            P(),
            P(),
            P(),
        ),
        check_vma=False,
    )
```

```python
import functools

import jax
import jax.numpy as jnp
from jax import lax
from jax.experimental import pallas as pl
from jax.experimental.pallas import tpu as pltpu
from jax.sharding import PartitionSpec as P

HEADS = 16
HEAD_DIM = 64
NBUCKET = 32
COLS = 256
SLOTS = 2
RING = 6
RING_ONE = 5
COLORS = "yxyxzxyxyxzxyxzxyxyxzxyxzxyxyxyx"
epsilon = 1e-05
masked_score = -1e30


LOW = jnp.bfloat16
WIDE = jnp.float32
NN = (((1,), (0,)), ((), ()))
NT = (((1,), (1,)), ((), ()))


def dot(left, right, dims=NN):
    return lax.dot_general(left, right, dims, preferred_element_type=WIDE)


def flip(block):
    return jnp.transpose(block.astype(WIDE))


def places():
    dp, sq = lax.axis_index("dp"), lax.axis_index("seq")
    core, ypos = sq % 2, sq // 2
    return dp, sq, core, ypos, (dp, sq + 1 - 2 * core), (dp, sq + 2 - 4 * ypos)


def remote_copy(src, dst, send_sem, recv_sem, peer):
    return pltpu.make_async_remote_copy(
        src_ref=src,
        dst_ref=dst,
        send_sem=send_sem,
        recv_sem=recv_sem,
        device_id=peer,
        device_id_type=MESH_ID,
    )


def greet(peers):
    barrier = pltpu.get_barrier_semaphore()
    for peer in peers:
        pl.semaphore_signal(barrier, inc=1, device_id=peer, device_id_type=MESH_ID)
    pl.semaphore_wait(barrier, len(peers))


def tiles(count, size, body):
    def step(index, carry):
        body(pl.ds(pl.multiple_of(index * size, size), size))
        return carry

    lax.fori_loop(0, count, step, 0)


def project_to(dst, left, weight, scale=None):
    product = dot(left[...], weight[...])
    if scale is not None:
        product = product * scale
    dst[...] = product.astype(dst.dtype)


def norm_stats(rows):
    centre = jnp.mean(rows, axis=-1, keepdims=True)
    centred = rows - centre
    spread = jnp.mean(centred * centred, axis=-1, keepdims=True)
    return centred, lax.rsqrt(spread + epsilon)


def norm_backward(unit, scale, gain, incoming):
    scaled = incoming * gain
    first = jnp.mean(scaled, axis=-1, keepdims=True)
    second = jnp.mean(scaled * unit, axis=-1, keepdims=True)
    grads = scale * (scaled - first - unit * second)
    d_gain = jnp.sum(incoming * unit, axis=0, keepdims=True)
    return grads, d_gain, jnp.sum(incoming, axis=0, keepdims=True)


def valid_rows(sq, length, count):
    position = sq * count + lax.broadcasted_iota(jnp.int32, (count, 1), 0)
    return (position < length).astype(WIDE)


def sum_squares(rows, mask):
    return jnp.sum(rows * rows * mask, axis=0, keepdims=True)


def half_rows(block, side):
    row = lax.broadcasted_iota(jnp.int32, block.shape, 0)
    return jnp.where(row // HEAD_DIM == side, block, 0.0).astype(LOW)


def half_lanes(block, side):
    lane = lax.broadcasted_iota(jnp.int32, block.shape, 1)
    return jnp.where(lane // HEAD_DIM == side, block.astype(WIDE), 0.0).astype(LOW)


def front_kernel(*refs):
    stream, encoded, length_ref, bucket_row, position_bias = refs[:5]
    gain_one, shift_one, gain_two, shift_two = refs[5:9]
    hbm_weights = refs[9:17]
    outs, probs_out, cross_probs_out = refs[17:34], refs[34], refs[35]
    held, refs = refs[36:53], refs[53:]
    (query, own_key, own_value, main_key, main_value, context, unit_one, first_norm) = held[:8]
    (cross_query, cross_key, cross_value, cross_context, unit_two, second_norm) = held[8:14]
    scales, own_probs, stats = held[14:]
    weights = refs[:8]
    main_all, source_all, kept, bias, masks, branch_out, bias_table = refs[8:15]
    weight_sem, kept_sem, send_sem, recv_sem, out_sem = refs[15:]
    stores = [
        pltpu.make_async_copy(src, dst, out_sem.at[index])
        for index, (src, dst) in enumerate(zip(held, outs))
    ]
    w_query, w_key, w_value, w_out, c_query, c_key, c_value, c_out = weights
    dp, sq, core, ypos, core_peer, y_peer = places()
    length = length_ref[0]
    rows = stream.shape[1]
    full = main_all.shape[0] * rows
    loads = [
        pltpu.make_async_copy(src, dst, weight_sem.at[index])
        for index, (src, dst) in enumerate(zip(hbm_weights, weights))
    ]
    for load in loads:
        load.start()
    greet([core_peer, y_peer])
    sources = (stream.at[0], encoded)
    gathered = (main_all, source_all)
    firsts = []
    for index in range(2):
        for lane, peer in enumerate((y_peer, core_peer)):
            slot = index * 3 + lane
            firsts.append(
                remote_copy(
                    sources[index],
                    gathered[index].at[sq],
                    send_sem.at[slot],
                    recv_sem.at[slot],
                    peer,
                )
            )
    firsts[0].start()
    firsts[1].start()
    main_all[sq] = stream[0]
    source_all[sq] = encoded[...]
    bucket = lax.broadcasted_iota(jnp.int32, (NBUCKET, full), 0)
    table_hot = (bucket == bucket_row[...]).astype(WIDE).astype(LOW)
    by_distance = jnp.zeros((HEADS, full), WIDE)
    rest = position_bias[...]
    for _ in range(3):
        part = rest.astype(LOW)
        rest = rest - part.astype(WIDE)
        by_distance = by_distance + dot(part, table_hot)
    bias_table[...] = jnp.zeros_like(bias_table)
    for head in range(HEADS):
        bias_table[head, :, full:] = by_distance[head : head + 1]

    def passed_on(index):
        other = gathered[index].at[sq + 2 - 4 * ypos]
        slot = index * 3 + 2
        return remote_copy(other, other, send_sem.at[slot], recv_sem.at[slot], core_peer)

    flat = stream.reshape(3 * rows, stream.shape[2])
    loads[0].wait()
    project_to(query, flat, w_query, 0.125)
    stores[0].start()
    predicting = flat.at[rows:, :]
    loads[1].wait()
    project_to(own_key, predicting, w_key)
    loads[2].wait()
    project_to(own_value, predicting, w_value)
    key_row = lax.broadcasted_iota(jnp.int32, (full, rows), 0)
    distance = sq * rows + lax.broadcasted_iota(jnp.int32, (full, rows), 1) - key_row
    in_range = key_row < length
    masks[0] = jnp.where((distance >= 0) & in_range, 0.0, masked_score)
    masks[1] = jnp.where((distance > 0) & in_range, 0.0, masked_score)
    masks[2] = jnp.where(in_range, 0.0, masked_score)
    firsts[0].wait_recv()
    passed_on(0).start()
    firsts[2].start()
    firsts[3].start()
    stores[1].start()
    stores[2].start()
    firsts[1].wait_recv()
    passed_on(0).wait_recv()
    wide_main = main_all.reshape(full, main_all.shape[2])
    project_to(main_key, wide_main, w_key)
    project_to(main_value, wide_main, w_value)
    stores[3].start()
    stores[4].start()

    def kept_copy(pair, out):
        slot = pair % 2
        return pltpu.make_async_copy(kept.at[slot], out.at[pair], kept_sem.at[slot])

    def self_pair(pair, carry):
        @pl.when(pair >= 2)
        def _():
            kept_copy(pair - 2, probs_out).wait()

        slot = pair % 2
        cols = pl.ds(pl.multiple_of(pair * 128, 128), 128)
        keys = main_key[:, cols]
        query_t = flip(query[:, cols])
        value_t = flip(main_value[:, cols]).astype(LOW)
        own_key_t, own_value_t = flip(own_key[:, cols]), flip(own_value[:, cols])
        own_product = query_t[:, rows:] * own_key_t
        sides = []
        for side in range(2):
            head = 2 * pair + side
            span = slice(side * HEAD_DIM, (side + 1) * HEAD_DIM)
            scores = dot(keys, half_rows(query_t, side))
            own_bias = bias_table[head, :, full : full + 128][:, 0:1]
            own_score = jnp.sum(own_product[span], axis=0, keepdims=True) + own_bias
            for block in range(full // rows):
                start = pl.multiple_of((sq - block + full // rows - 1) * rows, 128)
                line = bias_table[head, :, pl.ds(start, 2 * rows)]
                wide = jnp.broadcast_to(line, (rows, 2 * rows))
                near = pltpu.roll(wide, 0, 1, stride=1, stride_axis=0)[:, rows:]
                part = slice(block * rows, (block + 1) * rows)
                for kind in range(2):
                    bias[kind, part, :] = near + masks[kind, part, :]
            owns = []
            for stream_id in range(3):
                lanes = slice(stream_id * rows, (stream_id + 1) * rows)
                score = scores[:, lanes] + bias[min(stream_id, 1)]
                top = jnp.max(score, axis=0, keepdims=True)
                if stream_id > 0:
                    own = own_score[:, (stream_id - 1) * rows : stream_id * rows]
                    top = jnp.maximum(top, own)
                expo = jnp.exp(score - top)
                total = jnp.sum(expo, axis=0, keepdims=True)
                if stream_id > 0:
                    expo_own = jnp.exp(own - top)
                    total = total + expo_own
                share = 1.0 / total
                kept[slot, side, :, lanes] = (expo * share).astype(LOW)
                owns.append(expo_own * share if stream_id > 0 else jnp.zeros_like(total))
            own_probs[head] = jnp.concatenate(owns, axis=1)
            mixed = dot(value_t[span], kept[slot, side])
            mixed_own = jnp.concatenate(owns[1:], axis=1) * own_value_t[span]
            sides.append(
                jnp.concatenate([mixed[:, :rows], mixed[:, rows:] + mixed_own], axis=1)
            )
        context[:, cols] = jnp.transpose(jnp.concatenate(sides, axis=0)).astype(LOW)
        kept_copy(pair, probs_out).start()
        return carry

    lax.fori_loop(0, HEADS // 2, self_pair, 0)
    for pair in range(HEADS // 2 - 2, HEADS // 2):
        kept_copy(pair, probs_out).wait()
    stores[5].start()
    stores[15].start()

    mask = valid_rows(sq, length, rows)
    loads[3].wait()
    project_to(branch_out, context, w_out)
    firsts[2].wait_recv()
    passed_on(1).start()
    seen = jnp.zeros((1, stream.shape[2]), WIDE)
    branch = jnp.zeros((1, stream.shape[2]), WIDE)
    for stream_id in range(3):
        part = slice(stream_id * rows, (stream_id + 1) * rows)
        source, attended = stream[stream_id].astype(WIDE), branch_out[part, :]
        seen = seen + sum_squares(source, mask)
        branch = branch + sum_squares(attended, mask)
        centred, scale = norm_stats(source + attended)
        unit = centred * scale
        unit_one[part, :] = unit.astype(LOW)
        scales[0, part, :] = jnp.broadcast_to(scale, (rows, 128))
        first_norm[part, :] = (unit * gain_one[...] + shift_one[...]).astype(LOW)
    stats[0:1, :] = seen
    stats[1:2, :] = branch
    loads[4].wait()
    project_to(cross_query, first_norm, c_query, 0.125)
    for index in (6, 7, 8):
        stores[index].start()
    firsts[3].wait_recv()
    passed_on(1).wait_recv()
    wide_source = source_all.reshape(full, source_all.shape[2])
    loads[5].wait()
    project_to(cross_key, wide_source, c_key)
    loads[6].wait()
    project_to(cross_value, wide_source, c_value)
    stores[9].start()
    stores[10].start()

    def cross_pair(pair, carry):
        @pl.when(pair >= 2)
        def _():
            kept_copy(pair - 2, cross_probs_out).wait()

        slot = pair % 2
        cols = pl.ds(pl.multiple_of(pair * 128, 128), 128)
        keys = cross_key[:, cols]
        query_t = flip(cross_query[:, cols])
        value_t = flip(cross_value[:, cols]).astype(LOW)
        sides = []
        for side in range(2):
            span = slice(side * HEAD_DIM, (side + 1) * HEAD_DIM)
            scores = dot(keys, half_rows(query_t, side))
            for stream_id in range(3):
                lanes = slice(stream_id * rows, (stream_id + 1) * rows)
                score = scores[:, lanes] + masks[2]
                expo = jnp.exp(score - jnp.max(score, axis=0, keepdims=True))
                share = 1.0 / jnp.sum(expo, axis=0, keepdims=True)
                kept[slot, side, :, lanes] = (expo * share).astype(LOW)
            sides.append(dot(value_t[span], kept[slot, side]))
        cross_context[:, cols] = jnp.transpose(jnp.concatenate(sides, axis=0)).astype(LOW)
        kept_copy(pair, cross_probs_out).start()
        return carry

    lax.fori_loop(0, HEADS // 2, cross_pair, 0)
    for pair in range(HEADS // 2 - 2, HEADS // 2):
        kept_copy(pair, cross_probs_out).wait()
    stores[11].start()
    loads[7].wait()
    project_to(branch_out, cross_context, c_out)
    branch = jnp.zeros((1, stream.shape[2]), WIDE)
    for stream_id in range(3):
        part = slice(stream_id * rows, (stream_id + 1) * rows)
        crossed = branch_out[part, :]
        branch = branch + sum_squares(crossed, mask)
        centred, scale = norm_stats(first_norm[part, :].astype(WIDE) + crossed)
        unit = centred * scale
        unit_two[part, :] = unit.astype(LOW)
        scales[1, part, :] = jnp.broadcast_to(scale, (rows, 128))
        second_norm[part, :] = (unit * gain_two[...] + shift_two[...]).astype(LOW)
    stats[2:3, :] = branch
    for index in (12, 13, 14, 16):
        stores[index].start()
    for store in stores:
        store.wait()
    for copy in firsts:
        copy.wait_send()
    for index in range(2):
        passed_on(index).wait_send()


def front(stream, encoded, length, bucket_row, position_bias, norms, weights):
    streams, rows, width = stream.shape
    seq = lax.axis_size("seq")
    full, tokens = seq * rows, streams * rows
    own = tokens - rows
    shape = jax.ShapeDtypeStruct
    pairs = HEADS // 2
    outs = [
        shape((tokens, width), LOW),
        shape((own, width), LOW),
        shape((own, width), LOW),
        shape((full, width), LOW),
        shape((full, width), LOW),
        shape((tokens, width), LOW),
        shape((tokens, width), LOW),
        shape((tokens, width), LOW),
        shape((tokens, width), LOW),
        shape((full, width), LOW),
        shape((full, width), LOW),
        shape((tokens, width), LOW),
        shape((tokens, width), LOW),
        shape((tokens, width), LOW),
        shape((2, tokens, 128), WIDE),
        shape((HEADS, 1, tokens), WIDE),
        shape((3, width), WIDE),
        shape((pairs, 2, full, tokens), LOW),
        shape((pairs, 2, full, tokens), LOW),
    ]
    vmem = pl.BlockSpec(memory_space=pltpu.VMEM)
    smem = pl.BlockSpec(memory_space=pltpu.SMEM)
    hbm = pl.BlockSpec(memory_space=pl.ANY)
    sem = pltpu.SemaphoreType.DMA
    return pl.pallas_call(
        front_kernel,
        out_shape=outs,
        in_specs=[vmem, vmem, smem] + [vmem] * 6 + [hbm] * 8,
        out_specs=[hbm] * 19,
        scratch_shapes=[pltpu.VMEM(out.shape, out.dtype) for out in outs[:17]]
        + [pltpu.VMEM(w.shape, LOW) for w in weights]
        + [
            pltpu.VMEM((seq, rows, width), LOW),
            pltpu.VMEM((seq, rows, width), LOW),
            pltpu.VMEM((2, 2, full, tokens), LOW),
            pltpu.VMEM((2, full, rows), WIDE),
            pltpu.VMEM((3, full, rows), WIDE),
            pltpu.VMEM((tokens, width), WIDE),
            pltpu.VMEM((HEADS, 1, 2 * full), WIDE),
            sem((8,)),
            sem((2,)),
            sem((6,)),
            sem((6,)),
            sem((17,)),
        ],
        compiler_params=pltpu.CompilerParams(
            collective_id=1, has_side_effects=True, vmem_limit_bytes=60 << 20
        ),
    )(stream, encoded, length, bucket_row, position_bias, *norms, *weights)


def middle_kernel(*refs):
    second_norm, cotangent, length_ref, gain_three, shift_three, hbm_in, hbm_back = refs[:7]
    outs, grads, stats = refs[7:12], refs[12], refs[13]
    output, activated, d_ffn, slope, total = refs[14:19]
    w_in, w_back, load_sem, out_sem = refs[19:]
    sq = lax.axis_index("seq")
    length = length_ref[0]
    tokens, width = second_norm.shape
    rows = tokens // 3
    hidden = w_in.shape[1]
    size = 1024
    steps = hidden // size
    stores = [
        pltpu.make_async_copy(src, dst, out_sem.at[index])
        for index, (src, dst) in enumerate(zip(refs[14:19], outs))
    ]

    def load_in(step):
        cols = pl.ds(pl.multiple_of(step * size, size), size)
        return pltpu.make_async_copy(hbm_in.at[:, cols], w_in.at[:, cols], load_sem.at[0, step])

    def load_back(step):
        cols = pl.ds(pl.multiple_of(step * size, size), size)
        return pltpu.make_async_copy(hbm_back.at[cols], w_back.at[cols], load_sem.at[1, step])

    for step in range(steps):
        load_in(step).start()
        load_back(step).start()
    total[...] = jnp.zeros_like(total)

    def forward(step, carry):
        cols = pl.ds(pl.multiple_of(step * size, size), size)
        load_in(step).wait()
        inner = dot(second_norm[...], w_in[:, cols])
        phi = 0.5 + 0.5 * lax.erf(inner * (0.5**0.5))
        bell = jnp.exp(inner * inner * -0.5) * (0.5 / jnp.pi) ** 0.5
        value = (inner * phi).astype(LOW)
        activated[:, cols] = value
        slope[:, cols] = (phi + inner * bell).astype(LOW)
        load_back(step).wait()
        total[...] += dot(value, w_back[cols, :])
        return carry

    lax.fori_loop(0, steps, forward, 0)
    stores[1].start()
    stores[3].start()
    mask = valid_rows(sq, length, rows)
    branch = jnp.zeros((1, width), WIDE)
    d_gain = jnp.zeros((1, width), WIDE)
    d_shift = jnp.zeros((1, width), WIDE)
    for stream_id in range(3):
        part = slice(stream_id * rows, (stream_id + 1) * rows)
        ffn = total[part, :]
        branch = branch + sum_squares(ffn, mask)
        resid = second_norm[part, :].astype(WIDE) + ffn
        centred, scale = norm_stats(resid)
        unit = centred * scale
        normed = unit * gain_three[...] + shift_three[...]
        output[part, :] = (normed * mask).astype(LOW)
        incoming = cotangent[part, :].astype(WIDE) * mask
        back, gain_part, shift_part = norm_backward(unit, scale, gain_three[...], incoming)
        d_gain, d_shift = d_gain + gain_part, d_shift + shift_part
        total[part, :] = back
        d_ffn[part, :] = back.astype(LOW)
    stats[...] = branch
    grads[0:1, :] = d_gain
    grads[1:2, :] = d_shift
    for index in (0, 2, 4):
        stores[index].start()
    for store in stores:
        store.wait()


def middle(second_norm, cotangent, length, norms, w_in, w_back):
    tokens, width = second_norm.shape
    hidden = w_in.shape[1]
    shape = jax.ShapeDtypeStruct
    vmem = pl.BlockSpec(memory_space=pltpu.VMEM)
    smem = pl.BlockSpec(memory_space=pltpu.SMEM)
    hbm = pl.BlockSpec(memory_space=pl.ANY)
    outs = [
        shape((tokens, width), LOW),
        shape((tokens, hidden), LOW),
        shape((tokens, width), LOW),
        shape((tokens, hidden), LOW),
        shape((tokens, width), WIDE),
    ]
    return pl.pallas_call(
        middle_kernel,
        out_shape=outs + [shape((2, width), WIDE), shape((1, width), WIDE)],
        in_specs=[vmem] * 2 + [smem] + [vmem] * 2 + [hbm] * 2,
        out_specs=[hbm] * 5 + [vmem] * 2,
        scratch_shapes=[pltpu.VMEM(out.shape, out.dtype) for out in outs]
        + [
            pltpu.VMEM(w_in.shape, LOW),
            pltpu.VMEM(w_back.shape, LOW),
            pltpu.SemaphoreType.DMA((2, hidden // 1024)),
            pltpu.SemaphoreType.DMA((5,)),
        ],
        compiler_params=pltpu.CompilerParams(vmem_limit_bytes=60 << 20),
    )(second_norm, cotangent, length, *norms, w_in, w_back)


def rear_kernel(units, dp_size, *refs):
    cross_query, unit_one, query, own_key, own_value, own_probs, gain_one = refs[:7]
    refs = (None,) + refs
    d_ffn, second_norm, cross_context, first_norm, mid_grads, ffn_stat, front_stats = refs[8:15]
    scales, gain_two, bucket_row, length_ref = refs[15:19]
    refs = refs[:15] + refs[19:]
    hbm_slope, hbm_activated, hbm_context, hbm_stream, hbm_source, hbm_resid = refs[15:21]
    hbm_unit, refs = refs[21], refs[:21] + refs[22:]
    hbm_sides, hbm_weights = refs[21:25], refs[25:33]
    hbm_ffn, refs = refs[33:35], refs[:33] + refs[35:]
    cross_probs, probs = refs[33:35]
    encoded_grad, stream_grad, small_out = refs[35:38]
    shares, in_share, back_share = refs[38:46], refs[46], refs[47]
    (d_cross_query, d_cross_key, d_cross_value, d_attended) = refs[48:52]
    (d_query, d_key, d_value, bias_sums, small_in) = refs[52:57]
    d_inner, activated = refs[57:59]
    weights = refs[59:62]
    kept, d_context, d_resid, parts, near_in, far_in, sides_held = refs[62:69]
    d_crossed, ffn_sem, refs = refs[69], refs[70], refs[:69] + refs[71:]
    weight_sem, kept_sem, core_s, core_r, far_s, far_r, small_s, small_r = refs[69:77]
    held = (0, 1, 2, 0, 1, 2, 1, 2)
    c_out, c_query, w_out, w_query, w_key, w_value, c_key, c_value = [weights[i] for i in held]
    chunk = 1024 // dp_size

    def emit(unit, item, total):
        part, cols = unit[3], slice(item * 128, (item + 1) * 128)
        if unit[2] == "in":
            in_share[:, part * COLS + item * 128 : part * COLS + (item + 1) * 128] = total
        elif unit[2] in ("back", "parted"):
            back_share[part * chunk : (part + 1) * chunk, cols] = total
        else:
            shares[part][:, cols] = total

    operands = (d_ffn, second_norm, d_inner, activated, cross_context, d_crossed, first_norm)
    operands += (d_cross_query, d_attended, d_cross_key, d_cross_value, d_query, d_key, d_value)
    turn, drain = reducer(units, COLORS, operands, emit, refs[77:], dp_size)
    small_copy, small_step = small_sums(small_out, small_in, small_s, small_r, dp_size)
    dp, sq, core, ypos, core_peer, y_peer = places()
    tokens, width = query.shape
    rows = tokens // 3
    full = sides_held.shape[1]
    blocks = full // rows
    keys_held, values_held = sides_held.at[0], sides_held.at[1]
    pairs = HEADS // 2
    loads = [
        pltpu.make_async_copy(src, weights[held[index]], weight_sem.at[index])
        for index, src in enumerate(hbm_weights)
    ]

    def load_extra(index, src, dst):
        return pltpu.make_async_copy(src, dst, weight_sem.at[12 + index])

    early = [
        load_extra(0, hbm_activated, activated),
        load_extra(1, hbm_slope, d_inner),
        load_extra(2, hbm_resid, d_resid),
        load_extra(6, hbm_unit, d_context),
    ]
    late = [
        load_extra(3, hbm_context, activated.at[:, :width]),
        load_extra(4, hbm_stream, activated.at[:, width : 2 * width]),
        load_extra(5, hbm_source, activated.at[:rows, 2 * width : 3 * width]),
    ]

    def load_side(index):
        return pltpu.make_async_copy(
            hbm_sides[index], sides_held.at[index % 2], weight_sem.at[8 + index]
        )

    def fetch(pair, source, base):
        slot = (pair + base) % 2
        return pltpu.make_async_copy(source.at[pair], kept.at[slot], kept_sem.at[slot])

    def keep_lines(base, lines):
        for row, line in enumerate(lines):
            for piece in range(8):
                at = 8 * (base + row) + piece
                small_out[at : at + 1, :] = line[:, 128 * piece : 128 * (piece + 1)]

    def ffn_load(index):
        span = pl.ds(index // 2 * width, width)
        source = hbm_ffn[0].at[span] if index % 2 == 0 else hbm_ffn[1].at[:, span]
        return pltpu.make_async_copy(source, weights[index % 3], ffn_sem.at[index])

    early[0].start()
    early[1].start()
    for index in range(3):
        ffn_load(index).start()
    early[2].start()
    early[3].start()
    fetch(0, cross_probs, 0).start()
    load_side(0).start()
    load_side(1).start()
    greet(reduce_peers(dp_size))
    early[0].wait()
    turn(0)
    turn(1)
    early[1].wait()
    early[2].wait()
    ffn_steps = hbm_ffn[0].shape[0] // width
    for step in range(ffn_steps):
        span = slice(step * width, (step + 1) * width)
        ffn_load(2 * step).wait()
        d_act = dot(d_ffn[...], weights[2 * step % 3][...], NT)
        d_inner[:, span] = (d_act * d_inner[:, span].astype(WIDE)).astype(LOW)
        ffn_load(2 * step + 1).wait()
        d_resid[...] += dot(d_inner[:, span], weights[(2 * step + 1) % 3][...], NT)
        for index in (2 * step + 3, 2 * step + 4):
            if index < 2 * ffn_steps:
                ffn_load(index).start()
        if step != 2:
            turn((2, 3, None, 4)[step])
    for index in range(3):
        loads[index].start()
    early[3].wait()
    d_gain_two = jnp.zeros((1, width), WIDE)
    d_shift_two = jnp.zeros((1, width), WIDE)
    for stream_id in range(3):
        part = slice(stream_id * rows, (stream_id + 1) * rows)
        unit, scale = d_context[part, :].astype(WIDE), scales[1, part, 0:1]
        back, gain_part, shift_part = norm_backward(unit, scale, gain_two[...], d_resid[part, :])
        d_gain_two, d_shift_two = d_gain_two + gain_part, d_shift_two + shift_part
        d_resid[part, :] = back
        d_crossed[part, :] = back.astype(LOW)
    keep_lines(2, [d_gain_two, d_shift_two])
    loads[0].wait()

    def back_to(dst, left, weight, add=False):
        def body(cols):
            product = dot(left[...], weight[cols, :], NT)
            if add:
                product = product + dst[:, cols]
            dst[:, cols] = product.astype(dst.dtype)

        tiles(width // 256, 256, body)

    back_to(d_context, d_crossed, c_out)
    loads[3].start()

    def core_copy(index):
        view = parts.at[index % 2].reshape(2, 2, rows, width)
        return remote_copy(
            view.at[:, 1 - core], near_in.at[index], core_s.at[index], core_r.at[index], core_peer
        )

    def far_copy(index):
        return remote_copy(
            near_in.at[index, 1 - ypos], far_in.at[index], far_s.at[index], far_r.at[index], y_peer
        )

    def near_sum(index):
        core_copy(index).wait_recv()
        for side in range(2):
            mine = parts[index % 2, side * 2 + core].astype(WIDE)
            near_in[index, side] = (near_in[index, side].astype(WIDE) + mine).astype(LOW)
        far_copy(index).start()

    def far_sum(index):
        far_copy(index).wait_recv()
        return (near_in[index, ypos].astype(WIDE) + far_in[index].astype(WIDE)).astype(LOW)

    def store_part(index, cols, block):
        for part in range(full // rows):
            parts[index % 2, part, :, cols] = block[part * rows : (part + 1) * rows].astype(LOW)

    def cross_pair(pair, carry):
        fetch(pair, cross_probs, 0).wait()

        @pl.when(pair + 1 < pairs)
        def _():
            fetch(pair + 1, cross_probs, 0).start()

        slot = pair % 2
        cols = pl.ds(pl.multiple_of(pair * 128, 128), 128)
        values = values_held[:, cols]
        key_t = flip(keys_held[:, cols]).astype(LOW)
        queries, d_ctx = cross_query[:, cols], d_context[:, cols]
        d_ctx_t = flip(d_ctx)
        d_query_t, d_scores = [], []
        for side in range(2):
            span = slice(side * HEAD_DIM, (side + 1) * HEAD_DIM)
            d_prob = dot(values, half_rows(d_ctx_t, side))
            prob = kept[slot, side].astype(WIDE)
            delta = jnp.sum(prob * d_prob, axis=0, keepdims=True)
            d_score = (prob * (d_prob - delta)).astype(LOW)
            d_query_t.append(dot(key_t[span], d_score))
            d_scores.append(d_score)
        d_cross_query[:, cols] = (
            jnp.transpose(jnp.concatenate(d_query_t, axis=0)) * 0.125
        ).astype(LOW)
        both = jnp.concatenate(d_scores, axis=1)
        split = jnp.concatenate([half_lanes(queries, 0), half_lanes(queries, 1)], axis=0)
        store_part(0, cols, dot(both, split))
        both = jnp.concatenate([kept[slot, 0], kept[slot, 1]], axis=1)
        split = jnp.concatenate([half_lanes(d_ctx, 0), half_lanes(d_ctx, 1)], axis=0)
        store_part(1, cols, dot(both, split))
        return carry

    load_side(0).wait()
    load_side(1).wait()
    lax.fori_loop(0, pairs // 2, cross_pair, 0)
    turn(5)
    lax.fori_loop(pairs // 2, pairs, cross_pair, 0)
    fetch(0, probs, 0).start()
    load_side(2).start()
    load_side(3).start()
    core_copy(0).start()
    core_copy(1).start()
    turn(6)
    loads[1].wait()
    back_to(d_resid, d_cross_query, c_query, True)
    loads[6].start()
    d_gain = jnp.zeros((1, width), WIDE)
    d_shift = jnp.zeros((1, width), WIDE)
    for stream_id in range(3):
        part = slice(stream_id * rows, (stream_id + 1) * rows)
        unit, scale = unit_one[part, :].astype(WIDE), scales[0, part, 0:1]
        back, gain_part, shift_part = norm_backward(
            unit, scale, gain_one[...], d_resid[part, :]
        )
        d_gain, d_shift = d_gain + gain_part, d_shift + shift_part
        d_resid[part, :] = back
        d_attended[part, :] = back.astype(LOW)
    keep_lines(0, [d_gain, d_shift])
    keep_lines(4, [mid_grads[row : row + 1, :] for row in range(2)])
    for row, line in enumerate([front_stats[row : row + 1, :] for row in range(3)] + [ffn_stat[...]]):
        folded = line[:, :128]
        for piece in range(1, 8):
            folded = folded + line[:, 128 * piece : 128 * (piece + 1)]
        small_out[64 + row : 65 + row, :] = folded
    mask = valid_rows(sq, length_ref[0], rows)
    count = jnp.sum(jnp.broadcast_to(mask, (rows, 128)), axis=0, keepdims=True)
    small_out[68:69, :] = count * (3.0 / 128.0)
    small_out[69:80, :] = jnp.zeros((11, 128), WIDE)
    near_sum(0)
    near_sum(1)
    turn(7)
    loads[2].wait()
    back_to(d_context, d_attended, w_out)
    loads[7].start()
    core_copy(0).wait_send()
    core_copy(1).wait_send()
    line = lax.broadcasted_iota(jnp.int32, (rows, rows), 0)
    turned = (line + lax.broadcasted_iota(jnp.int32, (rows, rows), 1) == rows - 1).astype(LOW)

    def self_pair(pair, carry):
        fetch(pair, probs, 0).wait()

        @pl.when(pair + 1 < pairs)
        def _():
            fetch(pair + 1, probs, 0).start()

        slot = pair % 2
        cols = pl.ds(pl.multiple_of(pair * 128, 128), 128)
        values = values_held[:, cols]
        key_t = flip(keys_held[:, cols]).astype(LOW)
        queries, d_ctx = query[:, cols], d_context[:, cols]
        d_ctx_t, query_t = flip(d_ctx), flip(queries)
        own_key_t, own_value_t = flip(own_key[:, cols]), flip(own_value[:, cols])
        own_product = d_ctx_t[:, rows:] * own_value_t
        d_query_t, d_scores, d_own_key, d_own_value = [], [], [], []
        for side in range(2):
            head = 2 * pair + side
            span = slice(side * HEAD_DIM, (side + 1) * HEAD_DIM)
            d_prob = dot(values, half_rows(d_ctx_t, side))
            prob = kept[slot, side].astype(WIDE)
            prob_own = own_probs[head][:, rows:]
            d_prob_own = jnp.sum(own_product[span], axis=0, keepdims=True)
            delta = jnp.sum(prob * d_prob, axis=0, keepdims=True)
            delta = jnp.concatenate(
                [delta[:, :rows], delta[:, rows:] + prob_own * d_prob_own], axis=1
            )
            d_score = (prob * (d_prob - delta)).astype(LOW)
            d_own = (prob_own * (d_prob_own - delta[:, rows:])).astype(LOW).astype(WIDE)
            bias_sums[head, blocks : blocks + 1, :] = d_own
            mixed = dot(key_t[span], d_score)
            d_query_t.append(
                jnp.concatenate(
                    [mixed[:, :rows], mixed[:, rows:] + d_own * own_key_t[span]], axis=1
                )
            )
            d_scores.append(d_score)
            d_own_key.append(d_own * query_t[span, rows:])
            d_own_value.append(prob_own * d_ctx_t[span, rows:])
            wide = d_score.astype(WIDE)
            summed = wide[:, :rows] + wide[:, rows : 2 * rows] + wide[:, 2 * rows :]
            mirrored = dot(summed.astype(LOW), turned)
            for block in range(full // rows):
                piece = mirrored[block * rows : (block + 1) * rows]
                piece = jnp.concatenate([piece, jnp.zeros_like(piece)], axis=1)
                aligned = pltpu.roll(piece, 0, 1, stride=1, stride_axis=0)
                bias_sums[head, block : block + 1, :] = jnp.sum(aligned, axis=0, keepdims=True)
        d_query[:, cols] = (jnp.transpose(jnp.concatenate(d_query_t, axis=0)) * 0.125).astype(LOW)
        d_key[rows:, cols] = jnp.transpose(jnp.concatenate(d_own_key, axis=0)).astype(LOW)
        d_value[rows:, cols] = jnp.transpose(jnp.concatenate(d_own_value, axis=0)).astype(LOW)
        both = jnp.concatenate(d_scores, axis=1)
        split = jnp.concatenate([half_lanes(queries, 0), half_lanes(queries, 1)], axis=0)
        store_part(2, cols, dot(both, split))
        both = jnp.concatenate([kept[slot, 0], kept[slot, 1]], axis=1)
        split = jnp.concatenate([half_lanes(d_ctx, 0), half_lanes(d_ctx, 1)], axis=0)
        store_part(3, cols, dot(both, split))
        return carry

    load_side(2).wait()
    load_side(3).wait()
    quarter = pairs // 4
    lax.fori_loop(0, quarter, self_pair, 0)
    turn(8)
    for load in late:
        load.start()
    lax.fori_loop(quarter, 2 * quarter, self_pair, 0)
    turn(9)
    lax.fori_loop(2 * quarter, 3 * quarter, self_pair, 0)
    for load in late:
        load.wait()
    turn(10)
    lax.fori_loop(3 * quarter, pairs, self_pair, 0)
    core_copy(2).start()
    core_copy(3).start()
    d_cross_key[...] = far_sum(0)
    d_cross_value[...] = far_sum(1)
    turn(11)
    near_sum(2)
    near_sum(3)
    turn(12)
    loads[6].wait()
    loads[7].wait()

    def source_body(cols):
        grad = dot(d_cross_key[...], c_key[cols, :], NT)
        grad = grad + dot(d_cross_value[...], c_value[cols, :], NT)
        encoded_grad[:, cols] = grad.astype(LOW)

    tiles(width // 256, 256, source_body)
    loads[4].start()
    loads[5].start()
    loads[3].wait()

    def query_body(cols):
        d_resid[:, cols] += dot(d_query[...], w_query[cols, :], NT)

    turn(13)
    tiles(width // 256, 256, query_body)
    bucket = lax.broadcasted_iota(jnp.int32, (128, full), 0)
    ones = jnp.ones((8, full), LOW)
    below = (bucket_row[...] < bucket).astype(WIDE).astype(LOW)
    upto = (bucket_row[...] <= bucket).astype(WIDE).astype(LOW)
    first, after = dot(ones, below, NT)[0:1], dot(ones, upto, NT)[0:1]
    lane = lax.broadcasted_iota(jnp.int32, (2 * rows, 128), 0)
    table = jnp.zeros((HEADS, 128), WIDE)
    for block in range(blocks + 1):
        reach = ((sq - block) * rows + rows - 1 - lane).astype(WIDE)
        if block == blocks:
            reach = jnp.zeros((2 * rows, 128), WIDE)
        window_hot = ((reach >= first) & (reach < after)).astype(WIDE).astype(LOW)
        rest = bias_sums[:, block, :]
        for _ in range(3):
            part = rest.astype(LOW)
            rest = rest - part.astype(WIDE)
            table = table + dot(part, window_hot)
    small_out[48:64, :] = table
    small_copy(0).start()
    d_key[:rows, :] = far_sum(2)
    d_value[:rows, :] = far_sum(3)
    turn(14)
    turn(15)
    loads[4].wait()
    loads[5].wait()

    def last_body(cols):
        grad = d_resid[:, cols] + dot(d_key[...], w_key[cols, :], NT)
        grad = grad + dot(d_value[...], w_value[cols, :], NT)
        stream_grad[:, cols] = grad.astype(LOW)

    tiles(width // 256, 256, last_body)
    for index in range(4):
        if index >= 2:
            core_copy(index).wait_send()
        far_copy(index).wait_send()
    last = len(units) + 9
    for index in range(16, last):
        turn(index)
        if index % 2 == 0 and (index - 16) // 2 <= dp_size.bit_length():
            small_step((index - 16) // 2)
    for step in range((last - 15) // 2, dp_size.bit_length() + 1):
        small_step(step)
    drain()


def rear(acts, hbm_acts, sides, weights, ffn_weights, cross_probs, probs, units, dp_size):
    tokens, width = acts[0].shape
    full = sides[0].shape[0]
    rows = tokens // 3
    shape = jax.ShapeDtypeStruct
    vmem = pl.BlockSpec(memory_space=pltpu.VMEM)
    smem = pl.BlockSpec(memory_space=pltpu.SMEM)
    hbm = pl.BlockSpec(memory_space=pl.ANY)
    sem = pltpu.SemaphoreType.DMA
    blocks = full // rows
    chunk = width // dp_size
    steps = dp_size.bit_length() + 1
    return pl.pallas_call(
        functools.partial(rear_kernel, units, dp_size),
        out_shape=[
            shape((rows, width), LOW),
            shape((tokens, width), LOW),
            shape((80, 128), WIDE),
        ]
        + [shape((chunk, COLS), WIDE)] * 8
        + [shape((chunk, 4 * COLS), WIDE), shape((4 * chunk, COLS), WIDE)],
        in_specs=[vmem] * (len(acts) - 1) + [smem] + [hbm] * (len(hbm_acts) + 16),
        out_specs=[vmem] * 13,
        scratch_shapes=[
            pltpu.VMEM((tokens, width), LOW),
            pltpu.VMEM((rows, width), LOW),
            pltpu.VMEM((rows, width), LOW),
            pltpu.VMEM((tokens, width), LOW),
            pltpu.VMEM((tokens, width), LOW),
            pltpu.VMEM((tokens, width), LOW),
            pltpu.VMEM((tokens, width), LOW),
            pltpu.VMEM((HEADS, blocks + 1, 2 * rows), WIDE),
            pltpu.VMEM((steps, 80, 128), WIDE),
            pltpu.VMEM((tokens, 4 * width), LOW),
            pltpu.VMEM((tokens, 4 * width), LOW),
        ]
        + [pltpu.VMEM(w.shape, LOW) for w in weights[:3]]
        + [
            pltpu.VMEM((2, 2, full, tokens), LOW),
            pltpu.VMEM((tokens, width), LOW),
            pltpu.VMEM((tokens, width), WIDE),
            pltpu.VMEM((2, blocks, rows, width), LOW),
            pltpu.VMEM((4, 2, rows, width), LOW),
            pltpu.VMEM((4, rows, width), LOW),
            pltpu.VMEM((2, full, width), LOW),
            pltpu.VMEM((tokens, width), LOW),
            sem((8,)),
            sem((19,)),
            sem((2,)),
            sem((4,)),
            sem((4,)),
            sem((4,)),
            sem((4,)),
            sem((steps,)),
            sem((steps,)),
        ]
        + reduce_buffers(COLORS, dp_size),
        compiler_params=pltpu.CompilerParams(
            collective_id=2, has_side_effects=True, vmem_limit_bytes=63 << 20
        ),
    )(*acts, *hbm_acts, *sides, *weights, *ffn_weights, cross_probs, probs)


def finish_kernel(num, *refs):
    ins, sums = refs[:num], refs[num]
    outs, lines, table, rms, sems = refs[num + 1 : 2 * num + 1], refs[-9:-3], *refs[-3:]
    copies = [
        pltpu.make_async_copy(src, dst, sems.at[index])
        for index, (src, dst) in enumerate(zip(ins, outs))
    ]
    for copy in copies:
        copy.start()
    for row, line in enumerate(lines):
        line[...] = sums[8 * row : 8 * row + 8, :]
    table[...] = sums[48:64, :NBUCKET]
    totals = jnp.sum(sums[64:72, :], axis=1, keepdims=True)
    rms[...] = jnp.broadcast_to(jnp.sqrt(totals / (totals[4:5] * 1024.0)), (8, 128))
    for copy in copies:
        copy.wait()


def finish(arrays, sums):
    shape = jax.ShapeDtypeStruct
    vmem = pl.BlockSpec(memory_space=pltpu.VMEM)
    hbm = pl.BlockSpec(memory_space=pl.ANY)
    num = len(arrays)
    return pl.pallas_call(
        functools.partial(finish_kernel, num),
        out_shape=[shape(array.shape, array.dtype) for array in arrays]
        + [shape((8, 128), WIDE)] * 6
        + [shape((HEADS, NBUCKET), WIDE), shape((8, 128), WIDE)],
        in_specs=[hbm] * num + [vmem],
        out_specs=[hbm] * num + [vmem] * 8,
        scratch_shapes=[pltpu.SemaphoreType.DMA((num,))],
        compiler_params=pltpu.CompilerParams(vmem_limit_bytes=60 << 20),
    )(*arrays, sums)


MESH_ID = pl.DeviceIdType.MESH


def reduce_peers(dp_size):
    dp, sq, core, ypos, core_peer, y_peer = places()
    xpos, zpos = dp % 2, dp // 2
    depth = dp_size // 2
    peers = [core_peer, y_peer, (dp + 1 - 2 * xpos, sq)]
    return peers + [((zpos + step) % depth * 2 + xpos, sq) for step in range(1, depth)]


def reducer(units, colors, ins, emit, buffers, dp_size):
    sent, core_in, first_y, first_x, second_y, second_x, third = buffers[:7]
    z_in, z_half, z_last = buffers[7:10]
    core_s, core_r, one_s, one_r, two_s, two_r, three_s, three_r = buffers[10:18]
    core_free, one_free, two_free = buffers[18:]
    dp, sq, core, ypos, core_peer, y_peer = places()
    xpos, zpos = dp % 2, dp // 2
    depth = dp_size // 2
    chunk = 1024 // dp_size
    x_peer = (dp + 1 - 2 * xpos, sq)
    count = len(units)
    remote = remote_copy
    nth = [colors[:item].count(colors[item]) for item in range(2 * count)]
    order = [item - colors[:item].count("z") for item in range(2 * count)]
    firsts = {"y": first_y, "x": first_x}
    seconds = {"y": second_y, "x": second_x}
    color_id = {"y": 0, "x": RING_ONE}
    first_peer = {"y": y_peer, "x": x_peer}
    second_peer = {"y": x_peer, "x": y_peer}

    def z_peer(step):
        return ((zpos + step) % depth * 2 + xpos, sq)

    def half_dots(unit, half, write):
        x_id, y_id, kind, part, base, tokens = units[unit]
        x_ref, y_ref = ins[x_id], ins[y_id]
        if kind == "back":
            starts = [device * 4 * chunk + part * chunk for device in range(dp_size)]
            left = jnp.concatenate([x_ref[:tokens, s : s + chunk] for s in starts], axis=1)
        else:
            left = x_ref[:tokens, base : base + 1024]
        for side in range(2):
            start = (side * 2 + half) * COLS
            if kind == "in":
                start = (side * 2 + half) * 1024 + part * COLS
            right = y_ref[:tokens, pl.ds(pl.multiple_of(start, COLS), COLS)]
            value = lax.dot_general(
                left, right, (((0,), (0,)), ((), ())), preferred_element_type=WIDE
            )
            write(0, side, value[:, :128])
            write(1, side, value[:, 128:])

    def landed(item):
        return core_in.at[item // 2 % RING, item % 2]

    def core_copy(unit):
        return remote(
            sent.at[unit % SLOTS],
            core_in.at[unit % RING],
            core_s.at[unit],
            core_r.at[unit],
            core_peer,
        )

    def one_copy(item):
        color, source = colors[item], landed(item)
        if color == "y":
            source = source.at[1 - ypos]
        else:
            source = source.reshape(2, depth, 2, chunk, 128).at[:, :, 1 - xpos]
        return remote(
            source,
            firsts[color].at[nth[item] % RING_ONE],
            one_s.at[item],
            one_r.at[item],
            first_peer[color],
        )

    def two_copy(item):
        color = colors[item]
        source = firsts[color].at[nth[item] % RING_ONE]
        if color == "y":
            source = source.reshape(depth, 2, chunk, 128).at[:, 1 - xpos]
        else:
            source = source.at[1 - ypos]
        return remote(
            source,
            seconds[color].at[nth[item] % RING_ONE],
            two_s.at[item],
            two_r.at[item],
            second_peer[color],
        )

    def three_copy(item, step):
        color = colors[item]
        return remote(
            seconds[color].at[nth[item] % RING_ONE, (zpos + step) % depth],
            third.at[order[item], step - 1],
            three_s.at[item, step - 1],
            three_r.at[item, step - 1],
            z_peer(step),
        )

    def z_copy(item, step):
        source = landed(item).reshape(2, depth, 2 * chunk, 128)
        return remote(
            source.at[:, (zpos + step) % depth],
            z_in.at[nth[item], step - 1],
            three_s.at[item, step - 1],
            three_r.at[item, step - 1],
            z_peer(step),
        )

    def zy_copy(item):
        return remote(
            z_in.at[nth[item], 0, 1 - ypos],
            z_half.at[nth[item]],
            one_s.at[item],
            one_r.at[item],
            y_peer,
        )

    def zx_copy(item):
        source = z_half.at[nth[item]].reshape(2, chunk, 128)
        return remote(
            source.at[1 - xpos], z_last.at[nth[item]], two_s.at[item], two_r.at[item], x_peer
        )

    def take(free, slot):
        pl.semaphore_wait(free.at[slot], 1)

    def allow(free, slot, peer):
        pl.semaphore_signal(free.at[slot], inc=1, device_id=peer, device_id_type=MESH_ID)

    def steps(action):
        def body(step, carry):
            action(step)
            return carry

        lax.fori_loop(1, depth, body, 0)

    def plus(left, right):
        return (left.astype(WIDE) + right.astype(WIDE)).astype(LOW)

    def products(unit):
        slot = unit % SLOTS
        if unit >= SLOTS:
            core_copy(unit - SLOTS).wait_send()

        def write(item, side, value):
            sent[slot, item, side] = value.astype(LOW)

        half_dots(unit, 1 - core, write)
        if unit >= RING:
            for item in range(2):
                take(core_free, unit % RING * 2 + item)
        core_copy(unit).start()

    def core_sum(unit):
        core_copy(unit).wait_recv()
        slot = unit % RING

        def write(item, side, value):
            old = core_in[slot, item, side].astype(WIDE)
            core_in[slot, item, side] = (value + old).astype(LOW)

        half_dots(unit, core, write)
        for item in (2 * unit, 2 * unit + 1):
            color = colors[item]
            if color == "z":
                steps(lambda step: z_copy(item, step).start())
                continue
            if nth[item] >= RING_ONE:
                take(one_free, color_id[color] + nth[item] % RING_ONE)
            one_copy(item).start()

    def core_done(item):
        if item // 2 + RING < count:
            allow(core_free, item // 2 % RING * 2 + item % 2, core_peer)

    def one_sum(item):
        color = colors[item]
        if color == "z":
            return
        one_copy(item).wait_recv()
        slot, base, own = nth[item] % RING_ONE, item // 2 % RING, item % 2
        if color == "y":

            def body(step, carry):
                rows = pl.ds(pl.multiple_of(step * 256, 256), 256)
                first_y[slot, rows, :] = plus(
                    first_y[slot, rows, :], core_in[base, own, ypos, rows, :]
                )
                return carry

            lax.fori_loop(0, 4, body, 0)
        else:

            def body(layer, carry):
                rows = pl.ds(pl.multiple_of((layer * 2 + xpos) * chunk, chunk), chunk)
                for side in range(2):
                    first_x[slot, side, layer] = plus(
                        first_x[slot, side, layer], core_in[base, own, side, rows, :]
                    )
                return carry

            lax.fori_loop(0, depth, body, 0)
        if nth[item] >= RING_ONE:
            take(two_free, color_id[color] + nth[item] % RING_ONE)
        two_copy(item).start()
        one_copy(item).wait_send()
        core_done(item)

    def z_sum(item):
        base, own = item // 2 % RING, item % 2
        rows = pl.ds(pl.multiple_of(zpos * 2 * chunk, 2 * chunk), 2 * chunk)
        steps(lambda step: z_copy(item, step).wait_recv())
        for side in range(2):

            def body(step, total):
                return total + z_in[nth[item], step - 1, side].astype(WIDE)

            mine = core_in[base, own, side, rows, :].astype(WIDE)
            z_in[nth[item], 0, side] = lax.fori_loop(1, depth, body, mine).astype(LOW)
        zy_copy(item).start()
        steps(lambda step: z_copy(item, step).wait_send())
        core_done(item)

    def two_sum(item):
        color = colors[item]
        if color == "z":
            z_sum(item)
            return
        two_copy(item).wait_recv()
        slot = nth[item] % RING_ONE
        second = seconds[color]

        def body(layer, carry):
            if color == "y":
                rows = pl.ds(pl.multiple_of((layer * 2 + xpos) * chunk, chunk), chunk)
                old = first_y[slot, rows, :]
            else:
                old = first_x[slot, ypos, layer]
            second[slot, layer] = plus(second[slot, layer], old)
            return carry

        lax.fori_loop(0, depth, body, 0)
        steps(lambda step: three_copy(item, step).start())
        two_copy(item).wait_send()
        if nth[item] + RING_ONE < colors.count(color):
            allow(one_free, color_id[color] + slot, first_peer[color])

    def last_sum(item):
        color = colors[item]
        if color == "z":
            zy_copy(item).wait_recv()
            z_half[nth[item]] = plus(z_half[nth[item]], z_in[nth[item], 0, ypos])
            zx_copy(item).start()
            zy_copy(item).wait_send()
            return
        slot = nth[item] % RING_ONE

        def body(step, total):
            three_copy(item, step).wait_recv()
            return total + third[order[item], step - 1].astype(WIDE)

        total = lax.fori_loop(1, depth, body, seconds[color][slot, zpos].astype(WIDE))
        emit(units[item // 2], item % 2, total)
        steps(lambda step: three_copy(item, step).wait_send())
        if nth[item] + RING_ONE < colors.count(color):
            allow(two_free, color_id[color] + slot, second_peer[color])

    def z_end(item):
        if colors[item] == "z":
            zx_copy(item).wait_recv()
            rows = pl.ds(pl.multiple_of(xpos * chunk, chunk), chunk)
            mine = z_half[nth[item], rows, :].astype(WIDE)
            emit(units[item // 2], item % 2, mine + z_last[nth[item]].astype(WIDE))
            zx_copy(item).wait_send()

    def turn(index):
        for stage, lag in ((products, 0), (core_sum, 1)):
            if 0 <= index - lag < count:
                stage(index - lag)
        for stage, lag in ((one_sum, 3), (two_sum, 5), (last_sum, 7), (z_end, 9)):
            for item in (2 * (index - lag), 2 * (index - lag) + 1):
                if 0 <= item < 2 * count:
                    stage(item)

    def drain():
        for unit in range(count - SLOTS, count):
            core_copy(unit).wait_send()

    return turn, drain


def reduce_buffers(colors, dp_size):
    depth, chunk = dp_size // 2, 1024 // dp_size
    count, slow = len(colors), max(colors.count("z"), 1)
    sem = pltpu.SemaphoreType.DMA
    credit = pltpu.SemaphoreType.REGULAR
    return (
        [
            pltpu.VMEM((SLOTS, 2, 2, 1024, 128), LOW),
            pltpu.VMEM((RING, 2, 2, 1024, 128), LOW),
            pltpu.VMEM((RING_ONE, 1024, 128), LOW),
            pltpu.VMEM((RING_ONE, 2, depth, chunk, 128), LOW),
            pltpu.VMEM((RING_ONE, depth, chunk, 128), LOW),
            pltpu.VMEM((RING_ONE, depth, chunk, 128), LOW),
            pltpu.VMEM((count - colors.count("z"), depth - 1, chunk, 128), LOW),
            pltpu.VMEM((slow, depth - 1, 2, 2 * chunk, 128), LOW),
            pltpu.VMEM((slow, 2 * chunk, 128), LOW),
            pltpu.VMEM((slow, chunk, 128), LOW),
        ]
        + [sem((count // 2,))] * 2
        + [sem((count,))] * 4
        + [sem((count, depth - 1))] * 2
        + [credit((2 * RING,)), credit((2 * RING_ONE,)), credit((2 * RING_ONE,))]
    )


def small_sums(small, small_in, small_s, small_r, dp_size):
    dp, sq, core, ypos, core_peer, y_peer = places()

    def copy(step):
        flip = 1 << max(step - 2, 0)
        peer = (dp + flip - 2 * flip * (dp // flip % 2), sq)
        peer = (core_peer, y_peer, peer)[min(step, 2)]
        return remote_copy(small, small_in.at[step], small_s.at[step], small_r.at[step], peer)

    def advance(step):
        copy(step).wait()
        small[...] = small[...] + small_in[step]
        if step < dp_size.bit_length():
            copy(step + 1).start()

    return copy, advance


def per_device(
    stream,
    encoded,
    cotangent,
    lengths,
    bucket_table,
    w_query,
    w_key,
    w_value,
    w_out,
    c_query,
    c_key,
    c_value,
    c_out,
    w_in,
    w_back,
    gain_one,
    shift_one,
    gain_two,
    shift_two,
    gain_three,
    shift_three,
    position_bias,
):
    num_rows, num_streams, local_len, model_width = stream.shape
    full_len = local_len * lax.axis_size("seq")
    dp_size = lax.axis_size("dp")
    chunk = model_width // dp_size
    bucket_row = bucket_table.reshape(1, full_len)
    flat_rows = stream.reshape(-1, model_width)
    source_rows = encoded.reshape(-1, model_width)
    flat_cotangent = cotangent.reshape(-1, model_width)

    def line(values):
        return values.reshape(1, model_width)

    fronts = front(
        stream.reshape(num_streams, local_len, model_width),
        source_rows,
        lengths,
        bucket_row,
        jnp.transpose(position_bias),
        (line(gain_one), line(shift_one), line(gain_two), line(shift_two)),
        (w_query, w_key, w_value, w_out, c_query, c_key, c_value, c_out),
    )
    query, own_key, own_value, main_key, main_value, context_low, unit_one, first_norm = fronts[:8]
    cross_query, cross_key, cross_value, cross_low, unit_two, second_norm = fronts[8:14]
    scales, own_probs, front_stats, probs, cross_probs = fronts[14:]
    layer_output, activated, d_ffn_out, slope, d_resid_three, mid_grads, ffn_stat = middle(
        second_norm,
        flat_cotangent,
        lengths,
        (line(gain_three), line(shift_three)),
        w_in,
        w_back,
    )
    units = []
    tokens = num_streams * local_len
    spread = activated
    if chunk % 128 != 0:
        spread = activated.reshape(-1, dp_size, 4, chunk)
        spread = jnp.transpose(spread, (0, 2, 1, 3)).reshape(activated.shape)
    for part in range(4):
        if chunk % 128 == 0:
            units.append((3, 0, "back", part, 0, tokens))
        else:
            units.append((3, 0, "parted", part, part * model_width, tokens))
    for part in range(4):
        units.append((1, 2, "in", part, 0, tokens))
    units += [(4, 5, "", 7, 0, tokens), (6, 7, "", 4, 0, tokens), (3, 8, "", 3, 0, tokens)]
    units += [(3, 9, "", 5, 2 * model_width, local_len), (3, 10, "", 6, 2 * model_width, local_len)]
    units += [(3, 11 + part, "", part, model_width, tokens) for part in range(3)]
    rears = rear(
        (
            cross_query,
            unit_one,
            query,
            own_key,
            own_value,
            own_probs,
            line(gain_one),
            d_ffn_out,
            second_norm,
            cross_low,
            first_norm,
            mid_grads,
            ffn_stat,
            front_stats,
            scales,
            line(gain_two),
            bucket_row,
            lengths,
        ),
        (slope, spread, context_low, flat_rows, source_rows, d_resid_three, unit_two),
        (cross_key, cross_value, main_key, main_value),
        (c_out, c_query, w_out, w_query, w_key, w_value, c_key, c_value),
        (w_back, w_in),
        cross_probs,
        probs,
        tuple(units),
        dp_size,
    )
    ends = finish(list(rears[:2]) + list(rears[3:]), rears[2])
    encoded_grad, stream_grad = ends[:2]
    shares, lines, table_grad = ends[2:12], ends[12:18], ends[18]
    rms = ends[19][:4, 0]
    return (
        layer_output.reshape(stream.shape),
        stream_grad.reshape(stream.shape),
        encoded_grad.reshape(encoded.shape),
        shares[0],
        shares[1],
        shares[2],
        shares[3],
        shares[4],
        shares[5],
        shares[6],
        shares[7],
        shares[8],
        shares[9],
        lines[0].reshape(model_width),
        lines[1].reshape(model_width),
        lines[2].reshape(model_width),
        lines[3].reshape(model_width),
        lines[4].reshape(model_width),
        lines[5].reshape(model_width),
        jnp.transpose(table_grad),
        rms,
    )


def solution(mesh):
    placed = (
        P("dp", None, "seq", None),
        P("dp", "seq", None),
        P("dp", None, "seq", None),
        P("dp"),
        P(),
        P(),
        P(),
        P(),
        P(),
        P(),
        P(),
        P(),
        P(),
        P(),
        P(),
        P(),
        P(),
        P(),
        P(),
        P(),
        P(),
        P(),
    )
    return jax.shard_map(
        per_device,
        mesh=mesh,
        in_specs=placed,
        out_specs=(
            P("dp", None, "seq", None),
            P("dp", None, "seq", None),
            P("dp", "seq", None),
            P("dp", "seq"),
            P("dp", "seq"),
            P("dp", "seq"),
            P("dp", "seq"),
            P("dp", "seq"),
            P("dp", "seq"),
            P("dp", "seq"),
            P("dp", "seq"),
            P("dp", "seq"),
            P("dp", "seq"),
            P(),
            P(),
            P(),
            P(),
            P(),
            P(),
            P(),
            P(),
        ),
        check_vma=False,
    )
```

```python
import functools

import jax
import jax.numpy as jnp
from jax import lax
from jax.experimental import pallas as pl
from jax.experimental.pallas import tpu as pltpu
from jax.sharding import PartitionSpec as P

HEADS = 16
HEAD_DIM = 64
NBUCKET = 32
COLS = 256
SLOTS = 2
RING = 6
RING_ONE = 5
COLORS = "yxyxzxyxyxzxyxzxyxyxzxyxzxyxyxyx"
epsilon = 1e-05
masked_score = -1e30


LOW = jnp.bfloat16
WIDE = jnp.float32
NN = (((1,), (0,)), ((), ()))
NT = (((1,), (1,)), ((), ()))


def dot(left, right, dims=NN):
    return lax.dot_general(left, right, dims, preferred_element_type=WIDE)


def flip(block):
    return jnp.transpose(block.astype(WIDE))


def places():
    dp, sq = lax.axis_index("dp"), lax.axis_index("seq")
    core, ypos = sq % 2, sq // 2
    return dp, sq, core, ypos, (dp, sq + 1 - 2 * core), (dp, sq + 2 - 4 * ypos)


def remote_copy(src, dst, send_sem, recv_sem, peer):
    return pltpu.make_async_remote_copy(
        src_ref=src,
        dst_ref=dst,
        send_sem=send_sem,
        recv_sem=recv_sem,
        device_id=peer,
        device_id_type=MESH_ID,
    )


def greet(peers):
    barrier = pltpu.get_barrier_semaphore()
    for peer in peers:
        pl.semaphore_signal(barrier, inc=1, device_id=peer, device_id_type=MESH_ID)
    pl.semaphore_wait(barrier, len(peers))


def tiles(count, size, body):
    def step(index, carry):
        body(pl.ds(pl.multiple_of(index * size, size), size))
        return carry

    lax.fori_loop(0, count, step, 0)


def project_to(dst, left, weight, scale=None):
    product = dot(left[...], weight[...])
    if scale is not None:
        product = product * scale
    dst[...] = product.astype(dst.dtype)


def norm_stats(rows):
    centre = jnp.mean(rows, axis=-1, keepdims=True)
    centred = rows - centre
    spread = jnp.mean(centred * centred, axis=-1, keepdims=True)
    return centred, lax.rsqrt(spread + epsilon)


def norm_backward(unit, scale, gain, incoming):
    scaled = incoming * gain
    first = jnp.mean(scaled, axis=-1, keepdims=True)
    second = jnp.mean(scaled * unit, axis=-1, keepdims=True)
    grads = scale * (scaled - first - unit * second)
    d_gain = jnp.sum(incoming * unit, axis=0, keepdims=True)
    return grads, d_gain, jnp.sum(incoming, axis=0, keepdims=True)


def valid_rows(sq, length, count):
    position = sq * count + lax.broadcasted_iota(jnp.int32, (count, 1), 0)
    return (position < length).astype(WIDE)


def sum_squares(rows, mask):
    return jnp.sum(rows * rows * mask, axis=0, keepdims=True)


def half_rows(block, side):
    row = lax.broadcasted_iota(jnp.int32, block.shape, 0)
    return jnp.where(row // HEAD_DIM == side, block, 0.0).astype(LOW)


def half_lanes(block, side):
    lane = lax.broadcasted_iota(jnp.int32, block.shape, 1)
    return jnp.where(lane // HEAD_DIM == side, block.astype(WIDE), 0.0).astype(LOW)


def front_kernel(*refs):
    stream, encoded, length_ref, bucket_row, position_bias = refs[:5]
    gain_one, shift_one, gain_two, shift_two = refs[5:9]
    hbm_weights = refs[9:17]
    outs, probs_out, cross_probs_out = refs[17:34], refs[34], refs[35]
    held, refs = refs[36:53], refs[53:]
    (query, own_key, own_value, main_key, main_value, context, unit_one, first_norm) = held[:8]
    (cross_query, cross_key, cross_value, cross_context, unit_two, second_norm) = held[8:14]
    scales, own_probs, stats = held[14:]
    weights = refs[:8]
    main_all, source_all, kept, bias, masks, branch_out, bias_table = refs[8:15]
    weight_sem, kept_sem, send_sem, recv_sem, out_sem = refs[15:]
    stores = [
        pltpu.make_async_copy(src, dst, out_sem.at[index])
        for index, (src, dst) in enumerate(zip(held, outs))
    ]
    w_query, w_key, w_value, w_out, c_query, c_key, c_value, c_out = weights
    dp, sq, core, ypos, core_peer, y_peer = places()
    length = length_ref[0]
    rows = stream.shape[1]
    full = main_all.shape[0] * rows
    loads = [
        pltpu.make_async_copy(src, dst, weight_sem.at[index])
        for index, (src, dst) in enumerate(zip(hbm_weights, weights))
    ]
    for load in loads:
        load.start()
    greet([core_peer, y_peer])
    sources = (stream.at[0], encoded)
    gathered = (main_all, source_all)
    firsts = []
    for index in range(2):
        for lane, peer in enumerate((y_peer, core_peer)):
            slot = index * 3 + lane
            firsts.append(
                remote_copy(
                    sources[index],
                    gathered[index].at[sq],
                    send_sem.at[slot],
                    recv_sem.at[slot],
                    peer,
                )
            )
    firsts[0].start()
    firsts[1].start()
    main_all[sq] = stream[0]
    source_all[sq] = encoded[...]
    bucket = lax.broadcasted_iota(jnp.int32, (NBUCKET, full), 0)
    table_hot = (bucket == bucket_row[...]).astype(WIDE).astype(LOW)
    by_distance = jnp.zeros((HEADS, full), WIDE)
    rest = position_bias[...]
    for _ in range(3):
        part = rest.astype(LOW)
        rest = rest - part.astype(WIDE)
        by_distance = by_distance + dot(part, table_hot)
    bias_table[...] = jnp.zeros_like(bias_table)
    for head in range(HEADS):
        bias_table[head, :, full:] = by_distance[head : head + 1]

    def passed_on(index):
        other = gathered[index].at[sq + 2 - 4 * ypos]
        slot = index * 3 + 2
        return remote_copy(other, other, send_sem.at[slot], recv_sem.at[slot], core_peer)

    flat = stream.reshape(3 * rows, stream.shape[2])
    loads[0].wait()
    project_to(query, flat, w_query, 0.125)
    stores[0].start()
    predicting = flat.at[rows:, :]
    loads[1].wait()
    project_to(own_key, predicting, w_key)
    loads[2].wait()
    project_to(own_value, predicting, w_value)
    key_row = lax.broadcasted_iota(jnp.int32, (full, rows), 0)
    distance = sq * rows + lax.broadcasted_iota(jnp.int32, (full, rows), 1) - key_row
    in_range = key_row < length
    masks[0] = jnp.where((distance >= 0) & in_range, 0.0, masked_score)
    masks[1] = jnp.where((distance > 0) & in_range, 0.0, masked_score)
    masks[2] = jnp.where(in_range, 0.0, masked_score)
    firsts[0].wait_recv()
    passed_on(0).start()
    firsts[2].start()
    firsts[3].start()
    stores[1].start()
    stores[2].start()
    firsts[1].wait_recv()
    passed_on(0).wait_recv()
    wide_main = main_all.reshape(full, main_all.shape[2])
    project_to(main_key, wide_main, w_key)
    project_to(main_value, wide_main, w_value)
    stores[3].start()
    stores[4].start()

    def kept_copy(pair, out):
        slot = pair % 2
        return pltpu.make_async_copy(kept.at[slot], out.at[pair], kept_sem.at[slot])

    def self_pair(pair, carry):
        @pl.when(pair >= 2)
        def _():
            kept_copy(pair - 2, probs_out).wait()

        slot = pair % 2
        cols = pl.ds(pl.multiple_of(pair * 128, 128), 128)
        keys = main_key[:, cols]
        query_t = flip(query[:, cols])
        value_t = flip(main_value[:, cols]).astype(LOW)
        own_key_t, own_value_t = flip(own_key[:, cols]), flip(own_value[:, cols])
        own_product = query_t[:, rows:] * own_key_t
        sides = []
        for side in range(2):
            head = 2 * pair + side
            span = slice(side * HEAD_DIM, (side + 1) * HEAD_DIM)
            scores = dot(keys, half_rows(query_t, side))
            own_bias = bias_table[head, :, full : full + 128][:, 0:1]
            own_score = jnp.sum(own_product[span], axis=0, keepdims=True) + own_bias
            for block in range(full // rows):
                start = pl.multiple_of((sq - block + full // rows - 1) * rows, 128)
                line = bias_table[head, :, pl.ds(start, 2 * rows)]
                wide = jnp.broadcast_to(line, (rows, 2 * rows))
                near = pltpu.roll(wide, 0, 1, stride=1, stride_axis=0)[:, rows:]
                part = slice(block * rows, (block + 1) * rows)
                for kind in range(2):
                    bias[kind, part, :] = near + masks[kind, part, :]
            owns = []
            for stream_id in range(3):
                lanes = slice(stream_id * rows, (stream_id + 1) * rows)
                score = scores[:, lanes] + bias[min(stream_id, 1)]
                top = jnp.max(score, axis=0, keepdims=True)
                if stream_id > 0:
                    own = own_score[:, (stream_id - 1) * rows : stream_id * rows]
                    top = jnp.maximum(top, own)
                expo = jnp.exp(score - top)
                total = jnp.sum(expo, axis=0, keepdims=True)
                if stream_id > 0:
                    expo_own = jnp.exp(own - top)
                    total = total + expo_own
                share = 1.0 / total
                kept[slot, side, :, lanes] = (expo * share).astype(LOW)
                owns.append(expo_own * share if stream_id > 0 else jnp.zeros_like(total))
            own_probs[head] = jnp.concatenate(owns, axis=1)
            mixed = dot(value_t[span], kept[slot, side])
            mixed_own = jnp.concatenate(owns[1:], axis=1) * own_value_t[span]
            sides.append(
                jnp.concatenate([mixed[:, :rows], mixed[:, rows:] + mixed_own], axis=1)
            )
        context[:, cols] = jnp.transpose(jnp.concatenate(sides, axis=0)).astype(LOW)
        kept_copy(pair, probs_out).start()
        return carry

    lax.fori_loop(0, HEADS // 2, self_pair, 0)
    for pair in range(HEADS // 2 - 2, HEADS // 2):
        kept_copy(pair, probs_out).wait()
    stores[5].start()
    stores[15].start()

    mask = valid_rows(sq, length, rows)
    loads[3].wait()
    project_to(branch_out, context, w_out)
    firsts[2].wait_recv()
    passed_on(1).start()
    seen = jnp.zeros((1, stream.shape[2]), WIDE)
    branch = jnp.zeros((1, stream.shape[2]), WIDE)
    for stream_id in range(3):
        part = slice(stream_id * rows, (stream_id + 1) * rows)
        source, attended = stream[stream_id].astype(WIDE), branch_out[part, :]
        seen = seen + sum_squares(source, mask)
        branch = branch + sum_squares(attended, mask)
        centred, scale = norm_stats(source + attended)
        unit = centred * scale
        unit_one[part, :] = unit.astype(LOW)
        scales[0, part, :] = jnp.broadcast_to(scale, (rows, 128))
        first_norm[part, :] = (unit * gain_one[...] + shift_one[...]).astype(LOW)
    stats[0:1, :] = seen
    stats[1:2, :] = branch
    loads[4].wait()
    project_to(cross_query, first_norm, c_query, 0.125)
    for index in (6, 7, 8):
        stores[index].start()
    firsts[3].wait_recv()
    passed_on(1).wait_recv()
    wide_source = source_all.reshape(full, source_all.shape[2])
    loads[5].wait()
    project_to(cross_key, wide_source, c_key)
    loads[6].wait()
    project_to(cross_value, wide_source, c_value)
    stores[9].start()
    stores[10].start()

    def cross_pair(pair, carry):
        @pl.when(pair >= 2)
        def _():
            kept_copy(pair - 2, cross_probs_out).wait()

        slot = pair % 2
        cols = pl.ds(pl.multiple_of(pair * 128, 128), 128)
        keys = cross_key[:, cols]
        query_t = flip(cross_query[:, cols])
        value_t = flip(cross_value[:, cols]).astype(LOW)
        sides = []
        for side in range(2):
            span = slice(side * HEAD_DIM, (side + 1) * HEAD_DIM)
            scores = dot(keys, half_rows(query_t, side))
            for stream_id in range(3):
                lanes = slice(stream_id * rows, (stream_id + 1) * rows)
                score = scores[:, lanes] + masks[2]
                expo = jnp.exp(score - jnp.max(score, axis=0, keepdims=True))
                share = 1.0 / jnp.sum(expo, axis=0, keepdims=True)
                kept[slot, side, :, lanes] = (expo * share).astype(LOW)
            sides.append(dot(value_t[span], kept[slot, side]))
        cross_context[:, cols] = jnp.transpose(jnp.concatenate(sides, axis=0)).astype(LOW)
        kept_copy(pair, cross_probs_out).start()
        return carry

    lax.fori_loop(0, HEADS // 2, cross_pair, 0)
    for pair in range(HEADS // 2 - 2, HEADS // 2):
        kept_copy(pair, cross_probs_out).wait()
    stores[11].start()
    loads[7].wait()
    project_to(branch_out, cross_context, c_out)
    branch = jnp.zeros((1, stream.shape[2]), WIDE)
    for stream_id in range(3):
        part = slice(stream_id * rows, (stream_id + 1) * rows)
        crossed = branch_out[part, :]
        branch = branch + sum_squares(crossed, mask)
        centred, scale = norm_stats(first_norm[part, :].astype(WIDE) + crossed)
        unit = centred * scale
        unit_two[part, :] = unit.astype(LOW)
        scales[1, part, :] = jnp.broadcast_to(scale, (rows, 128))
        second_norm[part, :] = (unit * gain_two[...] + shift_two[...]).astype(LOW)
    stats[2:3, :] = branch
    for index in (12, 13, 14, 16):
        stores[index].start()
    for store in stores:
        store.wait()
    for copy in firsts:
        copy.wait_send()
    for index in range(2):
        passed_on(index).wait_send()


def front(stream, encoded, length, bucket_row, position_bias, norms, weights):
    streams, rows, width = stream.shape
    seq = lax.axis_size("seq")
    full, tokens = seq * rows, streams * rows
    own = tokens - rows
    shape = jax.ShapeDtypeStruct
    pairs = HEADS // 2
    outs = [
        shape((tokens, width), LOW),
        shape((own, width), LOW),
        shape((own, width), LOW),
        shape((full, width), LOW),
        shape((full, width), LOW),
        shape((tokens, width), LOW),
        shape((tokens, width), LOW),
        shape((tokens, width), LOW),
        shape((tokens, width), LOW),
        shape((full, width), LOW),
        shape((full, width), LOW),
        shape((tokens, width), LOW),
        shape((tokens, width), LOW),
        shape((tokens, width), LOW),
        shape((2, tokens, 128), WIDE),
        shape((HEADS, 1, tokens), WIDE),
        shape((3, width), WIDE),
        shape((pairs, 2, full, tokens), LOW),
        shape((pairs, 2, full, tokens), LOW),
    ]
    vmem = pl.BlockSpec(memory_space=pltpu.VMEM)
    smem = pl.BlockSpec(memory_space=pltpu.SMEM)
    hbm = pl.BlockSpec(memory_space=pl.ANY)
    sem = pltpu.SemaphoreType.DMA
    return pl.pallas_call(
        front_kernel,
        out_shape=outs,
        in_specs=[vmem, vmem, smem] + [vmem] * 6 + [hbm] * 8,
        out_specs=[hbm] * 19,
        scratch_shapes=[pltpu.VMEM(out.shape, out.dtype) for out in outs[:17]]
        + [pltpu.VMEM(w.shape, LOW) for w in weights]
        + [
            pltpu.VMEM((seq, rows, width), LOW),
            pltpu.VMEM((seq, rows, width), LOW),
            pltpu.VMEM((2, 2, full, tokens), LOW),
            pltpu.VMEM((2, full, rows), WIDE),
            pltpu.VMEM((3, full, rows), WIDE),
            pltpu.VMEM((tokens, width), WIDE),
            pltpu.VMEM((HEADS, 1, 2 * full), WIDE),
            sem((8,)),
            sem((2,)),
            sem((6,)),
            sem((6,)),
            sem((17,)),
        ],
        compiler_params=pltpu.CompilerParams(
            collective_id=1, has_side_effects=True, vmem_limit_bytes=60 << 20
        ),
    )(stream, encoded, length, bucket_row, position_bias, *norms, *weights)


def middle_kernel(*refs):
    second_norm, cotangent, length_ref, gain_three, shift_three, hbm_in, hbm_back = refs[:7]
    outs, grads, stats = refs[7:12], refs[12], refs[13]
    output, activated, d_ffn, slope, total = refs[14:19]
    w_in, w_back, load_sem, out_sem = refs[19:]
    sq = lax.axis_index("seq")
    length = length_ref[0]
    tokens, width = second_norm.shape
    rows = tokens // 3
    hidden = w_in.shape[1]
    size = 1024
    steps = hidden // size
    stores = [
        pltpu.make_async_copy(src, dst, out_sem.at[index])
        for index, (src, dst) in enumerate(zip(refs[14:19], outs))
    ]

    def load_in(step):
        cols = pl.ds(pl.multiple_of(step * size, size), size)
        return pltpu.make_async_copy(hbm_in.at[:, cols], w_in.at[:, cols], load_sem.at[0, step])

    def load_back(step):
        cols = pl.ds(pl.multiple_of(step * size, size), size)
        return pltpu.make_async_copy(hbm_back.at[cols], w_back.at[cols], load_sem.at[1, step])

    for step in range(steps):
        load_in(step).start()
        load_back(step).start()
    total[...] = jnp.zeros_like(total)

    def forward(step, carry):
        cols = pl.ds(pl.multiple_of(step * size, size), size)
        load_in(step).wait()
        inner = dot(second_norm[...], w_in[:, cols])
        phi = 0.5 + 0.5 * lax.erf(inner * (0.5**0.5))
        bell = jnp.exp(inner * inner * -0.5) * (0.5 / jnp.pi) ** 0.5
        value = (inner * phi).astype(LOW)
        activated[:, cols] = value
        slope[:, cols] = (phi + inner * bell).astype(LOW)
        load_back(step).wait()
        total[...] += dot(value, w_back[cols, :])
        return carry

    lax.fori_loop(0, steps, forward, 0)
    stores[1].start()
    stores[3].start()
    mask = valid_rows(sq, length, rows)
    branch = jnp.zeros((1, width), WIDE)
    d_gain = jnp.zeros((1, width), WIDE)
    d_shift = jnp.zeros((1, width), WIDE)
    for stream_id in range(3):
        part = slice(stream_id * rows, (stream_id + 1) * rows)
        ffn = total[part, :]
        branch = branch + sum_squares(ffn, mask)
        resid = second_norm[part, :].astype(WIDE) + ffn
        centred, scale = norm_stats(resid)
        unit = centred * scale
        normed = unit * gain_three[...] + shift_three[...]
        output[part, :] = (normed * mask).astype(LOW)
        incoming = cotangent[part, :].astype(WIDE) * mask
        back, gain_part, shift_part = norm_backward(unit, scale, gain_three[...], incoming)
        d_gain, d_shift = d_gain + gain_part, d_shift + shift_part
        total[part, :] = back
        d_ffn[part, :] = back.astype(LOW)
    stats[...] = branch
    grads[0:1, :] = d_gain
    grads[1:2, :] = d_shift
    for index in (0, 2, 4):
        stores[index].start()
    for store in stores:
        store.wait()


def middle(second_norm, cotangent, length, norms, w_in, w_back):
    tokens, width = second_norm.shape
    hidden = w_in.shape[1]
    shape = jax.ShapeDtypeStruct
    vmem = pl.BlockSpec(memory_space=pltpu.VMEM)
    smem = pl.BlockSpec(memory_space=pltpu.SMEM)
    hbm = pl.BlockSpec(memory_space=pl.ANY)
    outs = [
        shape((tokens, width), LOW),
        shape((tokens, hidden), LOW),
        shape((tokens, width), LOW),
        shape((tokens, hidden), LOW),
        shape((tokens, width), WIDE),
    ]
    return pl.pallas_call(
        middle_kernel,
        out_shape=outs + [shape((2, width), WIDE), shape((1, width), WIDE)],
        in_specs=[vmem] * 2 + [smem] + [vmem] * 2 + [hbm] * 2,
        out_specs=[hbm] * 5 + [vmem] * 2,
        scratch_shapes=[pltpu.VMEM(out.shape, out.dtype) for out in outs]
        + [
            pltpu.VMEM(w_in.shape, LOW),
            pltpu.VMEM(w_back.shape, LOW),
            pltpu.SemaphoreType.DMA((2, hidden // 1024)),
            pltpu.SemaphoreType.DMA((5,)),
        ],
        compiler_params=pltpu.CompilerParams(vmem_limit_bytes=60 << 20),
    )(second_norm, cotangent, length, *norms, w_in, w_back)


def rear_kernel(units, dp_size, *refs):
    cross_query, unit_one, query, own_key, own_value, own_probs, gain_one = refs[:7]
    refs = (None,) + refs
    d_ffn, second_norm, cross_context, first_norm, mid_grads, ffn_stat, front_stats = refs[8:15]
    scales, gain_two, bucket_row, length_ref = refs[15:19]
    refs = refs[:15] + refs[19:]
    hbm_slope, hbm_activated, hbm_context, hbm_stream, hbm_source, hbm_resid = refs[15:21]
    hbm_unit, refs = refs[21], refs[:21] + refs[22:]
    hbm_sides, hbm_weights = refs[21:25], refs[25:33]
    hbm_ffn, refs = refs[33:35], refs[:33] + refs[35:]
    cross_probs, probs = refs[33:35]
    encoded_grad, stream_grad, small_out = refs[35:38]
    shares, in_share, back_share = refs[38:46], refs[46], refs[47]
    (d_cross_query, d_cross_key, d_cross_value, d_attended) = refs[48:52]
    (d_query, d_key, d_value, bias_sums, small_in) = refs[52:57]
    d_inner, activated = refs[57:59]
    weights = refs[59:62]
    kept, d_context, d_resid, parts, near_in, far_in, sides_held = refs[62:69]
    d_crossed, ffn_sem, refs = refs[69], refs[70], refs[:69] + refs[71:]
    weight_sem, kept_sem, core_s, core_r, far_s, far_r, small_s, small_r = refs[69:77]
    held = (0, 1, 2, 0, 1, 2, 1, 2)
    c_out, c_query, w_out, w_query, w_key, w_value, c_key, c_value = [weights[i] for i in held]
    chunk = 1024 // dp_size

    def emit(unit, item, total):
        part, cols = unit[3], slice(item * 128, (item + 1) * 128)
        if unit[2] == "in":
            in_share[:, part * COLS + item * 128 : part * COLS + (item + 1) * 128] = total
        elif unit[2] in ("back", "parted"):
            back_share[part * chunk : (part + 1) * chunk, cols] = total
        else:
            shares[part][:, cols] = total

    operands = (d_ffn, second_norm, d_inner, activated, cross_context, d_crossed, first_norm)
    operands += (d_cross_query, d_attended, d_cross_key, d_cross_value, d_query, d_key, d_value)
    turn, drain = reducer(units, COLORS, operands, emit, refs[77:], dp_size)
    small_copy, small_step = small_sums(small_out, small_in, small_s, small_r, dp_size)
    dp, sq, core, ypos, core_peer, y_peer = places()
    tokens, width = query.shape
    rows = tokens // 3
    full = sides_held.shape[1]
    blocks = full // rows
    keys_held, values_held = sides_held.at[0], sides_held.at[1]
    pairs = HEADS // 2
    loads = [
        pltpu.make_async_copy(src, weights[held[index]], weight_sem.at[index])
        for index, src in enumerate(hbm_weights)
    ]

    def load_extra(index, src, dst):
        return pltpu.make_async_copy(src, dst, weight_sem.at[12 + index])

    early = [
        load_extra(0, hbm_activated, activated),
        load_extra(1, hbm_slope, d_inner),
        load_extra(2, hbm_resid, d_resid),
        load_extra(6, hbm_unit, d_context),
    ]
    late = [
        load_extra(3, hbm_context, activated.at[:, :width]),
        load_extra(4, hbm_stream, activated.at[:, width : 2 * width]),
        load_extra(5, hbm_source, activated.at[:rows, 2 * width : 3 * width]),
    ]

    def load_side(index):
        return pltpu.make_async_copy(
            hbm_sides[index], sides_held.at[index % 2], weight_sem.at[8 + index]
        )

    def fetch(pair, source, base):
        slot = (pair + base) % 2
        return pltpu.make_async_copy(source.at[pair], kept.at[slot], kept_sem.at[slot])

    def keep_lines(base, lines):
        for row, line in enumerate(lines):
            for piece in range(8):
                at = 8 * (base + row) + piece
                small_out[at : at + 1, :] = line[:, 128 * piece : 128 * (piece + 1)]

    def ffn_load(index):
        span = pl.ds(index // 2 * width, width)
        source = hbm_ffn[0].at[span] if index % 2 == 0 else hbm_ffn[1].at[:, span]
        return pltpu.make_async_copy(source, weights[index % 3], ffn_sem.at[index])

    early[0].start()
    early[1].start()
    for index in range(3):
        ffn_load(index).start()
    early[2].start()
    early[3].start()
    fetch(0, cross_probs, 0).start()
    load_side(0).start()
    load_side(1).start()
    greet(reduce_peers(dp_size))
    early[0].wait()
    turn(0)
    turn(1)
    early[1].wait()
    early[2].wait()
    ffn_steps = hbm_ffn[0].shape[0] // width
    for step in range(ffn_steps):
        span = slice(step * width, (step + 1) * width)
        ffn_load(2 * step).wait()
        d_act = dot(d_ffn[...], weights[2 * step % 3][...], NT)
        d_inner[:, span] = (d_act * d_inner[:, span].astype(WIDE)).astype(LOW)
        ffn_load(2 * step + 1).wait()
        d_resid[...] += dot(d_inner[:, span], weights[(2 * step + 1) % 3][...], NT)
        for index in (2 * step + 3, 2 * step + 4):
            if index < 2 * ffn_steps:
                ffn_load(index).start()
        if step != 2:
            turn((2, 3, None, 4)[step])
    for index in range(3):
        loads[index].start()
    early[3].wait()
    d_gain_two = jnp.zeros((1, width), WIDE)
    d_shift_two = jnp.zeros((1, width), WIDE)
    for stream_id in range(3):
        part = slice(stream_id * rows, (stream_id + 1) * rows)
        unit, scale = d_context[part, :].astype(WIDE), scales[1, part, 0:1]
        back, gain_part, shift_part = norm_backward(unit, scale, gain_two[...], d_resid[part, :])
        d_gain_two, d_shift_two = d_gain_two + gain_part, d_shift_two + shift_part
        d_resid[part, :] = back
        d_crossed[part, :] = back.astype(LOW)
    keep_lines(2, [d_gain_two, d_shift_two])
    loads[0].wait()

    def back_to(dst, left, weight, add=False):
        def body(cols):
            product = dot(left[...], weight[cols, :], NT)
            if add:
                product = product + dst[:, cols]
            dst[:, cols] = product.astype(dst.dtype)

        tiles(width // 256, 256, body)

    back_to(d_context, d_crossed, c_out)
    loads[3].start()

    def core_copy(index):
        view = parts.at[index % 2].reshape(2, 2, rows, width)
        return remote_copy(
            view.at[:, 1 - core], near_in.at[index], core_s.at[index], core_r.at[index], core_peer
        )

    def far_copy(index):
        return remote_copy(
            near_in.at[index, 1 - ypos], far_in.at[index], far_s.at[index], far_r.at[index], y_peer
        )

    def near_sum(index):
        core_copy(index).wait_recv()
        for side in range(2):
            mine = parts[index % 2, side * 2 + core].astype(WIDE)
            near_in[index, side] = (near_in[index, side].astype(WIDE) + mine).astype(LOW)
        far_copy(index).start()

    def far_sum(index):
        far_copy(index).wait_recv()
        return (near_in[index, ypos].astype(WIDE) + far_in[index].astype(WIDE)).astype(LOW)

    def store_part(index, cols, block):
        for part in range(full // rows):
            parts[index % 2, part, :, cols] = block[part * rows : (part + 1) * rows].astype(LOW)

    def cross_pair(pair, carry):
        fetch(pair, cross_probs, 0).wait()

        @pl.when(pair + 1 < pairs)
        def _():
            fetch(pair + 1, cross_probs, 0).start()

        slot = pair % 2
        cols = pl.ds(pl.multiple_of(pair * 128, 128), 128)
        values = values_held[:, cols]
        key_t = flip(keys_held[:, cols]).astype(LOW)
        queries, d_ctx = cross_query[:, cols], d_context[:, cols]
        d_ctx_t = flip(d_ctx)
        d_query_t, d_scores = [], []
        for side in range(2):
            span = slice(side * HEAD_DIM, (side + 1) * HEAD_DIM)
            d_prob = dot(values, half_rows(d_ctx_t, side))
            prob = kept[slot, side].astype(WIDE)
            delta = jnp.sum(prob * d_prob, axis=0, keepdims=True)
            d_score = (prob * (d_prob - delta)).astype(LOW)
            d_query_t.append(dot(key_t[span], d_score))
            d_scores.append(d_score)
        d_cross_query[:, cols] = (
            jnp.transpose(jnp.concatenate(d_query_t, axis=0)) * 0.125
        ).astype(LOW)
        both = jnp.concatenate(d_scores, axis=1)
        split = jnp.concatenate([half_lanes(queries, 0), half_lanes(queries, 1)], axis=0)
        store_part(0, cols, dot(both, split))
        both = jnp.concatenate([kept[slot, 0], kept[slot, 1]], axis=1)
        split = jnp.concatenate([half_lanes(d_ctx, 0), half_lanes(d_ctx, 1)], axis=0)
        store_part(1, cols, dot(both, split))
        return carry

    load_side(0).wait()
    load_side(1).wait()
    lax.fori_loop(0, pairs // 2, cross_pair, 0)
    turn(5)
    lax.fori_loop(pairs // 2, pairs, cross_pair, 0)
    fetch(0, probs, 0).start()
    load_side(2).start()
    load_side(3).start()
    core_copy(0).start()
    core_copy(1).start()
    turn(6)
    loads[1].wait()
    back_to(d_resid, d_cross_query, c_query, True)
    loads[6].start()
    d_gain = jnp.zeros((1, width), WIDE)
    d_shift = jnp.zeros((1, width), WIDE)
    for stream_id in range(3):
        part = slice(stream_id * rows, (stream_id + 1) * rows)
        unit, scale = unit_one[part, :].astype(WIDE), scales[0, part, 0:1]
        back, gain_part, shift_part = norm_backward(
            unit, scale, gain_one[...], d_resid[part, :]
        )
        d_gain, d_shift = d_gain + gain_part, d_shift + shift_part
        d_resid[part, :] = back
        d_attended[part, :] = back.astype(LOW)
    keep_lines(0, [d_gain, d_shift])
    keep_lines(4, [mid_grads[row : row + 1, :] for row in range(2)])
    for row, line in enumerate([front_stats[row : row + 1, :] for row in range(3)] + [ffn_stat[...]]):
        folded = line[:, :128]
        for piece in range(1, 8):
            folded = folded + line[:, 128 * piece : 128 * (piece + 1)]
        small_out[64 + row : 65 + row, :] = folded
    mask = valid_rows(sq, length_ref[0], rows)
    count = jnp.sum(jnp.broadcast_to(mask, (rows, 128)), axis=0, keepdims=True)
    small_out[68:69, :] = count * (3.0 / 128.0)
    small_out[69:80, :] = jnp.zeros((11, 128), WIDE)
    near_sum(0)
    near_sum(1)
    turn(7)
    loads[2].wait()
    back_to(d_context, d_attended, w_out)
    loads[7].start()
    core_copy(0).wait_send()
    core_copy(1).wait_send()
    line = lax.broadcasted_iota(jnp.int32, (rows, rows), 0)
    turned = (line + lax.broadcasted_iota(jnp.int32, (rows, rows), 1) == rows - 1).astype(LOW)

    def self_pair(pair, carry):
        fetch(pair, probs, 0).wait()

        @pl.when(pair + 1 < pairs)
        def _():
            fetch(pair + 1, probs, 0).start()

        slot = pair % 2
        cols = pl.ds(pl.multiple_of(pair * 128, 128), 128)
        values = values_held[:, cols]
        key_t = flip(keys_held[:, cols]).astype(LOW)
        queries, d_ctx = query[:, cols], d_context[:, cols]
        d_ctx_t, query_t = flip(d_ctx), flip(queries)
        own_key_t, own_value_t = flip(own_key[:, cols]), flip(own_value[:, cols])
        own_product = d_ctx_t[:, rows:] * own_value_t
        d_query_t, d_scores, d_own_key, d_own_value = [], [], [], []
        for side in range(2):
            head = 2 * pair + side
            span = slice(side * HEAD_DIM, (side + 1) * HEAD_DIM)
            d_prob = dot(values, half_rows(d_ctx_t, side))
            prob = kept[slot, side].astype(WIDE)
            prob_own = own_probs[head][:, rows:]
            d_prob_own = jnp.sum(own_product[span], axis=0, keepdims=True)
            delta = jnp.sum(prob * d_prob, axis=0, keepdims=True)
            delta = jnp.concatenate(
                [delta[:, :rows], delta[:, rows:] + prob_own * d_prob_own], axis=1
            )
            d_score = (prob * (d_prob - delta)).astype(LOW)
            d_own = (prob_own * (d_prob_own - delta[:, rows:])).astype(LOW).astype(WIDE)
            bias_sums[head, blocks : blocks + 1, :] = d_own
            mixed = dot(key_t[span], d_score)
            d_query_t.append(
                jnp.concatenate(
                    [mixed[:, :rows], mixed[:, rows:] + d_own * own_key_t[span]], axis=1
                )
            )
            d_scores.append(d_score)
            d_own_key.append(d_own * query_t[span, rows:])
            d_own_value.append(prob_own * d_ctx_t[span, rows:])
            wide = d_score.astype(WIDE)
            summed = wide[:, :rows] + wide[:, rows : 2 * rows] + wide[:, 2 * rows :]
            mirrored = dot(summed.astype(LOW), turned)
            for block in range(full // rows):
                piece = mirrored[block * rows : (block + 1) * rows]
                piece = jnp.concatenate([piece, jnp.zeros_like(piece)], axis=1)
                aligned = pltpu.roll(piece, 0, 1, stride=1, stride_axis=0)
                bias_sums[head, block : block + 1, :] = jnp.sum(aligned, axis=0, keepdims=True)
        d_query[:, cols] = (jnp.transpose(jnp.concatenate(d_query_t, axis=0)) * 0.125).astype(LOW)
        d_key[rows:, cols] = jnp.transpose(jnp.concatenate(d_own_key, axis=0)).astype(LOW)
        d_value[rows:, cols] = jnp.transpose(jnp.concatenate(d_own_value, axis=0)).astype(LOW)
        both = jnp.concatenate(d_scores, axis=1)
        split = jnp.concatenate([half_lanes(queries, 0), half_lanes(queries, 1)], axis=0)
        store_part(2, cols, dot(both, split))
        both = jnp.concatenate([kept[slot, 0], kept[slot, 1]], axis=1)
        split = jnp.concatenate([half_lanes(d_ctx, 0), half_lanes(d_ctx, 1)], axis=0)
        store_part(3, cols, dot(both, split))
        return carry

    load_side(2).wait()
    load_side(3).wait()
    quarter = pairs // 4
    lax.fori_loop(0, quarter, self_pair, 0)
    turn(8)
    for load in late:
        load.start()
    lax.fori_loop(quarter, 2 * quarter, self_pair, 0)
    turn(9)
    lax.fori_loop(2 * quarter, 3 * quarter, self_pair, 0)
    for load in late:
        load.wait()
    turn(10)
    lax.fori_loop(3 * quarter, pairs, self_pair, 0)
    core_copy(2).start()
    core_copy(3).start()
    d_cross_key[...] = far_sum(0)
    d_cross_value[...] = far_sum(1)
    turn(11)
    near_sum(2)
    near_sum(3)
    turn(12)
    loads[6].wait()
    loads[7].wait()

    def source_body(cols):
        grad = dot(d_cross_key[...], c_key[cols, :], NT)
        grad = grad + dot(d_cross_value[...], c_value[cols, :], NT)
        encoded_grad[:, cols] = grad.astype(LOW)

    tiles(width // 256, 256, source_body)
    loads[4].start()
    loads[5].start()
    loads[3].wait()

    def query_body(cols):
        d_resid[:, cols] += dot(d_query[...], w_query[cols, :], NT)

    turn(13)
    tiles(width // 256, 256, query_body)
    bucket = lax.broadcasted_iota(jnp.int32, (128, full), 0)
    ones = jnp.ones((8, full), LOW)
    below = (bucket_row[...] < bucket).astype(WIDE).astype(LOW)
    upto = (bucket_row[...] <= bucket).astype(WIDE).astype(LOW)
    first, after = dot(ones, below, NT)[0:1], dot(ones, upto, NT)[0:1]
    lane = lax.broadcasted_iota(jnp.int32, (2 * rows, 128), 0)
    table = jnp.zeros((HEADS, 128), WIDE)
    for block in range(blocks + 1):
        reach = ((sq - block) * rows + rows - 1 - lane).astype(WIDE)
        if block == blocks:
            reach = jnp.zeros((2 * rows, 128), WIDE)
        window_hot = ((reach >= first) & (reach < after)).astype(WIDE).astype(LOW)
        rest = bias_sums[:, block, :]
        for _ in range(3):
            part = rest.astype(LOW)
            rest = rest - part.astype(WIDE)
            table = table + dot(part, window_hot)
    small_out[48:64, :] = table
    small_copy(0).start()
    d_key[:rows, :] = far_sum(2)
    d_value[:rows, :] = far_sum(3)
    turn(14)
    turn(15)
    loads[4].wait()
    loads[5].wait()

    def last_body(cols):
        grad = d_resid[:, cols] + dot(d_key[...], w_key[cols, :], NT)
        grad = grad + dot(d_value[...], w_value[cols, :], NT)
        stream_grad[:, cols] = grad.astype(LOW)

    tiles(width // 256, 256, last_body)
    for index in range(4):
        if index >= 2:
            core_copy(index).wait_send()
        far_copy(index).wait_send()
    last = len(units) + 9
    for index in range(16, last):
        turn(index)
        if index % 2 == 0 and (index - 16) // 2 <= dp_size.bit_length():
            small_step((index - 16) // 2)
    for step in range((last - 15) // 2, dp_size.bit_length() + 1):
        small_step(step)
    drain()


def rear(acts, hbm_acts, sides, weights, ffn_weights, cross_probs, probs, units, dp_size):
    tokens, width = acts[0].shape
    full = sides[0].shape[0]
    rows = tokens // 3
    shape = jax.ShapeDtypeStruct
    vmem = pl.BlockSpec(memory_space=pltpu.VMEM)
    smem = pl.BlockSpec(memory_space=pltpu.SMEM)
    hbm = pl.BlockSpec(memory_space=pl.ANY)
    sem = pltpu.SemaphoreType.DMA
    blocks = full // rows
    chunk = width // dp_size
    steps = dp_size.bit_length() + 1
    return pl.pallas_call(
        functools.partial(rear_kernel, units, dp_size),
        out_shape=[
            shape((rows, width), LOW),
            shape((tokens, width), LOW),
            shape((80, 128), WIDE),
        ]
        + [shape((chunk, COLS), WIDE)] * 8
        + [shape((chunk, 4 * COLS), WIDE), shape((4 * chunk, COLS), WIDE)],
        in_specs=[vmem] * (len(acts) - 1) + [smem] + [hbm] * (len(hbm_acts) + 16),
        out_specs=[vmem] * 13,
        scratch_shapes=[
            pltpu.VMEM((tokens, width), LOW),
            pltpu.VMEM((rows, width), LOW),
            pltpu.VMEM((rows, width), LOW),
            pltpu.VMEM((tokens, width), LOW),
            pltpu.VMEM((tokens, width), LOW),
            pltpu.VMEM((tokens, width), LOW),
            pltpu.VMEM((tokens, width), LOW),
            pltpu.VMEM((HEADS, blocks + 1, 2 * rows), WIDE),
            pltpu.VMEM((steps, 80, 128), WIDE),
            pltpu.VMEM((tokens, 4 * width), LOW),
            pltpu.VMEM((tokens, 4 * width), LOW),
        ]
        + [pltpu.VMEM(w.shape, LOW) for w in weights[:3]]
        + [
            pltpu.VMEM((2, 2, full, tokens), LOW),
            pltpu.VMEM((tokens, width), LOW),
            pltpu.VMEM((tokens, width), WIDE),
            pltpu.VMEM((2, blocks, rows, width), LOW),
            pltpu.VMEM((4, 2, rows, width), LOW),
            pltpu.VMEM((4, rows, width), LOW),
            pltpu.VMEM((2, full, width), LOW),
            pltpu.VMEM((tokens, width), LOW),
            sem((8,)),
            sem((19,)),
            sem((2,)),
            sem((4,)),
            sem((4,)),
            sem((4,)),
            sem((4,)),
            sem((steps,)),
            sem((steps,)),
        ]
        + reduce_buffers(COLORS, dp_size),
        compiler_params=pltpu.CompilerParams(
            collective_id=2, has_side_effects=True, vmem_limit_bytes=63 << 20
        ),
    )(*acts, *hbm_acts, *sides, *weights, *ffn_weights, cross_probs, probs)


def finish_kernel(num, *refs):
    ins, sums = refs[:num], refs[num]
    outs, lines = refs[num + 1 : 2 * num + 1], refs[2 * num + 1 : 2 * num + 7]
    table, rms = refs[2 * num + 7 : 2 * num + 9]
    held, (in_sem, out_sem) = refs[2 * num + 9 : -2], refs[-2:]
    loads, stores = [], []
    for index, (src, mid, dst) in enumerate(zip(ins, held, outs)):
        loads.append(pltpu.make_async_copy(src, mid, in_sem.at[index]))
        stores.append(pltpu.make_async_copy(mid, dst, out_sem.at[index]))
    for load in loads:
        load.start()
    for row, line in enumerate(lines):
        line[...] = sums[8 * row : 8 * row + 8, :]
    table[...] = sums[48:64, :NBUCKET]
    totals = jnp.sum(sums[64:72, :], axis=1, keepdims=True)
    rms[...] = jnp.broadcast_to(jnp.sqrt(totals / (totals[4:5] * 1024.0)), (8, 128))
    for load, store in zip(loads, stores):
        load.wait()
        store.start()
    for store in stores:
        store.wait()


def finish(arrays, sums):
    shape = jax.ShapeDtypeStruct
    vmem = pl.BlockSpec(memory_space=pltpu.VMEM)
    hbm = pl.BlockSpec(memory_space=pl.ANY)
    num = len(arrays)
    return pl.pallas_call(
        functools.partial(finish_kernel, num),
        out_shape=[shape(array.shape, array.dtype) for array in arrays]
        + [shape((8, 128), WIDE)] * 6
        + [shape((HEADS, NBUCKET), WIDE), shape((8, 128), WIDE)],
        in_specs=[hbm] * num + [vmem],
        out_specs=[hbm] * num + [vmem] * 8,
        scratch_shapes=[pltpu.VMEM(array.shape, array.dtype) for array in arrays]
        + [pltpu.SemaphoreType.DMA((num,))] * 2,
        compiler_params=pltpu.CompilerParams(vmem_limit_bytes=60 << 20),
    )(*arrays, sums)


MESH_ID = pl.DeviceIdType.MESH


def reduce_peers(dp_size):
    dp, sq, core, ypos, core_peer, y_peer = places()
    xpos, zpos = dp % 2, dp // 2
    depth = dp_size // 2
    peers = [core_peer, y_peer, (dp + 1 - 2 * xpos, sq)]
    return peers + [((zpos + step) % depth * 2 + xpos, sq) for step in range(1, depth)]


def reducer(units, colors, ins, emit, buffers, dp_size):
    sent, core_in, first_y, first_x, second_y, second_x, third = buffers[:7]
    z_in, z_half, z_last = buffers[7:10]
    core_s, core_r, one_s, one_r, two_s, two_r, three_s, three_r = buffers[10:18]
    core_free, one_free, two_free = buffers[18:]
    dp, sq, core, ypos, core_peer, y_peer = places()
    xpos, zpos = dp % 2, dp // 2
    depth = dp_size // 2
    chunk = 1024 // dp_size
    x_peer = (dp + 1 - 2 * xpos, sq)
    count = len(units)
    remote = remote_copy
    nth = [colors[:item].count(colors[item]) for item in range(2 * count)]
    order = [item - colors[:item].count("z") for item in range(2 * count)]
    firsts = {"y": first_y, "x": first_x}
    seconds = {"y": second_y, "x": second_x}
    color_id = {"y": 0, "x": RING_ONE}
    first_peer = {"y": y_peer, "x": x_peer}
    second_peer = {"y": x_peer, "x": y_peer}

    def z_peer(step):
        return ((zpos + step) % depth * 2 + xpos, sq)

    def half_dots(unit, half, write):
        x_id, y_id, kind, part, base, tokens = units[unit]
        x_ref, y_ref = ins[x_id], ins[y_id]
        if kind == "back":
            starts = [device * 4 * chunk + part * chunk for device in range(dp_size)]
            left = jnp.concatenate([x_ref[:tokens, s : s + chunk] for s in starts], axis=1)
        else:
            left = x_ref[:tokens, base : base + 1024]
        for side in range(2):
            start = (side * 2 + half) * COLS
            if kind == "in":
                start = (side * 2 + half) * 1024 + part * COLS
            right = y_ref[:tokens, pl.ds(pl.multiple_of(start, COLS), COLS)]
            value = lax.dot_general(
                left, right, (((0,), (0,)), ((), ())), preferred_element_type=WIDE
            )
            write(0, side, value[:, :128])
            write(1, side, value[:, 128:])

    def landed(item):
        return core_in.at[item // 2 % RING, item % 2]

    def core_copy(unit):
        return remote(
            sent.at[unit % SLOTS],
            core_in.at[unit % RING],
            core_s.at[unit],
            core_r.at[unit],
            core_peer,
        )

    def one_copy(item):
        color, source = colors[item], landed(item)
        if color == "y":
            source = source.at[1 - ypos]
        else:
            source = source.reshape(2, depth, 2, chunk, 128).at[:, :, 1 - xpos]
        return remote(
            source,
            firsts[color].at[nth[item] % RING_ONE],
            one_s.at[item],
            one_r.at[item],
            first_peer[color],
        )

    def two_copy(item):
        color = colors[item]
        source = firsts[color].at[nth[item] % RING_ONE]
        if color == "y":
            source = source.reshape(depth, 2, chunk, 128).at[:, 1 - xpos]
        else:
            source = source.at[1 - ypos]
        return remote(
            source,
            seconds[color].at[nth[item] % RING_ONE],
            two_s.at[item],
            two_r.at[item],
            second_peer[color],
        )

    def three_copy(item, step):
        color = colors[item]
        return remote(
            seconds[color].at[nth[item] % RING_ONE, (zpos + step) % depth],
            third.at[order[item], step - 1],
            three_s.at[item, step - 1],
            three_r.at[item, step - 1],
            z_peer(step),
        )

    def z_copy(item, step):
        source = landed(item).reshape(2, depth, 2 * chunk, 128)
        return remote(
            source.at[:, (zpos + step) % depth],
            z_in.at[nth[item], step - 1],
            three_s.at[item, step - 1],
            three_r.at[item, step - 1],
            z_peer(step),
        )

    def zy_copy(item):
        return remote(
            z_in.at[nth[item], 0, 1 - ypos],
            z_half.at[nth[item]],
            one_s.at[item],
            one_r.at[item],
            y_peer,
        )

    def zx_copy(item):
        source = z_half.at[nth[item]].reshape(2, chunk, 128)
        return remote(
            source.at[1 - xpos], z_last.at[nth[item]], two_s.at[item], two_r.at[item], x_peer
        )

    def take(free, slot):
        pl.semaphore_wait(free.at[slot], 1)

    def allow(free, slot, peer):
        pl.semaphore_signal(free.at[slot], inc=1, device_id=peer, device_id_type=MESH_ID)

    def steps(action):
        def body(step, carry):
            action(step)
            return carry

        lax.fori_loop(1, depth, body, 0)

    def plus(left, right):
        return (left.astype(WIDE) + right.astype(WIDE)).astype(LOW)

    def products(unit):
        slot = unit % SLOTS
        if unit >= SLOTS:
            core_copy(unit - SLOTS).wait_send()

        def write(item, side, value):
            sent[slot, item, side] = value.astype(LOW)

        half_dots(unit, 1 - core, write)
        if unit >= RING:
            for item in range(2):
                take(core_free, unit % RING * 2 + item)
        core_copy(unit).start()

    def core_sum(unit):
        core_copy(unit).wait_recv()
        slot = unit % RING

        def write(item, side, value):
            old = core_in[slot, item, side].astype(WIDE)
            core_in[slot, item, side] = (value + old).astype(LOW)

        half_dots(unit, core, write)
        for item in (2 * unit, 2 * unit + 1):
            color = colors[item]
            if color == "z":
                steps(lambda step: z_copy(item, step).start())
                continue
            if nth[item] >= RING_ONE:
                take(one_free, color_id[color] + nth[item] % RING_ONE)
            one_copy(item).start()

    def core_done(item):
        if item // 2 + RING < count:
            allow(core_free, item // 2 % RING * 2 + item % 2, core_peer)

    def one_sum(item):
        color = colors[item]
        if color == "z":
            return
        one_copy(item).wait_recv()
        slot, base, own = nth[item] % RING_ONE, item // 2 % RING, item % 2
        if color == "y":

            def body(step, carry):
                rows = pl.ds(pl.multiple_of(step * 256, 256), 256)
                first_y[slot, rows, :] = plus(
                    first_y[slot, rows, :], core_in[base, own, ypos, rows, :]
                )
                return carry

            lax.fori_loop(0, 4, body, 0)
        else:

            def body(layer, carry):
                rows = pl.ds(pl.multiple_of((layer * 2 + xpos) * chunk, chunk), chunk)
                for side in range(2):
                    first_x[slot, side, layer] = plus(
                        first_x[slot, side, layer], core_in[base, own, side, rows, :]
                    )
                return carry

            lax.fori_loop(0, depth, body, 0)
        if nth[item] >= RING_ONE:
            take(two_free, color_id[color] + nth[item] % RING_ONE)
        two_copy(item).start()
        one_copy(item).wait_send()
        core_done(item)

    def z_sum(item):
        base, own = item // 2 % RING, item % 2
        rows = pl.ds(pl.multiple_of(zpos * 2 * chunk, 2 * chunk), 2 * chunk)
        steps(lambda step: z_copy(item, step).wait_recv())
        for side in range(2):

            def body(step, total):
                return total + z_in[nth[item], step - 1, side].astype(WIDE)

            mine = core_in[base, own, side, rows, :].astype(WIDE)
            z_in[nth[item], 0, side] = lax.fori_loop(1, depth, body, mine).astype(LOW)
        zy_copy(item).start()
        steps(lambda step: z_copy(item, step).wait_send())
        core_done(item)

    def two_sum(item):
        color = colors[item]
        if color == "z":
            z_sum(item)
            return
        two_copy(item).wait_recv()
        slot = nth[item] % RING_ONE
        second = seconds[color]

        def body(layer, carry):
            if color == "y":
                rows = pl.ds(pl.multiple_of((layer * 2 + xpos) * chunk, chunk), chunk)
                old = first_y[slot, rows, :]
            else:
                old = first_x[slot, ypos, layer]
            second[slot, layer] = plus(second[slot, layer], old)
            return carry

        lax.fori_loop(0, depth, body, 0)
        steps(lambda step: three_copy(item, step).start())
        two_copy(item).wait_send()
        if nth[item] + RING_ONE < colors.count(color):
            allow(one_free, color_id[color] + slot, first_peer[color])

    def last_sum(item):
        color = colors[item]
        if color == "z":
            zy_copy(item).wait_recv()
            z_half[nth[item]] = plus(z_half[nth[item]], z_in[nth[item], 0, ypos])
            zx_copy(item).start()
            zy_copy(item).wait_send()
            return
        slot = nth[item] % RING_ONE

        def body(step, total):
            three_copy(item, step).wait_recv()
            return total + third[order[item], step - 1].astype(WIDE)

        total = lax.fori_loop(1, depth, body, seconds[color][slot, zpos].astype(WIDE))
        emit(units[item // 2], item % 2, total)
        steps(lambda step: three_copy(item, step).wait_send())
        if nth[item] + RING_ONE < colors.count(color):
            allow(two_free, color_id[color] + slot, second_peer[color])

    def z_end(item):
        if colors[item] == "z":
            zx_copy(item).wait_recv()
            rows = pl.ds(pl.multiple_of(xpos * chunk, chunk), chunk)
            mine = z_half[nth[item], rows, :].astype(WIDE)
            emit(units[item // 2], item % 2, mine + z_last[nth[item]].astype(WIDE))
            zx_copy(item).wait_send()

    def turn(index):
        for stage, lag in ((products, 0), (core_sum, 1)):
            if 0 <= index - lag < count:
                stage(index - lag)
        for stage, lag in ((one_sum, 3), (two_sum, 5), (last_sum, 7), (z_end, 9)):
            for item in (2 * (index - lag), 2 * (index - lag) + 1):
                if 0 <= item < 2 * count:
                    stage(item)

    def drain():
        for unit in range(count - SLOTS, count):
            core_copy(unit).wait_send()

    return turn, drain


def reduce_buffers(colors, dp_size):
    depth, chunk = dp_size // 2, 1024 // dp_size
    count, slow = len(colors), max(colors.count("z"), 1)
    sem = pltpu.SemaphoreType.DMA
    credit = pltpu.SemaphoreType.REGULAR
    return (
        [
            pltpu.VMEM((SLOTS, 2, 2, 1024, 128), LOW),
            pltpu.VMEM((RING, 2, 2, 1024, 128), LOW),
            pltpu.VMEM((RING_ONE, 1024, 128), LOW),
            pltpu.VMEM((RING_ONE, 2, depth, chunk, 128), LOW),
            pltpu.VMEM((RING_ONE, depth, chunk, 128), LOW),
            pltpu.VMEM((RING_ONE, depth, chunk, 128), LOW),
            pltpu.VMEM((count - colors.count("z"), depth - 1, chunk, 128), LOW),
            pltpu.VMEM((slow, depth - 1, 2, 2 * chunk, 128), LOW),
            pltpu.VMEM((slow, 2 * chunk, 128), LOW),
            pltpu.VMEM((slow, chunk, 128), LOW),
        ]
        + [sem((count // 2,))] * 2
        + [sem((count,))] * 4
        + [sem((count, depth - 1))] * 2
        + [credit((2 * RING,)), credit((2 * RING_ONE,)), credit((2 * RING_ONE,))]
    )


def small_sums(small, small_in, small_s, small_r, dp_size):
    dp, sq, core, ypos, core_peer, y_peer = places()

    def copy(step):
        flip = 1 << max(step - 2, 0)
        peer = (dp + flip - 2 * flip * (dp // flip % 2), sq)
        peer = (core_peer, y_peer, peer)[min(step, 2)]
        return remote_copy(small, small_in.at[step], small_s.at[step], small_r.at[step], peer)

    def advance(step):
        copy(step).wait()
        small[...] = small[...] + small_in[step]
        if step < dp_size.bit_length():
            copy(step + 1).start()

    return copy, advance


def per_device(
    stream,
    encoded,
    cotangent,
    lengths,
    bucket_table,
    w_query,
    w_key,
    w_value,
    w_out,
    c_query,
    c_key,
    c_value,
    c_out,
    w_in,
    w_back,
    gain_one,
    shift_one,
    gain_two,
    shift_two,
    gain_three,
    shift_three,
    position_bias,
):
    num_rows, num_streams, local_len, model_width = stream.shape
    full_len = local_len * lax.axis_size("seq")
    dp_size = lax.axis_size("dp")
    chunk = model_width // dp_size
    bucket_row = bucket_table.reshape(1, full_len)
    flat_rows = stream.reshape(-1, model_width)
    source_rows = encoded.reshape(-1, model_width)
    flat_cotangent = cotangent.reshape(-1, model_width)

    def line(values):
        return values.reshape(1, model_width)

    fronts = front(
        stream.reshape(num_streams, local_len, model_width),
        source_rows,
        lengths,
        bucket_row,
        jnp.transpose(position_bias),
        (line(gain_one), line(shift_one), line(gain_two), line(shift_two)),
        (w_query, w_key, w_value, w_out, c_query, c_key, c_value, c_out),
    )
    query, own_key, own_value, main_key, main_value, context_low, unit_one, first_norm = fronts[:8]
    cross_query, cross_key, cross_value, cross_low, unit_two, second_norm = fronts[8:14]
    scales, own_probs, front_stats, probs, cross_probs = fronts[14:]
    layer_output, activated, d_ffn_out, slope, d_resid_three, mid_grads, ffn_stat = middle(
        second_norm,
        flat_cotangent,
        lengths,
        (line(gain_three), line(shift_three)),
        w_in,
        w_back,
    )
    units = []
    tokens = num_streams * local_len
    spread = activated
    if chunk % 128 != 0:
        spread = activated.reshape(-1, dp_size, 4, chunk)
        spread = jnp.transpose(spread, (0, 2, 1, 3)).reshape(activated.shape)
    for part in range(4):
        if chunk % 128 == 0:
            units.append((3, 0, "back", part, 0, tokens))
        else:
            units.append((3, 0, "parted", part, part * model_width, tokens))
    for part in range(4):
        units.append((1, 2, "in", part, 0, tokens))
    units += [(4, 5, "", 7, 0, tokens), (6, 7, "", 4, 0, tokens), (3, 8, "", 3, 0, tokens)]
    units += [(3, 9, "", 5, 2 * model_width, local_len), (3, 10, "", 6, 2 * model_width, local_len)]
    units += [(3, 11 + part, "", part, model_width, tokens) for part in range(3)]
    rears = rear(
        (
            cross_query,
            unit_one,
            query,
            own_key,
            own_value,
            own_probs,
            line(gain_one),
            d_ffn_out,
            second_norm,
            cross_low,
            first_norm,
            mid_grads,
            ffn_stat,
            front_stats,
            scales,
            line(gain_two),
            bucket_row,
            lengths,
        ),
        (slope, spread, context_low, flat_rows, source_rows, d_resid_three, unit_two),
        (cross_key, cross_value, main_key, main_value),
        (c_out, c_query, w_out, w_query, w_key, w_value, c_key, c_value),
        (w_back, w_in),
        cross_probs,
        probs,
        tuple(units),
        dp_size,
    )
    ends = finish(list(rears[:2]) + list(rears[3:]), rears[2])
    encoded_grad, stream_grad = ends[:2]
    shares, lines, table_grad = ends[2:12], ends[12:18], ends[18]
    rms = ends[19][:4, 0]
    return (
        layer_output.reshape(stream.shape),
        stream_grad.reshape(stream.shape),
        encoded_grad.reshape(encoded.shape),
        shares[0],
        shares[1],
        shares[2],
        shares[3],
        shares[4],
        shares[5],
        shares[6],
        shares[7],
        shares[8],
        shares[9],
        lines[0].reshape(model_width),
        lines[1].reshape(model_width),
        lines[2].reshape(model_width),
        lines[3].reshape(model_width),
        lines[4].reshape(model_width),
        lines[5].reshape(model_width),
        jnp.transpose(table_grad),
        rms,
    )


def solution(mesh):
    placed = (
        P("dp", None, "seq", None),
        P("dp", "seq", None),
        P("dp", None, "seq", None),
        P("dp"),
        P(),
        P(),
        P(),
        P(),
        P(),
        P(),
        P(),
        P(),
        P(),
        P(),
        P(),
        P(),
        P(),
        P(),
        P(),
        P(),
        P(),
        P(),
    )
    return jax.shard_map(
        per_device,
        mesh=mesh,
        in_specs=placed,
        out_specs=(
            P("dp", None, "seq", None),
            P("dp", None, "seq", None),
            P("dp", "seq", None),
            P("dp", "seq"),
            P("dp", "seq"),
            P("dp", "seq"),
            P("dp", "seq"),
            P("dp", "seq"),
            P("dp", "seq"),
            P("dp", "seq"),
            P("dp", "seq"),
            P("dp", "seq"),
            P("dp", "seq"),
            P(),
            P(),
            P(),
            P(),
            P(),
            P(),
            P(),
            P(),
        ),
        check_vma=False,
    )
```

```python
import functools

import jax
import jax.numpy as jnp
from jax import lax
from jax.experimental import pallas as pl
from jax.experimental.pallas import tpu as pltpu
from jax.sharding import PartitionSpec as P

HEADS = 16
HEAD_DIM = 64
NBUCKET = 32
COLS = 256
SLOTS = 2
LATER = (0, 1, 2, 3, 4, 9, 10)
RING = 6
RING_ONE = 5
COLORS = "yxyxzxyxyxzxyxzxyxyxzxyxzxyxyxyx"
epsilon = 1e-05
masked_score = -1e30


LOW = jnp.bfloat16
WIDE = jnp.float32
NN = (((1,), (0,)), ((), ()))
NT = (((1,), (1,)), ((), ()))


def dot(left, right, dims=NN):
    return lax.dot_general(left, right, dims, preferred_element_type=WIDE)


def flip(block):
    return jnp.transpose(block.astype(WIDE))


def places():
    dp, sq = lax.axis_index("dp"), lax.axis_index("seq")
    core, ypos = sq % 2, sq // 2
    return dp, sq, core, ypos, (dp, sq + 1 - 2 * core), (dp, sq + 2 - 4 * ypos)


def remote_copy(src, dst, send_sem, recv_sem, peer):
    return pltpu.make_async_remote_copy(
        src_ref=src,
        dst_ref=dst,
        send_sem=send_sem,
        recv_sem=recv_sem,
        device_id=peer,
        device_id_type=MESH_ID,
    )


def greet(peers):
    barrier = pltpu.get_barrier_semaphore()
    for peer in peers:
        pl.semaphore_signal(barrier, inc=1, device_id=peer, device_id_type=MESH_ID)
    pl.semaphore_wait(barrier, len(peers))


def tiles(count, size, body):
    def step(index, carry):
        body(pl.ds(pl.multiple_of(index * size, size), size))
        return carry

    lax.fori_loop(0, count, step, 0)


def project_to(dst, left, weight, scale=None):
    product = dot(left[...], weight[...])
    if scale is not None:
        product = product * scale
    dst[...] = product.astype(dst.dtype)


def norm_stats(rows):
    centre = jnp.mean(rows, axis=-1, keepdims=True)
    centred = rows - centre
    spread = jnp.mean(centred * centred, axis=-1, keepdims=True)
    return centred, lax.rsqrt(spread + epsilon)


def norm_backward(unit, scale, gain, incoming):
    scaled = incoming * gain
    first = jnp.mean(scaled, axis=-1, keepdims=True)
    second = jnp.mean(scaled * unit, axis=-1, keepdims=True)
    grads = scale * (scaled - first - unit * second)
    d_gain = jnp.sum(incoming * unit, axis=0, keepdims=True)
    return grads, d_gain, jnp.sum(incoming, axis=0, keepdims=True)


def valid_rows(sq, length, count):
    position = sq * count + lax.broadcasted_iota(jnp.int32, (count, 1), 0)
    return (position < length).astype(WIDE)


def sum_squares(rows, mask):
    return jnp.sum(rows * rows * mask, axis=0, keepdims=True)


def half_rows(block, side):
    row = lax.broadcasted_iota(jnp.int32, block.shape, 0)
    return jnp.where(row // HEAD_DIM == side, block, 0.0).astype(LOW)


def half_lanes(block, side):
    lane = lax.broadcasted_iota(jnp.int32, block.shape, 1)
    return jnp.where(lane // HEAD_DIM == side, block.astype(WIDE), 0.0).astype(LOW)


def front_kernel(*refs):
    stream, encoded, length_ref, bucket_row, position_bias = refs[:5]
    gain_one, shift_one, gain_two, shift_two = refs[5:9]
    hbm_weights = refs[9:17]
    outs, probs_out, cross_probs_out = refs[17:34], refs[34], refs[35]
    held, refs = refs[36:53], refs[53:]
    (query, own_key, own_value, main_key, main_value, context, unit_one, first_norm) = held[:8]
    (cross_query, cross_key, cross_value, cross_context, unit_two, second_norm) = held[8:14]
    scales, own_probs, stats = held[14:]
    weights = refs[:8]
    main_all, source_all, kept, bias, masks, branch_out, bias_table = refs[8:15]
    weight_sem, kept_sem, send_sem, recv_sem, out_sem = refs[15:]
    stores = [
        pltpu.make_async_copy(src, dst, out_sem.at[index])
        for index, (src, dst) in enumerate(zip(held, outs))
    ]
    w_query, w_key, w_value, w_out, c_query, c_key, c_value, c_out = weights
    dp, sq, core, ypos, core_peer, y_peer = places()
    length = length_ref[0]
    rows = stream.shape[1]
    full = main_all.shape[0] * rows
    loads = [
        pltpu.make_async_copy(src, dst, weight_sem.at[index])
        for index, (src, dst) in enumerate(zip(hbm_weights, weights))
    ]
    for load in loads:
        load.start()
    greet([core_peer, y_peer])
    sources = (stream.at[0], encoded)
    gathered = (main_all, source_all)
    firsts = []
    for index in range(2):
        for lane, peer in enumerate((y_peer, core_peer)):
            slot = index * 3 + lane
            firsts.append(
                remote_copy(
                    sources[index],
                    gathered[index].at[sq],
                    send_sem.at[slot],
                    recv_sem.at[slot],
                    peer,
                )
            )
    firsts[0].start()
    firsts[1].start()
    main_all[sq] = stream[0]
    source_all[sq] = encoded[...]
    bucket = lax.broadcasted_iota(jnp.int32, (NBUCKET, full), 0)
    table_hot = (bucket == bucket_row[...]).astype(WIDE).astype(LOW)
    by_distance = jnp.zeros((HEADS, full), WIDE)
    rest = position_bias[...]
    for _ in range(3):
        part = rest.astype(LOW)
        rest = rest - part.astype(WIDE)
        by_distance = by_distance + dot(part, table_hot)
    bias_table[...] = jnp.zeros_like(bias_table)
    for head in range(HEADS):
        bias_table[head, :, full:] = by_distance[head : head + 1]

    def passed_on(index):
        other = gathered[index].at[sq + 2 - 4 * ypos]
        slot = index * 3 + 2
        return remote_copy(other, other, send_sem.at[slot], recv_sem.at[slot], core_peer)

    flat = stream.reshape(3 * rows, stream.shape[2])
    loads[0].wait()
    project_to(query, flat, w_query, 0.125)
    stores[0].start()
    predicting = flat.at[rows:, :]
    loads[1].wait()
    project_to(own_key, predicting, w_key)
    loads[2].wait()
    project_to(own_value, predicting, w_value)
    key_row = lax.broadcasted_iota(jnp.int32, (full, rows), 0)
    distance = sq * rows + lax.broadcasted_iota(jnp.int32, (full, rows), 1) - key_row
    in_range = key_row < length
    masks[0] = jnp.where((distance >= 0) & in_range, 0.0, masked_score)
    masks[1] = jnp.where((distance > 0) & in_range, 0.0, masked_score)
    masks[2] = jnp.where(in_range, 0.0, masked_score)
    firsts[0].wait_recv()
    passed_on(0).start()
    firsts[2].start()
    firsts[3].start()
    stores[1].start()
    stores[2].start()
    firsts[1].wait_recv()
    passed_on(0).wait_recv()
    wide_main = main_all.reshape(full, main_all.shape[2])
    project_to(main_key, wide_main, w_key)
    project_to(main_value, wide_main, w_value)
    stores[3].start()
    stores[4].start()

    def kept_copy(pair, out):
        slot = pair % 2
        return pltpu.make_async_copy(kept.at[slot], out.at[pair], kept_sem.at[slot])

    def self_pair(pair, carry):
        @pl.when(pair >= 2)
        def _():
            kept_copy(pair - 2, probs_out).wait()

        slot = pair % 2
        cols = pl.ds(pl.multiple_of(pair * 128, 128), 128)
        keys = main_key[:, cols]
        query_t = flip(query[:, cols])
        value_t = flip(main_value[:, cols]).astype(LOW)
        own_key_t, own_value_t = flip(own_key[:, cols]), flip(own_value[:, cols])
        own_product = query_t[:, rows:] * own_key_t
        sides = []
        for side in range(2):
            head = 2 * pair + side
            span = slice(side * HEAD_DIM, (side + 1) * HEAD_DIM)
            scores = dot(keys, half_rows(query_t, side))
            own_bias = bias_table[head, :, full : full + 128][:, 0:1]
            own_score = jnp.sum(own_product[span], axis=0, keepdims=True) + own_bias
            for block in range(full // rows):
                start = pl.multiple_of((sq - block + full // rows - 1) * rows, 128)
                line = bias_table[head, :, pl.ds(start, 2 * rows)]
                wide = jnp.broadcast_to(line, (rows, 2 * rows))
                near = pltpu.roll(wide, 0, 1, stride=1, stride_axis=0)[:, rows:]
                part = slice(block * rows, (block + 1) * rows)
                for kind in range(2):
                    bias[kind, part, :] = near + masks[kind, part, :]
            owns = []
            for stream_id in range(3):
                lanes = slice(stream_id * rows, (stream_id + 1) * rows)
                score = scores[:, lanes] + bias[min(stream_id, 1)]
                top = jnp.max(score, axis=0, keepdims=True)
                if stream_id > 0:
                    own = own_score[:, (stream_id - 1) * rows : stream_id * rows]
                    top = jnp.maximum(top, own)
                expo = jnp.exp(score - top)
                total = jnp.sum(expo, axis=0, keepdims=True)
                if stream_id > 0:
                    expo_own = jnp.exp(own - top)
                    total = total + expo_own
                share = 1.0 / total
                kept[slot, side, :, lanes] = (expo * share).astype(LOW)
                owns.append(expo_own * share if stream_id > 0 else jnp.zeros_like(total))
            own_probs[head] = jnp.concatenate(owns, axis=1)
            mixed = dot(value_t[span], kept[slot, side])
            mixed_own = jnp.concatenate(owns[1:], axis=1) * own_value_t[span]
            sides.append(
                jnp.concatenate([mixed[:, :rows], mixed[:, rows:] + mixed_own], axis=1)
            )
        context[:, cols] = jnp.transpose(jnp.concatenate(sides, axis=0)).astype(LOW)
        kept_copy(pair, probs_out).start()
        return carry

    lax.fori_loop(0, HEADS // 2, self_pair, 0)
    for pair in range(HEADS // 2 - 2, HEADS // 2):
        kept_copy(pair, probs_out).wait()
    stores[5].start()
    stores[15].start()

    mask = valid_rows(sq, length, rows)
    loads[3].wait()
    project_to(branch_out, context, w_out)
    firsts[2].wait_recv()
    passed_on(1).start()
    seen = jnp.zeros((1, stream.shape[2]), WIDE)
    branch = jnp.zeros((1, stream.shape[2]), WIDE)
    for stream_id in range(3):
        part = slice(stream_id * rows, (stream_id + 1) * rows)
        source, attended = stream[stream_id].astype(WIDE), branch_out[part, :]
        seen = seen + sum_squares(source, mask)
        branch = branch + sum_squares(attended, mask)
        centred, scale = norm_stats(source + attended)
        unit = centred * scale
        unit_one[part, :] = unit.astype(LOW)
        scales[0, part, :] = jnp.broadcast_to(scale, (rows, 128))
        first_norm[part, :] = (unit * gain_one[...] + shift_one[...]).astype(LOW)
    stats[0:1, :] = seen
    stats[1:2, :] = branch
    loads[4].wait()
    project_to(cross_query, first_norm, c_query, 0.125)
    for index in (6, 7, 8):
        stores[index].start()
    firsts[3].wait_recv()
    passed_on(1).wait_recv()
    wide_source = source_all.reshape(full, source_all.shape[2])
    loads[5].wait()
    project_to(cross_key, wide_source, c_key)
    loads[6].wait()
    project_to(cross_value, wide_source, c_value)
    stores[9].start()
    stores[10].start()

    def cross_pair(pair, carry):
        @pl.when(pair >= 2)
        def _():
            kept_copy(pair - 2, cross_probs_out).wait()

        slot = pair % 2
        cols = pl.ds(pl.multiple_of(pair * 128, 128), 128)
        keys = cross_key[:, cols]
        query_t = flip(cross_query[:, cols])
        value_t = flip(cross_value[:, cols]).astype(LOW)
        sides = []
        for side in range(2):
            span = slice(side * HEAD_DIM, (side + 1) * HEAD_DIM)
            scores = dot(keys, half_rows(query_t, side))
            for stream_id in range(3):
                lanes = slice(stream_id * rows, (stream_id + 1) * rows)
                score = scores[:, lanes] + masks[2]
                expo = jnp.exp(score - jnp.max(score, axis=0, keepdims=True))
                share = 1.0 / jnp.sum(expo, axis=0, keepdims=True)
                kept[slot, side, :, lanes] = (expo * share).astype(LOW)
            sides.append(dot(value_t[span], kept[slot, side]))
        cross_context[:, cols] = jnp.transpose(jnp.concatenate(sides, axis=0)).astype(LOW)
        kept_copy(pair, cross_probs_out).start()
        return carry

    lax.fori_loop(0, HEADS // 2, cross_pair, 0)
    for pair in range(HEADS // 2 - 2, HEADS // 2):
        kept_copy(pair, cross_probs_out).wait()
    stores[11].start()
    loads[7].wait()
    project_to(branch_out, cross_context, c_out)
    branch = jnp.zeros((1, stream.shape[2]), WIDE)
    for stream_id in range(3):
        part = slice(stream_id * rows, (stream_id + 1) * rows)
        crossed = branch_out[part, :]
        branch = branch + sum_squares(crossed, mask)
        centred, scale = norm_stats(first_norm[part, :].astype(WIDE) + crossed)
        unit = centred * scale
        unit_two[part, :] = unit.astype(LOW)
        scales[1, part, :] = jnp.broadcast_to(scale, (rows, 128))
        second_norm[part, :] = (unit * gain_two[...] + shift_two[...]).astype(LOW)
    stats[2:3, :] = branch
    for index in (12, 13, 14, 16):
        stores[index].start()
    for store in stores:
        store.wait()
    for copy in firsts:
        copy.wait_send()
    for index in range(2):
        passed_on(index).wait_send()


def front(stream, encoded, length, bucket_row, position_bias, norms, weights):
    streams, rows, width = stream.shape
    seq = lax.axis_size("seq")
    full, tokens = seq * rows, streams * rows
    own = tokens - rows
    shape = jax.ShapeDtypeStruct
    pairs = HEADS // 2
    outs = [
        shape((tokens, width), LOW),
        shape((own, width), LOW),
        shape((own, width), LOW),
        shape((full, width), LOW),
        shape((full, width), LOW),
        shape((tokens, width), LOW),
        shape((tokens, width), LOW),
        shape((tokens, width), LOW),
        shape((tokens, width), LOW),
        shape((full, width), LOW),
        shape((full, width), LOW),
        shape((tokens, width), LOW),
        shape((tokens, width), LOW),
        shape((tokens, width), LOW),
        shape((2, tokens, 128), WIDE),
        shape((HEADS, 1, tokens), WIDE),
        shape((3, width), WIDE),
        shape((pairs, 2, full, tokens), LOW),
        shape((pairs, 2, full, tokens), LOW),
    ]
    vmem = pl.BlockSpec(memory_space=pltpu.VMEM)
    smem = pl.BlockSpec(memory_space=pltpu.SMEM)
    hbm = pl.BlockSpec(memory_space=pl.ANY)
    sem = pltpu.SemaphoreType.DMA
    return pl.pallas_call(
        front_kernel,
        out_shape=outs,
        in_specs=[vmem, vmem, smem] + [vmem] * 6 + [hbm] * 8,
        out_specs=[hbm] * 19,
        scratch_shapes=[pltpu.VMEM(out.shape, out.dtype) for out in outs[:17]]
        + [pltpu.VMEM(w.shape, LOW) for w in weights]
        + [
            pltpu.VMEM((seq, rows, width), LOW),
            pltpu.VMEM((seq, rows, width), LOW),
            pltpu.VMEM((2, 2, full, tokens), LOW),
            pltpu.VMEM((2, full, rows), WIDE),
            pltpu.VMEM((3, full, rows), WIDE),
            pltpu.VMEM((tokens, width), WIDE),
            pltpu.VMEM((HEADS, 1, 2 * full), WIDE),
            sem((8,)),
            sem((2,)),
            sem((6,)),
            sem((6,)),
            sem((17,)),
        ],
        compiler_params=pltpu.CompilerParams(
            collective_id=1, has_side_effects=True, vmem_limit_bytes=60 << 20
        ),
    )(stream, encoded, length, bucket_row, position_bias, *norms, *weights)


def middle_kernel(*refs):
    second_norm, cotangent, length_ref, gain_three, shift_three, hbm_in, hbm_back = refs[:7]
    outs, grads, stats = refs[7:12], refs[12], refs[13]
    output, activated, d_ffn, slope, total = refs[14:19]
    w_in, w_back, load_sem, out_sem = refs[19:]
    sq = lax.axis_index("seq")
    length = length_ref[0]
    tokens, width = second_norm.shape
    rows = tokens // 3
    hidden = w_in.shape[1]
    size = 1024
    steps = hidden // size
    stores = [
        pltpu.make_async_copy(src, dst, out_sem.at[index])
        for index, (src, dst) in enumerate(zip(refs[14:19], outs))
    ]

    def load_in(step):
        cols = pl.ds(pl.multiple_of(step * size, size), size)
        return pltpu.make_async_copy(hbm_in.at[:, cols], w_in.at[:, cols], load_sem.at[0, step])

    def load_back(step):
        cols = pl.ds(pl.multiple_of(step * size, size), size)
        return pltpu.make_async_copy(hbm_back.at[cols], w_back.at[cols], load_sem.at[1, step])

    for step in range(steps):
        load_in(step).start()
        load_back(step).start()
    total[...] = jnp.zeros_like(total)

    def forward(step, carry):
        cols = pl.ds(pl.multiple_of(step * size, size), size)
        load_in(step).wait()
        inner = dot(second_norm[...], w_in[:, cols])
        phi = 0.5 + 0.5 * lax.erf(inner * (0.5**0.5))
        bell = jnp.exp(inner * inner * -0.5) * (0.5 / jnp.pi) ** 0.5
        value = (inner * phi).astype(LOW)
        activated[:, cols] = value
        slope[:, cols] = (phi + inner * bell).astype(LOW)
        load_back(step).wait()
        total[...] += dot(value, w_back[cols, :])
        return carry

    lax.fori_loop(0, steps, forward, 0)
    stores[1].start()
    stores[3].start()
    mask = valid_rows(sq, length, rows)
    branch = jnp.zeros((1, width), WIDE)
    d_gain = jnp.zeros((1, width), WIDE)
    d_shift = jnp.zeros((1, width), WIDE)
    for stream_id in range(3):
        part = slice(stream_id * rows, (stream_id + 1) * rows)
        ffn = total[part, :]
        branch = branch + sum_squares(ffn, mask)
        resid = second_norm[part, :].astype(WIDE) + ffn
        centred, scale = norm_stats(resid)
        unit = centred * scale
        normed = unit * gain_three[...] + shift_three[...]
        output[part, :] = (normed * mask).astype(LOW)
        incoming = cotangent[part, :].astype(WIDE) * mask
        back, gain_part, shift_part = norm_backward(unit, scale, gain_three[...], incoming)
        d_gain, d_shift = d_gain + gain_part, d_shift + shift_part
        total[part, :] = back
        d_ffn[part, :] = back.astype(LOW)
    stats[...] = branch
    grads[0:1, :] = d_gain
    grads[1:2, :] = d_shift
    for index in (0, 2, 4):
        stores[index].start()
    for store in stores:
        store.wait()


def middle(second_norm, cotangent, length, norms, w_in, w_back):
    tokens, width = second_norm.shape
    hidden = w_in.shape[1]
    shape = jax.ShapeDtypeStruct
    vmem = pl.BlockSpec(memory_space=pltpu.VMEM)
    smem = pl.BlockSpec(memory_space=pltpu.SMEM)
    hbm = pl.BlockSpec(memory_space=pl.ANY)
    outs = [
        shape((tokens, width), LOW),
        shape((tokens, hidden), LOW),
        shape((tokens, width), LOW),
        shape((tokens, hidden), LOW),
        shape((tokens, width), WIDE),
    ]
    return pl.pallas_call(
        middle_kernel,
        out_shape=outs + [shape((2, width), WIDE), shape((1, width), WIDE)],
        in_specs=[vmem] * 2 + [smem] + [vmem] * 2 + [hbm] * 2,
        out_specs=[hbm] * 5 + [vmem] * 2,
        scratch_shapes=[pltpu.VMEM(out.shape, out.dtype) for out in outs]
        + [
            pltpu.VMEM(w_in.shape, LOW),
            pltpu.VMEM(w_back.shape, LOW),
            pltpu.SemaphoreType.DMA((2, hidden // 1024)),
            pltpu.SemaphoreType.DMA((5,)),
        ],
        compiler_params=pltpu.CompilerParams(vmem_limit_bytes=60 << 20),
    )(second_norm, cotangent, length, *norms, w_in, w_back)


def rear_kernel(units, dp_size, *refs):
    refs, act_held, act_sem = list(refs[: -len(LATER) - 1]), refs[-len(LATER) - 1 : -1], refs[-1]
    act_loads = []
    for index, (place, held_ref) in enumerate(zip(LATER, act_held)):
        act_loads.append(pltpu.make_async_copy(refs[place], held_ref, act_sem.at[index]))
        refs[place] = held_ref
    refs = tuple(refs)
    cross_query, unit_one, query, own_key, own_value, own_probs, gain_one = refs[:7]
    refs = (None,) + refs
    d_ffn, second_norm, cross_context, first_norm, mid_grads, ffn_stat, front_stats = refs[8:15]
    scales, gain_two, bucket_row, length_ref = refs[15:19]
    refs = refs[:15] + refs[19:]
    hbm_slope, hbm_activated, hbm_context, hbm_stream, hbm_source, hbm_resid = refs[15:21]
    hbm_unit, refs = refs[21], refs[:21] + refs[22:]
    hbm_sides, hbm_weights = refs[21:25], refs[25:33]
    hbm_ffn, refs = refs[33:35], refs[:33] + refs[35:]
    cross_probs, probs = refs[33:35]
    encoded_grad, stream_grad, small_out = refs[35:38]
    shares, in_share, back_share = refs[38:46], refs[46], refs[47]
    (d_cross_query, d_cross_key, d_cross_value, d_attended) = refs[48:52]
    (d_query, d_key, d_value, bias_sums, small_in) = refs[52:57]
    d_inner, activated = refs[57:59]
    weights = refs[59:62]
    kept, d_context, d_resid, parts, near_in, far_in, sides_held = refs[62:69]
    d_crossed, ffn_sem, refs = refs[69], refs[70], refs[:69] + refs[71:]
    weight_sem, kept_sem, core_s, core_r, far_s, far_r, small_s, small_r = refs[69:77]
    held = (0, 1, 2, 0, 1, 2, 1, 2)
    c_out, c_query, w_out, w_query, w_key, w_value, c_key, c_value = [weights[i] for i in held]
    chunk = 1024 // dp_size

    def emit(unit, item, total):
        part, cols = unit[3], slice(item * 128, (item + 1) * 128)
        if unit[2] == "in":
            in_share[:, part * COLS + item * 128 : part * COLS + (item + 1) * 128] = total
        elif unit[2] in ("back", "parted"):
            back_share[part * chunk : (part + 1) * chunk, cols] = total
        else:
            shares[part][:, cols] = total

    operands = (d_ffn, second_norm, d_inner, activated, cross_context, d_crossed, first_norm)
    operands += (d_cross_query, d_attended, d_cross_key, d_cross_value, d_query, d_key, d_value)
    turn, drain = reducer(units, COLORS, operands, emit, refs[77:], dp_size)
    small_copy, small_step = small_sums(small_out, small_in, small_s, small_r, dp_size)
    dp, sq, core, ypos, core_peer, y_peer = places()
    tokens, width = query.shape
    rows = tokens // 3
    full = sides_held.shape[1]
    blocks = full // rows
    keys_held, values_held = sides_held.at[0], sides_held.at[1]
    pairs = HEADS // 2
    loads = [
        pltpu.make_async_copy(src, weights[held[index]], weight_sem.at[index])
        for index, src in enumerate(hbm_weights)
    ]

    def load_extra(index, src, dst):
        return pltpu.make_async_copy(src, dst, weight_sem.at[12 + index])

    early = [
        load_extra(0, hbm_activated, activated),
        load_extra(1, hbm_slope, d_inner),
        load_extra(2, hbm_resid, d_resid),
        load_extra(6, hbm_unit, d_context),
    ]
    late = [
        load_extra(3, hbm_context, activated.at[:, :width]),
        load_extra(4, hbm_stream, activated.at[:, width : 2 * width]),
        load_extra(5, hbm_source, activated.at[:rows, 2 * width : 3 * width]),
    ]

    def load_side(index):
        return pltpu.make_async_copy(
            hbm_sides[index], sides_held.at[index % 2], weight_sem.at[8 + index]
        )

    def fetch(pair, source, base):
        slot = (pair + base) % 2
        return pltpu.make_async_copy(source.at[pair], kept.at[slot], kept_sem.at[slot])

    def keep_lines(base, lines):
        for row, line in enumerate(lines):
            for piece in range(8):
                at = 8 * (base + row) + piece
                small_out[at : at + 1, :] = line[:, 128 * piece : 128 * (piece + 1)]

    def ffn_load(index):
        span = pl.ds(index // 2 * width, width)
        source = hbm_ffn[0].at[span] if index % 2 == 0 else hbm_ffn[1].at[:, span]
        return pltpu.make_async_copy(source, weights[index % 3], ffn_sem.at[index])

    early[0].start()
    early[1].start()
    for index in range(3):
        ffn_load(index).start()
    early[2].start()
    early[3].start()
    fetch(0, cross_probs, 0).start()
    load_side(0).start()
    load_side(1).start()
    for load in act_loads:
        load.start()
    greet(reduce_peers(dp_size))
    early[0].wait()
    turn(0)
    turn(1)
    early[1].wait()
    early[2].wait()
    ffn_steps = hbm_ffn[0].shape[0] // width
    for step in range(ffn_steps):
        span = slice(step * width, (step + 1) * width)
        ffn_load(2 * step).wait()
        d_act = dot(d_ffn[...], weights[2 * step % 3][...], NT)
        d_inner[:, span] = (d_act * d_inner[:, span].astype(WIDE)).astype(LOW)
        ffn_load(2 * step + 1).wait()
        d_resid[...] += dot(d_inner[:, span], weights[(2 * step + 1) % 3][...], NT)
        for index in (2 * step + 3, 2 * step + 4):
            if index < 2 * ffn_steps:
                ffn_load(index).start()
        if step != 2:
            turn((2, 3, None, 4)[step])
    for index in range(3):
        loads[index].start()
    early[3].wait()
    d_gain_two = jnp.zeros((1, width), WIDE)
    d_shift_two = jnp.zeros((1, width), WIDE)
    for stream_id in range(3):
        part = slice(stream_id * rows, (stream_id + 1) * rows)
        unit, scale = d_context[part, :].astype(WIDE), scales[1, part, 0:1]
        back, gain_part, shift_part = norm_backward(unit, scale, gain_two[...], d_resid[part, :])
        d_gain_two, d_shift_two = d_gain_two + gain_part, d_shift_two + shift_part
        d_resid[part, :] = back
        d_crossed[part, :] = back.astype(LOW)
    keep_lines(2, [d_gain_two, d_shift_two])
    loads[0].wait()

    def back_to(dst, left, weight, add=False):
        def body(cols):
            product = dot(left[...], weight[cols, :], NT)
            if add:
                product = product + dst[:, cols]
            dst[:, cols] = product.astype(dst.dtype)

        tiles(width // 256, 256, body)

    back_to(d_context, d_crossed, c_out)
    loads[3].start()

    def core_copy(index):
        view = parts.at[index % 2].reshape(2, 2, rows, width)
        return remote_copy(
            view.at[:, 1 - core], near_in.at[index], core_s.at[index], core_r.at[index], core_peer
        )

    def far_copy(index):
        return remote_copy(
            near_in.at[index, 1 - ypos], far_in.at[index], far_s.at[index], far_r.at[index], y_peer
        )

    def near_sum(index):
        core_copy(index).wait_recv()
        for side in range(2):
            mine = parts[index % 2, side * 2 + core].astype(WIDE)
            near_in[index, side] = (near_in[index, side].astype(WIDE) + mine).astype(LOW)
        far_copy(index).start()

    def far_sum(index):
        far_copy(index).wait_recv()
        return (near_in[index, ypos].astype(WIDE) + far_in[index].astype(WIDE)).astype(LOW)

    def store_part(index, cols, block):
        for part in range(full // rows):
            parts[index % 2, part, :, cols] = block[part * rows : (part + 1) * rows].astype(LOW)

    def cross_pair(pair, carry):
        fetch(pair, cross_probs, 0).wait()

        @pl.when(pair + 1 < pairs)
        def _():
            fetch(pair + 1, cross_probs, 0).start()

        slot = pair % 2
        cols = pl.ds(pl.multiple_of(pair * 128, 128), 128)
        values = values_held[:, cols]
        key_t = flip(keys_held[:, cols]).astype(LOW)
        queries, d_ctx = cross_query[:, cols], d_context[:, cols]
        d_ctx_t = flip(d_ctx)
        d_query_t, d_scores = [], []
        for side in range(2):
            span = slice(side * HEAD_DIM, (side + 1) * HEAD_DIM)
            d_prob = dot(values, half_rows(d_ctx_t, side))
            prob = kept[slot, side].astype(WIDE)
            delta = jnp.sum(prob * d_prob, axis=0, keepdims=True)
            d_score = (prob * (d_prob - delta)).astype(LOW)
            d_query_t.append(dot(key_t[span], d_score))
            d_scores.append(d_score)
        d_cross_query[:, cols] = (
            jnp.transpose(jnp.concatenate(d_query_t, axis=0)) * 0.125
        ).astype(LOW)
        both = jnp.concatenate(d_scores, axis=1)
        split = jnp.concatenate([half_lanes(queries, 0), half_lanes(queries, 1)], axis=0)
        store_part(0, cols, dot(both, split))
        both = jnp.concatenate([kept[slot, 0], kept[slot, 1]], axis=1)
        split = jnp.concatenate([half_lanes(d_ctx, 0), half_lanes(d_ctx, 1)], axis=0)
        store_part(1, cols, dot(both, split))
        return carry

    load_side(0).wait()
    load_side(1).wait()
    for load in act_loads:
        load.wait()
    lax.fori_loop(0, pairs // 2, cross_pair, 0)
    turn(5)
    lax.fori_loop(pairs // 2, pairs, cross_pair, 0)
    fetch(0, probs, 0).start()
    load_side(2).start()
    load_side(3).start()
    core_copy(0).start()
    core_copy(1).start()
    turn(6)
    loads[1].wait()
    back_to(d_resid, d_cross_query, c_query, True)
    loads[6].start()
    d_gain = jnp.zeros((1, width), WIDE)
    d_shift = jnp.zeros((1, width), WIDE)
    for stream_id in range(3):
        part = slice(stream_id * rows, (stream_id + 1) * rows)
        unit, scale = unit_one[part, :].astype(WIDE), scales[0, part, 0:1]
        back, gain_part, shift_part = norm_backward(
            unit, scale, gain_one[...], d_resid[part, :]
        )
        d_gain, d_shift = d_gain + gain_part, d_shift + shift_part
        d_resid[part, :] = back
        d_attended[part, :] = back.astype(LOW)
    keep_lines(0, [d_gain, d_shift])
    keep_lines(4, [mid_grads[row : row + 1, :] for row in range(2)])
    for row, line in enumerate([front_stats[row : row + 1, :] for row in range(3)] + [ffn_stat[...]]):
        folded = line[:, :128]
        for piece in range(1, 8):
            folded = folded + line[:, 128 * piece : 128 * (piece + 1)]
        small_out[64 + row : 65 + row, :] = folded
    mask = valid_rows(sq, length_ref[0], rows)
    count = jnp.sum(jnp.broadcast_to(mask, (rows, 128)), axis=0, keepdims=True)
    small_out[68:69, :] = count * (3.0 / 128.0)
    small_out[69:80, :] = jnp.zeros((11, 128), WIDE)
    near_sum(0)
    near_sum(1)
    turn(7)
    loads[2].wait()
    back_to(d_context, d_attended, w_out)
    loads[7].start()
    core_copy(0).wait_send()
    core_copy(1).wait_send()
    line = lax.broadcasted_iota(jnp.int32, (rows, rows), 0)
    turned = (line + lax.broadcasted_iota(jnp.int32, (rows, rows), 1) == rows - 1).astype(LOW)

    def self_pair(pair, carry):
        fetch(pair, probs, 0).wait()

        @pl.when(pair + 1 < pairs)
        def _():
            fetch(pair + 1, probs, 0).start()

        slot = pair % 2
        cols = pl.ds(pl.multiple_of(pair * 128, 128), 128)
        values = values_held[:, cols]
        key_t = flip(keys_held[:, cols]).astype(LOW)
        queries, d_ctx = query[:, cols], d_context[:, cols]
        d_ctx_t, query_t = flip(d_ctx), flip(queries)
        own_key_t, own_value_t = flip(own_key[:, cols]), flip(own_value[:, cols])
        own_product = d_ctx_t[:, rows:] * own_value_t
        d_query_t, d_scores, d_own_key, d_own_value = [], [], [], []
        for side in range(2):
            head = 2 * pair + side
            span = slice(side * HEAD_DIM, (side + 1) * HEAD_DIM)
            d_prob = dot(values, half_rows(d_ctx_t, side))
            prob = kept[slot, side].astype(WIDE)
            prob_own = own_probs[head][:, rows:]
            d_prob_own = jnp.sum(own_product[span], axis=0, keepdims=True)
            delta = jnp.sum(prob * d_prob, axis=0, keepdims=True)
            delta = jnp.concatenate(
                [delta[:, :rows], delta[:, rows:] + prob_own * d_prob_own], axis=1
            )
            d_score = (prob * (d_prob - delta)).astype(LOW)
            d_own = (prob_own * (d_prob_own - delta[:, rows:])).astype(LOW).astype(WIDE)
            bias_sums[head, blocks : blocks + 1, :] = d_own
            mixed = dot(key_t[span], d_score)
            d_query_t.append(
                jnp.concatenate(
                    [mixed[:, :rows], mixed[:, rows:] + d_own * own_key_t[span]], axis=1
                )
            )
            d_scores.append(d_score)
            d_own_key.append(d_own * query_t[span, rows:])
            d_own_value.append(prob_own * d_ctx_t[span, rows:])
            wide = d_score.astype(WIDE)
            summed = wide[:, :rows] + wide[:, rows : 2 * rows] + wide[:, 2 * rows :]
            mirrored = dot(summed.astype(LOW), turned)
            for block in range(full // rows):
                piece = mirrored[block * rows : (block + 1) * rows]
                piece = jnp.concatenate([piece, jnp.zeros_like(piece)], axis=1)
                aligned = pltpu.roll(piece, 0, 1, stride=1, stride_axis=0)
                bias_sums[head, block : block + 1, :] = jnp.sum(aligned, axis=0, keepdims=True)
        d_query[:, cols] = (jnp.transpose(jnp.concatenate(d_query_t, axis=0)) * 0.125).astype(LOW)
        d_key[rows:, cols] = jnp.transpose(jnp.concatenate(d_own_key, axis=0)).astype(LOW)
        d_value[rows:, cols] = jnp.transpose(jnp.concatenate(d_own_value, axis=0)).astype(LOW)
        both = jnp.concatenate(d_scores, axis=1)
        split = jnp.concatenate([half_lanes(queries, 0), half_lanes(queries, 1)], axis=0)
        store_part(2, cols, dot(both, split))
        both = jnp.concatenate([kept[slot, 0], kept[slot, 1]], axis=1)
        split = jnp.concatenate([half_lanes(d_ctx, 0), half_lanes(d_ctx, 1)], axis=0)
        store_part(3, cols, dot(both, split))
        return carry

    load_side(2).wait()
    load_side(3).wait()
    quarter = pairs // 4
    lax.fori_loop(0, quarter, self_pair, 0)
    turn(8)
    for load in late:
        load.start()
    lax.fori_loop(quarter, 2 * quarter, self_pair, 0)
    turn(9)
    lax.fori_loop(2 * quarter, 3 * quarter, self_pair, 0)
    for load in late:
        load.wait()
    turn(10)
    lax.fori_loop(3 * quarter, pairs, self_pair, 0)
    core_copy(2).start()
    core_copy(3).start()
    d_cross_key[...] = far_sum(0)
    d_cross_value[...] = far_sum(1)
    turn(11)
    near_sum(2)
    near_sum(3)
    turn(12)
    loads[6].wait()
    loads[7].wait()

    def source_body(cols):
        grad = dot(d_cross_key[...], c_key[cols, :], NT)
        grad = grad + dot(d_cross_value[...], c_value[cols, :], NT)
        encoded_grad[:, cols] = grad.astype(LOW)

    tiles(width // 256, 256, source_body)
    loads[4].start()
    loads[5].start()
    loads[3].wait()

    def query_body(cols):
        d_resid[:, cols] += dot(d_query[...], w_query[cols, :], NT)

    turn(13)
    tiles(width // 256, 256, query_body)
    bucket = lax.broadcasted_iota(jnp.int32, (128, full), 0)
    ones = jnp.ones((8, full), LOW)
    below = (bucket_row[...] < bucket).astype(WIDE).astype(LOW)
    upto = (bucket_row[...] <= bucket).astype(WIDE).astype(LOW)
    first, after = dot(ones, below, NT)[0:1], dot(ones, upto, NT)[0:1]
    lane = lax.broadcasted_iota(jnp.int32, (2 * rows, 128), 0)
    table = jnp.zeros((HEADS, 128), WIDE)
    for block in range(blocks + 1):
        reach = ((sq - block) * rows + rows - 1 - lane).astype(WIDE)
        if block == blocks:
            reach = jnp.zeros((2 * rows, 128), WIDE)
        window_hot = ((reach >= first) & (reach < after)).astype(WIDE).astype(LOW)
        rest = bias_sums[:, block, :]
        for _ in range(3):
            part = rest.astype(LOW)
            rest = rest - part.astype(WIDE)
            table = table + dot(part, window_hot)
    small_out[48:64, :] = table
    small_copy(0).start()
    d_key[:rows, :] = far_sum(2)
    d_value[:rows, :] = far_sum(3)
    turn(14)
    turn(15)
    loads[4].wait()
    loads[5].wait()

    def last_body(cols):
        grad = d_resid[:, cols] + dot(d_key[...], w_key[cols, :], NT)
        grad = grad + dot(d_value[...], w_value[cols, :], NT)
        stream_grad[:, cols] = grad.astype(LOW)

    tiles(width // 256, 256, last_body)
    for index in range(4):
        if index >= 2:
            core_copy(index).wait_send()
        far_copy(index).wait_send()
    last = len(units) + 9
    for index in range(16, last):
        turn(index)
        if index % 2 == 0 and (index - 16) // 2 <= dp_size.bit_length():
            small_step((index - 16) // 2)
    for step in range((last - 15) // 2, dp_size.bit_length() + 1):
        small_step(step)
    drain()


def rear(acts, hbm_acts, sides, weights, ffn_weights, cross_probs, probs, units, dp_size):
    tokens, width = acts[0].shape
    full = sides[0].shape[0]
    rows = tokens // 3
    shape = jax.ShapeDtypeStruct
    vmem = pl.BlockSpec(memory_space=pltpu.VMEM)
    smem = pl.BlockSpec(memory_space=pltpu.SMEM)
    hbm = pl.BlockSpec(memory_space=pl.ANY)
    sem = pltpu.SemaphoreType.DMA
    blocks = full // rows
    chunk = width // dp_size
    steps = dp_size.bit_length() + 1
    return pl.pallas_call(
        functools.partial(rear_kernel, units, dp_size),
        out_shape=[
            shape((rows, width), LOW),
            shape((tokens, width), LOW),
            shape((80, 128), WIDE),
        ]
        + [shape((chunk, COLS), WIDE)] * 8
        + [shape((chunk, 4 * COLS), WIDE), shape((4 * chunk, COLS), WIDE)],
        in_specs=[hbm if place in LATER else vmem for place in range(len(acts) - 1)] + [smem] + [hbm] * (len(hbm_acts) + 16),
        out_specs=[vmem] * 13,
        scratch_shapes=[
            pltpu.VMEM((tokens, width), LOW),
            pltpu.VMEM((rows, width), LOW),
            pltpu.VMEM((rows, width), LOW),
            pltpu.VMEM((tokens, width), LOW),
            pltpu.VMEM((tokens, width), LOW),
            pltpu.VMEM((tokens, width), LOW),
            pltpu.VMEM((tokens, width), LOW),
            pltpu.VMEM((HEADS, blocks + 1, 2 * rows), WIDE),
            pltpu.VMEM((steps, 80, 128), WIDE),
            pltpu.VMEM((tokens, 4 * width), LOW),
            pltpu.VMEM((tokens, 4 * width), LOW),
        ]
        + [pltpu.VMEM(w.shape, LOW) for w in weights[:3]]
        + [
            pltpu.VMEM((2, 2, full, tokens), LOW),
            pltpu.VMEM((tokens, width), LOW),
            pltpu.VMEM((tokens, width), WIDE),
            pltpu.VMEM((2, blocks, rows, width), LOW),
            pltpu.VMEM((4, 2, rows, width), LOW),
            pltpu.VMEM((4, rows, width), LOW),
            pltpu.VMEM((2, full, width), LOW),
            pltpu.VMEM((tokens, width), LOW),
            sem((8,)),
            sem((19,)),
            sem((2,)),
            sem((4,)),
            sem((4,)),
            sem((4,)),
            sem((4,)),
            sem((steps,)),
            sem((steps,)),
        ]
        + reduce_buffers(COLORS, dp_size)
        + [pltpu.VMEM(acts[place].shape, LOW) for place in LATER]
        + [sem((len(LATER),))],
        compiler_params=pltpu.CompilerParams(
            collective_id=2, has_side_effects=True, vmem_limit_bytes=63 << 20
        ),
    )(*acts, *hbm_acts, *sides, *weights, *ffn_weights, cross_probs, probs)


def finish_kernel(num, *refs):
    ins, sums = refs[:num], refs[num]
    outs, lines = refs[num + 1 : 2 * num + 1], refs[2 * num + 1 : 2 * num + 7]
    table, rms = refs[2 * num + 7 : 2 * num + 9]
    held, (in_sem, out_sem) = refs[2 * num + 9 : -2], refs[-2:]
    loads, stores = [], []
    for index, (src, mid, dst) in enumerate(zip(ins, held, outs)):
        loads.append(pltpu.make_async_copy(src, mid, in_sem.at[index]))
        stores.append(pltpu.make_async_copy(mid, dst, out_sem.at[index]))
    for load in loads:
        load.start()
    for row, line in enumerate(lines):
        line[...] = sums[8 * row : 8 * row + 8, :]
    table[...] = sums[48:64, :NBUCKET]
    totals = jnp.sum(sums[64:72, :], axis=1, keepdims=True)
    rms[...] = jnp.broadcast_to(jnp.sqrt(totals / (totals[4:5] * 1024.0)), (8, 128))
    for load, store in zip(loads, stores):
        load.wait()
        store.start()
    for store in stores:
        store.wait()


def finish(arrays, sums):
    shape = jax.ShapeDtypeStruct
    vmem = pl.BlockSpec(memory_space=pltpu.VMEM)
    hbm = pl.BlockSpec(memory_space=pl.ANY)
    num = len(arrays)
    return pl.pallas_call(
        functools.partial(finish_kernel, num),
        out_shape=[shape(array.shape, array.dtype) for array in arrays]
        + [shape((8, 128), WIDE)] * 6
        + [shape((HEADS, NBUCKET), WIDE), shape((8, 128), WIDE)],
        in_specs=[hbm] * num + [vmem],
        out_specs=[hbm] * num + [vmem] * 8,
        scratch_shapes=[pltpu.VMEM(array.shape, array.dtype) for array in arrays]
        + [pltpu.SemaphoreType.DMA((num,))] * 2,
        compiler_params=pltpu.CompilerParams(vmem_limit_bytes=60 << 20),
    )(*arrays, sums)


MESH_ID = pl.DeviceIdType.MESH


def reduce_peers(dp_size):
    dp, sq, core, ypos, core_peer, y_peer = places()
    xpos, zpos = dp % 2, dp // 2
    depth = dp_size // 2
    peers = [core_peer, y_peer, (dp + 1 - 2 * xpos, sq)]
    return peers + [((zpos + step) % depth * 2 + xpos, sq) for step in range(1, depth)]


def reducer(units, colors, ins, emit, buffers, dp_size):
    sent, core_in, first_y, first_x, second_y, second_x, third = buffers[:7]
    z_in, z_half, z_last = buffers[7:10]
    core_s, core_r, one_s, one_r, two_s, two_r, three_s, three_r = buffers[10:18]
    core_free, one_free, two_free = buffers[18:]
    dp, sq, core, ypos, core_peer, y_peer = places()
    xpos, zpos = dp % 2, dp // 2
    depth = dp_size // 2
    chunk = 1024 // dp_size
    x_peer = (dp + 1 - 2 * xpos, sq)
    count = len(units)
    remote = remote_copy
    nth = [colors[:item].count(colors[item]) for item in range(2 * count)]
    order = [item - colors[:item].count("z") for item in range(2 * count)]
    firsts = {"y": first_y, "x": first_x}
    seconds = {"y": second_y, "x": second_x}
    color_id = {"y": 0, "x": RING_ONE}
    first_peer = {"y": y_peer, "x": x_peer}
    second_peer = {"y": x_peer, "x": y_peer}

    def z_peer(step):
        return ((zpos + step) % depth * 2 + xpos, sq)

    def half_dots(unit, half, write):
        x_id, y_id, kind, part, base, tokens = units[unit]
        x_ref, y_ref = ins[x_id], ins[y_id]
        if kind == "back":
            starts = [device * 4 * chunk + part * chunk for device in range(dp_size)]
            left = jnp.concatenate([x_ref[:tokens, s : s + chunk] for s in starts], axis=1)
        else:
            left = x_ref[:tokens, base : base + 1024]
        for side in range(2):
            start = (side * 2 + half) * COLS
            if kind == "in":
                start = (side * 2 + half) * 1024 + part * COLS
            right = y_ref[:tokens, pl.ds(pl.multiple_of(start, COLS), COLS)]
            value = lax.dot_general(
                left, right, (((0,), (0,)), ((), ())), preferred_element_type=WIDE
            )
            write(0, side, value[:, :128])
            write(1, side, value[:, 128:])

    def landed(item):
        return core_in.at[item // 2 % RING, item % 2]

    def core_copy(unit):
        return remote(
            sent.at[unit % SLOTS],
            core_in.at[unit % RING],
            core_s.at[unit],
            core_r.at[unit],
            core_peer,
        )

    def one_copy(item):
        color, source = colors[item], landed(item)
        if color == "y":
            source = source.at[1 - ypos]
        else:
            source = source.reshape(2, depth, 2, chunk, 128).at[:, :, 1 - xpos]
        return remote(
            source,
            firsts[color].at[nth[item] % RING_ONE],
            one_s.at[item],
            one_r.at[item],
            first_peer[color],
        )

    def two_copy(item):
        color = colors[item]
        source = firsts[color].at[nth[item] % RING_ONE]
        if color == "y":
            source = source.reshape(depth, 2, chunk, 128).at[:, 1 - xpos]
        else:
            source = source.at[1 - ypos]
        return remote(
            source,
            seconds[color].at[nth[item] % RING_ONE],
            two_s.at[item],
            two_r.at[item],
            second_peer[color],
        )

    def three_copy(item, step):
        color = colors[item]
        return remote(
            seconds[color].at[nth[item] % RING_ONE, (zpos + step) % depth],
            third.at[order[item], step - 1],
            three_s.at[item, step - 1],
            three_r.at[item, step - 1],
            z_peer(step),
        )

    def z_copy(item, step):
        source = landed(item).reshape(2, depth, 2 * chunk, 128)
        return remote(
            source.at[:, (zpos + step) % depth],
            z_in.at[nth[item], step - 1],
            three_s.at[item, step - 1],
            three_r.at[item, step - 1],
            z_peer(step),
        )

    def zy_copy(item):
        return remote(
            z_in.at[nth[item], 0, 1 - ypos],
            z_half.at[nth[item]],
            one_s.at[item],
            one_r.at[item],
            y_peer,
        )

    def zx_copy(item):
        source = z_half.at[nth[item]].reshape(2, chunk, 128)
        return remote(
            source.at[1 - xpos], z_last.at[nth[item]], two_s.at[item], two_r.at[item], x_peer
        )

    def take(free, slot):
        pl.semaphore_wait(free.at[slot], 1)

    def allow(free, slot, peer):
        pl.semaphore_signal(free.at[slot], inc=1, device_id=peer, device_id_type=MESH_ID)

    def steps(action):
        def body(step, carry):
            action(step)
            return carry

        lax.fori_loop(1, depth, body, 0)

    def plus(left, right):
        return (left.astype(WIDE) + right.astype(WIDE)).astype(LOW)

    def products(unit):
        slot = unit % SLOTS
        if unit >= SLOTS:
            core_copy(unit - SLOTS).wait_send()

        def write(item, side, value):
            sent[slot, item, side] = value.astype(LOW)

        half_dots(unit, 1 - core, write)
        if unit >= RING:
            for item in range(2):
                take(core_free, unit % RING * 2 + item)
        core_copy(unit).start()

    def core_sum(unit):
        core_copy(unit).wait_recv()
        slot = unit % RING

        def write(item, side, value):
            old = core_in[slot, item, side].astype(WIDE)
            core_in[slot, item, side] = (value + old).astype(LOW)

        half_dots(unit, core, write)
        for item in (2 * unit, 2 * unit + 1):
            color = colors[item]
            if color == "z":
                steps(lambda step: z_copy(item, step).start())
                continue
            if nth[item] >= RING_ONE:
                take(one_free, color_id[color] + nth[item] % RING_ONE)
            one_copy(item).start()

    def core_done(item):
        if item // 2 + RING < count:
            allow(core_free, item // 2 % RING * 2 + item % 2, core_peer)

    def one_sum(item):
        color = colors[item]
        if color == "z":
            return
        one_copy(item).wait_recv()
        slot, base, own = nth[item] % RING_ONE, item // 2 % RING, item % 2
        if color == "y":

            def body(step, carry):
                rows = pl.ds(pl.multiple_of(step * 256, 256), 256)
                first_y[slot, rows, :] = plus(
                    first_y[slot, rows, :], core_in[base, own, ypos, rows, :]
                )
                return carry

            lax.fori_loop(0, 4, body, 0)
        else:

            def body(layer, carry):
                rows = pl.ds(pl.multiple_of((layer * 2 + xpos) * chunk, chunk), chunk)
                for side in range(2):
                    first_x[slot, side, layer] = plus(
                        first_x[slot, side, layer], core_in[base, own, side, rows, :]
                    )
                return carry

            lax.fori_loop(0, depth, body, 0)
        if nth[item] >= RING_ONE:
            take(two_free, color_id[color] + nth[item] % RING_ONE)
        two_copy(item).start()
        one_copy(item).wait_send()
        core_done(item)

    def z_sum(item):
        base, own = item // 2 % RING, item % 2
        rows = pl.ds(pl.multiple_of(zpos * 2 * chunk, 2 * chunk), 2 * chunk)
        steps(lambda step: z_copy(item, step).wait_recv())
        for side in range(2):

            def body(step, total):
                return total + z_in[nth[item], step - 1, side].astype(WIDE)

            mine = core_in[base, own, side, rows, :].astype(WIDE)
            z_in[nth[item], 0, side] = lax.fori_loop(1, depth, body, mine).astype(LOW)
        zy_copy(item).start()
        steps(lambda step: z_copy(item, step).wait_send())
        core_done(item)

    def two_sum(item):
        color = colors[item]
        if color == "z":
            z_sum(item)
            return
        two_copy(item).wait_recv()
        slot = nth[item] % RING_ONE
        second = seconds[color]

        def body(layer, carry):
            if color == "y":
                rows = pl.ds(pl.multiple_of((layer * 2 + xpos) * chunk, chunk), chunk)
                old = first_y[slot, rows, :]
            else:
                old = first_x[slot, ypos, layer]
            second[slot, layer] = plus(second[slot, layer], old)
            return carry

        lax.fori_loop(0, depth, body, 0)
        steps(lambda step: three_copy(item, step).start())
        two_copy(item).wait_send()
        if nth[item] + RING_ONE < colors.count(color):
            allow(one_free, color_id[color] + slot, first_peer[color])

    def last_sum(item):
        color = colors[item]
        if color == "z":
            zy_copy(item).wait_recv()
            z_half[nth[item]] = plus(z_half[nth[item]], z_in[nth[item], 0, ypos])
            zx_copy(item).start()
            zy_copy(item).wait_send()
            return
        slot = nth[item] % RING_ONE

        def body(step, total):
            three_copy(item, step).wait_recv()
            return total + third[order[item], step - 1].astype(WIDE)

        total = lax.fori_loop(1, depth, body, seconds[color][slot, zpos].astype(WIDE))
        emit(units[item // 2], item % 2, total)
        steps(lambda step: three_copy(item, step).wait_send())
        if nth[item] + RING_ONE < colors.count(color):
            allow(two_free, color_id[color] + slot, second_peer[color])

    def z_end(item):
        if colors[item] == "z":
            zx_copy(item).wait_recv()
            rows = pl.ds(pl.multiple_of(xpos * chunk, chunk), chunk)
            mine = z_half[nth[item], rows, :].astype(WIDE)
            emit(units[item // 2], item % 2, mine + z_last[nth[item]].astype(WIDE))
            zx_copy(item).wait_send()

    def turn(index):
        for stage, lag in ((core_sum, 1), (products, 0)):
            if 0 <= index - lag < count:
                stage(index - lag)
        for stage, lag in ((one_sum, 3), (two_sum, 5), (last_sum, 7), (z_end, 9)):
            for item in (2 * (index - lag), 2 * (index - lag) + 1):
                if 0 <= item < 2 * count:
                    stage(item)

    def drain():
        for unit in range(count - SLOTS, count):
            core_copy(unit).wait_send()

    return turn, drain


def reduce_buffers(colors, dp_size):
    depth, chunk = dp_size // 2, 1024 // dp_size
    count, slow = len(colors), max(colors.count("z"), 1)
    sem = pltpu.SemaphoreType.DMA
    credit = pltpu.SemaphoreType.REGULAR
    return (
        [
            pltpu.VMEM((SLOTS, 2, 2, 1024, 128), LOW),
            pltpu.VMEM((RING, 2, 2, 1024, 128), LOW),
            pltpu.VMEM((RING_ONE, 1024, 128), LOW),
            pltpu.VMEM((RING_ONE, 2, depth, chunk, 128), LOW),
            pltpu.VMEM((RING_ONE, depth, chunk, 128), LOW),
            pltpu.VMEM((RING_ONE, depth, chunk, 128), LOW),
            pltpu.VMEM((count - colors.count("z"), depth - 1, chunk, 128), LOW),
            pltpu.VMEM((slow, depth - 1, 2, 2 * chunk, 128), LOW),
            pltpu.VMEM((slow, 2 * chunk, 128), LOW),
            pltpu.VMEM((slow, chunk, 128), LOW),
        ]
        + [sem((count // 2,))] * 2
        + [sem((count,))] * 4
        + [sem((count, depth - 1))] * 2
        + [credit((2 * RING,)), credit((2 * RING_ONE,)), credit((2 * RING_ONE,))]
    )


def small_sums(small, small_in, small_s, small_r, dp_size):
    dp, sq, core, ypos, core_peer, y_peer = places()

    def copy(step):
        flip = 1 << max(step - 2, 0)
        peer = (dp + flip - 2 * flip * (dp // flip % 2), sq)
        peer = (core_peer, y_peer, peer)[min(step, 2)]
        return remote_copy(small, small_in.at[step], small_s.at[step], small_r.at[step], peer)

    def advance(step):
        copy(step).wait()
        small[...] = small[...] + small_in[step]
        if step < dp_size.bit_length():
            copy(step + 1).start()

    return copy, advance


def per_device(
    stream,
    encoded,
    cotangent,
    lengths,
    bucket_table,
    w_query,
    w_key,
    w_value,
    w_out,
    c_query,
    c_key,
    c_value,
    c_out,
    w_in,
    w_back,
    gain_one,
    shift_one,
    gain_two,
    shift_two,
    gain_three,
    shift_three,
    position_bias,
):
    num_rows, num_streams, local_len, model_width = stream.shape
    full_len = local_len * lax.axis_size("seq")
    dp_size = lax.axis_size("dp")
    chunk = model_width // dp_size
    bucket_row = bucket_table.reshape(1, full_len)
    flat_rows = stream.reshape(-1, model_width)
    source_rows = encoded.reshape(-1, model_width)
    flat_cotangent = cotangent.reshape(-1, model_width)

    def line(values):
        return values.reshape(1, model_width)

    fronts = front(
        stream.reshape(num_streams, local_len, model_width),
        source_rows,
        lengths,
        bucket_row,
        jnp.transpose(position_bias),
        (line(gain_one), line(shift_one), line(gain_two), line(shift_two)),
        (w_query, w_key, w_value, w_out, c_query, c_key, c_value, c_out),
    )
    query, own_key, own_value, main_key, main_value, context_low, unit_one, first_norm = fronts[:8]
    cross_query, cross_key, cross_value, cross_low, unit_two, second_norm = fronts[8:14]
    scales, own_probs, front_stats, probs, cross_probs = fronts[14:]
    layer_output, activated, d_ffn_out, slope, d_resid_three, mid_grads, ffn_stat = middle(
        second_norm,
        flat_cotangent,
        lengths,
        (line(gain_three), line(shift_three)),
        w_in,
        w_back,
    )
    units = []
    tokens = num_streams * local_len
    spread = activated
    if chunk % 128 != 0:
        spread = activated.reshape(-1, dp_size, 4, chunk)
        spread = jnp.transpose(spread, (0, 2, 1, 3)).reshape(activated.shape)
    for part in range(4):
        if chunk % 128 == 0:
            units.append((3, 0, "back", part, 0, tokens))
        else:
            units.append((3, 0, "parted", part, part * model_width, tokens))
    for part in range(4):
        units.append((1, 2, "in", part, 0, tokens))
    units += [(4, 5, "", 7, 0, tokens), (6, 7, "", 4, 0, tokens), (3, 8, "", 3, 0, tokens)]
    units += [(3, 9, "", 5, 2 * model_width, local_len), (3, 10, "", 6, 2 * model_width, local_len)]
    units += [(3, 11 + part, "", part, model_width, tokens) for part in range(3)]
    rears = rear(
        (
            cross_query,
            unit_one,
            query,
            own_key,
            own_value,
            own_probs,
            line(gain_one),
            d_ffn_out,
            second_norm,
            cross_low,
            first_norm,
            mid_grads,
            ffn_stat,
            front_stats,
            scales,
            line(gain_two),
            bucket_row,
            lengths,
        ),
        (slope, spread, context_low, flat_rows, source_rows, d_resid_three, unit_two),
        (cross_key, cross_value, main_key, main_value),
        (c_out, c_query, w_out, w_query, w_key, w_value, c_key, c_value),
        (w_back, w_in),
        cross_probs,
        probs,
        tuple(units),
        dp_size,
    )
    ends = finish(list(rears[:2]) + list(rears[3:]), rears[2])
    encoded_grad, stream_grad = ends[:2]
    shares, lines, table_grad = ends[2:12], ends[12:18], ends[18]
    rms = ends[19][:4, 0]
    return (
        layer_output.reshape(stream.shape),
        stream_grad.reshape(stream.shape),
        encoded_grad.reshape(encoded.shape),
        shares[0],
        shares[1],
        shares[2],
        shares[3],
        shares[4],
        shares[5],
        shares[6],
        shares[7],
        shares[8],
        shares[9],
        lines[0].reshape(model_width),
        lines[1].reshape(model_width),
        lines[2].reshape(model_width),
        lines[3].reshape(model_width),
        lines[4].reshape(model_width),
        lines[5].reshape(model_width),
        jnp.transpose(table_grad),
        rms,
    )


def solution(mesh):
    placed = (
        P("dp", None, "seq", None),
        P("dp", "seq", None),
        P("dp", None, "seq", None),
        P("dp"),
        P(),
        P(),
        P(),
        P(),
        P(),
        P(),
        P(),
        P(),
        P(),
        P(),
        P(),
        P(),
        P(),
        P(),
        P(),
        P(),
        P(),
        P(),
    )
    return jax.shard_map(
        per_device,
        mesh=mesh,
        in_specs=placed,
        out_specs=(
            P("dp", None, "seq", None),
            P("dp", None, "seq", None),
            P("dp", "seq", None),
            P("dp", "seq"),
            P("dp", "seq"),
            P("dp", "seq"),
            P("dp", "seq"),
            P("dp", "seq"),
            P("dp", "seq"),
            P("dp", "seq"),
            P("dp", "seq"),
            P("dp", "seq"),
            P("dp", "seq"),
            P(),
            P(),
            P(),
            P(),
            P(),
            P(),
            P(),
            P(),
        ),
        check_vma=False,
    )
```
